32 devices in a mesh: groups: 2 (over x), replica: 2 (over core), tensor: 8 (over z, y).
Axes of the slice: x: 2, y: 2, z: 4, core: 2. Of those that a mesh axis runs over, the one named last changes fastest.
Arguments:
- layer_input_hidden: bfloat16 [3, 16, 8192], P(None, ('groups', 'replica')), parts along dimension 1, may hold values from -6 to 6
- rmsnorm_gain_weight: bfloat16 [8192], replicated, may hold values from 0.099609375 to 1.8984375
- wq: bfloat16 [8192, 8192], P(None, 'tensor'), may hold values from -0.0625 to 0.0625
- wk: bfloat16 [8192, 1024], P(None, 'tensor'), may hold values from -0.0625 to 0.0625
- wv: bfloat16 [8192, 1024], P(None, 'tensor'), may hold values from -0.0625 to 0.0625
- wo: bfloat16 [8192, 8192], P('tensor'), may hold values from -0.5 to 0.5
- adapter_down_stored: bfloat16 [8192, 128], P(('replica', 'tensor')), may hold values from -0.0625 to 0.0625
- adapter_up_query: bfloat16 [64, 8192], P('replica', 'tensor'), may hold values from -0.75 to 0.75
- adapter_up_value: bfloat16 [64, 1024], P('replica', 'tensor'), may hold values from -0.75 to 0.75
- adapter_block_owner: int32 [16], replicated, may hold values from 0 to 15, each once
- rotated_key_cache: bfloat16 [16, 8, 2048, 128], P(('groups', 'replica'), None, 'tensor'), parts along dimension 0, may hold values from -210 to 210
- cached_value_rows: bfloat16 [16, 8, 2048, 128], P(('groups', 'replica'), None, 'tensor'), parts along dimension 0, may hold values from -6 to 6
- cache_valid_lengths: int32 [16], P(('groups', 'replica')), parts along dimension 0, may hold values from 1 to 2048, as said below
Outputs:
- layer_out: bfloat16 [3, 16, 8192], P(None, ('groups', 'replica'), 'tensor'), parts along dimension 1
The draws below stay inside these ranges and needn't reach their ends.
There are 2 independent parts, one for each index of `groups`. The reference program is written for one: setup_inputs(seed, part) draws one part's arguments, and reference() takes and returns one part's arrays. A program takes and returns all parts, laid end to end along the dimension named above; an argument that names none is the same for every part. Nothing has to cross between parts.
Inputs may be any that keep to these rules, and one draw needn't show every extreme that they name: adapter_block_owner is a permutation of 0 to 15; block k of adapter_down_stored is stored on index k of replica+tensor. `cache_valid_lengths`: some sequence of every job has exactly 2048 valid positions.
All inputs are finite; a program needn't handle non-finite values.
Results may differ from the reference program's by a relative error of at most 0.028.
Values may be sent and summed in bfloat16 or wider, within the bound.
No kernel may reach another device: no remote copies, remote signals or barrier semaphores. Data moves between devices by JAX's collectives and lax.ppermute only.
A program may use at most 128 MiB of HBM per device.

```python
import math
import jax
import jax.numpy as jnp
from jax import lax

MODEL_DIM = 8192
QUERY_HEADS = 64
KEY_VALUE_HEADS = 8
HEAD_DIM = 128
ADAPTER_RANK = 64
CACHE = 2048
STEPS = 3
SEQS = 8
ROW_BLOCKS = 16
DOWN_BLOCK_ROWS = 512
N_TENSOR = 8


def draw_rotated_key_cache(key, part):
    key = jax.random.fold_in(key, 11)
    base_key = jax.random.fold_in(key, 0)
    array_shape = (SEQS, KEY_VALUE_HEADS, CACHE, HEAD_DIM)
    values = jnp.clip(jax.random.normal(base_key, array_shape, jnp.float32), -6.0, 6.0)
    return values.astype(jnp.bfloat16)


def draw_cache_valid_lengths(key, part):
    key = jax.random.fold_in(key, 5)
    length_key, full_key = jax.random.split(key)
    lengths = jax.random.randint(length_key, (SEQS,), 1, CACHE + 1)
    full_slot = jax.random.randint(full_key, (), 0, SEQS)
    return jnp.where(jnp.arange(SEQS, dtype=jnp.int32) == full_slot, CACHE, lengths).astype(jnp.int32)


def shard_levels(stream_key, extent, shards, least, high):
    level, own = 1.0, jax.random.fold_in(stream_key, 6)
    for dim, shards_of in shards:
        steps = jnp.exp(jax.random.uniform(jax.random.fold_in(own, dim), (shards_of,), jnp.float32, least / len(shards), high / len(shards)))
        level = level * jnp.repeat(steps, extent[dim] // shards_of).reshape([-1 if axis == dim else 1 for axis in range(len(extent))])
    return level


def bell_draw(key, dims, scale, bound, shards=(), kind=jnp.bfloat16):
    factor_of = shard_levels(key, dims, shards, -0.22, 0.18) if shards else 1.0
    entries = jax.random.normal(key, dims, jnp.float32) * scale * factor_of
    return jnp.minimum(jnp.maximum(entries, -bound), bound).astype(kind)


def setup_inputs(seed: int = 0, part: int = 0) -> dict:
    streams_of = jax.random.split(jax.random.key(seed), 14)
    own_keys = jax.random.split(jax.random.fold_in(streams_of[13], part), 14)
    return {
        "layer_input_hidden": bell_draw(own_keys[0], (STEPS, SEQS, MODEL_DIM), 1.0, 6.0, ((1, 2),)),
        "rmsnorm_gain_weight": jnp.clip(1.0 + 0.18 * jax.random.normal(streams_of[1], (MODEL_DIM,), jnp.float32), 0.099609375, 1.8984375).astype(jnp.bfloat16),
        "wq": bell_draw(streams_of[2], (MODEL_DIM, QUERY_HEADS * HEAD_DIM), MODEL_DIM ** -0.5, 0.0625, ((1, 8),)),
        "wk": bell_draw(streams_of[3], (MODEL_DIM, KEY_VALUE_HEADS * HEAD_DIM), MODEL_DIM ** -0.5, 0.0625, ((1, 8),)),
        "wv": bell_draw(streams_of[4], (MODEL_DIM, KEY_VALUE_HEADS * HEAD_DIM), MODEL_DIM ** -0.5, 0.0625, ((1, 8),)),
        "wo": bell_draw(streams_of[5], (QUERY_HEADS * HEAD_DIM, MODEL_DIM), HEAD_DIM ** -0.5, 0.5, ((0, 8),)),
        "adapter_down_stored": bell_draw(streams_of[6], (MODEL_DIM, 2 * ADAPTER_RANK), MODEL_DIM ** -0.5, 0.0625, ((0, 16),)),
        "adapter_up_query": bell_draw(streams_of[7], (ADAPTER_RANK, QUERY_HEADS * HEAD_DIM), ADAPTER_RANK ** -0.5, 0.75, ((0, 2), (1, 8))),
        "adapter_up_value": bell_draw(streams_of[8], (ADAPTER_RANK, KEY_VALUE_HEADS * HEAD_DIM), ADAPTER_RANK ** -0.5, 0.75, ((0, 2), (1, 8))),
        "adapter_block_owner": jax.random.permutation(streams_of[9], ROW_BLOCKS).astype(jnp.int32),
        "rotated_key_cache": draw_rotated_key_cache(jax.random.fold_in(jax.random.fold_in(streams_of[13], part), 71), part),
        "cached_value_rows": bell_draw(own_keys[11], (SEQS, KEY_VALUE_HEADS, CACHE, HEAD_DIM), 1.0, 6.0, ((0, 2), (2, 8))),
        "cache_valid_lengths": draw_cache_valid_lengths(jax.random.fold_in(jax.random.fold_in(streams_of[13], part), 71), part),
    }


adapter_scale = 2.0
rope_base = 500000.0
negative = -1e+30

def rms_normed(layer_input_hidden, rmsnorm_gain_weight):
    values = layer_input_hidden.astype(jnp.float32)
    factor = lax.rsqrt(lax.optimization_barrier(jnp.mean(values * values, axis=-1, keepdims=True)) + 1e-05)
    return (values * factor * rmsnorm_gain_weight.astype(jnp.float32)).astype(jnp.bfloat16)

def rotary(heads_in, positions):
    half_dim = heads_in.shape[-1] // 2
    exponent = jnp.arange(half_dim).astype(jnp.float32) * (2.0 / heads_in.shape[-1])
    frequency = rope_base ** (-exponent)
    angles = positions.astype(jnp.float32)[..., None, None] * frequency
    cosine = jnp.cos(angles)
    sine = jnp.sin(angles)
    values = heads_in.astype(jnp.float32)
    first = values[..., :half_dim]
    second = values[..., half_dim:]
    return jnp.concatenate([first * cosine - second * sine, second * cosine + first * sine], axis=-1).astype(jnp.bfloat16)

def reference(layer_input_hidden, rmsnorm_gain_weight, wq, wk, wv, wo, adapter_down_stored, adapter_up_query, adapter_up_value, adapter_block_owner, rotated_key_cache, cached_value_rows, cache_valid_lengths):
    normed = rms_normed(layer_input_hidden, rmsnorm_gain_weight)
    flattened_rows = normed.reshape(STEPS * SEQS, MODEL_DIM)
    adapter_down_matrix = adapter_down_stored.reshape(ROW_BLOCKS, DOWN_BLOCK_ROWS, 2 * ADAPTER_RANK)[adapter_block_owner].reshape(MODEL_DIM, 2 * ADAPTER_RANK)
    adapter_shrunk = jnp.dot(flattened_rows, adapter_down_matrix, preferred_element_type=jnp.float32).astype(jnp.bfloat16)
    query_unrotated = (jnp.dot(flattened_rows, wq, preferred_element_type=jnp.float32) + adapter_scale * jnp.dot(adapter_shrunk[:, :ADAPTER_RANK], adapter_up_query, preferred_element_type=jnp.float32)).astype(jnp.bfloat16)
    k_raw = jnp.dot(flattened_rows, wk, preferred_element_type=jnp.float32).astype(jnp.bfloat16)
    value_current = (jnp.dot(flattened_rows, wv, preferred_element_type=jnp.float32) + adapter_scale * jnp.dot(adapter_shrunk[:, ADAPTER_RANK:], adapter_up_value, preferred_element_type=jnp.float32)).astype(jnp.bfloat16)
    positions = cache_valid_lengths[None, :] + jnp.arange(STEPS, dtype=jnp.int32)[:, None]
    queries = rotary(query_unrotated.reshape(STEPS, SEQS, QUERY_HEADS, HEAD_DIM), positions)
    keys_new = rotary(k_raw.reshape(STEPS, SEQS, KEY_VALUE_HEADS, HEAD_DIM), positions)
    values_new = value_current.reshape(STEPS, SEQS, KEY_VALUE_HEADS, HEAD_DIM)
    group = QUERY_HEADS // KEY_VALUE_HEADS
    span = CACHE // N_TENSOR
    inv_root = 1.0 / math.sqrt(HEAD_DIM)

    def one_sequence(items):
        query, key_block, value_block, key_fresh, value_fresh, length = items
        query = query.reshape(STEPS, KEY_VALUE_HEADS, group, HEAD_DIM).astype(jnp.float32)
        cache_keys = key_block.reshape(KEY_VALUE_HEADS, N_TENSOR, span, HEAD_DIM).astype(jnp.float32)
        cache_values = value_block.reshape(KEY_VALUE_HEADS, N_TENSOR, span, HEAD_DIM).astype(jnp.float32)
        scores = jnp.einsum('skgd,kbcd->skgbc', query, cache_keys) * inv_root
        live = jnp.arange(CACHE, dtype=jnp.int32).reshape(N_TENSOR, span) < length
        masked = jnp.where(live, scores, negative)
        block_max = lax.optimization_barrier(jnp.max(masked, axis=-1))
        weights = jnp.where(live, jnp.exp(masked - block_max[..., None]), 0.0)
        block_sum = lax.optimization_barrier(jnp.sum(weights, axis=-1))
        rounded = lax.optimization_barrier(weights.astype(jnp.bfloat16))
        block_out = jnp.einsum('skgbc,kbcd->skgbd', rounded.astype(jnp.float32), cache_values)
        fresh_scores = jnp.einsum('skgd,tkd->skgt', query, key_fresh.astype(jnp.float32)) * inv_root
        causal = (jnp.arange(STEPS)[None, :] <= jnp.arange(STEPS)[:, None])[:, None, None, :]
        fresh_masked = jnp.where(causal, fresh_scores, negative)
        fresh_max = lax.optimization_barrier(jnp.max(fresh_masked, axis=-1))
        fresh_weights = jnp.where(causal, jnp.exp(fresh_masked - fresh_max[..., None]), 0.0)
        fresh_sum = lax.optimization_barrier(jnp.sum(fresh_weights, axis=-1))
        fresh_rounded = lax.optimization_barrier(fresh_weights.astype(jnp.bfloat16))
        fresh_out = jnp.einsum('skgt,tkd->skgd', fresh_rounded.astype(jnp.float32), value_fresh.astype(jnp.float32))
        top = jnp.maximum(lax.optimization_barrier(jnp.max(block_max, axis=-1)), fresh_max)
        block_factor = jnp.exp(block_max - top[..., None])
        fresh_factor = jnp.exp(fresh_max - top)
        total = lax.optimization_barrier(jnp.sum(block_sum * block_factor, axis=-1)) + fresh_sum * fresh_factor
        summed = lax.optimization_barrier(jnp.sum(block_out * block_factor[..., None], axis=-2)) + fresh_out * fresh_factor[..., None]
        return (summed / total[..., None]).reshape(STEPS, QUERY_HEADS * HEAD_DIM).astype(jnp.bfloat16)
    attended = lax.map(one_sequence, (jnp.transpose(queries, (1, 0, 2, 3)), rotated_key_cache, cached_value_rows, jnp.transpose(keys_new, (1, 0, 2, 3)), jnp.transpose(values_new, (1, 0, 2, 3)), cache_valid_lengths))
    attn = jnp.transpose(attended, (1, 0, 2)).reshape(STEPS * SEQS, QUERY_HEADS * HEAD_DIM)
    projected = jnp.dot(attn, wo, preferred_element_type=jnp.float32).reshape(STEPS, SEQS, MODEL_DIM)
    return (layer_input_hidden.astype(jnp.float32) + projected).astype(jnp.bfloat16)
```

```python
import math

import jax
import jax.numpy as jnp
from jax import lax
from jax.sharding import PartitionSpec as P

QUERY_HEADS = 64
KEY_VALUE_HEADS = 8
HEAD_DIM = 128
ADAPTER_RANK = 64


adapter_scale = 2.0
rope_base = 500000.0
negative = -1e30


def shifted(value, axis, shift):
    count = lax.axis_size(axis)
    pairs = [(source, (source + shift) % count) for source in range(count)]
    return jax.tree.map(lambda leaf: lax.ppermute(leaf, axis, pairs), value)


def spread(value, axis):
    return [value] + [shifted(value, axis, k) for k in range(1, lax.axis_size(axis))]


def swapped(value):
    return shifted(value, "replica", 1)


def rms_normed(layer_input_hidden, rmsnorm_gain_weight):
    values = layer_input_hidden.astype(jnp.float32)
    factor = lax.rsqrt(jnp.mean(values * values, axis=-1, keepdims=True) + 1e-05)
    return (values * factor * rmsnorm_gain_weight.astype(jnp.float32)).astype(jnp.bfloat16)


def rotary(heads_in, positions):
    half_dim = heads_in.shape[-1] // 2
    exponent = jnp.arange(half_dim).astype(jnp.float32) * (2.0 / heads_in.shape[-1])
    frequency = rope_base ** (-exponent)
    angles = positions.astype(jnp.float32)[..., None, None] * frequency
    cosine = jnp.cos(angles)
    sine = jnp.sin(angles)
    values = heads_in.astype(jnp.float32)
    first = values[..., :half_dim]
    second = values[..., half_dim:]
    return jnp.concatenate(
        [first * cosine - second * sine, second * cosine + first * sine], axis=-1
    ).astype(jnp.bfloat16)


def body(
    layer_input_hidden,
    rmsnorm_gain_weight,
    wq,
    wk,
    wv,
    wo,
    adapter_down_stored,
    adapter_up_query,
    adapter_up_value,
    adapter_block_owner,
    rotated_key_cache,
    cached_value_rows,
    cache_valid_lengths,
):
    step_count, seq_count, model_width = layer_input_hidden.shape
    tensor_count = lax.axis_size("tensor")
    tensor_index = lax.axis_index("tensor")
    replica_index = lax.axis_index("replica")
    rows = step_count * seq_count
    other_down, other_up_query, other_up_value = swapped(
        (adapter_down_stored, adapter_up_query, adapter_up_value)
    )
    normed = rms_normed(layer_input_hidden, rmsnorm_gain_weight)
    flattened_rows = normed.reshape(rows, model_width)

    block_rows = adapter_down_stored.shape[0]

    def block_product(stored, replica):
        held = replica * tensor_count + tensor_index
        place = jnp.argmax(adapter_block_owner == held)
        features = lax.dynamic_slice_in_dim(flattened_rows, place * block_rows, block_rows, 1)
        return jnp.dot(features, stored, preferred_element_type=jnp.float32)

    partial_shrunk = block_product(adapter_down_stored, replica_index) + block_product(
        other_down, 1 - replica_index
    )
    adapter_shrunk = sum(spread(partial_shrunk, "tensor")).astype(jnp.bfloat16)

    def ordered(own, other):
        first = replica_index == 0
        return jnp.concatenate([jnp.where(first, own, other), jnp.where(first, other, own)], axis=0)

    query_raw = (
        jnp.dot(flattened_rows, wq, preferred_element_type=jnp.float32)
        + adapter_scale
        * jnp.dot(
            adapter_shrunk[:, :ADAPTER_RANK],
            ordered(adapter_up_query, other_up_query),
            preferred_element_type=jnp.float32,
        )
    ).astype(jnp.bfloat16)
    key_raw = jnp.dot(flattened_rows, wk, preferred_element_type=jnp.float32).astype(jnp.bfloat16)
    value_raw = (
        jnp.dot(flattened_rows, wv, preferred_element_type=jnp.float32)
        + adapter_scale
        * jnp.dot(
            adapter_shrunk[:, ADAPTER_RANK:],
            ordered(adapter_up_value, other_up_value),
            preferred_element_type=jnp.float32,
        )
    ).astype(jnp.bfloat16)

    positions = cache_valid_lengths[None, :] + jnp.arange(step_count, dtype=jnp.int32)[:, None]
    local_heads = wq.shape[1] // HEAD_DIM
    group = QUERY_HEADS // KEY_VALUE_HEADS
    own_queries = rotary(query_raw.reshape(step_count, seq_count, local_heads, HEAD_DIM), positions)

    sources = (tensor_index - jnp.arange(tensor_count)) % tensor_count
    gathered = jnp.stack(spread(own_queries, "tensor"))
    all_queries = jnp.take(gathered, sources, axis=0)
    query_groups = jnp.transpose(all_queries, (1, 2, 0, 3, 4)).reshape(
        step_count, seq_count, KEY_VALUE_HEADS, group, HEAD_DIM
    )
    span = rotated_key_cache.shape[2]
    inv_root = 1.0 / math.sqrt(HEAD_DIM)
    scores = (
        jnp.einsum(
            "snkgd,nkcd->snkgc", query_groups, rotated_key_cache, preferred_element_type=jnp.float32
        )
        * inv_root
    )
    cache_spots = tensor_index * span + jnp.arange(span, dtype=jnp.int32)
    live = (cache_spots[None, :] < cache_valid_lengths[:, None])[None, :, None, None, :]
    masked = jnp.where(live, scores, negative)
    block_max = jnp.max(masked, axis=-1)
    weights = jnp.where(live, jnp.exp(masked - block_max[..., None]), 0.0)
    block_sum = jnp.sum(weights, axis=-1)
    block_out = jnp.einsum(
        "snkgc,nkcd->snkgd",
        weights.astype(jnp.bfloat16),
        cached_value_rows,
        preferred_element_type=jnp.float32,
    )
    mean_out = (block_out / jnp.maximum(block_sum, 1e-30)[..., None]).astype(jnp.bfloat16)

    def by_owner(value, tail):
        heads_apart = value.reshape((step_count, seq_count, tensor_count, local_heads) + tail)
        return jnp.moveaxis(heads_apart, 2, 0)

    statistics = jnp.stack([block_max, block_sum])
    statistics = jnp.moveaxis(
        statistics.reshape(2, step_count, seq_count, tensor_count, local_heads), 3, 0
    ).reshape(tensor_count, 2, rows * local_heads)
    per_owner = (by_owner(mean_out, (HEAD_DIM,)), statistics)

    def deal(value):
        received = []
        for k in range(tensor_count):
            share = jax.tree.map(
                lambda leaf: lax.dynamic_index_in_dim(
                    leaf, (tensor_index + k) % tensor_count, 0, keepdims=False
                ),
                value,
            )
            received.append(shifted(share, "tensor", k) if k else share)
        return received

    received = deal(per_owner)
    cache_mean = jnp.stack([part[0] for part in received]).astype(jnp.float32)
    cache_stat = jnp.stack([part[1] for part in received]).reshape(
        tensor_count, 2, step_count, seq_count, local_heads
    )

    if local_heads == group:
        own_keys = rotary(key_raw.reshape(step_count, seq_count, 1, HEAD_DIM), positions)[:, :, 0]
        own_values = value_raw.reshape(step_count, seq_count, HEAD_DIM)
    else:
        kv_index = tensor_index * local_heads // group

        def own_head(value):
            heads = lax.all_gather(value, "tensor", axis=1, tiled=True).reshape(
                step_count, seq_count, KEY_VALUE_HEADS, HEAD_DIM
            )
            return lax.dynamic_index_in_dim(heads, kv_index, 2, keepdims=True)

        own_keys = rotary(own_head(key_raw), positions)[:, :, 0]
        own_values = own_head(value_raw)[:, :, 0]

    fresh_scores = (
        jnp.einsum("snhd,tnd->snht", own_queries, own_keys, preferred_element_type=jnp.float32)
        * inv_root
    )
    causal = (jnp.arange(step_count)[None, :] <= jnp.arange(step_count)[:, None])[:, None, None, :]
    fresh_masked = jnp.where(causal, fresh_scores, negative)
    fresh_max = jnp.max(fresh_masked, axis=-1)
    fresh_weights = jnp.where(causal, jnp.exp(fresh_masked - fresh_max[..., None]), 0.0)
    fresh_total = jnp.sum(fresh_weights, axis=-1)
    fresh_out = jnp.einsum(
        "snht,tnd->snhd",
        fresh_weights.astype(jnp.bfloat16),
        own_values,
        preferred_element_type=jnp.float32,
    )
    top = jnp.maximum(jnp.max(cache_stat[:, 0], axis=0), fresh_max)
    cache_share = cache_stat[:, 1] * jnp.exp(cache_stat[:, 0] - top)
    fresh_factor = jnp.exp(fresh_max - top)
    total = jnp.sum(cache_share, axis=0) + fresh_total * fresh_factor
    summed = jnp.sum(cache_mean * cache_share[..., None], axis=0) + fresh_out * fresh_factor[..., None]
    attention = (
        (summed / total[..., None]).astype(jnp.bfloat16).reshape(rows, local_heads * HEAD_DIM)
    )
    projected = jnp.dot(attention, wo, preferred_element_type=jnp.float32)
    width = model_width // tensor_count
    shares = jnp.moveaxis(projected.reshape(rows, tensor_count, width), 1, 0).astype(jnp.bfloat16)
    share = sum(part.astype(jnp.float32) for part in deal(shares))
    residual = lax.dynamic_slice_in_dim(layer_input_hidden, tensor_index * width, width, 2)
    return (residual.astype(jnp.float32) + share.reshape(step_count, seq_count, width)).astype(
        jnp.bfloat16
    )


def solution(mesh):
    return jax.shard_map(
        body,
        mesh=mesh,
        in_specs=(
            P(None, ("groups", "replica"), None),
            P(),
            P(None, "tensor"),
            P(None, "tensor"),
            P(None, "tensor"),
            P("tensor", None),
            P(("replica", "tensor"), None),
            P("replica", "tensor"),
            P("replica", "tensor"),
            P(),
            P(("groups", "replica"), None, "tensor", None),
            P(("groups", "replica"), None, "tensor", None),
            P(("groups", "replica")),
        ),
        out_specs=P(None, ("groups", "replica"), "tensor"),
        check_vma=False,
    )
```

```python
import math

import jax
import jax.numpy as jnp
from jax import lax
from jax.sharding import PartitionSpec as P

QUERY_HEADS = 64
KEY_VALUE_HEADS = 8
HEAD_DIM = 128
ADAPTER_RANK = 64


adapter_scale = 2.0
rope_base = 500000.0
negative = -1e30


def shifted(value, axis, shift):
    count = lax.axis_size(axis)
    pairs = [(source, (source + shift) % count) for source in range(count)]
    return jax.tree.map(lambda leaf: lax.ppermute(leaf, axis, pairs), value)


def crossed(value, axis, mask):
    pairs = [(source, source ^ mask) for source in range(lax.axis_size(axis))]
    return lax.ppermute(value, axis, pairs)


def masks_of(count):
    masks = []
    mask = count // 2
    while mask:
        masks.append(mask)
        mask //= 2
    return masks


def gathered_by_mask(value, axis):
    held, order = value[None], [0]
    for mask in masks_of(lax.axis_size(axis)):
        held = jnp.concatenate([held, crossed(held, axis, mask)], axis=0)
        order = order + [place ^ mask for place in order]
    return held, order


def summed_over(value, axis):
    for mask in masks_of(lax.axis_size(axis)):
        value = value + crossed(value, axis, mask)
    return value


def swapped(value):
    return shifted(value, "replica", 1)


def rms_normed(layer_input_hidden, rmsnorm_gain_weight):
    values = layer_input_hidden.astype(jnp.float32)
    factor = lax.rsqrt(jnp.mean(values * values, axis=-1, keepdims=True) + 1e-05)
    return (values * factor * rmsnorm_gain_weight.astype(jnp.float32)).astype(jnp.bfloat16)


def rotary(heads_in, positions):
    half_dim = heads_in.shape[-1] // 2
    exponent = jnp.arange(half_dim).astype(jnp.float32) * (2.0 / heads_in.shape[-1])
    frequency = rope_base ** (-exponent)
    angles = positions.astype(jnp.float32)[..., None, None] * frequency
    cosine = jnp.cos(angles)
    sine = jnp.sin(angles)
    values = heads_in.astype(jnp.float32)
    first = values[..., :half_dim]
    second = values[..., half_dim:]
    return jnp.concatenate(
        [first * cosine - second * sine, second * cosine + first * sine], axis=-1
    ).astype(jnp.bfloat16)


def body(
    layer_input_hidden,
    rmsnorm_gain_weight,
    wq,
    wk,
    wv,
    wo,
    adapter_down_stored,
    adapter_up_query,
    adapter_up_value,
    adapter_block_owner,
    rotated_key_cache,
    cached_value_rows,
    cache_valid_lengths,
):
    step_count, seq_count, model_width = layer_input_hidden.shape
    tensor_count = lax.axis_size("tensor")
    tensor_index = lax.axis_index("tensor")
    replica_index = lax.axis_index("replica")
    rows = step_count * seq_count
    other_down, other_up_query, other_up_value = swapped(
        (adapter_down_stored, adapter_up_query, adapter_up_value)
    )
    normed = rms_normed(layer_input_hidden, rmsnorm_gain_weight)
    flattened_rows = normed.reshape(rows, model_width)

    block_rows = adapter_down_stored.shape[0]

    def block_product(stored, replica):
        held = replica * tensor_count + tensor_index
        place = jnp.argmax(adapter_block_owner == held)
        features = lax.dynamic_slice_in_dim(flattened_rows, place * block_rows, block_rows, 1)
        return jnp.dot(features, stored, preferred_element_type=jnp.float32)

    partial_shrunk = block_product(adapter_down_stored, replica_index) + block_product(
        other_down, 1 - replica_index
    )
    adapter_shrunk = summed_over(partial_shrunk, "tensor").astype(jnp.bfloat16)

    def ordered(own, other):
        first = replica_index == 0
        return jnp.concatenate([jnp.where(first, own, other), jnp.where(first, other, own)], axis=0)

    query_raw = (
        jnp.dot(flattened_rows, wq, preferred_element_type=jnp.float32)
        + adapter_scale
        * jnp.dot(
            adapter_shrunk[:, :ADAPTER_RANK],
            ordered(adapter_up_query, other_up_query),
            preferred_element_type=jnp.float32,
        )
    ).astype(jnp.bfloat16)
    key_raw = jnp.dot(flattened_rows, wk, preferred_element_type=jnp.float32).astype(jnp.bfloat16)
    value_raw = (
        jnp.dot(flattened_rows, wv, preferred_element_type=jnp.float32)
        + adapter_scale
        * jnp.dot(
            adapter_shrunk[:, ADAPTER_RANK:],
            ordered(adapter_up_value, other_up_value),
            preferred_element_type=jnp.float32,
        )
    ).astype(jnp.bfloat16)

    positions = cache_valid_lengths[None, :] + jnp.arange(step_count, dtype=jnp.int32)[:, None]
    local_heads = wq.shape[1] // HEAD_DIM
    group = QUERY_HEADS // KEY_VALUE_HEADS
    own_queries = rotary(query_raw.reshape(step_count, seq_count, local_heads, HEAD_DIM), positions)

    gathered, order = gathered_by_mask(own_queries, "tensor")
    place_of = [order.index(mask) for mask in range(tensor_count)]
    wanted = jnp.arange(tensor_count) ^ tensor_index
    all_queries = jnp.take(gathered, jnp.asarray(place_of)[wanted], axis=0)
    query_groups = jnp.transpose(all_queries, (1, 2, 0, 3, 4)).reshape(
        step_count, seq_count, KEY_VALUE_HEADS, group, HEAD_DIM
    )
    span = rotated_key_cache.shape[2]
    inv_root = 1.0 / math.sqrt(HEAD_DIM)
    scores = (
        jnp.einsum(
            "snkgd,nkcd->snkgc", query_groups, rotated_key_cache, preferred_element_type=jnp.float32
        )
        * inv_root
    )
    cache_spots = tensor_index * span + jnp.arange(span, dtype=jnp.int32)
    live = (cache_spots[None, :] < cache_valid_lengths[:, None])[None, :, None, None, :]
    masked = jnp.where(live, scores, negative)
    block_max = jnp.max(masked, axis=-1)
    weights = jnp.where(live, jnp.exp(masked - block_max[..., None]), 0.0)
    block_sum = jnp.sum(weights, axis=-1)
    block_out = jnp.einsum(
        "snkgc,nkcd->snkgd",
        weights.astype(jnp.bfloat16),
        cached_value_rows,
        preferred_element_type=jnp.float32,
    )
    mean_out = (block_out / jnp.maximum(block_sum, 1e-30)[..., None]).astype(jnp.bfloat16)

    def by_owner(value, tail):
        heads_apart = value.reshape((step_count, seq_count, tensor_count, local_heads) + tail)
        return jnp.moveaxis(heads_apart, 2, 0)

    statistics = jnp.stack([block_max, block_sum])
    statistics = jnp.moveaxis(
        statistics.reshape(2, step_count, seq_count, tensor_count, local_heads), 3, 0
    ).reshape(tensor_count, 2, rows * local_heads)
    per_owner = (by_owner(mean_out, (HEAD_DIM,)), statistics)

    def deal(value):
        return lax.all_to_all(value, "tensor", split_axis=0, concat_axis=0, tiled=True)

    cache_mean = deal(per_owner[0]).astype(jnp.float32)
    cache_stat = deal(per_owner[1]).reshape(
        tensor_count, 2, step_count, seq_count, local_heads
    )

    if local_heads == group:
        own_keys = rotary(key_raw.reshape(step_count, seq_count, 1, HEAD_DIM), positions)[:, :, 0]
        own_values = value_raw.reshape(step_count, seq_count, HEAD_DIM)
    else:
        kv_index = tensor_index * local_heads // group

        def own_head(value):
            heads = lax.all_gather(value, "tensor", axis=1, tiled=True).reshape(
                step_count, seq_count, KEY_VALUE_HEADS, HEAD_DIM
            )
            return lax.dynamic_index_in_dim(heads, kv_index, 2, keepdims=True)

        own_keys = rotary(own_head(key_raw), positions)[:, :, 0]
        own_values = own_head(value_raw)[:, :, 0]

    fresh_scores = (
        jnp.einsum("snhd,tnd->snht", own_queries, own_keys, preferred_element_type=jnp.float32)
        * inv_root
    )
    causal = (jnp.arange(step_count)[None, :] <= jnp.arange(step_count)[:, None])[:, None, None, :]
    fresh_masked = jnp.where(causal, fresh_scores, negative)
    fresh_max = jnp.max(fresh_masked, axis=-1)
    fresh_weights = jnp.where(causal, jnp.exp(fresh_masked - fresh_max[..., None]), 0.0)
    fresh_total = jnp.sum(fresh_weights, axis=-1)
    fresh_out = jnp.einsum(
        "snht,tnd->snhd",
        fresh_weights.astype(jnp.bfloat16),
        own_values,
        preferred_element_type=jnp.float32,
    )
    top = jnp.maximum(jnp.max(cache_stat[:, 0], axis=0), fresh_max)
    cache_share = cache_stat[:, 1] * jnp.exp(cache_stat[:, 0] - top)
    fresh_factor = jnp.exp(fresh_max - top)
    total = jnp.sum(cache_share, axis=0) + fresh_total * fresh_factor
    summed = jnp.sum(cache_mean * cache_share[..., None], axis=0) + fresh_out * fresh_factor[..., None]
    attention = (
        (summed / total[..., None]).astype(jnp.bfloat16).reshape(rows, local_heads * HEAD_DIM)
    )
    projected = lax.optimization_barrier(
        jnp.dot(attention, wo, preferred_element_type=jnp.float32)
    )
    width = model_width // tensor_count
    shares = jnp.moveaxis(projected.reshape(rows, tensor_count, width), 1, 0).astype(jnp.bfloat16)
    share = jnp.sum(deal(shares).astype(jnp.float32), axis=0)
    residual = lax.dynamic_slice_in_dim(layer_input_hidden, tensor_index * width, width, 2)
    return (residual.astype(jnp.float32) + share.reshape(step_count, seq_count, width)).astype(
        jnp.bfloat16
    )


def solution(mesh):
    return jax.shard_map(
        body,
        mesh=mesh,
        in_specs=(
            P(None, ("groups", "replica"), None),
            P(),
            P(None, "tensor"),
            P(None, "tensor"),
            P(None, "tensor"),
            P("tensor", None),
            P(("replica", "tensor"), None),
            P("replica", "tensor"),
            P("replica", "tensor"),
            P(),
            P(("groups", "replica"), None, "tensor", None),
            P(("groups", "replica"), None, "tensor", None),
            P(("groups", "replica")),
        ),
        out_specs=P(None, ("groups", "replica"), "tensor"),
        check_vma=False,
    )
```

```python
import functools
import math

import jax
import jax.numpy as jnp
from jax import lax
from jax.experimental import pallas as pl
from jax.experimental.pallas import tpu as pltpu
from jax.sharding import PartitionSpec as P

QUERY_HEADS = 64
KEY_VALUE_HEADS = 8
HEAD_DIM = 128
ADAPTER_RANK = 64


adapter_scale = 2.0
rope_base = 500000.0
negative = -1e30
inv_root = 1.0 / math.sqrt(HEAD_DIM)
MIB = 1 << 20

vmem = pl.BlockSpec(memory_space=pltpu.VMEM)
smem = pl.BlockSpec(memory_space=pltpu.SMEM)
far = pl.BlockSpec(memory_space=pl.ANY)


def padded(count, multiple):
    return -(-count // multiple) * multiple


def rows_padded(value, rows):
    if value.shape[0] == rows:
        return value
    filler = jnp.zeros((rows - value.shape[0],) + value.shape[1:], value.dtype)
    return jnp.concatenate([value, filler], axis=0)


def kernel_call(kernel, outs, specs, out_specs, scratch=(), limit=16, moved=0, flops=0):
    call = pl.pallas_call(
        kernel,
        out_shape=outs,
        in_specs=specs,
        out_specs=out_specs,
        scratch_shapes=list(scratch),
        compiler_params=pltpu.CompilerParams(vmem_limit_bytes=limit * MIB),
        cost_estimate=pl.CostEstimate(flops=flops, bytes_accessed=moved, transcendentals=0),
    )

    def run(*operands):
        return call(
            *[
                pltpu.with_memory_space_constraint(operand, pltpu.HBM) if spec is far else operand
                for operand, spec in zip(operands, specs)
            ]
        )

    return run


def norm_kernel(x_ref, gain_ref, wk_ref, wv_ref, normed_ref, key_ref, value_ref, wk_buf, wv_buf, sem):
    copies = [
        pltpu.make_async_copy(wk_ref, wk_buf, sem.at[0]),
        pltpu.make_async_copy(wv_ref, wv_buf, sem.at[1]),
    ]
    for copy in copies:
        copy.start()
    steps = x_ref.shape[0]
    values = jnp.concatenate([x_ref[s].astype(jnp.float32) for s in range(steps)], axis=0)
    factor = lax.rsqrt(jnp.mean(values * values, axis=-1, keepdims=True) + 1e-05)
    normed = (values * factor * gain_ref[...].astype(jnp.float32)).astype(jnp.bfloat16)
    normed_ref[...] = normed
    copies[0].wait()
    key_ref[...] = jnp.dot(normed, wk_buf[...], preferred_element_type=jnp.float32)
    copies[1].wait()
    value_ref[...] = jnp.dot(normed, wv_buf[...], preferred_element_type=jnp.float32)


def shrink_kernel(owner_ref, normed_ref, own_ref, other_ref, out_ref):
    replica, tensor = lax.axis_index("replica"), lax.axis_index("tensor")
    peers, block_rows = out_ref.shape[0], own_ref.shape[0]

    def product(held, stored):
        place = jnp.int32(0)
        for j in range(owner_ref.shape[0]):
            place = jnp.where(owner_ref[j] == held, jnp.int32(j), place)
        columns = pl.ds(pl.multiple_of(place * block_rows, block_rows), block_rows)
        return jnp.dot(normed_ref[:, columns], stored[...], preferred_element_type=jnp.float32)

    total = product(replica * peers + tensor, own_ref) + product(
        (1 - replica) * peers + tensor, other_ref
    )
    for peer in range(peers):
        out_ref[peer] = total


def query_kernel(chunks, normed_ref, wq_ref, out_ref, wq_buf, sem):
    span = wq_ref.shape[0] // chunks

    def part(c):
        rows = pl.ds(c * span, span)
        return pltpu.make_async_copy(wq_ref.at[rows], wq_buf.at[rows], sem.at[c])

    for c in range(chunks):
        part(c).start()
    total = jnp.zeros(out_ref.shape, jnp.float32)
    for c in range(chunks):
        part(c).wait()
        total = total + jnp.dot(
            normed_ref[:, c * span : (c + 1) * span],
            wq_buf[c * span : (c + 1) * span, :],
            preferred_element_type=jnp.float32,
        )
    out_ref[...] = total


def rotated(values, cosine, sine):
    half = HEAD_DIM // 2
    turned = jnp.concatenate([values[:, half:], values[:, :half]], axis=1)
    return values * cosine + turned * sine


def finish_kernel(
    seq_count, acc_ref, key_ref, value_ref, parts_ref, uq_own, uq_other, uv_own, uv_other,
    cos_ref, sin_ref, query_ref, keyout_ref, valueout_ref, wide, tall,
):
    first = lax.axis_index("replica") == 0
    rows = acc_ref.shape[0]
    steps = rows // seq_count
    heads = acc_ref.shape[1] // HEAD_DIM
    peers = parts_ref.shape[0]
    shrunk = parts_ref[0]
    for peer in range(1, peers):
        shrunk = shrunk + parts_ref[peer]
    shrunk = shrunk.astype(jnp.bfloat16).astype(jnp.float32)
    half = ADAPTER_RANK // 2

    def lifted(low, high, own, other):
        mine = jnp.where(first, low, high).astype(jnp.bfloat16)
        theirs = jnp.where(first, high, low).astype(jnp.bfloat16)
        return adapter_scale * (
            jnp.dot(mine, own[...], preferred_element_type=jnp.float32)
            + jnp.dot(theirs, other[...], preferred_element_type=jnp.float32)
        )

    raw = acc_ref[...] + lifted(shrunk[:, :half], shrunk[:, half : 2 * half], uq_own, uq_other)
    raw = raw.astype(jnp.bfloat16).astype(jnp.float32)
    cosine, sine = cos_ref[...], sin_ref[...]
    for h in range(heads):
        columns = slice(h * HEAD_DIM, (h + 1) * HEAD_DIM)
        wide[h, 0:rows, :] = rotated(raw[:, columns], cosine, sine)
    for n in range(seq_count):
        for h in range(heads):
            tall[pl.ds((n * heads + h) * steps, steps), :] = wide[
                h, pl.ds(n, steps, stride=seq_count), :
            ]
    queries = tall[...].astype(jnp.bfloat16)
    for peer in range(peers):
        query_ref[peer] = queries
    keyout_ref[...] = key_ref[...].astype(jnp.bfloat16)
    value = value_ref[...] + lifted(
        shrunk[:, 2 * half : 3 * half], shrunk[:, 3 * half :], uv_own, uv_other
    )
    valueout_ref[...] = value.astype(jnp.bfloat16)


def fetch_kernel(
    seq_count, chunks, query_ref, key_ref, value_ref, cos_ref, sin_ref, wo_ref, kc_ref, vc_ref,
    fresh_ref, level_ref, wo_out, kc_out, vc_out, sem,
):
    span = wo_ref.shape[0] // chunks
    copies = [
        pltpu.make_async_copy(kc_ref, kc_out, sem.at[chunks]),
        pltpu.make_async_copy(vc_ref, vc_out, sem.at[chunks + 1]),
    ]
    for c in range(chunks):
        part = pl.ds(c * span, span)
        copies.append(pltpu.make_async_copy(wo_ref.at[part], wo_out.at[part], sem.at[c]))
    for copy in copies:
        copy.start()
    steps = key_ref.shape[0] // seq_count
    per_seq = fresh_ref.shape[0] // seq_count
    queries = query_ref[0].astype(jnp.float32)
    keys = rotated(key_ref[...].astype(jnp.float32), cos_ref[...], sin_ref[...])
    keys = keys.astype(jnp.bfloat16).astype(jnp.float32)
    values = value_ref[...].astype(jnp.float32)
    step = lax.rem(lax.broadcasted_iota(jnp.int32, (per_seq, 1), 0), steps)
    for n in range(seq_count):
        rows = slice(n * per_seq, (n + 1) * per_seq)
        query = queries[rows]
        scores = []
        for t in range(steps):
            place = t * seq_count + n
            score = jnp.sum(query * keys[place : place + 1], axis=-1, keepdims=True) * inv_root
            scores.append(jnp.where(step >= t, score, negative))
        top = functools.reduce(jnp.maximum, scores)
        weights = [
            jnp.where(step >= t, jnp.exp(score - top), 0.0) for t, score in enumerate(scores)
        ]
        total = functools.reduce(jnp.add, weights)
        summed = jnp.zeros((per_seq, HEAD_DIM), jnp.float32)
        for t, weight in enumerate(weights):
            place = t * seq_count + n
            summed = summed + weight.astype(jnp.bfloat16).astype(jnp.float32) * values[
                place : place + 1
            ]
        fresh_ref[rows, :] = summed / total
        level_ref[rows, :] = jnp.broadcast_to(top + jnp.log(total), (per_seq, HEAD_DIM))
    for copy in copies:
        copy.wait()


def cache_kernel(lengths_ref, query_ref, kc_ref, vc_ref, out_ref):
    peers, held_rows, _ = query_ref.shape
    seq_count, kv_heads, span, _ = kc_ref.shape
    per_seq = held_rows // seq_count
    sharers = peers // kv_heads
    mean_rows = padded(held_rows, 16)
    level_rows = out_ref.shape[1] - mean_rows
    spots = lax.axis_index("tensor") * span + lax.broadcasted_iota(jnp.int32, (1, span), 1)
    lane = lax.broadcasted_iota(jnp.int32, (1, HEAD_DIM), 1)
    for g in range(kv_heads):
        owners = range(g * sharers, (g + 1) * sharers)
        queries = [query_ref[owner].astype(jnp.float32) for owner in owners]
        means = [[] for _ in owners]
        levels = jnp.zeros((per_seq * sharers, HEAD_DIM), jnp.float32)
        for n in range(seq_count):
            rows = [query[n * per_seq : (n + 1) * per_seq] for query in queries]
            rows = (jnp.concatenate(rows, axis=0) if sharers > 1 else rows[0]).astype(jnp.bfloat16)
            scores = (
                lax.dot_general(
                    rows,
                    kc_ref[n, g],
                    (((1,), (1,)), ((), ())),
                    preferred_element_type=jnp.float32,
                )
                * inv_root
            )
            live = spots < lengths_ref[n]
            scores = jnp.where(live, scores, negative)
            top = jnp.max(scores, axis=-1, keepdims=True)
            weights = jnp.where(live, jnp.exp(scores - top), 0.0)
            total = jnp.sum(weights, axis=-1, keepdims=True)
            summed = jnp.dot(
                weights.astype(jnp.bfloat16), vc_ref[n, g], preferred_element_type=jnp.float32
            )
            some = jnp.where(total > 0.0, total, 1.0)
            mean = summed / some
            level = jnp.where(total > 0.0, top + jnp.log(some), negative)
            for o in range(sharers):
                means[o].append(mean[o * per_seq : (o + 1) * per_seq])
            left = level
            for c in range(3):
                piece = left.astype(jnp.bfloat16).astype(jnp.float32)
                left = left - piece
                levels = jnp.where(lane == 3 * n + c, piece, levels)
        for o, owner in enumerate(owners):
            mean = rows_padded(jnp.concatenate(means[o], axis=0), mean_rows)
            out_ref[owner, 0:mean_rows, :] = mean.astype(jnp.bfloat16)
            level = rows_padded(levels[o * per_seq : (o + 1) * per_seq], level_rows)
            out_ref[owner, mean_rows:, :] = level.astype(jnp.bfloat16)


def output_kernel(seq_count, parts_ref, fresh_ref, level_ref, wo_ref, out_ref, wide):
    peers, rows, width = out_ref.shape
    steps = rows // seq_count
    held_rows = fresh_ref.shape[0]
    per_seq = held_rows // seq_count
    heads = per_seq // steps
    mean_rows = padded(held_rows, 16)
    means = [parts_ref[b, 0:mean_rows, :].astype(jnp.float32) for b in range(peers)]
    levels = []
    for b in range(peers):
        pieces = parts_ref[b, mean_rows:, :].astype(jnp.float32)[0:per_seq]
        levels.append(pieces)
    for n in range(seq_count):
        part = slice(n * per_seq, (n + 1) * per_seq)
        own = [
            level[:, 3 * n : 3 * n + 1]
            + (level[:, 3 * n + 1 : 3 * n + 2] + level[:, 3 * n + 2 : 3 * n + 3])
            for level in levels
        ]
        fresh_level = level_ref[part, 0:1]
        top = functools.reduce(jnp.maximum, own + [fresh_level])
        share = jnp.exp(fresh_level - top)
        total = share
        summed = share * fresh_ref[part, :]
        for b in range(peers):
            share = jnp.exp(own[b] - top)
            total = total + share
            summed = summed + share * means[b][part]
        mixed = summed / total
        for h in range(heads):
            wide[h, pl.ds(n, steps, stride=seq_count), :] = mixed[h * steps : (h + 1) * steps]
    attention = jnp.concatenate([wide[h, 0:rows, :] for h in range(heads)], axis=1)
    attention = attention.astype(jnp.bfloat16)
    for peer in range(peers):
        out_ref[peer] = jnp.dot(
            attention,
            wo_ref[:, peer * width : (peer + 1) * width],
            preferred_element_type=jnp.float32,
        ).astype(jnp.bfloat16)


def exchanged(value):
    return lax.all_to_all(value, "tensor", split_axis=0, concat_axis=0, tiled=True)


def body(
    layer_input_hidden,
    rmsnorm_gain_weight,
    wq,
    wk,
    wv,
    wo,
    adapter_down_stored,
    adapter_up_query,
    adapter_up_value,
    adapter_block_owner,
    rotated_key_cache,
    cached_value_rows,
    cache_valid_lengths,
):
    f32, bf16 = jnp.float32, jnp.bfloat16
    shape = jax.ShapeDtypeStruct
    steps, seqs, model_width = layer_input_hidden.shape
    peers = lax.axis_size("tensor")
    tensor_index = lax.axis_index("tensor")
    rows = steps * seqs
    local_heads = wq.shape[1] // HEAD_DIM
    held_rows = rows * local_heads
    kv_width = wk.shape[1]
    width = model_width // peers
    group = QUERY_HEADS // KEY_VALUE_HEADS

    pairs = [(0, 1), (1, 0)]
    other_down = lax.ppermute(adapter_down_stored, "replica", pairs)
    other_up_query = lax.ppermute(adapter_up_query, "replica", pairs)
    other_up_value = lax.ppermute(adapter_up_value, "replica", pairs)

    positions = cache_valid_lengths[None, :] + jnp.arange(steps, dtype=jnp.int32)[:, None]
    half = HEAD_DIM // 2
    exponent = jnp.arange(half).astype(f32) * (2.0 / HEAD_DIM)
    angles = positions.astype(f32).reshape(rows, 1) * (rope_base ** (-exponent))
    cosine, sine = jnp.cos(angles), jnp.sin(angles)
    cosine = jnp.concatenate([cosine, cosine], axis=1)
    sine = jnp.concatenate([-sine, sine], axis=1)

    normed, key_sum, value_sum = kernel_call(
        norm_kernel,
        (
            shape((rows, model_width), bf16),
            shape((rows, kv_width), f32),
            shape((rows, kv_width), f32),
        ),
        [vmem, vmem, far, far],
        (vmem, vmem, vmem),
        [pltpu.VMEM(wk.shape, bf16), pltpu.VMEM(wv.shape, bf16), pltpu.SemaphoreType.DMA((2,))],
        limit=16,
        moved=2 * wk.size * 2,
    )(layer_input_hidden, rmsnorm_gain_weight.reshape(1, model_width), wk, wv)

    partial = kernel_call(
        shrink_kernel,
        shape((peers, rows, 2 * ADAPTER_RANK), f32),
        [smem, vmem, vmem, vmem],
        vmem,
        limit=8,
    )(adapter_block_owner, normed, adapter_down_stored, other_down)
    shrink_parts = exchanged(partial)

    chunks = 16
    query_sum = kernel_call(
        functools.partial(query_kernel, chunks),
        shape((rows, wq.shape[1]), f32),
        [vmem, far],
        vmem,
        [pltpu.VMEM(wq.shape, bf16), pltpu.SemaphoreType.DMA((chunks,))],
        limit=24,
        moved=wq.size * 2,
        flops=2 * rows * wq.size,
    )(normed, wq)

    queries, key_raw, value_raw = kernel_call(
        functools.partial(finish_kernel, seqs),
        (
            shape((peers, held_rows, HEAD_DIM), bf16),
            shape((rows, kv_width), bf16),
            shape((rows, kv_width), bf16),
        ),
        [vmem] * 10,
        (vmem,) * 3,
        [
            pltpu.VMEM((local_heads, padded(rows, 8), HEAD_DIM), f32),
            pltpu.VMEM((held_rows, HEAD_DIM), f32),
        ],
        limit=16,
    )(
        query_sum, key_sum, value_sum, shrink_parts, adapter_up_query, other_up_query,
        adapter_up_value, other_up_value, cosine, sine,
    )
    all_queries = exchanged(queries)

    if kv_width != HEAD_DIM:
        kv_index = tensor_index * local_heads // group

        def own_head(value):
            heads = lax.all_gather(value, "tensor", axis=1, tiled=True)
            return lax.dynamic_slice_in_dim(heads, kv_index * HEAD_DIM, HEAD_DIM, 1)

        key_raw, value_raw = own_head(key_raw), own_head(value_raw)

    fresh, fresh_level, wo_near, keys_near, values_near = kernel_call(
        functools.partial(fetch_kernel, seqs, 8),
        (
            shape((held_rows, HEAD_DIM), f32),
            shape((held_rows, HEAD_DIM), f32),
            shape(wo.shape, bf16),
            shape(rotated_key_cache.shape, bf16),
            shape(cached_value_rows.shape, bf16),
        ),
        [vmem] * 5 + [far] * 3,
        (vmem,) * 5,
        [pltpu.SemaphoreType.DMA((10,))],
        limit=24,
        moved=2 * (wo.size + 2 * rotated_key_cache.size),
    )(queries, key_raw, value_raw, cosine, sine, wo, rotated_key_cache, cached_value_rows)

    level_rows = padded(held_rows // seqs, 16)
    partials = kernel_call(
        cache_kernel,
        shape((peers, padded(held_rows, 16) + level_rows, HEAD_DIM), bf16),
        [smem, vmem, vmem, vmem],
        vmem,
        limit=16,
    )(cache_valid_lengths, all_queries, keys_near, values_near)
    received = exchanged(partials)

    shares = kernel_call(
        functools.partial(output_kernel, seqs),
        shape((peers, rows, width), bf16),
        [vmem] * 4,
        vmem,
        [pltpu.VMEM((local_heads, padded(rows, 8), HEAD_DIM), f32)],
        limit=16,
    )(received, fresh, fresh_level, wo_near)
    share = jnp.sum(exchanged(shares).astype(f32), axis=0)
    residual = lax.dynamic_slice_in_dim(layer_input_hidden, tensor_index * width, width, 2)
    return (residual.astype(f32) + share.reshape(steps, seqs, width)).astype(bf16)


def solution(mesh):
    return jax.shard_map(
        body,
        mesh=mesh,
        in_specs=(
            P(None, ("groups", "replica"), None),
            P(),
            P(None, "tensor"),
            P(None, "tensor"),
            P(None, "tensor"),
            P("tensor", None),
            P(("replica", "tensor"), None),
            P("replica", "tensor"),
            P("replica", "tensor"),
            P(),
            P(("groups", "replica"), None, "tensor", None),
            P(("groups", "replica"), None, "tensor", None),
            P(("groups", "replica")),
        ),
        out_specs=P(None, ("groups", "replica"), "tensor"),
        check_vma=False,
    )
```

```python
import functools
import math

import jax
import jax.numpy as jnp
from jax import lax
from jax.experimental import pallas as pl
from jax.experimental.pallas import tpu as pltpu
from jax.sharding import PartitionSpec as P

QUERY_HEADS = 64
KEY_VALUE_HEADS = 8
HEAD_DIM = 128
ADAPTER_RANK = 64


adapter_scale = 2.0
rope_base = 500000.0
negative = -1e30
inv_root = 1.0 / math.sqrt(HEAD_DIM)
MIB = 1 << 20

vmem = pl.BlockSpec(memory_space=pltpu.VMEM)
smem = pl.BlockSpec(memory_space=pltpu.SMEM)
far = pl.BlockSpec(memory_space=pl.ANY)


def padded(count, multiple):
    return -(-count // multiple) * multiple


def rows_padded(value, rows):
    if value.shape[0] == rows:
        return value
    filler = jnp.zeros((rows - value.shape[0],) + value.shape[1:], value.dtype)
    return jnp.concatenate([value, filler], axis=0)


def kernel_call(kernel, outs, specs, out_specs, scratch=(), limit=16, moved=0, flops=0):
    call = pl.pallas_call(
        kernel,
        out_shape=outs,
        in_specs=specs,
        out_specs=out_specs,
        scratch_shapes=list(scratch),
        compiler_params=pltpu.CompilerParams(vmem_limit_bytes=limit * MIB),
        cost_estimate=pl.CostEstimate(flops=flops, bytes_accessed=moved, transcendentals=0),
    )

    def run(*operands):
        return call(
            *[
                pltpu.with_memory_space_constraint(operand, pltpu.HBM) if spec is far else operand
                for operand, spec in zip(operands, specs)
            ]
        )

    return run


def norm_kernel(lengths_ref, x_ref, gain_ref, normed_ref, cos_ref, sin_ref, rest_ref, x_buf, sem):
    copy = pltpu.make_async_copy(x_ref, x_buf, sem)
    copy.start()
    steps, seqs, _ = x_ref.shape
    rows, width = rest_ref.shape
    half = HEAD_DIM // 2
    row = lax.broadcasted_iota(jnp.int32, (rows, HEAD_DIM), 0)
    lane = lax.broadcasted_iota(jnp.int32, (rows, HEAD_DIM), 1)
    positions = jnp.zeros((rows, HEAD_DIM), jnp.int32)
    for s in range(steps):
        for n in range(seqs):
            positions = jnp.where(row == s * seqs + n, lengths_ref[n] + s, positions)
    low = lane < half
    exponent = jnp.where(low, lane, lane - half).astype(jnp.float32) * (2.0 / HEAD_DIM)
    angles = positions.astype(jnp.float32) * jnp.exp(exponent * -math.log(rope_base))
    sine = jnp.sin(angles)
    cos_ref[...] = jnp.cos(angles)
    sin_ref[...] = jnp.where(low, -sine, sine)
    copy.wait()
    values = jnp.concatenate([x_buf[s].astype(jnp.float32) for s in range(steps)], axis=0)
    factor = lax.rsqrt(jnp.mean(values * values, axis=-1, keepdims=True) + 1e-05)
    normed = values * factor * gain_ref[...].astype(jnp.float32)
    normed_ref[...] = normed.astype(jnp.bfloat16)
    start = lax.axis_index("tensor") * width
    for s in range(steps):
        part = x_buf[s, :, pl.ds(pl.multiple_of(start, width), width)]
        rest_ref[s * seqs : (s + 1) * seqs, :] = part.astype(jnp.float32)


def shrink_kernel(peers, owner_ref, normed_ref, own_ref, other_ref, out_ref):
    replica, tensor = lax.axis_index("replica"), lax.axis_index("tensor")
    block_rows = own_ref.shape[0]

    def product(held, stored):
        place = jnp.int32(0)
        for j in range(owner_ref.shape[0]):
            place = jnp.where(owner_ref[j] == held, jnp.int32(j), place)
        columns = pl.ds(pl.multiple_of(place * block_rows, block_rows), block_rows)
        return jnp.dot(normed_ref[:, columns], stored[...], preferred_element_type=jnp.float32)

    out_ref[...] = product(replica * peers + tensor, own_ref) + product(
        (1 - replica) * peers + tensor, other_ref
    )


def key_value_kernel(normed_ref, wk_ref, wv_ref, key_ref, value_ref, wk_buf, wv_buf, sem):
    halves = 2
    span = wk_ref.shape[0] // halves
    copies = []
    for far_ref, near, out, k in ((wk_ref, wk_buf, key_ref, 0), (wv_ref, wv_buf, value_ref, 1)):
        for c in range(halves):
            part = pl.ds(c * span, span)
            copies.append(
                pltpu.make_async_copy(far_ref.at[part], near.at[part], sem.at[halves * k + c])
            )
    for copy in copies:
        copy.start()
    for near, out, k in ((wk_buf, key_ref, 0), (wv_buf, value_ref, 1)):
        total = jnp.zeros(out.shape, jnp.float32)
        for c in range(halves):
            copies[halves * k + c].wait()
            total = total + jnp.dot(
                normed_ref[:, c * span : (c + 1) * span],
                near[c * span : (c + 1) * span, :],
                preferred_element_type=jnp.float32,
            )
        out[...] = total


def query_kernel(chunks, normed_ref, wq_ref, out_ref, wq_buf, sem):
    span = wq_ref.shape[0] // chunks

    def part(c):
        rows = pl.ds(c * span, span)
        return pltpu.make_async_copy(wq_ref.at[rows], wq_buf.at[rows], sem.at[c])

    for c in range(chunks):
        part(c).start()
    total = jnp.zeros(out_ref.shape, jnp.float32)
    for c in range(chunks):
        part(c).wait()
        total = total + jnp.dot(
            normed_ref[:, c * span : (c + 1) * span],
            wq_buf[c * span : (c + 1) * span, :],
            preferred_element_type=jnp.float32,
        )
    out_ref[...] = total


def rotated(values, cosine, sine):
    half = HEAD_DIM // 2
    turned = jnp.concatenate([values[:, half:], values[:, :half]], axis=1)
    return values * cosine + turned * sine


def finish_kernel(
    seq_count, acc_ref, key_ref, value_ref, parts_ref, uq_own, uq_other, uv_own, uv_other,
    cos_ref, sin_ref, query_ref, keyout_ref, valueout_ref, wide, tall,
):
    first = lax.axis_index("replica") == 0
    rows = acc_ref.shape[0]
    steps = rows // seq_count
    heads = acc_ref.shape[1] // HEAD_DIM
    shrunk = functools.reduce(jnp.add, [parts_ref[b] for b in range(parts_ref.shape[0])])
    shrunk = shrunk.astype(jnp.bfloat16).astype(jnp.float32)
    half = ADAPTER_RANK // 2

    def lifted(low, high, own, other):
        mine = jnp.where(first, low, high).astype(jnp.bfloat16)
        theirs = jnp.where(first, high, low).astype(jnp.bfloat16)
        return adapter_scale * (
            jnp.dot(mine, own[...], preferred_element_type=jnp.float32)
            + jnp.dot(theirs, other[...], preferred_element_type=jnp.float32)
        )

    raw = acc_ref[...] + lifted(shrunk[:, :half], shrunk[:, half : 2 * half], uq_own, uq_other)
    raw = raw.astype(jnp.bfloat16).astype(jnp.float32)
    cosine, sine = cos_ref[...], sin_ref[...]
    for h in range(heads):
        columns = slice(h * HEAD_DIM, (h + 1) * HEAD_DIM)
        wide[h, 0:rows, :] = rotated(raw[:, columns], cosine, sine)
    for n in range(seq_count):
        for h in range(heads):
            tall[pl.ds((n * heads + h) * steps, steps), :] = wide[
                h, pl.ds(n, steps, stride=seq_count), :
            ]
    query_ref[...] = tall[...].astype(jnp.bfloat16)
    keyout_ref[...] = key_ref[...].astype(jnp.bfloat16)
    value = value_ref[...] + lifted(
        shrunk[:, 2 * half : 3 * half], shrunk[:, 3 * half :], uv_own, uv_other
    )
    valueout_ref[...] = value.astype(jnp.bfloat16)


def fetches(pairs, sem):
    copies = [
        pltpu.make_async_copy(far_ref, near, sem.at[k]) for k, (far_ref, near) in enumerate(pairs)
    ]
    for copy in copies:
        copy.start()
    return copies


def row_parts(far_ref, near, first, pieces):
    span = near.shape[0] // pieces
    return [
        (far_ref.at[pl.ds(first + c * span, span)], near.at[pl.ds(c * span, span)])
        for c in range(pieces)
    ]


def fresh_kernel(
    seq_count, query_ref, key_ref, value_ref, cos_ref, sin_ref, kc_ref, vc_ref,
    fresh_ref, level_ref, kc_out, vc_out, sem,
):
    copies = fetches([(kc_ref, kc_out), (vc_ref, vc_out)], sem)
    steps = key_ref.shape[0] // seq_count
    per_seq = fresh_ref.shape[0] // seq_count
    queries = query_ref[...].astype(jnp.float32)
    keys = rotated(key_ref[...].astype(jnp.float32), cos_ref[...], sin_ref[...])
    keys = keys.astype(jnp.bfloat16).astype(jnp.float32)
    values = value_ref[...].astype(jnp.float32)
    step = lax.rem(lax.broadcasted_iota(jnp.int32, (per_seq, 1), 0), steps)
    for n in range(seq_count):
        rows = slice(n * per_seq, (n + 1) * per_seq)
        query = queries[rows]
        scores = []
        for t in range(steps):
            place = t * seq_count + n
            score = jnp.sum(query * keys[place : place + 1], axis=-1, keepdims=True) * inv_root
            scores.append(jnp.where(step >= t, score, negative))
        top = functools.reduce(jnp.maximum, scores)
        weights = [
            jnp.where(step >= t, jnp.exp(score - top), 0.0) for t, score in enumerate(scores)
        ]
        total = functools.reduce(jnp.add, weights)
        summed = jnp.zeros((per_seq, HEAD_DIM), jnp.float32)
        for t, weight in enumerate(weights):
            place = t * seq_count + n
            summed = summed + weight.astype(jnp.bfloat16).astype(jnp.float32) * values[
                place : place + 1
            ]
        fresh_ref[rows, :] = summed / total
        level_ref[rows, :] = jnp.broadcast_to(top + jnp.log(total), (per_seq, HEAD_DIM))
    for copy in copies:
        copy.wait()


def cache_kernel(odd, first, lengths_ref, query_ref, kc_ref, vc_ref, wo_ref, out_ref, wo_out, sem):
    copies = fetches(row_parts(wo_ref, wo_out, first, 4), sem)
    entries, held_rows, _ = query_ref.shape
    seq_count, kv_heads, span, _ = kc_ref.shape
    peers = 2 * entries
    per_seq = held_rows // seq_count
    mean_rows = padded(held_rows, 16)
    level_rows = out_ref.shape[1] - mean_rows
    tensor = lax.axis_index("tensor")
    spots = tensor * span + lax.broadcasted_iota(jnp.int32, (1, span), 1)
    lane = lax.broadcasted_iota(jnp.int32, (1, HEAD_DIM), 1)
    lives = [
        jnp.broadcast_to(spots, (per_seq, span)) < lengths_ref[n] for n in range(seq_count)
    ]
    batch = 2
    for lead in range(0, entries, batch):
        group = range(lead, min(lead + batch, entries))
        heads = [lax.bitwise_xor(tensor, 2 * e + odd) * kv_heads // peers for e in group]
        cases = [(g, e, n) for g, e in zip(heads, group) for n in range(seq_count)]
        held = {e: query_ref[e].astype(jnp.float32) for e in group}
        scores = [
            lax.dot_general(
                held[e][n * per_seq : (n + 1) * per_seq].astype(jnp.bfloat16),
                kc_ref[n, g],
                (((1,), (1,)), ((), ())),
                preferred_element_type=jnp.float32,
            )
            for g, e, n in cases
        ]
        scores = [
            jnp.where(lives[n], score * inv_root, negative)
            for score, (g, e, n) in zip(scores, cases)
        ]
        tops = [jnp.max(score, axis=-1, keepdims=True) for score in scores]
        weights = [
            jnp.where(lives[n], jnp.exp(score - top), 0.0)
            for score, top, (g, e, n) in zip(scores, tops, cases)
        ]
        totals = [jnp.sum(weight, axis=-1, keepdims=True) for weight in weights]
        sums = [
            jnp.dot(weight.astype(jnp.bfloat16), vc_ref[n, g], preferred_element_type=jnp.float32)
            for weight, (g, e, n) in zip(weights, cases)
        ]
        somes = [jnp.where(total > 0.0, total, 1.0) for total in totals]
        means = [total / some for total, some in zip(sums, somes)]
        levels = [
            jnp.where(total > 0.0, top + jnp.log(some), negative)
            for total, top, some in zip(totals, tops, somes)
        ]
        for k, e in enumerate(group):
            part = slice(k * seq_count, (k + 1) * seq_count)
            mean = rows_padded(jnp.concatenate(means[part], axis=0), mean_rows)
            out_ref[e, 0:mean_rows, :] = mean.astype(jnp.bfloat16)
            packed = jnp.zeros((per_seq, HEAD_DIM), jnp.float32)
            for n, level in enumerate(levels[part]):
                left = level
                for c in range(3):
                    piece = left.astype(jnp.bfloat16).astype(jnp.float32)
                    left = left - piece
                    packed = jnp.where(lane == 3 * n + c, piece, packed)
            out_ref[e, mean_rows:, :] = rows_padded(packed, level_rows).astype(jnp.bfloat16)
    for copy in copies:
        copy.wait()


def order_kernel(even_ref, odd_ref, out_ref):
    tensor = lax.axis_index("tensor")
    for e in range(even_ref.shape[0]):
        out_ref[lax.bitwise_xor(tensor, 2 * e)] = even_ref[e]
        out_ref[lax.bitwise_xor(tensor, 2 * e + 1)] = odd_ref[e]


def merge_kernel(
    seq_count, parts_ref, fresh_ref, level_ref, low_ref, high_ref, mixed_ref, out_ref, wide
):
    peers = parts_ref.shape[0]
    rows = mixed_ref.shape[0]
    steps = rows // seq_count
    held_rows = fresh_ref.shape[0]
    per_seq = held_rows // seq_count
    heads = per_seq // steps
    mean_rows = padded(held_rows, 16)
    means = [parts_ref[b, 0:mean_rows, :].astype(jnp.float32) for b in range(peers)]
    levels = [
        parts_ref[b, mean_rows:, :].astype(jnp.float32)[0:per_seq] for b in range(peers)
    ]
    for n in range(seq_count):
        part = slice(n * per_seq, (n + 1) * per_seq)
        own = [
            level[:, 3 * n : 3 * n + 1]
            + (level[:, 3 * n + 1 : 3 * n + 2] + level[:, 3 * n + 2 : 3 * n + 3])
            for level in levels
        ]
        fresh_level = level_ref[part, 0:1]
        top = functools.reduce(jnp.maximum, own + [fresh_level])
        share = jnp.exp(fresh_level - top)
        total = share
        summed = share * fresh_ref[part, :]
        for b in range(peers):
            share = jnp.exp(own[b] - top)
            total = total + share
            summed = summed + share * means[b][part]
        mixed = summed / total
        for h in range(heads):
            wide[h, pl.ds(n, steps, stride=seq_count), :] = mixed[h * steps : (h + 1) * steps]
    attention = jnp.concatenate([wide[h, 0:rows, :] for h in range(heads)], axis=1)
    attention = attention.astype(jnp.bfloat16)
    mixed_ref[...] = attention
    project(attention, low_ref, high_ref, out_ref, 1 - lax.rem(lax.axis_index("tensor"), 2))


def project(attention, low_ref, high_ref, out_ref, y):
    width = out_ref.shape[2]
    cut = low_ref.shape[0]
    for p in range(out_ref.shape[0]):
        columns = pl.ds(pl.multiple_of((2 * p + y) * width, width), width)
        out_ref[p] = (
            jnp.dot(attention[:, :cut], low_ref[:, columns], preferred_element_type=jnp.float32)
            + jnp.dot(attention[:, cut:], high_ref[:, columns], preferred_element_type=jnp.float32)
        ).astype(out_ref.dtype)


def stay_kernel(attention_ref, low_ref, high_ref, out_ref):
    y = lax.rem(lax.axis_index("tensor"), 2)
    project(attention_ref[...], low_ref, high_ref, out_ref, y)


def sum_kernel(parts_ref, rest_ref, out_ref):
    total = rest_ref[...]
    for b in range(parts_ref.shape[0]):
        total = total + parts_ref[b].astype(jnp.float32)
    seqs = out_ref.shape[1]
    for s in range(out_ref.shape[0]):
        out_ref[s] = total[s * seqs : (s + 1) * seqs].astype(jnp.bfloat16)


def crossed(value, mask):
    pairs = [(source, source ^ mask) for source in range(lax.axis_size("tensor"))]
    return lax.ppermute(value, "tensor", pairs)


def exchanged_along_z(value):
    peers = lax.axis_size("tensor")
    groups = [list(range(y, peers, 2)) for y in range(2)]
    return lax.all_to_all(
        value, "tensor", split_axis=0, concat_axis=0, tiled=True, axis_index_groups=groups
    )


def exchanged(value):
    return lax.all_to_all(value, "tensor", split_axis=0, concat_axis=0, tiled=True)


def body(
    layer_input_hidden,
    rmsnorm_gain_weight,
    wq,
    wk,
    wv,
    wo,
    adapter_down_stored,
    adapter_up_query,
    adapter_up_value,
    adapter_block_owner,
    rotated_key_cache,
    cached_value_rows,
    cache_valid_lengths,
):
    f32, bf16 = jnp.float32, jnp.bfloat16
    shape = jax.ShapeDtypeStruct
    steps, seqs, model_width = layer_input_hidden.shape
    peers = lax.axis_size("tensor")
    tensor_index = lax.axis_index("tensor")
    rows = steps * seqs
    local_heads = wq.shape[1] // HEAD_DIM
    held_rows = rows * local_heads
    kv_width = wk.shape[1]
    width = model_width // peers
    group = QUERY_HEADS // KEY_VALUE_HEADS

    pairs = [(0, 1), (1, 0)]
    other_down = lax.ppermute(adapter_down_stored, "replica", pairs)
    other_up_query = lax.ppermute(adapter_up_query, "replica", pairs)
    other_up_value = lax.ppermute(adapter_up_value, "replica", pairs)

    normed, cosine, sine, rest = kernel_call(
        norm_kernel,
        (
            shape((rows, model_width), bf16),
            shape((rows, HEAD_DIM), f32),
            shape((rows, HEAD_DIM), f32),
            shape((rows, width), f32),
        ),
        [smem, far, vmem],
        (vmem,) * 4,
        [pltpu.VMEM(layer_input_hidden.shape, bf16), pltpu.SemaphoreType.DMA],
        limit=8,
    )(cache_valid_lengths, layer_input_hidden, rmsnorm_gain_weight.reshape(1, model_width))

    partial = kernel_call(
        functools.partial(shrink_kernel, peers),
        shape((rows, 2 * ADAPTER_RANK), f32),
        [smem, vmem, vmem, vmem],
        vmem,
        limit=4,
    )(adapter_block_owner, normed, adapter_down_stored, other_down)

    key_sum, value_sum = kernel_call(
        key_value_kernel,
        (shape((rows, kv_width), f32), shape((rows, kv_width), f32)),
        [vmem, far, far],
        (vmem, vmem),
        [pltpu.VMEM(wk.shape, bf16), pltpu.VMEM(wv.shape, bf16), pltpu.SemaphoreType.DMA((4,))],
        limit=8,
        moved=2 * wk.size * 2,
    )(normed, wk, wv)
    partial = partial + crossed(partial, 1)
    partial, normed, key_sum = lax.optimization_barrier((partial, normed, key_sum))
    shrink_parts = exchanged_along_z(
        jnp.broadcast_to(partial[None], (peers // 2,) + partial.shape)
    )

    chunks = 16
    query_sum = kernel_call(
        functools.partial(query_kernel, chunks),
        shape((rows, wq.shape[1]), f32),
        [vmem, far],
        vmem,
        [pltpu.VMEM(wq.shape, bf16), pltpu.SemaphoreType.DMA((chunks,))],
        limit=20,
        moved=wq.size * 2,
        flops=2 * rows * wq.size,
    )(normed, wq)

    queries, key_raw, value_raw = kernel_call(
        functools.partial(finish_kernel, seqs),
        (
            shape((held_rows, HEAD_DIM), bf16),
            shape((rows, kv_width), bf16),
            shape((rows, kv_width), bf16),
        ),
        [vmem] * 10,
        (vmem,) * 3,
        [
            pltpu.VMEM((local_heads, padded(rows, 8), HEAD_DIM), f32),
            pltpu.VMEM((held_rows, HEAD_DIM), f32),
        ],
        limit=4,
    )(
        query_sum, key_sum, value_sum, shrink_parts, adapter_up_query, other_up_query,
        adapter_up_value, other_up_value, cosine, sine,
    )
    held = jnp.stack([queries] + [crossed(queries, mask) for mask in range(2, peers, 2)])

    if kv_width != HEAD_DIM:
        kv_index = tensor_index * local_heads // group

        def own_head(value):
            heads = lax.all_gather(value, "tensor", axis=1, tiled=True)
            return lax.dynamic_slice_in_dim(heads, kv_index * HEAD_DIM, HEAD_DIM, 1)

        key_raw, value_raw = own_head(key_raw), own_head(value_raw)

    cache_shape = shape(rotated_key_cache.shape, bf16)
    fresh, fresh_level, keys_near, values_near = kernel_call(
        functools.partial(fresh_kernel, seqs),
        (
            shape((held_rows, HEAD_DIM), f32),
            shape((held_rows, HEAD_DIM), f32),
            cache_shape,
            cache_shape,
        ),
        [vmem] * 5 + [far] * 2,
        (vmem,) * 4,
        [pltpu.SemaphoreType.DMA((2,))],
        limit=4,
        moved=4 * rotated_key_cache.size,
    )(queries, key_raw, value_raw, cosine, sine, rotated_key_cache, cached_value_rows)

    others = crossed(held, 1)
    level_rows = padded(held_rows // seqs, 16)
    cut = wo.shape[0] // 2

    def cache_part(odd, queries_held):
        return kernel_call(
            functools.partial(cache_kernel, odd, odd * cut),
            (
                shape((peers // 2, padded(held_rows, 16) + level_rows, HEAD_DIM), bf16),
                shape((cut, wo.shape[1]), bf16),
            ),
            [smem, vmem, vmem, vmem, far],
            (vmem, vmem),
            [pltpu.SemaphoreType.DMA((4,))],
            limit=6,
            moved=wo.size,
        )(cache_valid_lengths, queries_held, keys_near, values_near, wo)

    even_parts, wo_low = cache_part(0, held)
    odd_parts, wo_high = cache_part(1, others)
    partials = kernel_call(
        order_kernel,
        shape((peers,) + even_parts.shape[1:], bf16),
        [vmem, vmem],
        vmem,
        limit=4,
    )(even_parts, odd_parts)
    received = exchanged(partials)

    mixed, shares_sent = kernel_call(
        functools.partial(merge_kernel, seqs),
        (shape((rows, local_heads * HEAD_DIM), bf16), shape((peers // 2, rows, width), bf16)),
        [vmem] * 5,
        (vmem, vmem),
        [pltpu.VMEM((local_heads, padded(rows, 8), HEAD_DIM), f32)],
        limit=6,
    )(received, fresh, fresh_level, wo_low, wo_high)
    shares_met = crossed(shares_sent, 1)
    shares_kept = kernel_call(
        stay_kernel,
        shape((peers // 2, rows, width), f32),
        [vmem] * 3,
        vmem,
        limit=4,
        moved=wo.size,
    )(mixed, wo_low, wo_high)
    shares = (shares_kept + shares_met.astype(f32)).astype(bf16)
    return kernel_call(
        sum_kernel,
        shape((steps, seqs, width), bf16),
        [vmem, vmem],
        vmem,
        limit=4,
    )(exchanged_along_z(shares), rest)


def solution(mesh):
    return jax.shard_map(
        body,
        mesh=mesh,
        in_specs=(
            P(None, ("groups", "replica"), None),
            P(),
            P(None, "tensor"),
            P(None, "tensor"),
            P(None, "tensor"),
            P("tensor", None),
            P(("replica", "tensor"), None),
            P("replica", "tensor"),
            P("replica", "tensor"),
            P(),
            P(("groups", "replica"), None, "tensor", None),
            P(("groups", "replica"), None, "tensor", None),
            P(("groups", "replica")),
        ),
        out_specs=P(None, ("groups", "replica"), "tensor"),
        check_vma=False,
    )
```

```python
import functools
import math

import jax
import jax.numpy as jnp
from jax import lax
from jax.experimental import pallas as pl
from jax.experimental.pallas import tpu as pltpu
from jax.sharding import PartitionSpec as P

QUERY_HEADS = 64
KEY_VALUE_HEADS = 8
HEAD_DIM = 128
ADAPTER_RANK = 64


adapter_scale = 2.0
rope_base = 500000.0
negative = -1e30
inv_root = 1.0 / math.sqrt(HEAD_DIM)
MIB = 1 << 20

vmem = pl.BlockSpec(memory_space=pltpu.VMEM)
smem = pl.BlockSpec(memory_space=pltpu.SMEM)
far = pl.BlockSpec(memory_space=pl.ANY)


def padded(count, multiple):
    return -(-count // multiple) * multiple


def rows_padded(value, rows):
    if value.shape[0] == rows:
        return value
    filler = jnp.zeros((rows - value.shape[0],) + value.shape[1:], value.dtype)
    return jnp.concatenate([value, filler], axis=0)


def kernel_call(kernel, outs, specs, out_specs, scratch=(), limit=16, moved=0, flops=0):
    call = pl.pallas_call(
        kernel,
        out_shape=outs,
        in_specs=specs,
        out_specs=out_specs,
        scratch_shapes=list(scratch),
        compiler_params=pltpu.CompilerParams(vmem_limit_bytes=limit * MIB),
        cost_estimate=pl.CostEstimate(flops=flops, bytes_accessed=moved, transcendentals=0),
    )

    def run(*operands):
        return call(
            *[
                pltpu.with_memory_space_constraint(operand, pltpu.HBM) if spec is far else operand
                for operand, spec in zip(operands, specs)
            ]
        )

    return run


def fetches(pairs, sem):
    copies = [
        pltpu.make_async_copy(far_ref, near, sem.at[k]) for k, (far_ref, near) in enumerate(pairs)
    ]
    for copy in copies:
        copy.start()
    return copies


def row_parts(far_ref, near, first, pieces):
    span = near.shape[0] // pieces
    return [
        (far_ref.at[pl.ds(first + c * span, span)], near.at[pl.ds(c * span, span)])
        for c in range(pieces)
    ]


def place_of(owner_ref, held):
    place = jnp.int32(0)
    for j in range(owner_ref.shape[0]):
        place = jnp.where(owner_ref[j] == held, jnp.int32(j), place)
    return place


def block_product(normed_ref, place, stored):
    block_rows = stored.shape[0]
    columns = pl.ds(pl.multiple_of(place * block_rows, block_rows), block_rows)
    return jnp.dot(normed_ref[:, columns], stored[...], preferred_element_type=jnp.float32)


def norm_kernel(
    peers, heads, lengths_ref, owner_ref, x_ref, down_ref, gain_ref,
    normed_ref, cos_ref, sin_ref, rest_ref, reach_ref, shrunk_ref, other_ref,
    lengths, owner, x_buf, down_buf, sem,
):
    copies = fetches(
        [(lengths_ref, lengths), (owner_ref, owner), (x_ref, x_buf), (down_ref, down_buf)], sem
    )
    steps, seqs, _ = x_ref.shape
    rows, width = rest_ref.shape
    half = HEAD_DIM // 2
    row = lax.broadcasted_iota(jnp.int32, (rows, HEAD_DIM), 0)
    lane = lax.broadcasted_iota(jnp.int32, (rows, HEAD_DIM), 1)
    copies[0].wait()
    positions = jnp.zeros((rows, HEAD_DIM), jnp.int32)
    for s in range(steps):
        for n in range(seqs):
            positions = jnp.where(row == s * seqs + n, lengths[n] + s, positions)
    low = lane < half
    exponent = jnp.where(low, lane, lane - half).astype(jnp.float32) * (2.0 / HEAD_DIM)
    angles = positions.astype(jnp.float32) * jnp.exp(exponent * -math.log(rope_base))
    sine = jnp.sin(angles)
    cos_ref[...] = jnp.cos(angles)
    sin_ref[...] = jnp.where(low, -sine, sine)
    place = lax.broadcasted_iota(jnp.int32, reach_ref.shape, 1)
    reach = jnp.zeros(reach_ref.shape, jnp.int32)
    per_seq = heads * steps
    for n in range(seqs):
        mine = jnp.logical_and(place >= n * per_seq, place < (n + 1) * per_seq)
        reach = jnp.where(mine, lengths[n], reach)
    reach_ref[...] = reach
    copies[2].wait()
    values = jnp.concatenate([x_buf[s].astype(jnp.float32) for s in range(steps)], axis=0)
    factor = lax.rsqrt(jnp.mean(values * values, axis=-1, keepdims=True) + 1e-05)
    normed = values * factor * gain_ref[...].astype(jnp.float32)
    normed_ref[...] = normed.astype(jnp.bfloat16)
    replica, tensor = lax.axis_index("replica"), lax.axis_index("tensor")
    for s in range(steps):
        part = x_buf[s, :, pl.ds(pl.multiple_of(tensor * width, width), width)]
        rest_ref[s * seqs : (s + 1) * seqs, :] = part.astype(jnp.float32)
    copies[1].wait()
    copies[3].wait()
    shrunk_ref[...] = block_product(
        normed_ref, place_of(owner, replica * peers + tensor), down_buf
    )
    other_ref[0] = place_of(owner, (1 - replica) * peers + tensor)


def shrink_kernel(place_ref, normed_ref, other_ref, own_ref, out_ref):
    out_ref[...] = own_ref[...] + block_product(normed_ref, place_ref[0], other_ref)


def key_value_kernel(normed_ref, wk_ref, wv_ref, key_ref, value_ref, wk_buf, wv_buf, sem):
    halves = 2
    span = wk_ref.shape[0] // halves
    copies = []
    for far_ref, near, out, k in ((wk_ref, wk_buf, key_ref, 0), (wv_ref, wv_buf, value_ref, 1)):
        for c in range(halves):
            part = pl.ds(c * span, span)
            copies.append(
                pltpu.make_async_copy(far_ref.at[part], near.at[part], sem.at[halves * k + c])
            )
    for copy in copies:
        copy.start()
    for near, out, k in ((wk_buf, key_ref, 0), (wv_buf, value_ref, 1)):
        total = jnp.zeros(out.shape, jnp.float32)
        for c in range(halves):
            copies[halves * k + c].wait()
            total = total + jnp.dot(
                normed_ref[:, c * span : (c + 1) * span],
                near[c * span : (c + 1) * span, :],
                preferred_element_type=jnp.float32,
            )
        out[...] = total


def query_kernel(chunks, normed_ref, wq_ref, out_ref, wq_buf, sem):
    span = wq_ref.shape[0] // chunks

    def part(c):
        rows = pl.ds(c * span, span)
        return pltpu.make_async_copy(wq_ref.at[rows], wq_buf.at[rows], sem.at[c])

    for c in range(chunks):
        part(c).start()
    total = jnp.zeros(out_ref.shape, jnp.float32)
    for c in range(chunks):
        part(c).wait()
        total = total + jnp.dot(
            normed_ref[:, c * span : (c + 1) * span],
            wq_buf[c * span : (c + 1) * span, :],
            preferred_element_type=jnp.float32,
        )
    out_ref[...] = total


def rotated(values, cosine, sine):
    half = HEAD_DIM // 2
    turned = jnp.concatenate([values[:, half:], values[:, :half]], axis=1)
    return values * cosine + turned * sine


def finish_kernel(
    seq_count, acc_ref, key_ref, value_ref, uq_own, uq_other, uv_own, uv_other,
    cos_ref, sin_ref, *parts_and_outs,
):
    parts, (query_ref, keyout_ref, valueout_ref, wide, tall) = parts_and_outs[:-5], parts_and_outs[-5:]
    first = lax.axis_index("replica") == 0
    rows = acc_ref.shape[0]
    steps = rows // seq_count
    heads = acc_ref.shape[1] // HEAD_DIM
    shrunk = functools.reduce(jnp.add, [part[...] for part in parts])
    shrunk = shrunk.astype(jnp.bfloat16).astype(jnp.float32)
    half = ADAPTER_RANK // 2

    def lifted(low, high, own, other):
        mine = jnp.where(first, low, high).astype(jnp.bfloat16)
        theirs = jnp.where(first, high, low).astype(jnp.bfloat16)
        return adapter_scale * (
            jnp.dot(mine, own[...], preferred_element_type=jnp.float32)
            + jnp.dot(theirs, other[...], preferred_element_type=jnp.float32)
        )

    raw = acc_ref[...] + lifted(shrunk[:, :half], shrunk[:, half : 2 * half], uq_own, uq_other)
    raw = raw.astype(jnp.bfloat16).astype(jnp.float32)
    cosine, sine = cos_ref[...], sin_ref[...]
    for h in range(heads):
        columns = slice(h * HEAD_DIM, (h + 1) * HEAD_DIM)
        wide[h, 0:rows, :] = rotated(raw[:, columns], cosine, sine)
    for n in range(seq_count):
        for h in range(heads):
            tall[pl.ds((n * heads + h) * steps, steps), :] = wide[
                h, pl.ds(n, steps, stride=seq_count), :
            ]
    query_ref[...] = tall[...].astype(jnp.bfloat16)
    keyout_ref[...] = key_ref[...].astype(jnp.bfloat16)
    value = value_ref[...] + lifted(
        shrunk[:, 2 * half : 3 * half], shrunk[:, 3 * half :], uv_own, uv_other
    )
    valueout_ref[...] = value.astype(jnp.bfloat16)


def fresh_kernel(
    seq_count, query_ref, key_ref, value_ref, cos_ref, sin_ref, kc_ref, vc_ref,
    fresh_ref, level_ref, query_out, kc_out, vc_out, sem,
):
    copies = fetches([(kc_ref, kc_out), (vc_ref, vc_out)], sem)
    lane = lax.broadcasted_iota(jnp.int32, (1, HEAD_DIM), 1)
    columns = []
    steps = key_ref.shape[0] // seq_count
    per_seq = fresh_ref.shape[0] // seq_count
    query_out[...] = query_ref[...]
    queries = query_ref[...].astype(jnp.float32)
    keys = rotated(key_ref[...].astype(jnp.float32), cos_ref[...], sin_ref[...])
    keys = keys.astype(jnp.bfloat16).astype(jnp.float32)
    values = value_ref[...].astype(jnp.float32)
    step = lax.rem(lax.broadcasted_iota(jnp.int32, (per_seq, 1), 0), steps)
    for n in range(seq_count):
        rows = slice(n * per_seq, (n + 1) * per_seq)
        query = queries[rows]
        scores = []
        for t in range(steps):
            place = t * seq_count + n
            score = jnp.sum(query * keys[place : place + 1], axis=-1, keepdims=True) * inv_root
            scores.append(jnp.where(step >= t, score, negative))
        top = functools.reduce(jnp.maximum, scores)
        weights = [
            jnp.where(step >= t, jnp.exp(score - top), 0.0) for t, score in enumerate(scores)
        ]
        total = functools.reduce(jnp.add, weights)
        summed = jnp.zeros((per_seq, HEAD_DIM), jnp.float32)
        for t, weight in enumerate(weights):
            place = t * seq_count + n
            summed = summed + weight.astype(jnp.bfloat16).astype(jnp.float32) * values[
                place : place + 1
            ]
        fresh_ref[rows, :] = summed
        columns.append(jnp.where(lane == 0, top, jnp.where(lane == 1, total, 0.0)))
    columns = rows_padded(jnp.concatenate(columns, axis=0), HEAD_DIM)
    level_ref[...] = jnp.transpose(columns)[0 : level_ref.shape[0], :]
    for copy in copies:
        copy.wait()


def pieces_of(top, total):
    rows = lax.broadcasted_iota(jnp.int32, (16, HEAD_DIM), 0)
    packed = jnp.zeros((16, HEAD_DIM), jnp.float32)
    for first, left in ((0, top), (3, total)):
        for c in range(3):
            piece = left.astype(jnp.bfloat16).astype(jnp.float32)
            left = left - piece
            packed = jnp.where(rows == first + c, piece, packed)
    return packed.astype(jnp.bfloat16)


def top_and_total(part_ref, held_rows):
    pieces = part_ref[padded(held_rows, 16) :, :].astype(jnp.float32)
    return (
        pieces[0:1] + (pieces[1:2] + pieces[2:3]),
        pieces[3:4] + (pieces[4:5] + pieces[5:6]),
    )


def turned_rows(rows):
    count = padded(len(rows), 8)
    place = lax.broadcasted_iota(jnp.int32, (count, HEAD_DIM), 0)
    stacked = jnp.zeros((count, HEAD_DIM), jnp.float32)
    for k, row in enumerate(rows):
        stacked = jnp.where(place == k, row, stacked)
    return jnp.transpose(rows_padded(stacked, HEAD_DIM))


def cache_kernel(
    done_ref, reach_ref, even_ref, odd_ref, kc_ref, vc_ref, wo_ref,
    even_out, odd_out, wo_out, sem, *, first,
):
    copies = fetches(row_parts(wo_ref, wo_out, first, 2), sem)
    entries, held_rows, _ = even_ref.shape
    seq_count, kv_heads, span, _ = kc_ref.shape
    peers = 2 * entries
    per_seq = held_rows // seq_count
    mean_rows = padded(held_rows, 16)
    tensor = lax.axis_index("tensor")
    spots = tensor * span + lax.broadcasted_iota(jnp.int32, (span, HEAD_DIM), 0)
    live = spots < reach_ref[0:1, :]
    lane = lax.broadcasted_iota(jnp.int32, (span, HEAD_DIM), 1)
    for e in range(peers):
        query_ref, out_ref = (odd_ref, odd_out) if e % 2 else (even_ref, even_out)
        head = lax.bitwise_xor(tensor, e) * kv_heads // peers
        queries = rows_padded(query_ref[e // 2].astype(jnp.float32), HEAD_DIM)
        turned = jnp.transpose(queries).astype(jnp.bfloat16)
        scores = None
        for n in range(seq_count):
            score = jnp.dot(kc_ref[n, head], turned, preferred_element_type=jnp.float32)
            scores = score if n == 0 else jnp.where(lane < n * per_seq, scores, score)
        scores = jnp.where(live, scores, negative)
        top = jnp.maximum(jnp.max(scores, axis=0, keepdims=True), 0.1 * negative)
        weights = jnp.exp((scores - top) * inv_root)
        total = jnp.sum(weights, axis=0, keepdims=True)
        weights = jnp.transpose(weights)
        sums = [
            jnp.dot(
                weights[n * per_seq : (n + 1) * per_seq].astype(jnp.bfloat16),
                vc_ref[n, head],
                preferred_element_type=jnp.float32,
            )
            for n in range(seq_count)
        ]
        sums = rows_padded(jnp.concatenate(sums, axis=0), mean_rows)
        out_ref[e // 2, 0:mean_rows, :] = sums.astype(jnp.bfloat16)
        out_ref[e // 2, mean_rows:, :] = pieces_of(top * inv_root, total)
    for copy in copies:
        copy.wait()


def fetch_kernel(after_ref, wo_ref, wo_out, done_out, sem, *, first):
    copies = fetches(row_parts(wo_ref, wo_out, first, 2), sem)
    done_out[...] = jnp.zeros(done_out.shape, jnp.float32)
    for copy in copies:
        copy.wait()


def blend_kernel(held_rows, done_ref, own_ref, met_ref, *outs):
    mean_rows = padded(held_rows, 16)
    rows, kept = [], []
    for p in range(len(outs)):
        own_top, own_total = top_and_total(own_ref.at[p], held_rows)
        met_top, met_total = top_and_total(met_ref.at[p], held_rows)
        top = jnp.maximum(own_top, met_top)
        own_factor, met_factor = jnp.exp(own_top - top), jnp.exp(met_top - top)
        rows += [own_factor, met_factor]
        kept.append((top, own_factor * own_total + met_factor * met_total))
    columns = turned_rows(rows)
    for p, out_ref in enumerate(outs):
        sums = (
            own_ref[p, 0:mean_rows, :].astype(jnp.float32) * columns[0:mean_rows, 2 * p : 2 * p + 1]
            + met_ref[p, 0:mean_rows, :].astype(jnp.float32)
            * columns[0:mean_rows, 2 * p + 1 : 2 * p + 2]
        )
        out_ref[0:mean_rows, :] = sums.astype(jnp.bfloat16)
        out_ref[mean_rows:, :] = pieces_of(*kept[p])


def merge_kernel(seq_count, block_count, *refs):
    blocks, refs = refs[:block_count], refs[block_count:]
    fresh_ref, level_ref, refs = refs[0], refs[1], refs[2:]
    wo_refs, (mixed_ref, out_ref, wide) = refs[:-3], refs[-3:]
    rows = mixed_ref.shape[0]
    steps = rows // seq_count
    held_rows = fresh_ref.shape[0]
    per_seq = held_rows // seq_count
    heads = per_seq // steps
    stats = [top_and_total(block, held_rows) for block in blocks]
    stats.append((level_ref[0:1, :], level_ref[1:2, :]))
    top = functools.reduce(jnp.maximum, [stat[0] for stat in stats])
    factors = [jnp.exp(stat[0] - top) for stat in stats]
    total = functools.reduce(jnp.add, [factor * stat[1] for factor, stat in zip(factors, stats)])
    total = jnp.where(total > 0.0, total, 1.0)
    columns = turned_rows([factor / total for factor in factors])
    mixed = fresh_ref[...] * columns[0:held_rows, block_count : block_count + 1]
    for b, block in enumerate(blocks):
        mixed = mixed + (
            block[0 : padded(held_rows, 16), :].astype(jnp.float32)[0:held_rows]
            * columns[0:held_rows, b : b + 1]
        )
    for n in range(seq_count):
        for h in range(heads):
            first = n * per_seq + h * steps
            wide[h, pl.ds(n, steps, stride=seq_count), :] = mixed[first : first + steps]
    attention = jnp.concatenate([wide[h, 0:rows, :] for h in range(heads)], axis=1)
    attention = attention.astype(jnp.bfloat16)
    mixed_ref[...] = attention
    project(attention, wo_refs, out_ref, 1)


def project(attention, wo_refs, out_ref, odd):
    rows = attention.shape[0]
    folds = out_ref.shape[1] // rows
    lanes = out_ref.shape[2]
    width = folds * lanes
    cut = wo_refs[0].shape[0]
    tensor = lax.axis_index("tensor")
    for p in range(out_ref.shape[0]):
        first = lax.bitwise_xor(tensor, 2 * p + odd) * width
        columns = pl.ds(pl.multiple_of(first, width), width)
        total = functools.reduce(
            jnp.add,
            [
                jnp.dot(
                    attention[:, k * cut : (k + 1) * cut],
                    wo_ref[:, columns],
                    preferred_element_type=jnp.float32,
                )
                for k, wo_ref in enumerate(wo_refs)
            ],
        )
        if folds > 1:
            total = jnp.concatenate(
                [total[:, c * lanes : (c + 1) * lanes] for c in range(folds)], axis=0
            )
        out_ref[p] = total.astype(out_ref.dtype)


def stay_kernel(attention_ref, *refs):
    project(attention_ref[...], refs[:-1], refs[-1], 0)


def sum_kernel(rest_ref, *refs):
    parts, out_ref = refs[:-1], refs[-1]
    total = functools.reduce(jnp.add, [part[...].astype(jnp.float32) for part in parts])
    rows = rest_ref.shape[0]
    steps, seqs, _ = out_ref.shape
    folds, lanes = total.shape[0] // rows, total.shape[1]
    for c in range(folds):
        columns = slice(c * lanes, (c + 1) * lanes)
        piece = total[c * rows : (c + 1) * rows] + rest_ref[:, columns]
        for s in range(steps):
            out_ref[s, :, columns] = piece[s * seqs : (s + 1) * seqs].astype(jnp.bfloat16)


def crossed(value, mask):
    pairs = [(source, source ^ mask) for source in range(lax.axis_size("tensor"))]
    return lax.ppermute(value, "tensor", pairs)


def along_z(values):
    return [values[0]] + [crossed(value, 2 * p) for p, value in enumerate(values) if p]


def body(
    layer_input_hidden,
    rmsnorm_gain_weight,
    wq,
    wk,
    wv,
    wo,
    adapter_down_stored,
    adapter_up_query,
    adapter_up_value,
    adapter_block_owner,
    rotated_key_cache,
    cached_value_rows,
    cache_valid_lengths,
):
    f32, bf16 = jnp.float32, jnp.bfloat16
    shape = jax.ShapeDtypeStruct
    steps, seqs, model_width = layer_input_hidden.shape
    peers = lax.axis_size("tensor")
    tensor_index = lax.axis_index("tensor")
    rows = steps * seqs
    local_heads = wq.shape[1] // HEAD_DIM
    held_rows = rows * local_heads
    kv_width = wk.shape[1]
    width = model_width // peers
    group = QUERY_HEADS // KEY_VALUE_HEADS

    pairs = [(0, 1), (1, 0)]
    other_down = lax.ppermute(adapter_down_stored, "replica", pairs)
    other_up_query = lax.ppermute(adapter_up_query, "replica", pairs)
    other_up_value = lax.ppermute(adapter_up_value, "replica", pairs)

    block_shape = (padded(held_rows, 16) + 16, HEAD_DIM)
    normed, cosine, sine, rest, reach, own_shrunk, place = kernel_call(
        functools.partial(norm_kernel, peers, local_heads),
        (
            shape((rows, model_width), bf16),
            shape((rows, HEAD_DIM), f32),
            shape((rows, HEAD_DIM), f32),
            shape((rows, width), f32),
            shape((8, HEAD_DIM), jnp.int32),
            shape((rows, 2 * ADAPTER_RANK), f32),
            shape((1,), jnp.int32),
        ),
        [far] * 4 + [vmem],
        (vmem,) * 6 + (smem,),
        [
            pltpu.SMEM(cache_valid_lengths.shape, jnp.int32),
            pltpu.SMEM(adapter_block_owner.shape, jnp.int32),
            pltpu.VMEM(layer_input_hidden.shape, bf16),
            pltpu.VMEM(adapter_down_stored.shape, bf16),
            pltpu.SemaphoreType.DMA((4,)),
        ],
        limit=8,
    )(
        cache_valid_lengths, adapter_block_owner, layer_input_hidden, adapter_down_stored,
        rmsnorm_gain_weight.reshape(1, model_width),
    )
    own_shrunk, other_down, other_up_query, other_up_value = lax.optimization_barrier(
        (own_shrunk, other_down, other_up_query, other_up_value)
    )
    partial = kernel_call(
        shrink_kernel,
        shape((rows, 2 * ADAPTER_RANK), f32),
        [smem, vmem, vmem, vmem],
        vmem,
        limit=4,
    )(place, normed, other_down, own_shrunk)

    key_sum, value_sum = kernel_call(
        key_value_kernel,
        (shape((rows, kv_width), f32), shape((rows, kv_width), f32)),
        [vmem, far, far],
        (vmem, vmem),
        [pltpu.VMEM(wk.shape, bf16), pltpu.VMEM(wv.shape, bf16), pltpu.SemaphoreType.DMA((4,))],
        limit=8,
        moved=2 * wk.size * 2,
    )(normed, wk, wv)
    partial = partial + crossed(partial, 1)
    partial, normed, key_sum = lax.optimization_barrier((partial, normed, key_sum))
    shrink_parts = along_z([partial] * (peers // 2))

    chunks = 16
    query_sum = kernel_call(
        functools.partial(query_kernel, chunks),
        shape((rows, wq.shape[1]), f32),
        [vmem, far],
        vmem,
        [pltpu.VMEM(wq.shape, bf16), pltpu.SemaphoreType.DMA((chunks,))],
        limit=20,
        moved=wq.size * 2,
        flops=2 * rows * wq.size,
    )(normed, wq)

    queries, key_raw, value_raw = kernel_call(
        functools.partial(finish_kernel, seqs),
        (
            shape((held_rows, HEAD_DIM), bf16),
            shape((rows, kv_width), bf16),
            shape((rows, kv_width), bf16),
        ),
        [vmem] * (9 + peers // 2),
        (vmem,) * 3,
        [
            pltpu.VMEM((local_heads, padded(rows, 8), HEAD_DIM), f32),
            pltpu.VMEM((held_rows, HEAD_DIM), f32),
        ],
        limit=4,
    )(
        query_sum, key_sum, value_sum, adapter_up_query, other_up_query,
        adapter_up_value, other_up_value, cosine, sine, *shrink_parts,
    )
    met_queries = along_z([queries] * (peers // 2))[1:]

    if kv_width != HEAD_DIM:
        kv_index = tensor_index * local_heads // group

        def own_head(value):
            heads = lax.all_gather(value, "tensor", axis=1, tiled=True)
            return lax.dynamic_slice_in_dim(heads, kv_index * HEAD_DIM, HEAD_DIM, 1)

        key_raw, value_raw = own_head(key_raw), own_head(value_raw)

    cache_shape = shape(rotated_key_cache.shape, bf16)
    fresh, fresh_level, queries, keys_near, values_near = kernel_call(
        functools.partial(fresh_kernel, seqs),
        (
            shape((held_rows, HEAD_DIM), f32),
            shape((8, HEAD_DIM), f32),
            shape((held_rows, HEAD_DIM), bf16),
            cache_shape,
            cache_shape,
        ),
        [vmem] * 5 + [far] * 2,
        (vmem,) * 5,
        [pltpu.SemaphoreType.DMA((2,))],
        limit=4,
        moved=4 * rotated_key_cache.size,
    )(queries, key_raw, value_raw, cosine, sine, rotated_key_cache, cached_value_rows)

    held = jnp.stack([queries] + met_queries)

    cut = wo.shape[0] // 4
    wo_shape = shape((cut, wo.shape[1]), bf16)

    def wo_part(k, after):
        return kernel_call(
            functools.partial(fetch_kernel, first=k * cut),
            (wo_shape, shape((8, HEAD_DIM), f32)),
            [vmem, far],
            (vmem, vmem),
            [pltpu.SemaphoreType.DMA((2,))],
            limit=2,
            moved=wo.size // 2,
        )(after, wo)

    others = crossed(held, 1)
    wo_near, done = wo_part(0, held)
    wo_parts = [wo_near]
    parts_shape = shape((peers // 2,) + block_shape, bf16)
    even_parts, odd_parts, wo_near = kernel_call(
        functools.partial(cache_kernel, first=cut),
        (parts_shape, parts_shape, wo_shape),
        [vmem] * 6 + [far],
        (vmem,) * 3,
        [pltpu.SemaphoreType.DMA((2,))],
        limit=8,
        moved=wo.size // 2,
    )(done, reach, held, others, keys_near, values_near, wo)
    wo_parts.append(wo_near)

    met_parts = crossed(odd_parts, 1)
    wo_near, done = wo_part(2, odd_parts)
    wo_parts.append(wo_near)
    blended = kernel_call(
        functools.partial(blend_kernel, held_rows),
        (shape(block_shape, bf16),) * (peers // 2),
        [vmem] * 3,
        (vmem,) * (peers // 2),
        limit=4,
    )(done, even_parts, met_parts)
    wo_parts.append(wo_part(3, blended[0])[0])
    received = along_z(blended)

    folds = width // 256 if (rows * (width // 256)) % 16 == 0 else 1
    share_shape = (peers // 2, rows * folds, width // folds)
    mixed, shares_sent = kernel_call(
        functools.partial(merge_kernel, seqs, peers // 2),
        (shape((rows, local_heads * HEAD_DIM), bf16), shape(share_shape, bf16)),
        [vmem] * (peers // 2 + 6),
        (vmem, vmem),
        [pltpu.VMEM((local_heads, padded(rows, 8), HEAD_DIM), f32)],
        limit=6,
    )(*received, fresh, fresh_level, *wo_parts)
    shares_met = crossed(shares_sent, 1)
    shares_kept = kernel_call(
        stay_kernel,
        shape(share_shape, f32),
        [vmem] * 5,
        vmem,
        limit=4,
        moved=wo.size,
    )(mixed, *wo_parts)
    shares = (shares_kept + shares_met.astype(f32)).astype(bf16)
    return kernel_call(
        sum_kernel,
        shape((steps, seqs, width), bf16),
        [vmem] * (1 + peers // 2),
        vmem,
        limit=4,
    )(rest, *along_z([shares[p] for p in range(peers // 2)]))


def solution(mesh):
    return jax.shard_map(
        body,
        mesh=mesh,
        in_specs=(
            P(None, ("groups", "replica"), None),
            P(),
            P(None, "tensor"),
            P(None, "tensor"),
            P(None, "tensor"),
            P("tensor", None),
            P(("replica", "tensor"), None),
            P("replica", "tensor"),
            P("replica", "tensor"),
            P(),
            P(("groups", "replica"), None, "tensor", None),
            P(("groups", "replica"), None, "tensor", None),
            P(("groups", "replica")),
        ),
        out_specs=P(None, ("groups", "replica"), "tensor"),
        check_vma=False,
    )
```

```python
import functools
import math

import jax
import jax.numpy as jnp
from jax import lax
from jax.experimental import pallas as pl
from jax.experimental.pallas import tpu as pltpu
from jax.sharding import PartitionSpec as P

QUERY_HEADS = 64
KEY_VALUE_HEADS = 8
HEAD_DIM = 128
ADAPTER_RANK = 64


adapter_scale = 2.0
rope_base = 500000.0
negative = -1e30
inv_root = 1.0 / math.sqrt(HEAD_DIM)
MIB = 1 << 20

vmem = pl.BlockSpec(memory_space=pltpu.VMEM)
smem = pl.BlockSpec(memory_space=pltpu.SMEM)
far = pl.BlockSpec(memory_space=pl.ANY)


def padded(count, multiple):
    return -(-count // multiple) * multiple


def rows_padded(value, rows):
    if value.shape[0] == rows:
        return value
    filler = jnp.zeros((rows - value.shape[0],) + value.shape[1:], value.dtype)
    return jnp.concatenate([value, filler], axis=0)


def kernel_call(kernel, outs, specs, out_specs, scratch=(), limit=16, moved=0, flops=0):
    call = pl.pallas_call(
        kernel,
        out_shape=outs,
        in_specs=specs,
        out_specs=out_specs,
        scratch_shapes=list(scratch),
        compiler_params=pltpu.CompilerParams(vmem_limit_bytes=limit * MIB),
        cost_estimate=pl.CostEstimate(flops=flops, bytes_accessed=moved, transcendentals=0),
    )

    def run(*operands):
        return call(
            *[
                pltpu.with_memory_space_constraint(operand, pltpu.HBM) if spec is far else operand
                for operand, spec in zip(operands, specs)
            ]
        )

    return run


def fetches(pairs, sem):
    copies = [
        pltpu.make_async_copy(far_ref, near, sem.at[k]) for k, (far_ref, near) in enumerate(pairs)
    ]
    for copy in copies:
        copy.start()
    return copies


def row_parts(far_ref, near, first, pieces):
    span = near.shape[0] // pieces
    return [
        (far_ref.at[pl.ds(first + c * span, span)], near.at[pl.ds(c * span, span)])
        for c in range(pieces)
    ]


def place_of(owner_ref, held):
    place = jnp.int32(0)
    for j in range(owner_ref.shape[0]):
        place = jnp.where(owner_ref[j] == held, jnp.int32(j), place)
    return place


def block_product(normed_ref, place, stored):
    block_rows = stored.shape[0]
    columns = pl.ds(pl.multiple_of(place * block_rows, block_rows), block_rows)
    return jnp.dot(normed_ref[:, columns], stored[...], preferred_element_type=jnp.float32)


def norm_kernel(
    peers, heads, lengths_ref, owner_ref, x_ref, down_ref, gain_ref, other_ref,
    normed_ref, cos_ref, sin_ref, rest_ref, reach_ref, shrunk_ref,
    lengths, owner, x_buf, down_buf, gain, sem,
):
    copies = fetches(
        [
            (lengths_ref, lengths),
            (owner_ref, owner),
            (x_ref, x_buf),
            (down_ref, down_buf),
            (gain_ref, gain),
        ],
        sem,
    )
    steps, seqs, _ = x_ref.shape
    rows, width = rest_ref.shape
    half = HEAD_DIM // 2
    row = lax.broadcasted_iota(jnp.int32, (rows, HEAD_DIM), 0)
    lane = lax.broadcasted_iota(jnp.int32, (rows, HEAD_DIM), 1)
    copies[0].wait()
    positions = jnp.zeros((rows, HEAD_DIM), jnp.int32)
    for s in range(steps):
        for n in range(seqs):
            positions = jnp.where(row == s * seqs + n, lengths[n] + s, positions)
    low = lane < half
    exponent = jnp.where(low, lane, lane - half).astype(jnp.float32) * (2.0 / HEAD_DIM)
    angles = positions.astype(jnp.float32) * jnp.exp(exponent * -math.log(rope_base))
    sine = jnp.sin(angles)
    cos_ref[...] = jnp.cos(angles)
    sin_ref[...] = jnp.where(low, -sine, sine)
    place = lax.broadcasted_iota(jnp.int32, reach_ref.shape, 1)
    reach = jnp.zeros(reach_ref.shape, jnp.int32)
    per_seq = heads * steps
    for n in range(seqs):
        mine = jnp.logical_and(place >= n * per_seq, place < (n + 1) * per_seq)
        reach = jnp.where(mine, lengths[n], reach)
    reach_ref[...] = reach
    copies[2].wait()
    values = jnp.concatenate([x_buf[s].astype(jnp.float32) for s in range(steps)], axis=0)
    factor = lax.rsqrt(jnp.mean(values * values, axis=-1, keepdims=True) + 1e-05)
    copies[4].wait()
    normed = values * factor * gain[...].astype(jnp.float32).reshape(1, -1)
    normed_ref[...] = normed.astype(jnp.bfloat16)
    replica, tensor = lax.axis_index("replica"), lax.axis_index("tensor")
    for s in range(steps):
        part = x_buf[s, :, pl.ds(pl.multiple_of(tensor * width, width), width)]
        rest_ref[s * seqs : (s + 1) * seqs, :] = part.astype(jnp.float32)
    copies[1].wait()
    copies[3].wait()
    shrunk_ref[...] = block_product(
        normed_ref, place_of(owner, replica * peers + tensor), down_buf
    ) + block_product(normed_ref, place_of(owner, (1 - replica) * peers + tensor), other_ref)


def key_value_kernel(chunks, normed_ref, wk_ref, wv_ref, key_ref, value_ref, both, sem):
    width = wk_ref.shape[1]
    span = wk_ref.shape[0] // chunks
    joined = len(both.shape) == 2

    def near(k, c):
        rows = pl.ds(c * span, span)
        return both.at[rows, pl.ds(k * width, width)] if joined else both.at[k, rows]

    copies = [
        [
            pltpu.make_async_copy(far_ref.at[pl.ds(c * span, span)], near(k, c), sem.at[k, c])
            for k, far_ref in enumerate((wk_ref, wv_ref))
        ]
        for c in range(chunks)
    ]
    for pair in copies:
        for copy in pair:
            copy.start()
    total = jnp.zeros((normed_ref.shape[0], 2 * width), jnp.float32)
    for c, pair in enumerate(copies):
        for copy in pair:
            copy.wait()
        rows = slice(c * span, (c + 1) * span)
        if joined:
            weights = both[rows, :]
        else:
            weights = jnp.concatenate([both[k, rows, :] for k in range(2)], axis=1)
        total = total + jnp.dot(normed_ref[:, rows], weights, preferred_element_type=jnp.float32)
    key_ref[...] = total[:, :width]
    value_ref[...] = total[:, width:]


def query_kernel(chunks, normed_ref, wq_ref, out_ref, wq_buf, sem):
    span = wq_ref.shape[0] // chunks

    def part(c):
        rows = pl.ds(c * span, span)
        return pltpu.make_async_copy(wq_ref.at[rows], wq_buf.at[rows], sem.at[c])

    for c in range(chunks):
        part(c).start()
    total = jnp.zeros(out_ref.shape, jnp.float32)
    for c in range(chunks):
        part(c).wait()
        total = total + jnp.dot(
            normed_ref[:, c * span : (c + 1) * span],
            wq_buf[c * span : (c + 1) * span, :],
            preferred_element_type=jnp.float32,
        )
    out_ref[...] = total


def rotated(values, cosine, sine):
    half = HEAD_DIM // 2
    turned = jnp.concatenate([values[:, half:], values[:, :half]], axis=1)
    return values * cosine + turned * sine


def finish_kernel(
    seq_count, acc_ref, key_ref, value_ref, uq_own, uq_other, uv_own, uv_other,
    cos_ref, sin_ref, *parts_and_outs,
):
    parts, (query_ref, keyout_ref, valueout_ref, wide, tall) = parts_and_outs[:-5], parts_and_outs[-5:]
    first = lax.axis_index("replica") == 0
    rows = acc_ref.shape[0]
    steps = rows // seq_count
    heads = acc_ref.shape[1] // HEAD_DIM
    shrunk = functools.reduce(jnp.add, [part[...] for part in parts])
    shrunk = shrunk.astype(jnp.bfloat16).astype(jnp.float32)
    half = ADAPTER_RANK // 2

    def lifted(low, high, own, other):
        mine = jnp.where(first, low, high).astype(jnp.bfloat16)
        theirs = jnp.where(first, high, low).astype(jnp.bfloat16)
        return adapter_scale * (
            jnp.dot(mine, own[...], preferred_element_type=jnp.float32)
            + jnp.dot(theirs, other[...], preferred_element_type=jnp.float32)
        )

    raw = acc_ref[...] + lifted(shrunk[:, :half], shrunk[:, half : 2 * half], uq_own, uq_other)
    raw = raw.astype(jnp.bfloat16).astype(jnp.float32)
    cosine, sine = cos_ref[...], sin_ref[...]
    for h in range(heads):
        columns = slice(h * HEAD_DIM, (h + 1) * HEAD_DIM)
        wide[h, 0:rows, :] = rotated(raw[:, columns], cosine, sine)
    for n in range(seq_count):
        for h in range(heads):
            tall[pl.ds((n * heads + h) * steps, steps), :] = wide[
                h, pl.ds(n, steps, stride=seq_count), :
            ]
    query_ref[...] = tall[...].astype(jnp.bfloat16)
    keyout_ref[...] = key_ref[...].astype(jnp.bfloat16)
    value = value_ref[...] + lifted(
        shrunk[:, 2 * half : 3 * half], shrunk[:, 3 * half :], uv_own, uv_other
    )
    valueout_ref[...] = value.astype(jnp.bfloat16)


def fresh_kernel(
    seq_count, query_ref, key_ref, value_ref, cos_ref, sin_ref, kc_ref, vc_ref, wo_ref,
    fresh_ref, level_ref, query_out, kc_out, vc_out, wo_out, sem,
):
    pairs = [(kc_ref.at[n], kc_out.at[n]) for n in range(seq_count)]
    pairs += [(vc_ref.at[n], vc_out.at[n]) for n in range(seq_count)]
    copies = fetches(pairs + row_parts(wo_ref, wo_out, 0, 4), sem)
    lane = lax.broadcasted_iota(jnp.int32, (1, HEAD_DIM), 1)
    columns = []
    steps = key_ref.shape[0] // seq_count
    per_seq = fresh_ref.shape[0] // seq_count
    query_out[...] = query_ref[...]
    queries = query_ref[...].astype(jnp.float32)
    keys = rotated(key_ref[...].astype(jnp.float32), cos_ref[...], sin_ref[...])
    keys = keys.astype(jnp.bfloat16).astype(jnp.float32)
    values = value_ref[...].astype(jnp.float32)
    step = lax.rem(lax.broadcasted_iota(jnp.int32, (per_seq, 1), 0), steps)
    for n in range(seq_count):
        rows = slice(n * per_seq, (n + 1) * per_seq)
        query = queries[rows]
        scores = []
        for t in range(steps):
            place = t * seq_count + n
            score = jnp.sum(query * keys[place : place + 1], axis=-1, keepdims=True) * inv_root
            scores.append(jnp.where(step >= t, score, negative))
        top = functools.reduce(jnp.maximum, scores)
        weights = [
            jnp.where(step >= t, jnp.exp(score - top), 0.0) for t, score in enumerate(scores)
        ]
        total = functools.reduce(jnp.add, weights)
        summed = jnp.zeros((per_seq, HEAD_DIM), jnp.float32)
        for t, weight in enumerate(weights):
            place = t * seq_count + n
            summed = summed + weight.astype(jnp.bfloat16).astype(jnp.float32) * values[
                place : place + 1
            ]
        fresh_ref[rows, :] = summed
        columns.append(jnp.where(lane == 0, top, jnp.where(lane == 1, total, 0.0)))
    columns = rows_padded(jnp.concatenate(columns, axis=0), HEAD_DIM)
    level_ref[...] = jnp.transpose(columns)[0 : level_ref.shape[0], :]
    for copy in copies:
        copy.wait()


def pieces_of(top, total):
    rows = lax.broadcasted_iota(jnp.int32, (16, HEAD_DIM), 0)
    packed = jnp.zeros((16, HEAD_DIM), jnp.float32)
    for first, left in ((0, top), (3, total)):
        for c in range(3):
            piece = left.astype(jnp.bfloat16).astype(jnp.float32)
            left = left - piece
            packed = jnp.where(rows == first + c, piece, packed)
    return packed.astype(jnp.bfloat16)


def top_and_total(part_ref, held_rows):
    pieces = part_ref[padded(held_rows, 16) :, :].astype(jnp.float32)
    return (
        pieces[0:1] + (pieces[1:2] + pieces[2:3]),
        pieces[3:4] + (pieces[4:5] + pieces[5:6]),
    )


def turned_rows(rows):
    count = padded(len(rows), 8)
    place = lax.broadcasted_iota(jnp.int32, (count, HEAD_DIM), 0)
    stacked = jnp.zeros((count, HEAD_DIM), jnp.float32)
    for k, row in enumerate(rows):
        stacked = jnp.where(place == k, row, stacked)
    return jnp.transpose(rows_padded(stacked, HEAD_DIM))


def cache_kernel(
    odd, first, reach_ref, query_ref, kc_ref, vc_ref, wo_ref, *refs
):
    earlier = refs[:-5]
    out_ref, wo_out, scores_buf, weights_buf, sem = refs[-5:]
    copies = fetches(row_parts(wo_ref, wo_out, first, sem.shape[0]), sem)
    entries, held_rows, _ = query_ref.shape
    seq_count, kv_heads, span, _ = kc_ref.shape
    peers = 2 * entries
    per_seq = held_rows // seq_count
    mean_rows = padded(held_rows, 16)
    tensor = lax.axis_index("tensor")
    spots = tensor * span + lax.broadcasted_iota(jnp.int32, (span, HEAD_DIM), 0)
    live = spots < reach_ref[0:1, :]
    lane = lax.broadcasted_iota(jnp.int32, (span, HEAD_DIM), 1)
    owners = [lax.bitwise_xor(tensor, 2 * e + odd) for e in range(entries)]
    heads = [owner * kv_heads // peers for owner in owners]
    for blocks in earlier:
        for e in range(entries):
            place = lax.bitwise_xor(tensor, 2 * e + 1 - odd)
            out_ref[place] = blocks[place]
    batch = 4
    for lead in range(0, entries, batch):
        part = range(lead, min(lead + batch, entries))
        turned = [
            jnp.transpose(rows_padded(query_ref[e].astype(jnp.float32), HEAD_DIM)).astype(
                jnp.bfloat16
            )
            for e in part
        ]
        for k, e in enumerate(part):
            scores = None
            for n in range(seq_count):
                score = jnp.dot(
                    kc_ref[n, heads[e]], turned[k], preferred_element_type=jnp.float32
                )
                scores = score if n == 0 else jnp.where(lane < n * per_seq, scores, score)
            scores_buf[k] = jnp.where(live, scores, negative)
        tops = [
            jnp.maximum(jnp.max(scores_buf[k], axis=0, keepdims=True), 0.1 * negative)
            for k in range(len(part))
        ]
        for k, e in enumerate(part):
            weights = jnp.exp((scores_buf[k] - tops[k]) * inv_root)
            total = jnp.sum(weights, axis=0, keepdims=True)
            out_ref[owners[e], mean_rows:, :] = pieces_of(tops[k] * inv_root, total)
            weights_buf[k] = jnp.transpose(weights)
        for k, e in enumerate(part):
            sums = [
                jnp.dot(
                    weights_buf[k, n * per_seq : (n + 1) * per_seq, :].astype(jnp.bfloat16),
                    vc_ref[n, heads[e]],
                    preferred_element_type=jnp.float32,
                )
                for n in range(seq_count)
            ]
            sums = rows_padded(jnp.concatenate(sums, axis=0), mean_rows)
            out_ref[owners[e], 0:mean_rows, :] = sums.astype(jnp.bfloat16)
    for copy in copies:
        copy.wait()


def merge_kernel(seq_count, blocks_ref, fresh_ref, level_ref, *refs):
    wo_refs, (out_ref, wide) = refs[:-2], refs[-2:]
    peers, folded, lanes = out_ref.shape
    heads = wide.shape[0]
    held_rows = fresh_ref.shape[0]
    rows = held_rows // heads
    steps = rows // seq_count
    folds = folded // rows
    per_seq = heads * steps
    mean_rows = padded(held_rows, 16)
    stats = [top_and_total(blocks_ref.at[b], held_rows) for b in range(peers)]
    stats.append((level_ref[0:1, :], level_ref[1:2, :]))
    top = functools.reduce(jnp.maximum, [stat[0] for stat in stats])
    factors = [jnp.exp(stat[0] - top) for stat in stats]
    total = functools.reduce(jnp.add, [factor * stat[1] for factor, stat in zip(factors, stats)])
    total = jnp.where(total > 0.0, total, 1.0)
    columns = turned_rows([factor / total for factor in factors])
    mixed = fresh_ref[...] * columns[0:held_rows, peers : peers + 1]
    for b in range(peers):
        mixed = mixed + (
            blocks_ref[b, 0:mean_rows, :].astype(jnp.float32)[0:held_rows]
            * columns[0:held_rows, b : b + 1]
        )
    for n in range(seq_count):
        for h in range(heads):
            first = n * per_seq + h * steps
            wide[h, pl.ds(n, steps, stride=seq_count), :] = mixed[first : first + steps]
    attention = jnp.concatenate([wide[h, 0:rows, :] for h in range(heads)], axis=1)
    attention = attention.astype(jnp.bfloat16)
    width = folds * lanes
    starts = [0]
    for wo_ref in wo_refs:
        starts.append(starts[-1] + wo_ref.shape[0])
    for p in range(peers):
        share = functools.reduce(
            jnp.add,
            [
                jnp.dot(
                    attention[:, start : start + wo_ref.shape[0]],
                    wo_ref[:, p * width : (p + 1) * width],
                    preferred_element_type=jnp.float32,
                )
                for start, wo_ref in zip(starts, wo_refs)
            ],
        )
        if folds > 1:
            share = jnp.concatenate(
                [share[:, c * lanes : (c + 1) * lanes] for c in range(folds)], axis=0
            )
        out_ref[p] = share.astype(out_ref.dtype)


def sum_kernel(rest_ref, parts_ref, out_ref):
    total = functools.reduce(
        jnp.add, [parts_ref[b].astype(jnp.float32) for b in range(parts_ref.shape[0])]
    )
    rows = rest_ref.shape[0]
    steps, seqs, _ = out_ref.shape
    folds, lanes = total.shape[0] // rows, total.shape[1]
    for c in range(folds):
        columns = slice(c * lanes, (c + 1) * lanes)
        piece = total[c * rows : (c + 1) * rows] + rest_ref[:, columns]
        for s in range(steps):
            out_ref[s, :, columns] = piece[s * seqs : (s + 1) * seqs].astype(jnp.bfloat16)


def crossed(value, mask):
    pairs = [(source, source ^ mask) for source in range(lax.axis_size("tensor"))]
    return lax.ppermute(value, "tensor", pairs)


def exchanged(value):
    return lax.all_to_all(value, "tensor", split_axis=0, concat_axis=0, tiled=True)


def along_z(values):
    return [values[0]] + [crossed(value, 2 * p) for p, value in enumerate(values) if p]


def body(
    layer_input_hidden,
    rmsnorm_gain_weight,
    wq,
    wk,
    wv,
    wo,
    adapter_down_stored,
    adapter_up_query,
    adapter_up_value,
    adapter_block_owner,
    rotated_key_cache,
    cached_value_rows,
    cache_valid_lengths,
):
    f32, bf16 = jnp.float32, jnp.bfloat16
    shape = jax.ShapeDtypeStruct
    steps, seqs, model_width = layer_input_hidden.shape
    peers = lax.axis_size("tensor")
    tensor_index = lax.axis_index("tensor")
    rows = steps * seqs
    local_heads = wq.shape[1] // HEAD_DIM
    held_rows = rows * local_heads
    kv_width = wk.shape[1]
    width = model_width // peers
    group = QUERY_HEADS // KEY_VALUE_HEADS

    pairs = [(0, 1), (1, 0)]
    other_down = lax.ppermute(adapter_down_stored, "replica", pairs)
    other_up_query = lax.ppermute(adapter_up_query, "replica", pairs)
    other_up_value = lax.ppermute(adapter_up_value, "replica", pairs)
    other_down, other_up_query, other_up_value = lax.optimization_barrier(
        (other_down, other_up_query, other_up_value)
    )

    normed, cosine, sine, rest, reach, partial = kernel_call(
        functools.partial(norm_kernel, peers, local_heads),
        (
            shape((rows, model_width), bf16),
            shape((rows, HEAD_DIM), f32),
            shape((rows, HEAD_DIM), f32),
            shape((rows, width), f32),
            shape((8, HEAD_DIM), jnp.int32),
            shape((rows, 2 * ADAPTER_RANK), f32),
        ),
        [far] * 5 + [vmem],
        (vmem,) * 6,
        [
            pltpu.SMEM(cache_valid_lengths.shape, jnp.int32),
            pltpu.SMEM(adapter_block_owner.shape, jnp.int32),
            pltpu.VMEM(layer_input_hidden.shape, bf16),
            pltpu.VMEM(adapter_down_stored.shape, bf16),
            pltpu.VMEM(rmsnorm_gain_weight.shape, bf16),
            pltpu.SemaphoreType.DMA((5,)),
        ],
        limit=8,
    )(
        cache_valid_lengths, adapter_block_owner, layer_input_hidden, adapter_down_stored,
        rmsnorm_gain_weight, other_down,
    )

    kv_chunks = 4
    key_sum, value_sum = kernel_call(
        functools.partial(key_value_kernel, kv_chunks),
        (shape((rows, kv_width), f32), shape((rows, kv_width), f32)),
        [vmem, far, far],
        (vmem, vmem),
        [
            pltpu.VMEM(
                (2, model_width, kv_width) if kv_width % 128 else (model_width, 2 * kv_width), bf16
            ),
            pltpu.SemaphoreType.DMA((2, kv_chunks)),
        ],
        limit=8,
        moved=2 * wk.size * 2,
    )(normed, wk, wv)
    partial = partial + crossed(partial, 1)
    partial, normed, key_sum = lax.optimization_barrier((partial, normed, key_sum))
    shrink_parts = along_z([partial] * (peers // 2))

    chunks = 16
    query_sum = kernel_call(
        functools.partial(query_kernel, chunks),
        shape((rows, wq.shape[1]), f32),
        [vmem, far],
        vmem,
        [pltpu.VMEM(wq.shape, bf16), pltpu.SemaphoreType.DMA((chunks,))],
        limit=20,
        moved=wq.size * 2,
        flops=2 * rows * wq.size,
    )(normed, wq)

    queries, key_raw, value_raw = kernel_call(
        functools.partial(finish_kernel, seqs),
        (
            shape((held_rows, HEAD_DIM), bf16),
            shape((rows, kv_width), bf16),
            shape((rows, kv_width), bf16),
        ),
        [vmem] * (9 + peers // 2),
        (vmem,) * 3,
        [
            pltpu.VMEM((local_heads, padded(rows, 8), HEAD_DIM), f32),
            pltpu.VMEM((held_rows, HEAD_DIM), f32),
        ],
        limit=4,
    )(
        query_sum, key_sum, value_sum, adapter_up_query, other_up_query,
        adapter_up_value, other_up_value, cosine, sine, *shrink_parts,
    )
    met_queries = along_z([queries] * (peers // 2))[1:]

    if kv_width != HEAD_DIM:
        kv_index = tensor_index * local_heads // group

        def own_head(value):
            heads = lax.all_gather(value, "tensor", axis=1, tiled=True)
            return lax.dynamic_slice_in_dim(heads, kv_index * HEAD_DIM, HEAD_DIM, 1)

        key_raw, value_raw = own_head(key_raw), own_head(value_raw)

    cache_shape = shape(rotated_key_cache.shape, bf16)
    quarter = wo.shape[0] // 4
    fresh, fresh_level, queries, keys_near, values_near, wo_first = kernel_call(
        functools.partial(fresh_kernel, seqs),
        (
            shape((held_rows, HEAD_DIM), f32),
            shape((8, HEAD_DIM), f32),
            shape((held_rows, HEAD_DIM), bf16),
            cache_shape,
            cache_shape,
            shape((quarter, model_width), bf16),
        ),
        [vmem] * 5 + [far] * 3,
        (vmem,) * 6,
        [pltpu.SemaphoreType.DMA((2 * seqs + 4,))],
        limit=4,
        moved=4 * rotated_key_cache.size + wo.size // 2,
    )(queries, key_raw, value_raw, cosine, sine, rotated_key_cache, cached_value_rows, wo)
    held = jnp.stack([queries] + met_queries)
    others = crossed(held, 1)

    def cache_part(odd, first, count, *operands):
        return kernel_call(
            functools.partial(cache_kernel, odd, first),
            (
                shape((peers, padded(held_rows, 16) + 16, HEAD_DIM), bf16),
                shape((count, model_width), bf16),
            ),
            [vmem] * 4 + [far] + [vmem] * (len(operands) - 1),
            (vmem, vmem),
            [
                pltpu.VMEM((4, rotated_key_cache.shape[2], HEAD_DIM), f32),
                pltpu.VMEM((4, HEAD_DIM, rotated_key_cache.shape[2]), f32),
                pltpu.SemaphoreType.DMA((8,)),
            ],
            limit=8,
            moved=2 * count * model_width,
        )(reach, operands[0], keys_near, values_near, wo, *operands[1:])

    even_blocks, wo_second = cache_part(0, quarter, 2 * quarter, held)
    blocks, wo_third = cache_part(1, 3 * quarter, quarter, others, even_blocks)

    folds = width // 256 if (rows * (width // 256)) % 16 == 0 else 1
    shares = kernel_call(
        functools.partial(merge_kernel, seqs),
        shape((peers, rows * folds, width // folds), bf16),
        [vmem] * 6,
        vmem,
        [pltpu.VMEM((local_heads, padded(rows, 8), HEAD_DIM), f32)],
        limit=6,
    )(exchanged(blocks), fresh, fresh_level, wo_first, wo_second, wo_third)
    return kernel_call(
        sum_kernel,
        shape((steps, seqs, width), bf16),
        [vmem] * 2,
        vmem,
        limit=4,
    )(rest, exchanged(shares))


def solution(mesh):
    return jax.shard_map(
        body,
        mesh=mesh,
        in_specs=(
            P(None, ("groups", "replica"), None),
            P(),
            P(None, "tensor"),
            P(None, "tensor"),
            P(None, "tensor"),
            P("tensor", None),
            P(("replica", "tensor"), None),
            P("replica", "tensor"),
            P("replica", "tensor"),
            P(),
            P(("groups", "replica"), None, "tensor", None),
            P(("groups", "replica"), None, "tensor", None),
            P(("groups", "replica")),
        ),
        out_specs=P(None, ("groups", "replica"), "tensor"),
        check_vma=False,
    )
```

```python
import functools
import math

import jax
import jax.numpy as jnp
from jax import lax
from jax.experimental import pallas as pl
from jax.experimental.pallas import tpu as pltpu
from jax.sharding import PartitionSpec as P

QUERY_HEADS = 64
KEY_VALUE_HEADS = 8
HEAD_DIM = 128
ADAPTER_RANK = 64


adapter_scale = 2.0
rope_base = 500000.0
negative = -1e30
inv_root = 1.0 / math.sqrt(HEAD_DIM)
MIB = 1 << 20

vmem = pl.BlockSpec(memory_space=pltpu.VMEM)
smem = pl.BlockSpec(memory_space=pltpu.SMEM)
far = pl.BlockSpec(memory_space=pl.ANY)


def padded(count, multiple):
    return -(-count // multiple) * multiple


def rows_padded(value, rows):
    if value.shape[0] == rows:
        return value
    filler = jnp.zeros((rows - value.shape[0],) + value.shape[1:], value.dtype)
    return jnp.concatenate([value, filler], axis=0)


def kernel_call(kernel, outs, specs, out_specs, scratch=(), limit=16, moved=0, flops=0):
    call = pl.pallas_call(
        kernel,
        out_shape=outs,
        in_specs=specs,
        out_specs=out_specs,
        scratch_shapes=list(scratch),
        compiler_params=pltpu.CompilerParams(vmem_limit_bytes=limit * MIB),
        cost_estimate=pl.CostEstimate(flops=flops, bytes_accessed=moved, transcendentals=0),
    )

    def run(*operands):
        return call(
            *[
                pltpu.with_memory_space_constraint(operand, pltpu.HBM) if spec is far else operand
                for operand, spec in zip(operands, specs)
            ]
        )

    return run


def fetches(pairs, sem):
    copies = [
        pltpu.make_async_copy(far_ref, near, sem.at[k]) for k, (far_ref, near) in enumerate(pairs)
    ]
    for copy in copies:
        copy.start()
    return copies


def row_parts(far_ref, near, first, pieces):
    span = near.shape[0] // pieces
    return [
        (far_ref.at[pl.ds(first + c * span, span)], near.at[pl.ds(c * span, span)])
        for c in range(pieces)
    ]


def place_of(owner_ref, held):
    place = jnp.int32(0)
    for j in range(owner_ref.shape[0]):
        place = jnp.where(owner_ref[j] == held, jnp.int32(j), place)
    return place


def block_product(normed_ref, place, stored):
    block_rows = stored.shape[0]
    columns = pl.ds(pl.multiple_of(place * block_rows, block_rows), block_rows)
    return jnp.dot(normed_ref[:, columns], stored[...], preferred_element_type=jnp.float32)


def norm_kernel(
    peers, heads, lengths_ref, owner_ref, x_ref, down_ref, gain_ref, other_ref,
    normed_ref, cos_ref, sin_ref, rest_ref, reach_ref, shrunk_ref,
    lengths, owner, x_buf, down_buf, gain, sem,
):
    copies = fetches(
        [
            (lengths_ref, lengths),
            (owner_ref, owner),
            (x_ref, x_buf),
            (down_ref, down_buf),
            (gain_ref, gain),
        ],
        sem,
    )
    steps, seqs, _ = x_ref.shape
    rows, width = rest_ref.shape
    half = HEAD_DIM // 2
    row = lax.broadcasted_iota(jnp.int32, (rows, HEAD_DIM), 0)
    lane = lax.broadcasted_iota(jnp.int32, (rows, HEAD_DIM), 1)
    copies[0].wait()
    positions = jnp.zeros((rows, HEAD_DIM), jnp.int32)
    for s in range(steps):
        for n in range(seqs):
            positions = jnp.where(row == s * seqs + n, lengths[n] + s, positions)
    low = lane < half
    exponent = jnp.where(low, lane, lane - half).astype(jnp.float32) * (2.0 / HEAD_DIM)
    angles = positions.astype(jnp.float32) * jnp.exp(exponent * -math.log(rope_base))
    sine = jnp.sin(angles)
    cos_ref[...] = jnp.cos(angles)
    sin_ref[...] = jnp.where(low, -sine, sine)
    place = lax.broadcasted_iota(jnp.int32, reach_ref.shape, 1)
    reach = jnp.zeros(reach_ref.shape, jnp.int32)
    per_seq = heads * steps
    for n in range(seqs):
        mine = jnp.logical_and(place >= n * per_seq, place < (n + 1) * per_seq)
        reach = jnp.where(mine, lengths[n], reach)
    reach_ref[...] = reach
    copies[2].wait()
    values = jnp.concatenate([x_buf[s].astype(jnp.float32) for s in range(steps)], axis=0)
    factor = lax.rsqrt(jnp.mean(values * values, axis=-1, keepdims=True) + 1e-05)
    copies[4].wait()
    normed = values * factor * gain[...].astype(jnp.float32).reshape(1, -1)
    normed_ref[...] = normed.astype(jnp.bfloat16)
    replica, tensor = lax.axis_index("replica"), lax.axis_index("tensor")
    for s in range(steps):
        part = x_buf[s, :, pl.ds(pl.multiple_of(tensor * width, width), width)]
        rest_ref[s * seqs : (s + 1) * seqs, :] = part.astype(jnp.float32)
    copies[1].wait()
    copies[3].wait()
    shrunk_ref[...] = block_product(
        normed_ref, place_of(owner, replica * peers + tensor), down_buf
    ) + block_product(normed_ref, place_of(owner, (1 - replica) * peers + tensor), other_ref)


def rotated(values, cosine, sine):
    half = HEAD_DIM // 2
    turned = jnp.concatenate([values[:, half:], values[:, :half]], axis=1)
    return values * cosine + turned * sine


def finish_kernel(
    seq_count, acc_ref, key_ref, value_ref, uq_own, uq_other, uv_own, uv_other,
    cos_ref, sin_ref, *parts_and_outs,
):
    parts, (query_ref, keyout_ref, valueout_ref, wide, tall) = parts_and_outs[:-5], parts_and_outs[-5:]
    first = lax.axis_index("replica") == 0
    rows = acc_ref.shape[0]
    steps = rows // seq_count
    heads = acc_ref.shape[1] // HEAD_DIM
    shrunk = functools.reduce(jnp.add, [part[...] for part in parts])
    shrunk = shrunk.astype(jnp.bfloat16).astype(jnp.float32)
    half = ADAPTER_RANK // 2

    def lifted(low, high, own, other):
        mine = jnp.where(first, low, high).astype(jnp.bfloat16)
        theirs = jnp.where(first, high, low).astype(jnp.bfloat16)
        return adapter_scale * (
            jnp.dot(mine, own[...], preferred_element_type=jnp.float32)
            + jnp.dot(theirs, other[...], preferred_element_type=jnp.float32)
        )

    raw = acc_ref[...] + lifted(shrunk[:, :half], shrunk[:, half : 2 * half], uq_own, uq_other)
    raw = raw.astype(jnp.bfloat16).astype(jnp.float32)
    cosine, sine = cos_ref[...], sin_ref[...]
    for h in range(heads):
        columns = slice(h * HEAD_DIM, (h + 1) * HEAD_DIM)
        wide[h, 0:rows, :] = rotated(raw[:, columns], cosine, sine)
    for n in range(seq_count):
        for h in range(heads):
            tall[pl.ds((n * heads + h) * steps, steps), :] = wide[
                h, pl.ds(n, steps, stride=seq_count), :
            ]
    query_ref[...] = tall[...].astype(jnp.bfloat16)
    keyout_ref[...] = key_ref[...].astype(jnp.bfloat16)
    value = value_ref[...] + lifted(
        shrunk[:, 2 * half : 3 * half], shrunk[:, 3 * half :], uv_own, uv_other
    )
    valueout_ref[...] = value.astype(jnp.bfloat16)


def fresh_kernel(
    seq_count, query_ref, key_ref, value_ref, cos_ref, sin_ref, kc_ref, vc_ref, wo_ref,
    fresh_ref, level_ref, query_out, kc_out, vc_out, wo_out, sem,
):
    pairs = [(kc_ref.at[n], kc_out.at[n]) for n in range(seq_count)]
    pairs += [(vc_ref.at[n], vc_out.at[n]) for n in range(seq_count)]
    copies = fetches(pairs + row_parts(wo_ref, wo_out, 0, 4), sem)
    lane = lax.broadcasted_iota(jnp.int32, (1, HEAD_DIM), 1)
    columns = []
    steps = key_ref.shape[0] // seq_count
    per_seq = fresh_ref.shape[0] // seq_count
    query_out[...] = query_ref[...]
    queries = query_ref[...].astype(jnp.float32)
    keys = rotated(key_ref[...].astype(jnp.float32), cos_ref[...], sin_ref[...])
    keys = keys.astype(jnp.bfloat16).astype(jnp.float32)
    values = value_ref[...].astype(jnp.float32)
    step = lax.rem(lax.broadcasted_iota(jnp.int32, (per_seq, 1), 0), steps)
    for n in range(seq_count):
        rows = slice(n * per_seq, (n + 1) * per_seq)
        query = queries[rows]
        scores = []
        for t in range(steps):
            place = t * seq_count + n
            score = jnp.sum(query * keys[place : place + 1], axis=-1, keepdims=True) * inv_root
            scores.append(jnp.where(step >= t, score, negative))
        top = functools.reduce(jnp.maximum, scores)
        weights = [
            jnp.where(step >= t, jnp.exp(score - top), 0.0) for t, score in enumerate(scores)
        ]
        total = functools.reduce(jnp.add, weights)
        summed = jnp.zeros((per_seq, HEAD_DIM), jnp.float32)
        for t, weight in enumerate(weights):
            place = t * seq_count + n
            summed = summed + weight.astype(jnp.bfloat16).astype(jnp.float32) * values[
                place : place + 1
            ]
        fresh_ref[rows, :] = summed
        columns.append(jnp.where(lane == 0, top, jnp.where(lane == 1, total, 0.0)))
    columns = rows_padded(jnp.concatenate(columns, axis=0), HEAD_DIM)
    level_ref[...] = jnp.transpose(columns)[0 : level_ref.shape[0], :]
    for copy in copies:
        copy.wait()


def pieces_of(top, total):
    rows = lax.broadcasted_iota(jnp.int32, (16, HEAD_DIM), 0)
    packed = jnp.zeros((16, HEAD_DIM), jnp.float32)
    for first, left in ((0, top), (3, total)):
        for c in range(3):
            piece = left.astype(jnp.bfloat16).astype(jnp.float32)
            left = left - piece
            packed = jnp.where(rows == first + c, piece, packed)
    return packed.astype(jnp.bfloat16)


def top_and_total(part_ref, held_rows):
    pieces = part_ref[padded(held_rows, 16) :, :].astype(jnp.float32)
    return (
        pieces[0:1] + (pieces[1:2] + pieces[2:3]),
        pieces[3:4] + (pieces[4:5] + pieces[5:6]),
    )


def turned_rows(rows):
    count = padded(len(rows), 8)
    place = lax.broadcasted_iota(jnp.int32, (count, HEAD_DIM), 0)
    stacked = jnp.zeros((count, HEAD_DIM), jnp.float32)
    for k, row in enumerate(rows):
        stacked = jnp.where(place == k, row, stacked)
    return jnp.transpose(rows_padded(stacked, HEAD_DIM))


def cache_kernel(
    odd, first, reach_ref, query_ref, kc_ref, vc_ref, wo_ref, *refs
):
    copies = []
    if first is not None:
        *refs, wo_out, scores_buf, weights_buf, sem = refs
        copies = fetches(row_parts(wo_ref, wo_out, first, sem.shape[0]), sem)
    else:
        *refs, scores_buf, weights_buf = refs
    *earlier, out_ref = refs
    entries, held_rows, _ = query_ref.shape
    seq_count, kv_heads, span, _ = kc_ref.shape
    peers = 2 * entries
    per_seq = held_rows // seq_count
    mean_rows = padded(held_rows, 16)
    tensor = lax.axis_index("tensor")
    spots = tensor * span + lax.broadcasted_iota(jnp.int32, (span, HEAD_DIM), 0)
    live = spots < reach_ref[0:1, :]
    lane = lax.broadcasted_iota(jnp.int32, (span, HEAD_DIM), 1)
    owners = [lax.bitwise_xor(tensor, 2 * e + odd) for e in range(entries)]
    heads = [owner * kv_heads // peers for owner in owners]
    for blocks in earlier:
        for e in range(entries):
            place = lax.bitwise_xor(tensor, 2 * e + 1 - odd)
            out_ref[place] = blocks[place]
    batch = 4
    for lead in range(0, entries, batch):
        part = range(lead, min(lead + batch, entries))
        turned = [
            jnp.transpose(rows_padded(query_ref[e].astype(jnp.float32), HEAD_DIM)).astype(
                jnp.bfloat16
            )
            for e in part
        ]
        for k, e in enumerate(part):
            scores = None
            for n in range(seq_count):
                score = jnp.dot(
                    kc_ref[n, heads[e]], turned[k], preferred_element_type=jnp.float32
                )
                scores = score if n == 0 else jnp.where(lane < n * per_seq, scores, score)
            scores_buf[k] = jnp.where(live, scores, negative)
        tops = [
            jnp.maximum(jnp.max(scores_buf[k], axis=0, keepdims=True), 0.1 * negative)
            for k in range(len(part))
        ]
        for k, e in enumerate(part):
            weights = jnp.exp((scores_buf[k] - tops[k]) * inv_root)
            total = jnp.sum(weights, axis=0, keepdims=True)
            out_ref[owners[e], mean_rows:, :] = pieces_of(tops[k] * inv_root, total)
            weights_buf[k] = jnp.transpose(weights)
        for k, e in enumerate(part):
            sums = [
                jnp.dot(
                    weights_buf[k, n * per_seq : (n + 1) * per_seq, :].astype(jnp.bfloat16),
                    vc_ref[n, heads[e]],
                    preferred_element_type=jnp.float32,
                )
                for n in range(seq_count)
            ]
            sums = rows_padded(jnp.concatenate(sums, axis=0), mean_rows)
            out_ref[owners[e], 0:mean_rows, :] = sums.astype(jnp.bfloat16)
    for copy in copies:
        copy.wait()


def merge_kernel(seq_count, blocks_ref, fresh_ref, level_ref, wo_ref, *refs):
    *wo_refs, out_ref, wide, wo_buf, sums, sem = refs
    last = wo_ref.shape[0] - wo_buf.shape[0]
    copies = fetches(row_parts(wo_ref, wo_buf, last, sem.shape[0]), sem)
    peers, folded, lanes = out_ref.shape
    heads = wide.shape[0]
    held_rows = fresh_ref.shape[0]
    rows = held_rows // heads
    steps = rows // seq_count
    folds = folded // rows
    per_seq = heads * steps
    mean_rows = padded(held_rows, 16)
    stats = [top_and_total(blocks_ref.at[b], held_rows) for b in range(peers)]
    stats.append((level_ref[0:1, :], level_ref[1:2, :]))
    top = functools.reduce(jnp.maximum, [stat[0] for stat in stats])
    factors = [jnp.exp(stat[0] - top) for stat in stats]
    total = functools.reduce(jnp.add, [factor * stat[1] for factor, stat in zip(factors, stats)])
    total = jnp.where(total > 0.0, total, 1.0)
    columns = turned_rows([factor / total for factor in factors])
    mixed = fresh_ref[...] * columns[0:held_rows, peers : peers + 1]
    for b in range(peers):
        mixed = mixed + (
            blocks_ref[b, 0:mean_rows, :].astype(jnp.float32)[0:held_rows]
            * columns[0:held_rows, b : b + 1]
        )
    for n in range(seq_count):
        for h in range(heads):
            first = n * per_seq + h * steps
            wide[h, pl.ds(n, steps, stride=seq_count), :] = mixed[first : first + steps]
    attention = jnp.concatenate([wide[h, 0:rows, :] for h in range(heads)], axis=1)
    attention = attention.astype(jnp.bfloat16)
    width = folds * lanes

    def product(p, first, weights):
        return jnp.dot(
            attention[:, first : first + weights.shape[0]],
            weights[:, p * width : (p + 1) * width],
            preferred_element_type=jnp.float32,
        )

    for p in range(peers):
        share, first = 0.0, 0
        for weights in wo_refs:
            share = share + product(p, first, weights)
            first = first + weights.shape[0]
        sums[p] = share
    for copy in copies:
        copy.wait()
    for p in range(peers):
        share = sums[p] + product(p, last, wo_buf)
        if folds > 1:
            share = jnp.concatenate(
                [share[:, c * lanes : (c + 1) * lanes] for c in range(folds)], axis=0
            )
        out_ref[p] = share.astype(out_ref.dtype)


def sum_kernel(rest_ref, parts_ref, out_ref):
    total = functools.reduce(
        jnp.add, [parts_ref[b].astype(jnp.float32) for b in range(parts_ref.shape[0])]
    )
    rows = rest_ref.shape[0]
    steps, seqs, _ = out_ref.shape
    folds, lanes = total.shape[0] // rows, total.shape[1]
    for c in range(folds):
        columns = slice(c * lanes, (c + 1) * lanes)
        piece = total[c * rows : (c + 1) * rows] + rest_ref[:, columns]
        for s in range(steps):
            out_ref[s, :, columns] = piece[s * seqs : (s + 1) * seqs].astype(jnp.bfloat16)


def crossed(value, mask):
    pairs = [(source, source ^ mask) for source in range(lax.axis_size("tensor"))]
    return lax.ppermute(value, "tensor", pairs)


def exchanged(value):
    return lax.all_to_all(value, "tensor", split_axis=0, concat_axis=0, tiled=True)


def along_z(values):
    return [values[0]] + [crossed(value, 2 * p) for p, value in enumerate(values) if p]


def body(
    layer_input_hidden,
    rmsnorm_gain_weight,
    wq,
    wk,
    wv,
    wo,
    adapter_down_stored,
    adapter_up_query,
    adapter_up_value,
    adapter_block_owner,
    rotated_key_cache,
    cached_value_rows,
    cache_valid_lengths,
):
    f32, bf16 = jnp.float32, jnp.bfloat16
    shape = jax.ShapeDtypeStruct
    steps, seqs, model_width = layer_input_hidden.shape
    peers = lax.axis_size("tensor")
    tensor_index = lax.axis_index("tensor")
    rows = steps * seqs
    local_heads = wq.shape[1] // HEAD_DIM
    held_rows = rows * local_heads
    kv_width = wk.shape[1]
    width = model_width // peers
    group = QUERY_HEADS // KEY_VALUE_HEADS

    pairs = [(0, 1), (1, 0)]
    other_down = lax.ppermute(adapter_down_stored, "replica", pairs)
    other_up_query = lax.ppermute(adapter_up_query, "replica", pairs)
    other_up_value = lax.ppermute(adapter_up_value, "replica", pairs)
    other_down, other_up_query, other_up_value = lax.optimization_barrier(
        (other_down, other_up_query, other_up_value)
    )

    normed, cosine, sine, rest, reach, partial = kernel_call(
        functools.partial(norm_kernel, peers, local_heads),
        (
            shape((rows, model_width), bf16),
            shape((rows, HEAD_DIM), f32),
            shape((rows, HEAD_DIM), f32),
            shape((rows, width), f32),
            shape((8, HEAD_DIM), jnp.int32),
            shape((rows, 2 * ADAPTER_RANK), f32),
        ),
        [far] * 5 + [vmem],
        (vmem,) * 6,
        [
            pltpu.SMEM(cache_valid_lengths.shape, jnp.int32),
            pltpu.SMEM(adapter_block_owner.shape, jnp.int32),
            pltpu.VMEM(layer_input_hidden.shape, bf16),
            pltpu.VMEM(adapter_down_stored.shape, bf16),
            pltpu.VMEM(rmsnorm_gain_weight.shape, bf16),
            pltpu.SemaphoreType.DMA((5,)),
        ],
        limit=8,
    )(
        cache_valid_lengths, adapter_block_owner, layer_input_hidden, adapter_down_stored,
        rmsnorm_gain_weight, other_down,
    )

    key_sum = jnp.dot(normed, wk, preferred_element_type=f32)
    value_sum = jnp.dot(normed, wv, preferred_element_type=f32)
    partial = partial + crossed(partial, 1)
    partial, normed, key_sum = lax.optimization_barrier((partial, normed, key_sum))
    shrink_parts = along_z([partial] * (peers // 2))

    query_sum = jnp.dot(normed, wq, preferred_element_type=f32)

    queries, key_raw, value_raw = kernel_call(
        functools.partial(finish_kernel, seqs),
        (
            shape((held_rows, HEAD_DIM), bf16),
            shape((rows, kv_width), bf16),
            shape((rows, kv_width), bf16),
        ),
        [vmem] * (9 + peers // 2),
        (vmem,) * 3,
        [
            pltpu.VMEM((local_heads, padded(rows, 8), HEAD_DIM), f32),
            pltpu.VMEM((held_rows, HEAD_DIM), f32),
        ],
        limit=4,
    )(
        query_sum, key_sum, value_sum, adapter_up_query, other_up_query,
        adapter_up_value, other_up_value, cosine, sine, *shrink_parts,
    )
    met_queries = along_z([queries] * (peers // 2))[1:]

    if kv_width != HEAD_DIM:
        kv_index = tensor_index * local_heads // group

        def own_head(value):
            heads = lax.all_gather(value, "tensor", axis=1, tiled=True)
            return lax.dynamic_slice_in_dim(heads, kv_index * HEAD_DIM, HEAD_DIM, 1)

        key_raw, value_raw = own_head(key_raw), own_head(value_raw)

    cache_shape = shape(rotated_key_cache.shape, bf16)
    quarter = wo.shape[0] // 4
    fresh, fresh_level, queries, keys_near, values_near, wo_first = kernel_call(
        functools.partial(fresh_kernel, seqs),
        (
            shape((held_rows, HEAD_DIM), f32),
            shape((8, HEAD_DIM), f32),
            shape((held_rows, HEAD_DIM), bf16),
            cache_shape,
            cache_shape,
            shape((quarter, model_width), bf16),
        ),
        [vmem] * 5 + [far] * 3,
        (vmem,) * 6,
        [pltpu.SemaphoreType.DMA((2 * seqs + 4,))],
        limit=4,
        moved=4 * rotated_key_cache.size + wo.size // 2,
    )(queries, key_raw, value_raw, cosine, sine, rotated_key_cache, cached_value_rows, wo)
    held = jnp.stack([queries] + met_queries)
    others = crossed(held, 1)

    span = rotated_key_cache.shape[2]
    blocks_shape = shape((peers, padded(held_rows, 16) + 16, HEAD_DIM), bf16)
    buffers = [pltpu.VMEM((4, span, HEAD_DIM), f32), pltpu.VMEM((4, HEAD_DIM, span), f32)]
    even_blocks, wo_second = kernel_call(
        functools.partial(cache_kernel, 0, quarter),
        (blocks_shape, shape((2 * quarter, model_width), bf16)),
        [vmem] * 4 + [far],
        (vmem, vmem),
        buffers + [pltpu.SemaphoreType.DMA((8,))],
        limit=8,
        moved=wo.size,
    )(reach, held, keys_near, values_near, wo)
    blocks = kernel_call(
        functools.partial(cache_kernel, 1, None),
        blocks_shape,
        [vmem] * 4 + [far, vmem],
        vmem,
        buffers,
        limit=8,
    )(reach, others, keys_near, values_near, wo, even_blocks)

    folds = width // 256 if (rows * (width // 256)) % 16 == 0 else 1
    shares = kernel_call(
        functools.partial(merge_kernel, seqs),
        shape((peers, rows * folds, width // folds), bf16),
        [vmem] * 3 + [far] + [vmem] * 2,
        vmem,
        [
            pltpu.VMEM((local_heads, padded(rows, 8), HEAD_DIM), f32),
            pltpu.VMEM((quarter, model_width), bf16),
            pltpu.VMEM((peers, rows, width), f32),
            pltpu.SemaphoreType.DMA((4,)),
        ],
        limit=10,
        moved=wo.size,
    )(exchanged(blocks), fresh, fresh_level, wo, wo_first, wo_second)
    return kernel_call(
        sum_kernel,
        shape((steps, seqs, width), bf16),
        [vmem] * 2,
        vmem,
        limit=4,
    )(rest, exchanged(shares))


def solution(mesh):
    return jax.shard_map(
        body,
        mesh=mesh,
        in_specs=(
            P(None, ("groups", "replica"), None),
            P(),
            P(None, "tensor"),
            P(None, "tensor"),
            P(None, "tensor"),
            P("tensor", None),
            P(("replica", "tensor"), None),
            P("replica", "tensor"),
            P("replica", "tensor"),
            P(),
            P(("groups", "replica"), None, "tensor", None),
            P(("groups", "replica"), None, "tensor", None),
            P(("groups", "replica")),
        ),
        out_specs=P(None, ("groups", "replica"), "tensor"),
        check_vma=False,
    )
```

```python
import functools
import math

import jax
import jax.numpy as jnp
from jax import lax
from jax.experimental import pallas as pl
from jax.experimental.pallas import tpu as pltpu
from jax.sharding import PartitionSpec as P

QUERY_HEADS = 64
KEY_VALUE_HEADS = 8
HEAD_DIM = 128
ADAPTER_RANK = 64


adapter_scale = 2.0
rope_base = 500000.0
negative = -1e30
inv_root = 1.0 / math.sqrt(HEAD_DIM)
MIB = 1 << 20

vmem = pl.BlockSpec(memory_space=pltpu.VMEM)
smem = pl.BlockSpec(memory_space=pltpu.SMEM)
far = pl.BlockSpec(memory_space=pl.ANY)


def padded(count, multiple):
    return -(-count // multiple) * multiple


def rows_padded(value, rows):
    if value.shape[0] == rows:
        return value
    filler = jnp.zeros((rows - value.shape[0],) + value.shape[1:], value.dtype)
    return jnp.concatenate([value, filler], axis=0)


def kernel_call(kernel, outs, specs, out_specs, scratch=(), limit=16, moved=0, flops=0):
    call = pl.pallas_call(
        kernel,
        out_shape=outs,
        in_specs=specs,
        out_specs=out_specs,
        scratch_shapes=list(scratch),
        compiler_params=pltpu.CompilerParams(vmem_limit_bytes=limit * MIB),
        cost_estimate=pl.CostEstimate(flops=flops, bytes_accessed=moved, transcendentals=0),
    )

    def run(*operands):
        return call(
            *[
                pltpu.with_memory_space_constraint(operand, pltpu.HBM) if spec is far else operand
                for operand, spec in zip(operands, specs)
            ]
        )

    return run


def fetches(pairs, sem):
    copies = [
        pltpu.make_async_copy(far_ref, near, sem.at[k]) for k, (far_ref, near) in enumerate(pairs)
    ]
    for copy in copies:
        copy.start()
    return copies


def row_parts(far_ref, near, first, pieces):
    span = near.shape[0] // pieces
    return [
        (far_ref.at[pl.ds(first + c * span, span)], near.at[pl.ds(c * span, span)])
        for c in range(pieces)
    ]


def place_of(owner_ref, held):
    place = jnp.int32(0)
    for j in range(owner_ref.shape[0]):
        place = jnp.where(owner_ref[j] == held, jnp.int32(j), place)
    return place


def block_product(normed_ref, place, stored):
    block_rows = stored.shape[0]
    columns = pl.ds(pl.multiple_of(place * block_rows, block_rows), block_rows)
    return jnp.dot(normed_ref[:, columns], stored[...], preferred_element_type=jnp.float32)


def norm_kernel(
    peers, heads, lengths_ref, owner_ref, x_ref, down_ref, gain_ref, wq_ref,
    normed_ref, cos_ref, sin_ref, rest_ref, reach_ref, shrunk_ref, place_ref, wq_out,
    lengths, owner, x_buf, down_buf, gain, sem,
):
    copies = fetches(
        [
            (lengths_ref, lengths),
            (owner_ref, owner),
            (x_ref, x_buf),
            (down_ref, down_buf),
            (gain_ref, gain),
        ]
        + row_parts(wq_ref, wq_out, 0, 4),
        sem,
    )
    steps, seqs, _ = x_ref.shape
    rows, width = rest_ref.shape
    half = HEAD_DIM // 2
    row = lax.broadcasted_iota(jnp.int32, (rows, HEAD_DIM), 0)
    lane = lax.broadcasted_iota(jnp.int32, (rows, HEAD_DIM), 1)
    copies[0].wait()
    positions = jnp.zeros((rows, HEAD_DIM), jnp.int32)
    for s in range(steps):
        for n in range(seqs):
            positions = jnp.where(row == s * seqs + n, lengths[n] + s, positions)
    low = lane < half
    exponent = jnp.where(low, lane, lane - half).astype(jnp.float32) * (2.0 / HEAD_DIM)
    angles = positions.astype(jnp.float32) * jnp.exp(exponent * -math.log(rope_base))
    sine = jnp.sin(angles)
    cos_ref[...] = jnp.cos(angles)
    sin_ref[...] = jnp.where(low, -sine, sine)
    place = lax.broadcasted_iota(jnp.int32, reach_ref.shape, 1)
    reach = jnp.zeros(reach_ref.shape, jnp.int32)
    per_seq = heads * steps
    for n in range(seqs):
        mine = jnp.logical_and(place >= n * per_seq, place < (n + 1) * per_seq)
        reach = jnp.where(mine, lengths[n], reach)
    reach_ref[...] = reach
    copies[2].wait()
    values = jnp.concatenate([x_buf[s].astype(jnp.float32) for s in range(steps)], axis=0)
    factor = lax.rsqrt(jnp.mean(values * values, axis=-1, keepdims=True) + 1e-05)
    copies[4].wait()
    normed = values * factor * gain[...].astype(jnp.float32).reshape(1, -1)
    normed_ref[...] = normed.astype(jnp.bfloat16)
    replica, tensor = lax.axis_index("replica"), lax.axis_index("tensor")
    for s in range(steps):
        part = x_buf[s, :, pl.ds(pl.multiple_of(tensor * width, width), width)]
        rest_ref[s * seqs : (s + 1) * seqs, :] = part.astype(jnp.float32)
    copies[1].wait()
    copies[3].wait()
    shrunk_ref[...] = block_product(
        normed_ref, place_of(owner, replica * peers + tensor), down_buf
    )
    place_ref[0] = place_of(owner, (1 - replica) * peers + tensor)
    for copy in copies[5:]:
        copy.wait()


def shrink_kernel(place_ref, normed_ref, other_ref, own_ref, out_ref):
    out_ref[...] = own_ref[...] + block_product(normed_ref, place_ref[0], other_ref)


def fetch_kernel(first, after_ref, weights_ref, out_ref, sem):
    for copy in fetches(row_parts(weights_ref, out_ref, first, sem.shape[0]), sem):
        copy.wait()


def query_kernel(normed_ref, wq_ref, *refs):
    *near_refs, out_ref, wq_buf, sem = refs
    first = sum(near_ref.shape[0] for near_ref in near_refs)
    chunks = sem.shape[0]
    span = wq_buf.shape[0] // chunks
    copies = fetches(row_parts(wq_ref, wq_buf, first, chunks), sem)
    total, start = jnp.zeros(out_ref.shape, jnp.float32), 0
    for near_ref in near_refs:
        stop = start + near_ref.shape[0]
        total = total + jnp.dot(
            normed_ref[:, start:stop], near_ref[...], preferred_element_type=jnp.float32
        )
        start = stop
    for c, copy in enumerate(copies):
        copy.wait()
        total = total + jnp.dot(
            normed_ref[:, first + c * span : first + (c + 1) * span],
            wq_buf[c * span : (c + 1) * span, :],
            preferred_element_type=jnp.float32,
        )
    out_ref[...] = total


def rotated(values, cosine, sine):
    half = HEAD_DIM // 2
    turned = jnp.concatenate([values[:, half:], values[:, :half]], axis=1)
    return values * cosine + turned * sine


def finish_kernel(
    seq_count, acc_ref, key_ref, value_ref, uq_own, uq_other, uv_own, uv_other,
    cos_ref, sin_ref, *parts_and_outs,
):
    parts, (query_ref, keyout_ref, valueout_ref, wide, tall) = parts_and_outs[:-5], parts_and_outs[-5:]
    first = lax.axis_index("replica") == 0
    rows = acc_ref.shape[0]
    steps = rows // seq_count
    heads = acc_ref.shape[1] // HEAD_DIM
    shrunk = functools.reduce(jnp.add, [part[...] for part in parts])
    shrunk = shrunk.astype(jnp.bfloat16).astype(jnp.float32)
    half = ADAPTER_RANK // 2

    def lifted(low, high, own, other):
        mine = jnp.where(first, low, high).astype(jnp.bfloat16)
        theirs = jnp.where(first, high, low).astype(jnp.bfloat16)
        return adapter_scale * (
            jnp.dot(mine, own[...], preferred_element_type=jnp.float32)
            + jnp.dot(theirs, other[...], preferred_element_type=jnp.float32)
        )

    raw = acc_ref[...] + lifted(shrunk[:, :half], shrunk[:, half : 2 * half], uq_own, uq_other)
    raw = raw.astype(jnp.bfloat16).astype(jnp.float32)
    cosine, sine = cos_ref[...], sin_ref[...]
    for h in range(heads):
        columns = slice(h * HEAD_DIM, (h + 1) * HEAD_DIM)
        wide[h, 0:rows, :] = rotated(raw[:, columns], cosine, sine)
    for n in range(seq_count):
        for h in range(heads):
            tall[pl.ds((n * heads + h) * steps, steps), :] = wide[
                h, pl.ds(n, steps, stride=seq_count), :
            ]
    query_ref[...] = tall[...].astype(jnp.bfloat16)
    keyout_ref[...] = key_ref[...].astype(jnp.bfloat16)
    value = value_ref[...] + lifted(
        shrunk[:, 2 * half : 3 * half], shrunk[:, 3 * half :], uv_own, uv_other
    )
    valueout_ref[...] = value.astype(jnp.bfloat16)


def fresh_kernel(
    seq_count, query_ref, key_ref, value_ref, cos_ref, sin_ref, wo_ref,
    fresh_ref, level_ref, query_out, wo_out, sem,
):
    copies = fetches(row_parts(wo_ref, wo_out, 0, sem.shape[0]), sem)
    lane = lax.broadcasted_iota(jnp.int32, (1, HEAD_DIM), 1)
    columns = []
    steps = key_ref.shape[0] // seq_count
    per_seq = fresh_ref.shape[0] // seq_count
    query_out[...] = query_ref[...]
    queries = query_ref[...].astype(jnp.float32)
    keys = rotated(key_ref[...].astype(jnp.float32), cos_ref[...], sin_ref[...])
    keys = keys.astype(jnp.bfloat16).astype(jnp.float32)
    values = value_ref[...].astype(jnp.float32)
    step = lax.rem(lax.broadcasted_iota(jnp.int32, (per_seq, 1), 0), steps)
    for n in range(seq_count):
        rows = slice(n * per_seq, (n + 1) * per_seq)
        query = queries[rows]
        scores = []
        for t in range(steps):
            place = t * seq_count + n
            score = jnp.sum(query * keys[place : place + 1], axis=-1, keepdims=True) * inv_root
            scores.append(jnp.where(step >= t, score, negative))
        top = functools.reduce(jnp.maximum, scores)
        weights = [
            jnp.where(step >= t, jnp.exp(score - top), 0.0) for t, score in enumerate(scores)
        ]
        total = functools.reduce(jnp.add, weights)
        summed = jnp.zeros((per_seq, HEAD_DIM), jnp.float32)
        for t, weight in enumerate(weights):
            place = t * seq_count + n
            summed = summed + weight.astype(jnp.bfloat16).astype(jnp.float32) * values[
                place : place + 1
            ]
        fresh_ref[rows, :] = summed
        columns.append(jnp.where(lane == 0, top, jnp.where(lane == 1, total, 0.0)))
    columns = rows_padded(jnp.concatenate(columns, axis=0), HEAD_DIM)
    level_ref[...] = jnp.transpose(columns)[0 : level_ref.shape[0], :]
    for copy in copies:
        copy.wait()


def pieces_of(top, total):
    rows = lax.broadcasted_iota(jnp.int32, (16, HEAD_DIM), 0)
    packed = jnp.zeros((16, HEAD_DIM), jnp.float32)
    for first, left in ((0, top), (3, total)):
        for c in range(3):
            piece = left.astype(jnp.bfloat16).astype(jnp.float32)
            left = left - piece
            packed = jnp.where(rows == first + c, piece, packed)
    return packed.astype(jnp.bfloat16)


def top_and_total(part_ref, held_rows):
    pieces = part_ref[padded(held_rows, 16) :, :].astype(jnp.float32)
    return (
        pieces[0:1] + (pieces[1:2] + pieces[2:3]),
        pieces[3:4] + (pieces[4:5] + pieces[5:6]),
    )


def turned_rows(rows):
    count = padded(len(rows), 8)
    place = lax.broadcasted_iota(jnp.int32, (count, HEAD_DIM), 0)
    stacked = jnp.zeros((count, HEAD_DIM), jnp.float32)
    for k, row in enumerate(rows):
        stacked = jnp.where(place == k, row, stacked)
    return jnp.transpose(rows_padded(stacked, HEAD_DIM))


def cache_kernel(
    odd, first, reach_ref, query_ref, kc_ref, vc_ref, wo_ref, *refs
):
    copies = []
    if first is not None:
        *refs, wo_out, scores_buf, weights_buf, sem = refs
        copies = fetches(row_parts(wo_ref, wo_out, first, sem.shape[0]), sem)
    else:
        *refs, scores_buf, weights_buf = refs
    *earlier, out_ref = refs
    entries, held_rows, _ = query_ref.shape
    seq_count, kv_heads, span, _ = kc_ref.shape
    peers = 2 * entries
    per_seq = held_rows // seq_count
    mean_rows = padded(held_rows, 16)
    tensor = lax.axis_index("tensor")
    spots = tensor * span + lax.broadcasted_iota(jnp.int32, (span, HEAD_DIM), 0)
    live = spots < reach_ref[0:1, :]
    lane = lax.broadcasted_iota(jnp.int32, (span, HEAD_DIM), 1)
    owners = [lax.bitwise_xor(tensor, 2 * e + odd) for e in range(entries)]
    heads = [owner * kv_heads // peers for owner in owners]
    for blocks in earlier:
        for e in range(entries):
            place = lax.bitwise_xor(tensor, 2 * e + 1 - odd)
            out_ref[place] = blocks[place]
    batch = 4
    for lead in range(0, entries, batch):
        part = range(lead, min(lead + batch, entries))
        turned = [
            jnp.transpose(rows_padded(query_ref[e].astype(jnp.float32), HEAD_DIM)).astype(
                jnp.bfloat16
            )
            for e in part
        ]
        for k, e in enumerate(part):
            scores = None
            for n in range(seq_count):
                score = jnp.dot(
                    kc_ref[n, heads[e]], turned[k], preferred_element_type=jnp.float32
                )
                scores = score if n == 0 else jnp.where(lane < n * per_seq, scores, score)
            scores_buf[k] = jnp.where(live, scores, negative)
        tops = [
            jnp.maximum(jnp.max(scores_buf[k], axis=0, keepdims=True), 0.1 * negative)
            for k in range(len(part))
        ]
        for k, e in enumerate(part):
            weights = jnp.exp((scores_buf[k] - tops[k]) * inv_root)
            total = jnp.sum(weights, axis=0, keepdims=True)
            out_ref[owners[e], mean_rows:, :] = pieces_of(tops[k] * inv_root, total)
            weights_buf[k] = jnp.transpose(weights)
        for k, e in enumerate(part):
            sums = [
                jnp.dot(
                    weights_buf[k, n * per_seq : (n + 1) * per_seq, :].astype(jnp.bfloat16),
                    vc_ref[n, heads[e]],
                    preferred_element_type=jnp.float32,
                )
                for n in range(seq_count)
            ]
            sums = rows_padded(jnp.concatenate(sums, axis=0), mean_rows)
            out_ref[owners[e], 0:mean_rows, :] = sums.astype(jnp.bfloat16)
    for copy in copies:
        copy.wait()


def merge_kernel(seq_count, blocks_ref, fresh_ref, level_ref, *refs):
    wo_refs, (out_ref, wide) = refs[:-2], refs[-2:]
    peers, folded, lanes = out_ref.shape
    heads = wide.shape[0]
    held_rows = fresh_ref.shape[0]
    rows = held_rows // heads
    steps = rows // seq_count
    folds = folded // rows
    per_seq = heads * steps
    mean_rows = padded(held_rows, 16)
    stats = [top_and_total(blocks_ref.at[b], held_rows) for b in range(peers)]
    stats.append((level_ref[0:1, :], level_ref[1:2, :]))
    top = functools.reduce(jnp.maximum, [stat[0] for stat in stats])
    factors = [jnp.exp(stat[0] - top) for stat in stats]
    total = functools.reduce(jnp.add, [factor * stat[1] for factor, stat in zip(factors, stats)])
    total = jnp.where(total > 0.0, total, 1.0)
    columns = turned_rows([factor / total for factor in factors])
    mixed = fresh_ref[...] * columns[0:held_rows, peers : peers + 1]
    for b in range(peers):
        mixed = mixed + (
            blocks_ref[b, 0:mean_rows, :].astype(jnp.float32)[0:held_rows]
            * columns[0:held_rows, b : b + 1]
        )
    for n in range(seq_count):
        for h in range(heads):
            first = n * per_seq + h * steps
            wide[h, pl.ds(n, steps, stride=seq_count), :] = mixed[first : first + steps]
    attention = jnp.concatenate([wide[h, 0:rows, :] for h in range(heads)], axis=1)
    attention = attention.astype(jnp.bfloat16)
    width = folds * lanes
    starts = [0]
    for wo_ref in wo_refs:
        starts.append(starts[-1] + wo_ref.shape[0])
    for p in range(peers):
        share = functools.reduce(
            jnp.add,
            [
                jnp.dot(
                    attention[:, start : start + wo_ref.shape[0]],
                    wo_ref[:, p * width : (p + 1) * width],
                    preferred_element_type=jnp.float32,
                )
                for start, wo_ref in zip(starts, wo_refs)
            ],
        )
        if folds > 1:
            share = jnp.concatenate(
                [share[:, c * lanes : (c + 1) * lanes] for c in range(folds)], axis=0
            )
        out_ref[p] = share.astype(out_ref.dtype)


def sum_kernel(rest_ref, parts_ref, out_ref):
    total = functools.reduce(
        jnp.add, [parts_ref[b].astype(jnp.float32) for b in range(parts_ref.shape[0])]
    )
    rows = rest_ref.shape[0]
    steps, seqs, _ = out_ref.shape
    folds, lanes = total.shape[0] // rows, total.shape[1]
    for c in range(folds):
        columns = slice(c * lanes, (c + 1) * lanes)
        piece = total[c * rows : (c + 1) * rows] + rest_ref[:, columns]
        for s in range(steps):
            out_ref[s, :, columns] = piece[s * seqs : (s + 1) * seqs].astype(jnp.bfloat16)


def crossed(value, mask):
    pairs = [(source, source ^ mask) for source in range(lax.axis_size("tensor"))]
    return lax.ppermute(value, "tensor", pairs)


def exchanged(value):
    return lax.all_to_all(value, "tensor", split_axis=0, concat_axis=0, tiled=True)


def along_z(values):
    return [values[0]] + [crossed(value, 2 * p) for p, value in enumerate(values) if p]


def body(
    layer_input_hidden,
    rmsnorm_gain_weight,
    wq,
    wk,
    wv,
    wo,
    adapter_down_stored,
    adapter_up_query,
    adapter_up_value,
    adapter_block_owner,
    rotated_key_cache,
    cached_value_rows,
    cache_valid_lengths,
):
    f32, bf16 = jnp.float32, jnp.bfloat16
    shape = jax.ShapeDtypeStruct
    steps, seqs, model_width = layer_input_hidden.shape
    peers = lax.axis_size("tensor")
    tensor_index = lax.axis_index("tensor")
    rows = steps * seqs
    local_heads = wq.shape[1] // HEAD_DIM
    held_rows = rows * local_heads
    kv_width = wk.shape[1]
    width = model_width // peers
    group = QUERY_HEADS // KEY_VALUE_HEADS

    pairs = [(0, 1), (1, 0)]
    other_down = lax.ppermute(adapter_down_stored, "replica", pairs)
    other_up_query = lax.ppermute(adapter_up_query, "replica", pairs)
    other_up_value = lax.ppermute(adapter_up_value, "replica", pairs)

    near_rows = model_width // 4
    near_shape = shape((near_rows, wq.shape[1]), bf16)
    normed, cosine, sine, rest, reach, own_shrunk, place, wq_first = kernel_call(
        functools.partial(norm_kernel, peers, local_heads),
        (
            shape((rows, model_width), bf16),
            shape((rows, HEAD_DIM), f32),
            shape((rows, HEAD_DIM), f32),
            shape((rows, width), f32),
            shape((8, HEAD_DIM), jnp.int32),
            shape((rows, 2 * ADAPTER_RANK), f32),
            shape((1,), jnp.int32),
            near_shape,
        ),
        [far] * 6,
        (vmem,) * 6 + (smem, vmem),
        [
            pltpu.SMEM(cache_valid_lengths.shape, jnp.int32),
            pltpu.SMEM(adapter_block_owner.shape, jnp.int32),
            pltpu.VMEM(layer_input_hidden.shape, bf16),
            pltpu.VMEM(adapter_down_stored.shape, bf16),
            pltpu.VMEM(rmsnorm_gain_weight.shape, bf16),
            pltpu.SemaphoreType.DMA((9,)),
        ],
        limit=8,
        moved=wq.size // 2,
    )(
        cache_valid_lengths, adapter_block_owner, layer_input_hidden, adapter_down_stored,
        rmsnorm_gain_weight, wq,
    )
    own_shrunk, other_down, other_up_query, other_up_value = lax.optimization_barrier(
        (own_shrunk, other_down, other_up_query, other_up_value)
    )
    partial = kernel_call(
        shrink_kernel,
        shape((rows, 2 * ADAPTER_RANK), f32),
        [smem, vmem, vmem, vmem],
        vmem,
        limit=4,
    )(place, normed, other_down, own_shrunk)
    wq_second = kernel_call(
        functools.partial(fetch_kernel, near_rows),
        near_shape,
        [vmem, far],
        vmem,
        [pltpu.SemaphoreType.DMA((4,))],
        limit=2,
        moved=wq.size // 2,
    )(partial, wq)

    key_sum = jnp.dot(normed, wk, preferred_element_type=f32)
    value_sum = jnp.dot(normed, wv, preferred_element_type=f32)
    partial = partial + crossed(partial, 1)
    partial, normed, key_sum = lax.optimization_barrier((partial, normed, key_sum))
    shrink_parts = along_z([partial] * (peers // 2))

    query_sum = kernel_call(
        query_kernel,
        shape((rows, wq.shape[1]), f32),
        [vmem, far, vmem, vmem],
        vmem,
        [
            pltpu.VMEM((model_width - 2 * near_rows, wq.shape[1]), bf16),
            pltpu.SemaphoreType.DMA((8,)),
        ],
        limit=12,
        moved=wq.size,
        flops=2 * rows * wq.size,
    )(normed, wq, wq_first, wq_second)

    queries, key_raw, value_raw = kernel_call(
        functools.partial(finish_kernel, seqs),
        (
            shape((held_rows, HEAD_DIM), bf16),
            shape((rows, kv_width), bf16),
            shape((rows, kv_width), bf16),
        ),
        [vmem] * (9 + peers // 2),
        (vmem,) * 3,
        [
            pltpu.VMEM((local_heads, padded(rows, 8), HEAD_DIM), f32),
            pltpu.VMEM((held_rows, HEAD_DIM), f32),
        ],
        limit=4,
    )(
        query_sum, key_sum, value_sum, adapter_up_query, other_up_query,
        adapter_up_value, other_up_value, cosine, sine, *shrink_parts,
    )
    met_queries = along_z([queries] * (peers // 2))[1:]

    if kv_width != HEAD_DIM:
        kv_index = tensor_index * local_heads // group

        def own_head(value):
            heads = lax.all_gather(value, "tensor", axis=1, tiled=True)
            return lax.dynamic_slice_in_dim(heads, kv_index * HEAD_DIM, HEAD_DIM, 1)

        key_raw, value_raw = own_head(key_raw), own_head(value_raw)

    cut = wo.shape[0] // 2
    wo_shape = shape((cut, model_width), bf16)
    fresh, fresh_level, queries, wo_first = kernel_call(
        functools.partial(fresh_kernel, seqs),
        (
            shape((held_rows, HEAD_DIM), f32),
            shape((8, HEAD_DIM), f32),
            shape((held_rows, HEAD_DIM), bf16),
            wo_shape,
        ),
        [vmem] * 5 + [far],
        (vmem,) * 4,
        [pltpu.SemaphoreType.DMA((8,))],
        limit=4,
        moved=wo.size,
    )(queries, key_raw, value_raw, cosine, sine, wo)
    held = jnp.stack([queries] + met_queries)
    others = crossed(held, 1)

    span = rotated_key_cache.shape[2]
    blocks_shape = shape((peers, padded(held_rows, 16) + 16, HEAD_DIM), bf16)
    buffers = [pltpu.VMEM((4, span, HEAD_DIM), f32), pltpu.VMEM((4, HEAD_DIM, span), f32)]
    even_blocks, wo_second = kernel_call(
        functools.partial(cache_kernel, 0, cut),
        (blocks_shape, wo_shape),
        [vmem] * 4 + [far],
        (vmem, vmem),
        buffers + [pltpu.SemaphoreType.DMA((8,))],
        limit=8,
        moved=wo.size,
    )(reach, held, rotated_key_cache, cached_value_rows, wo)
    blocks = kernel_call(
        functools.partial(cache_kernel, 1, None),
        blocks_shape,
        [vmem] * 4 + [far, vmem],
        vmem,
        buffers,
        limit=8,
    )(reach, others, rotated_key_cache, cached_value_rows, wo, even_blocks)

    folds = width // 256 if (rows * (width // 256)) % 16 == 0 else 1
    shares = kernel_call(
        functools.partial(merge_kernel, seqs),
        shape((peers, rows * folds, width // folds), bf16),
        [vmem] * 5,
        vmem,
        [pltpu.VMEM((local_heads, padded(rows, 8), HEAD_DIM), f32)],
        limit=6,
    )(exchanged(blocks), fresh, fresh_level, wo_first, wo_second)
    return kernel_call(
        sum_kernel,
        shape((steps, seqs, width), bf16),
        [vmem] * 2,
        vmem,
        limit=4,
    )(rest, exchanged(shares))


def solution(mesh):
    return jax.shard_map(
        body,
        mesh=mesh,
        in_specs=(
            P(None, ("groups", "replica"), None),
            P(),
            P(None, "tensor"),
            P(None, "tensor"),
            P(None, "tensor"),
            P("tensor", None),
            P(("replica", "tensor"), None),
            P("replica", "tensor"),
            P("replica", "tensor"),
            P(),
            P(("groups", "replica"), None, "tensor", None),
            P(("groups", "replica"), None, "tensor", None),
            P(("groups", "replica")),
        ),
        out_specs=P(None, ("groups", "replica"), "tensor"),
        check_vma=False,
    )
```

```python
import functools
import math

import jax
import jax.numpy as jnp
from jax import lax
from jax.experimental import pallas as pl
from jax.experimental.pallas import tpu as pltpu
from jax.sharding import PartitionSpec as P

QUERY_HEADS = 64
KEY_VALUE_HEADS = 8
HEAD_DIM = 128
ADAPTER_RANK = 64


adapter_scale = 2.0
rope_base = 500000.0
negative = -1e30
inv_root = 1.0 / math.sqrt(HEAD_DIM)
MIB = 1 << 20

vmem = pl.BlockSpec(memory_space=pltpu.VMEM)
smem = pl.BlockSpec(memory_space=pltpu.SMEM)
far = pl.BlockSpec(memory_space=pl.ANY)


def padded(count, multiple):
    return -(-count // multiple) * multiple


def rows_padded(value, rows):
    if value.shape[0] == rows:
        return value
    filler = jnp.zeros((rows - value.shape[0],) + value.shape[1:], value.dtype)
    return jnp.concatenate([value, filler], axis=0)


def kernel_call(kernel, outs, specs, out_specs, scratch=(), limit=16, moved=0, flops=0):
    call = pl.pallas_call(
        kernel,
        out_shape=outs,
        in_specs=specs,
        out_specs=out_specs,
        scratch_shapes=list(scratch),
        compiler_params=pltpu.CompilerParams(vmem_limit_bytes=limit * MIB),
        cost_estimate=pl.CostEstimate(flops=flops, bytes_accessed=moved, transcendentals=0),
    )

    def run(*operands):
        return call(
            *[
                pltpu.with_memory_space_constraint(operand, pltpu.HBM) if spec is far else operand
                for operand, spec in zip(operands, specs)
            ]
        )

    return run


def fetches(pairs, sem):
    copies = [
        pltpu.make_async_copy(far_ref, near, sem.at[k]) for k, (far_ref, near) in enumerate(pairs)
    ]
    for copy in copies:
        copy.start()
    return copies


def row_parts(far_ref, near, first, pieces):
    span = near.shape[0] // pieces
    return [
        (far_ref.at[pl.ds(first + c * span, span)], near.at[pl.ds(c * span, span)])
        for c in range(pieces)
    ]


def features_of(normed_ref, owner_ref, held, block_rows):
    place = jnp.int32(0)
    for j in range(owner_ref.shape[0]):
        place = jnp.where(owner_ref[j] == held, jnp.int32(j), place)
    return normed_ref[:, pl.ds(pl.multiple_of(place * block_rows, block_rows), block_rows)]


def norm_kernel(
    peers, heads, lengths_ref, owner_ref, x_ref, down_ref, gain_ref,
    normed_ref, cos_ref, sin_ref, rest_ref, reach_ref, shrunk_ref, features_ref,
    lengths, owner, x_buf, down_buf, gain, sem,
):
    copies = fetches(
        [
            (lengths_ref, lengths),
            (owner_ref, owner),
            (x_ref, x_buf),
            (down_ref, down_buf),
            (gain_ref, gain),
        ],
        sem,
    )
    steps, seqs, _ = x_ref.shape
    rows, width = rest_ref.shape
    half = HEAD_DIM // 2
    row = lax.broadcasted_iota(jnp.int32, (rows, HEAD_DIM), 0)
    lane = lax.broadcasted_iota(jnp.int32, (rows, HEAD_DIM), 1)
    copies[0].wait()
    positions = jnp.zeros((rows, HEAD_DIM), jnp.int32)
    for s in range(steps):
        for n in range(seqs):
            positions = jnp.where(row == s * seqs + n, lengths[n] + s, positions)
    low = lane < half
    exponent = jnp.where(low, lane, lane - half).astype(jnp.float32) * (2.0 / HEAD_DIM)
    angles = positions.astype(jnp.float32) * jnp.exp(exponent * -math.log(rope_base))
    sine = jnp.sin(angles)
    cos_ref[...] = jnp.cos(angles)
    sin_ref[...] = jnp.where(low, -sine, sine)
    place = lax.broadcasted_iota(jnp.int32, reach_ref.shape, 1)
    reach = jnp.zeros(reach_ref.shape, jnp.int32)
    per_seq = heads * steps
    for n in range(seqs):
        mine = jnp.logical_and(place >= n * per_seq, place < (n + 1) * per_seq)
        reach = jnp.where(mine, lengths[n], reach)
    reach_ref[...] = reach
    copies[2].wait()
    values = jnp.concatenate([x_buf[s].astype(jnp.float32) for s in range(steps)], axis=0)
    factor = lax.rsqrt(jnp.mean(values * values, axis=-1, keepdims=True) + 1e-05)
    copies[4].wait()
    normed = values * factor * gain[...].astype(jnp.float32).reshape(1, -1)
    normed_ref[...] = normed.astype(jnp.bfloat16)
    replica, tensor = lax.axis_index("replica"), lax.axis_index("tensor")
    for s in range(steps):
        part = x_buf[s, :, pl.ds(pl.multiple_of(tensor * width, width), width)]
        rest_ref[s * seqs : (s + 1) * seqs, :] = part.astype(jnp.float32)
    copies[1].wait()
    copies[3].wait()
    block_rows = down_ref.shape[0]
    features_ref[...] = features_of(
        normed_ref, owner, (1 - replica) * peers + tensor, block_rows
    )
    shrunk_ref[...] = jnp.dot(
        features_of(normed_ref, owner, replica * peers + tensor, block_rows),
        down_buf[...],
        preferred_element_type=jnp.float32,
    )


def shrink_kernel(features_ref, other_ref, own_ref, normed_ref, out_ref, normed_out):
    normed_out[...] = normed_ref[...]
    out_ref[...] = own_ref[...] + jnp.dot(
        features_ref[...], other_ref[...], preferred_element_type=jnp.float32
    )


def fetch_kernel(first, value_ref, weights_ref, value_out, weights_out, sem):
    copies = fetches(row_parts(weights_ref, weights_out, first, sem.shape[0]), sem)
    value_out[...] = value_ref[...]
    for copy in copies:
        copy.wait()


def query_kernel(normed_ref, wq_ref, *refs):
    *near_refs, out_ref, wq_buf, sem = refs
    first = sum(near_ref.shape[0] for near_ref in near_refs)
    chunks = sem.shape[0]
    span = wq_buf.shape[0] // chunks
    copies = fetches(row_parts(wq_ref, wq_buf, first, chunks), sem)
    total, start = jnp.zeros(out_ref.shape, jnp.float32), 0
    for near_ref in near_refs:
        stop = start + near_ref.shape[0]
        total = total + jnp.dot(
            normed_ref[:, start:stop], near_ref[...], preferred_element_type=jnp.float32
        )
        start = stop
    for c, copy in enumerate(copies):
        copy.wait()
        total = total + jnp.dot(
            normed_ref[:, first + c * span : first + (c + 1) * span],
            wq_buf[c * span : (c + 1) * span, :],
            preferred_element_type=jnp.float32,
        )
    out_ref[...] = total


def rotated(values, cosine, sine):
    half = HEAD_DIM // 2
    turned = jnp.concatenate([values[:, half:], values[:, :half]], axis=1)
    return values * cosine + turned * sine


def finish_kernel(
    seq_count, acc_ref, key_ref, value_ref, uq_own, uq_other, uv_own, uv_other,
    cos_ref, sin_ref, *parts_and_outs,
):
    parts, (query_ref, keyout_ref, valueout_ref, wide, tall) = parts_and_outs[:-5], parts_and_outs[-5:]
    first = lax.axis_index("replica") == 0
    rows = acc_ref.shape[0]
    steps = rows // seq_count
    heads = acc_ref.shape[1] // HEAD_DIM
    shrunk = functools.reduce(jnp.add, [part[...] for part in parts])
    shrunk = shrunk.astype(jnp.bfloat16).astype(jnp.float32)
    half = ADAPTER_RANK // 2

    def lifted(low, high, own, other):
        mine = jnp.where(first, low, high).astype(jnp.bfloat16)
        theirs = jnp.where(first, high, low).astype(jnp.bfloat16)
        return adapter_scale * (
            jnp.dot(mine, own[...], preferred_element_type=jnp.float32)
            + jnp.dot(theirs, other[...], preferred_element_type=jnp.float32)
        )

    raw = acc_ref[...] + lifted(shrunk[:, :half], shrunk[:, half : 2 * half], uq_own, uq_other)
    raw = raw.astype(jnp.bfloat16).astype(jnp.float32)
    cosine, sine = cos_ref[...], sin_ref[...]
    for h in range(heads):
        columns = slice(h * HEAD_DIM, (h + 1) * HEAD_DIM)
        wide[h, 0:rows, :] = rotated(raw[:, columns], cosine, sine)
    for n in range(seq_count):
        for h in range(heads):
            tall[pl.ds((n * heads + h) * steps, steps), :] = wide[
                h, pl.ds(n, steps, stride=seq_count), :
            ]
    query_ref[...] = tall[...].astype(jnp.bfloat16)
    keyout_ref[...] = key_ref[...].astype(jnp.bfloat16)
    value = value_ref[...] + lifted(
        shrunk[:, 2 * half : 3 * half], shrunk[:, 3 * half :], uv_own, uv_other
    )
    valueout_ref[...] = value.astype(jnp.bfloat16)


def fresh_kernel(
    seq_count, query_ref, key_ref, value_ref, cos_ref, sin_ref, wo_ref,
    fresh_ref, level_ref, query_out, wo_out, sem,
):
    copies = fetches(row_parts(wo_ref, wo_out, 0, sem.shape[0]), sem)
    lane = lax.broadcasted_iota(jnp.int32, (1, HEAD_DIM), 1)
    columns = []
    steps = key_ref.shape[0] // seq_count
    per_seq = fresh_ref.shape[0] // seq_count
    query_out[...] = query_ref[...]
    queries = query_ref[...].astype(jnp.float32)
    keys = rotated(key_ref[...].astype(jnp.float32), cos_ref[...], sin_ref[...])
    keys = keys.astype(jnp.bfloat16).astype(jnp.float32)
    values = value_ref[...].astype(jnp.float32)
    step = lax.rem(lax.broadcasted_iota(jnp.int32, (per_seq, 1), 0), steps)
    for n in range(seq_count):
        rows = slice(n * per_seq, (n + 1) * per_seq)
        query = queries[rows]
        scores = []
        for t in range(steps):
            place = t * seq_count + n
            score = jnp.sum(query * keys[place : place + 1], axis=-1, keepdims=True) * inv_root
            scores.append(jnp.where(step >= t, score, negative))
        top = functools.reduce(jnp.maximum, scores)
        weights = [
            jnp.where(step >= t, jnp.exp(score - top), 0.0) for t, score in enumerate(scores)
        ]
        total = functools.reduce(jnp.add, weights)
        summed = jnp.zeros((per_seq, HEAD_DIM), jnp.float32)
        for t, weight in enumerate(weights):
            place = t * seq_count + n
            summed = summed + weight.astype(jnp.bfloat16).astype(jnp.float32) * values[
                place : place + 1
            ]
        fresh_ref[rows, :] = summed
        columns.append(jnp.where(lane == 0, top, jnp.where(lane == 1, total, 0.0)))
    columns = rows_padded(jnp.concatenate(columns, axis=0), HEAD_DIM)
    level_ref[...] = jnp.transpose(columns)[0 : level_ref.shape[0], :]
    for copy in copies:
        copy.wait()


def pieces_of(top, total):
    rows = lax.broadcasted_iota(jnp.int32, (16, HEAD_DIM), 0)
    packed = jnp.zeros((16, HEAD_DIM), jnp.float32)
    for first, left in ((0, top), (3, total)):
        for c in range(3):
            piece = left.astype(jnp.bfloat16).astype(jnp.float32)
            left = left - piece
            packed = jnp.where(rows == first + c, piece, packed)
    return packed.astype(jnp.bfloat16)


def top_and_total(part_ref, held_rows):
    pieces = part_ref[padded(held_rows, 16) :, :].astype(jnp.float32)
    return (
        pieces[0:1] + (pieces[1:2] + pieces[2:3]),
        pieces[3:4] + (pieces[4:5] + pieces[5:6]),
    )


def turned_rows(rows):
    count = padded(len(rows), 8)
    place = lax.broadcasted_iota(jnp.int32, (count, HEAD_DIM), 0)
    stacked = jnp.zeros((count, HEAD_DIM), jnp.float32)
    for k, row in enumerate(rows):
        stacked = jnp.where(place == k, row, stacked)
    return jnp.transpose(rows_padded(stacked, HEAD_DIM))


def cache_kernel(
    masks, first, reach_ref, query_ref, kc_ref, vc_ref, wo_ref, *refs
):
    copies = []
    if first is not None:
        *refs, wo_out, scores_buf, weights_buf, sem = refs
        copies = fetches(row_parts(wo_ref, wo_out, first, sem.shape[0]), sem)
    else:
        *refs, scores_buf, weights_buf = refs
    *earlier, out_ref = refs
    entries, held_rows, _ = query_ref.shape
    seq_count, kv_heads, span, _ = kc_ref.shape
    peers = 2 * entries
    per_seq = held_rows // seq_count
    mean_rows = padded(held_rows, 16)
    tensor = lax.axis_index("tensor")
    spots = tensor * span + lax.broadcasted_iota(jnp.int32, (span, HEAD_DIM), 0)
    live = spots < reach_ref[0:1, :]
    lane = lax.broadcasted_iota(jnp.int32, (span, HEAD_DIM), 1)
    owners = [lax.bitwise_xor(tensor, mask) for mask in masks]
    heads = [owner * kv_heads // peers for owner in owners]
    for blocks in earlier:
        for e in range(entries):
            place = lax.bitwise_xor(tensor, masks[e] ^ 1)
            out_ref[place] = blocks[place]
    batch = 4
    for lead in range(0, entries, batch):
        part = range(lead, min(lead + batch, entries))
        turned = [
            jnp.transpose(rows_padded(query_ref[e].astype(jnp.float32), HEAD_DIM)).astype(
                jnp.bfloat16
            )
            for e in part
        ]
        for k, e in enumerate(part):
            scores = None
            for n in range(seq_count):
                score = jnp.dot(
                    kc_ref[n, heads[e]], turned[k], preferred_element_type=jnp.float32
                )
                scores = score if n == 0 else jnp.where(lane < n * per_seq, scores, score)
            scores_buf[k] = jnp.where(live, scores, negative)
        tops = [
            jnp.maximum(jnp.max(scores_buf[k], axis=0, keepdims=True), 0.1 * negative)
            for k in range(len(part))
        ]
        for k, e in enumerate(part):
            weights = jnp.exp((scores_buf[k] - tops[k]) * inv_root)
            total = jnp.sum(weights, axis=0, keepdims=True)
            out_ref[owners[e], mean_rows:, :] = pieces_of(tops[k] * inv_root, total)
            weights_buf[k] = jnp.transpose(weights)
        for k, e in enumerate(part):
            sums = [
                jnp.dot(
                    weights_buf[k, n * per_seq : (n + 1) * per_seq, :].astype(jnp.bfloat16),
                    vc_ref[n, heads[e]],
                    preferred_element_type=jnp.float32,
                )
                for n in range(seq_count)
            ]
            sums = rows_padded(jnp.concatenate(sums, axis=0), mean_rows)
            out_ref[owners[e], 0:mean_rows, :] = sums.astype(jnp.bfloat16)
    for copy in copies:
        copy.wait()


def merge_kernel(seq_count, blocks_ref, fresh_ref, level_ref, *refs):
    wo_refs, (out_ref, wide) = refs[:-2], refs[-2:]
    peers, folded, lanes = out_ref.shape
    heads = wide.shape[0]
    held_rows = fresh_ref.shape[0]
    rows = held_rows // heads
    steps = rows // seq_count
    folds = folded // rows
    per_seq = heads * steps
    mean_rows = padded(held_rows, 16)
    stats = [top_and_total(blocks_ref.at[b], held_rows) for b in range(peers)]
    stats.append((level_ref[0:1, :], level_ref[1:2, :]))
    top = functools.reduce(jnp.maximum, [stat[0] for stat in stats])
    factors = [jnp.exp(stat[0] - top) for stat in stats]
    total = functools.reduce(jnp.add, [factor * stat[1] for factor, stat in zip(factors, stats)])
    total = jnp.where(total > 0.0, total, 1.0)
    columns = turned_rows([factor / total for factor in factors])
    mixed = fresh_ref[...] * columns[0:held_rows, peers : peers + 1]
    for b in range(peers):
        mixed = mixed + (
            blocks_ref[b, 0:mean_rows, :].astype(jnp.float32)[0:held_rows]
            * columns[0:held_rows, b : b + 1]
        )
    for n in range(seq_count):
        for h in range(heads):
            first = n * per_seq + h * steps
            wide[h, pl.ds(n, steps, stride=seq_count), :] = mixed[first : first + steps]
    attention = jnp.concatenate([wide[h, 0:rows, :] for h in range(heads)], axis=1)
    attention = attention.astype(jnp.bfloat16)
    width = folds * lanes
    starts = [0]
    for wo_ref in wo_refs:
        starts.append(starts[-1] + wo_ref.shape[0])
    for p in range(peers):
        share = functools.reduce(
            jnp.add,
            [
                jnp.dot(
                    attention[:, start : start + wo_ref.shape[0]],
                    wo_ref[:, p * width : (p + 1) * width],
                    preferred_element_type=jnp.float32,
                )
                for start, wo_ref in zip(starts, wo_refs)
            ],
        )
        if folds > 1:
            share = jnp.concatenate(
                [share[:, c * lanes : (c + 1) * lanes] for c in range(folds)], axis=0
            )
        out_ref[p] = share.astype(out_ref.dtype)


def sum_kernel(rest_ref, parts_ref, out_ref):
    total = functools.reduce(
        jnp.add, [parts_ref[b].astype(jnp.float32) for b in range(parts_ref.shape[0])]
    )
    rows = rest_ref.shape[0]
    steps, seqs, _ = out_ref.shape
    folds, lanes = total.shape[0] // rows, total.shape[1]
    for c in range(folds):
        columns = slice(c * lanes, (c + 1) * lanes)
        piece = total[c * rows : (c + 1) * rows] + rest_ref[:, columns]
        for s in range(steps):
            out_ref[s, :, columns] = piece[s * seqs : (s + 1) * seqs].astype(jnp.bfloat16)


def crossed(value, mask):
    pairs = [(source, source ^ mask) for source in range(lax.axis_size("tensor"))]
    return lax.ppermute(value, "tensor", pairs)


def exchanged(value):
    return lax.all_to_all(value, "tensor", split_axis=0, concat_axis=0, tiled=True)


def z_masks():
    masks = [lax.axis_size("tensor") // 2]
    while masks[-1] > 2:
        masks.append(masks[-1] // 2)
    return masks


def body(
    layer_input_hidden,
    rmsnorm_gain_weight,
    wq,
    wk,
    wv,
    wo,
    adapter_down_stored,
    adapter_up_query,
    adapter_up_value,
    adapter_block_owner,
    rotated_key_cache,
    cached_value_rows,
    cache_valid_lengths,
):
    f32, bf16 = jnp.float32, jnp.bfloat16
    shape = jax.ShapeDtypeStruct
    steps, seqs, model_width = layer_input_hidden.shape
    peers = lax.axis_size("tensor")
    tensor_index = lax.axis_index("tensor")
    rows = steps * seqs
    local_heads = wq.shape[1] // HEAD_DIM
    held_rows = rows * local_heads
    kv_width = wk.shape[1]
    width = model_width // peers
    group = QUERY_HEADS // KEY_VALUE_HEADS

    pairs = [(0, 1), (1, 0)]
    other_down = lax.ppermute(adapter_down_stored, "replica", pairs)
    other_up_query = lax.ppermute(adapter_up_query, "replica", pairs)
    other_up_value = lax.ppermute(adapter_up_value, "replica", pairs)

    normed, cosine, sine, rest, reach, own_shrunk, features = kernel_call(
        functools.partial(norm_kernel, peers, local_heads),
        (
            shape((rows, model_width), bf16),
            shape((rows, HEAD_DIM), f32),
            shape((rows, HEAD_DIM), f32),
            shape((rows, width), f32),
            shape((8, HEAD_DIM), jnp.int32),
            shape((rows, 2 * ADAPTER_RANK), f32),
            shape((rows, adapter_down_stored.shape[0]), bf16),
        ),
        [far] * 5,
        (vmem,) * 7,
        [
            pltpu.SMEM(cache_valid_lengths.shape, jnp.int32),
            pltpu.SMEM(adapter_block_owner.shape, jnp.int32),
            pltpu.VMEM(layer_input_hidden.shape, bf16),
            pltpu.VMEM(adapter_down_stored.shape, bf16),
            pltpu.VMEM(rmsnorm_gain_weight.shape, bf16),
            pltpu.SemaphoreType.DMA((5,)),
        ],
        limit=8,
    )(
        cache_valid_lengths, adapter_block_owner, layer_input_hidden, adapter_down_stored,
        rmsnorm_gain_weight,
    )
    own_shrunk, other_down, other_up_query, other_up_value = lax.optimization_barrier(
        (own_shrunk, other_down, other_up_query, other_up_value)
    )
    partial, normed = kernel_call(
        shrink_kernel,
        (shape((rows, 2 * ADAPTER_RANK), f32), shape((rows, model_width), bf16)),
        [vmem] * 4,
        (vmem, vmem),
        limit=4,
    )(features, other_down, own_shrunk, normed)

    def fetched(value, weights, quarter):
        span = weights.shape[0] // 4
        return kernel_call(
            functools.partial(fetch_kernel, quarter * span),
            (shape(value.shape, value.dtype), shape((span, weights.shape[1]), bf16)),
            [vmem, far],
            (vmem, vmem),
            [pltpu.SemaphoreType.DMA((4,))],
            limit=2,
            moved=weights.size // 2,
        )(value, weights)

    wq_parts = []
    for mask in [1] + z_masks()[:-1]:
        met = crossed(partial, mask)
        if len(wq_parts) < 2:
            partial, near = fetched(partial, wq, len(wq_parts))
            wq_parts.append(near)
        partial = partial + met
    shrink_parts = [partial, crossed(partial, 2)]

    key_sum = jnp.dot(normed, wk, preferred_element_type=f32)
    value_sum = jnp.dot(normed, wv, preferred_element_type=f32)
    query_sum = kernel_call(
        query_kernel,
        shape((rows, wq.shape[1]), f32),
        [vmem, far, vmem, vmem],
        vmem,
        [
            pltpu.VMEM((model_width // 2, wq.shape[1]), bf16),
            pltpu.SemaphoreType.DMA((8,)),
        ],
        limit=12,
        moved=wq.size,
        flops=2 * rows * wq.size,
    )(normed, wq, *wq_parts)

    queries, key_raw, value_raw = kernel_call(
        functools.partial(finish_kernel, seqs),
        (
            shape((held_rows, HEAD_DIM), bf16),
            shape((rows, kv_width), bf16),
            shape((rows, kv_width), bf16),
        ),
        [vmem] * (9 + len(shrink_parts)),
        (vmem,) * 3,
        [
            pltpu.VMEM((local_heads, padded(rows, 8), HEAD_DIM), f32),
            pltpu.VMEM((held_rows, HEAD_DIM), f32),
        ],
        limit=4,
    )(
        query_sum, key_sum, value_sum, adapter_up_query, other_up_query,
        adapter_up_value, other_up_value, cosine, sine, *shrink_parts,
    )
    if kv_width != HEAD_DIM:
        kv_index = tensor_index * local_heads // group

        def own_head(value):
            heads = lax.all_gather(value, "tensor", axis=1, tiled=True)
            return lax.dynamic_slice_in_dim(heads, kv_index * HEAD_DIM, HEAD_DIM, 1)

        key_raw, value_raw = own_head(key_raw), own_head(value_raw)

    quarter = wo.shape[0] // 4
    met = crossed(queries, z_masks()[0])
    fresh, fresh_level, queries, wo_near = kernel_call(
        functools.partial(fresh_kernel, seqs),
        (
            shape((held_rows, HEAD_DIM), f32),
            shape((8, HEAD_DIM), f32),
            shape((held_rows, HEAD_DIM), bf16),
            shape((quarter, model_width), bf16),
        ),
        [vmem] * 5 + [far],
        (vmem,) * 4,
        [pltpu.SemaphoreType.DMA((4,))],
        limit=4,
        moved=wo.size // 2,
    )(queries, key_raw, value_raw, cosine, sine, wo)
    held, masks, wo_parts = jnp.stack([queries, met]), [0, z_masks()[0]], [wo_near]
    for mask in z_masks()[1:]:
        met = crossed(held, mask)
        if len(wo_parts) < 2:
            held, wo_near = fetched(held, wo, 1)
            wo_parts.append(wo_near)
        held, masks = jnp.concatenate([held, met]), masks + [mask ^ other for other in masks]
    others = crossed(held, 1)

    span = rotated_key_cache.shape[2]
    blocks_shape = shape((peers, padded(held_rows, 16) + 16, HEAD_DIM), bf16)
    buffers = [pltpu.VMEM((4, span, HEAD_DIM), f32), pltpu.VMEM((4, HEAD_DIM, span), f32)]
    even_blocks, wo_near = kernel_call(
        functools.partial(cache_kernel, masks, 2 * quarter),
        (blocks_shape, shape((2 * quarter, model_width), bf16)),
        [vmem] * 4 + [far],
        (vmem, vmem),
        buffers + [pltpu.SemaphoreType.DMA((8,))],
        limit=8,
        moved=wo.size,
    )(reach, held, rotated_key_cache, cached_value_rows, wo)
    blocks = kernel_call(
        functools.partial(cache_kernel, [mask ^ 1 for mask in masks], None),
        blocks_shape,
        [vmem] * 4 + [far, vmem],
        vmem,
        buffers,
        limit=8,
    )(reach, others, rotated_key_cache, cached_value_rows, wo, even_blocks)

    folds = width // 256 if (rows * (width // 256)) % 16 == 0 else 1
    shares = kernel_call(
        functools.partial(merge_kernel, seqs),
        shape((peers, rows * folds, width // folds), bf16),
        [vmem] * (4 + len(wo_parts)),
        vmem,
        [pltpu.VMEM((local_heads, padded(rows, 8), HEAD_DIM), f32)],
        limit=6,
    )(exchanged(blocks), fresh, fresh_level, *wo_parts, wo_near)
    return kernel_call(
        sum_kernel,
        shape((steps, seqs, width), bf16),
        [vmem] * 2,
        vmem,
        limit=4,
    )(rest, exchanged(shares))


def solution(mesh):
    return jax.shard_map(
        body,
        mesh=mesh,
        in_specs=(
            P(None, ("groups", "replica"), None),
            P(),
            P(None, "tensor"),
            P(None, "tensor"),
            P(None, "tensor"),
            P("tensor", None),
            P(("replica", "tensor"), None),
            P("replica", "tensor"),
            P("replica", "tensor"),
            P(),
            P(("groups", "replica"), None, "tensor", None),
            P(("groups", "replica"), None, "tensor", None),
            P(("groups", "replica")),
        ),
        out_specs=P(None, ("groups", "replica"), "tensor"),
        check_vma=False,
    )
```

```python
import functools
import math

import jax
import jax.numpy as jnp
from jax import lax
from jax.experimental import pallas as pl
from jax.experimental.pallas import tpu as pltpu
from jax.sharding import PartitionSpec as P

QUERY_HEADS = 64
KEY_VALUE_HEADS = 8
HEAD_DIM = 128
ADAPTER_RANK = 64


adapter_scale = 2.0
rope_base = 500000.0
negative = -1e30
inv_root = 1.0 / math.sqrt(HEAD_DIM)
MIB = 1 << 20

vmem = pl.BlockSpec(memory_space=pltpu.VMEM)
smem = pl.BlockSpec(memory_space=pltpu.SMEM)
far = pl.BlockSpec(memory_space=pl.ANY)


def padded(count, multiple):
    return -(-count // multiple) * multiple


def rows_padded(value, rows):
    if value.shape[0] == rows:
        return value
    filler = jnp.zeros((rows - value.shape[0],) + value.shape[1:], value.dtype)
    return jnp.concatenate([value, filler], axis=0)


def kernel_call(kernel, outs, specs, out_specs, scratch=(), limit=16, moved=0, flops=0):
    call = pl.pallas_call(
        kernel,
        out_shape=outs,
        in_specs=specs,
        out_specs=out_specs,
        scratch_shapes=list(scratch),
        compiler_params=pltpu.CompilerParams(vmem_limit_bytes=limit * MIB),
        cost_estimate=pl.CostEstimate(flops=flops, bytes_accessed=moved, transcendentals=0),
    )

    def run(*operands):
        return call(
            *[
                pltpu.with_memory_space_constraint(operand, pltpu.HBM) if spec is far else operand
                for operand, spec in zip(operands, specs)
            ]
        )

    return run


def fetches(pairs, sem):
    copies = [
        pltpu.make_async_copy(far_ref, near, sem.at[k]) for k, (far_ref, near) in enumerate(pairs)
    ]
    for copy in copies:
        copy.start()
    return copies


def features_of(normed_ref, owner_ref, held, block_rows):
    place = jnp.int32(0)
    for j in range(owner_ref.shape[0]):
        place = jnp.where(owner_ref[j] == held, jnp.int32(j), place)
    return normed_ref[:, pl.ds(pl.multiple_of(place * block_rows, block_rows), block_rows)]


def norm_kernel(
    peers, heads, lengths_ref, owner_ref, x_ref, down_ref, gain_ref,
    normed_ref, cos_ref, sin_ref, rest_ref, reach_ref, shrunk_ref, features_ref,
    lengths, owner, x_buf, down_buf, gain, sem,
):
    copies = fetches(
        [
            (lengths_ref, lengths),
            (owner_ref, owner),
            (x_ref, x_buf),
            (down_ref, down_buf),
            (gain_ref, gain),
        ],
        sem,
    )
    steps, seqs, _ = x_ref.shape
    rows, width = rest_ref.shape
    half = HEAD_DIM // 2
    row = lax.broadcasted_iota(jnp.int32, (rows, HEAD_DIM), 0)
    lane = lax.broadcasted_iota(jnp.int32, (rows, HEAD_DIM), 1)
    copies[0].wait()
    positions = jnp.zeros((rows, HEAD_DIM), jnp.int32)
    for s in range(steps):
        for n in range(seqs):
            positions = jnp.where(row == s * seqs + n, lengths[n] + s, positions)
    low = lane < half
    exponent = jnp.where(low, lane, lane - half).astype(jnp.float32) * (2.0 / HEAD_DIM)
    angles = positions.astype(jnp.float32) * jnp.exp(exponent * -math.log(rope_base))
    sine = jnp.sin(angles)
    cos_ref[...] = jnp.cos(angles)
    sin_ref[...] = jnp.where(low, -sine, sine)
    place = lax.broadcasted_iota(jnp.int32, reach_ref.shape, 1)
    reach = jnp.zeros(reach_ref.shape, jnp.int32)
    per_seq = heads * steps
    for n in range(seqs):
        mine = jnp.logical_and(place >= n * per_seq, place < (n + 1) * per_seq)
        reach = jnp.where(mine, lengths[n], reach)
    reach_ref[...] = reach
    copies[2].wait()
    values = jnp.concatenate([x_buf[s].astype(jnp.float32) for s in range(steps)], axis=0)
    factor = lax.rsqrt(jnp.mean(values * values, axis=-1, keepdims=True) + 1e-05)
    copies[4].wait()
    normed = values * factor * gain[...].astype(jnp.float32).reshape(1, -1)
    normed_ref[...] = normed.astype(jnp.bfloat16)
    replica, tensor = lax.axis_index("replica"), lax.axis_index("tensor")
    for s in range(steps):
        part = x_buf[s, :, pl.ds(pl.multiple_of(tensor * width, width), width)]
        rest_ref[s * seqs : (s + 1) * seqs, :] = part.astype(jnp.float32)
    copies[1].wait()
    copies[3].wait()
    block_rows = down_ref.shape[0]
    features_ref[...] = features_of(
        normed_ref, owner, (1 - replica) * peers + tensor, block_rows
    )
    shrunk_ref[...] = jnp.dot(
        features_of(normed_ref, owner, replica * peers + tensor, block_rows),
        down_buf[...],
        preferred_element_type=jnp.float32,
    )


def shrink_kernel(features_ref, other_ref, own_ref, normed_ref, out_ref, normed_out):
    normed_out[...] = normed_ref[...]
    out_ref[...] = own_ref[...] + jnp.dot(
        features_ref[...], other_ref[...], preferred_element_type=jnp.float32
    )


def query_kernel(normed_ref, wq_ref, out_ref):
    out_ref[...] = jnp.dot(normed_ref[...], wq_ref[...], preferred_element_type=jnp.float32)


def rotated(values, cosine, sine):
    half = HEAD_DIM // 2
    turned = jnp.concatenate([values[:, half:], values[:, :half]], axis=1)
    return values * cosine + turned * sine


def finish_kernel(
    seq_count, acc_ref, key_ref, value_ref, uq_own, uq_other, uv_own, uv_other,
    cos_ref, sin_ref, *parts_and_outs,
):
    parts, (query_ref, keyout_ref, valueout_ref, wide, tall) = parts_and_outs[:-5], parts_and_outs[-5:]
    first = lax.axis_index("replica") == 0
    rows = acc_ref.shape[0]
    steps = rows // seq_count
    heads = acc_ref.shape[1] // HEAD_DIM
    shrunk = functools.reduce(jnp.add, [part[...] for part in parts])
    shrunk = shrunk.astype(jnp.bfloat16).astype(jnp.float32)
    half = ADAPTER_RANK // 2

    def lifted(low, high, own, other):
        mine = jnp.where(first, low, high).astype(jnp.bfloat16)
        theirs = jnp.where(first, high, low).astype(jnp.bfloat16)
        return adapter_scale * (
            jnp.dot(mine, own[...], preferred_element_type=jnp.float32)
            + jnp.dot(theirs, other[...], preferred_element_type=jnp.float32)
        )

    raw = acc_ref[...] + lifted(shrunk[:, :half], shrunk[:, half : 2 * half], uq_own, uq_other)
    raw = raw.astype(jnp.bfloat16).astype(jnp.float32)
    cosine, sine = cos_ref[...], sin_ref[...]
    for h in range(heads):
        columns = slice(h * HEAD_DIM, (h + 1) * HEAD_DIM)
        wide[h, 0:rows, :] = rotated(raw[:, columns], cosine, sine)
    for n in range(seq_count):
        for h in range(heads):
            tall[pl.ds((n * heads + h) * steps, steps), :] = wide[
                h, pl.ds(n, steps, stride=seq_count), :
            ]
    query_ref[...] = tall[...].astype(jnp.bfloat16)
    keyout_ref[...] = key_ref[...].astype(jnp.bfloat16)
    value = value_ref[...] + lifted(
        shrunk[:, 2 * half : 3 * half], shrunk[:, 3 * half :], uv_own, uv_other
    )
    valueout_ref[...] = value.astype(jnp.bfloat16)


def fresh_kernel(
    seq_count, query_ref, key_ref, value_ref, cos_ref, sin_ref, fresh_ref, level_ref, query_out
):
    lane = lax.broadcasted_iota(jnp.int32, (1, HEAD_DIM), 1)
    columns = []
    steps = key_ref.shape[0] // seq_count
    per_seq = fresh_ref.shape[0] // seq_count
    query_out[...] = query_ref[...]
    queries = query_ref[...].astype(jnp.float32)
    keys = rotated(key_ref[...].astype(jnp.float32), cos_ref[...], sin_ref[...])
    keys = keys.astype(jnp.bfloat16).astype(jnp.float32)
    values = value_ref[...].astype(jnp.float32)
    step = lax.rem(lax.broadcasted_iota(jnp.int32, (per_seq, 1), 0), steps)
    for n in range(seq_count):
        rows = slice(n * per_seq, (n + 1) * per_seq)
        query = queries[rows]
        scores = []
        for t in range(steps):
            place = t * seq_count + n
            score = jnp.sum(query * keys[place : place + 1], axis=-1, keepdims=True) * inv_root
            scores.append(jnp.where(step >= t, score, negative))
        top = functools.reduce(jnp.maximum, scores)
        weights = [
            jnp.where(step >= t, jnp.exp(score - top), 0.0) for t, score in enumerate(scores)
        ]
        total = functools.reduce(jnp.add, weights)
        summed = jnp.zeros((per_seq, HEAD_DIM), jnp.float32)
        for t, weight in enumerate(weights):
            place = t * seq_count + n
            summed = summed + weight.astype(jnp.bfloat16).astype(jnp.float32) * values[
                place : place + 1
            ]
        fresh_ref[rows, :] = summed
        columns.append(jnp.where(lane == 0, top, jnp.where(lane == 1, total, 0.0)))
    columns = rows_padded(jnp.concatenate(columns, axis=0), HEAD_DIM)
    level_ref[...] = jnp.transpose(columns)[0 : level_ref.shape[0], :]


def pieces_of(top, total):
    rows = lax.broadcasted_iota(jnp.int32, (16, HEAD_DIM), 0)
    packed = jnp.zeros((16, HEAD_DIM), jnp.float32)
    for first, left in ((0, top), (3, total)):
        for c in range(3):
            piece = left.astype(jnp.bfloat16).astype(jnp.float32)
            left = left - piece
            packed = jnp.where(rows == first + c, piece, packed)
    return packed.astype(jnp.bfloat16)


def top_and_total(part_ref, held_rows):
    pieces = part_ref[padded(held_rows, 16) :, :].astype(jnp.float32)
    return (
        pieces[0:1] + (pieces[1:2] + pieces[2:3]),
        pieces[3:4] + (pieces[4:5] + pieces[5:6]),
    )


def turned_rows(rows):
    count = padded(len(rows), 8)
    place = lax.broadcasted_iota(jnp.int32, (count, HEAD_DIM), 0)
    stacked = jnp.zeros((count, HEAD_DIM), jnp.float32)
    for k, row in enumerate(rows):
        stacked = jnp.where(place == k, row, stacked)
    return jnp.transpose(rows_padded(stacked, HEAD_DIM))


def cache_kernel(
    masks, reach_ref, query_ref, kc_ref, vc_ref, *refs
):
    *earlier, out_ref, scores_buf, weights_buf = refs
    entries, held_rows, _ = query_ref.shape
    seq_count, kv_heads, span, _ = kc_ref.shape
    peers = 2 * entries
    per_seq = held_rows // seq_count
    mean_rows = padded(held_rows, 16)
    tensor = lax.axis_index("tensor")
    spots = tensor * span + lax.broadcasted_iota(jnp.int32, (span, HEAD_DIM), 0)
    live = spots < reach_ref[0:1, :]
    lane = lax.broadcasted_iota(jnp.int32, (span, HEAD_DIM), 1)
    owners = [lax.bitwise_xor(tensor, mask) for mask in masks]
    heads = [owner * kv_heads // peers for owner in owners]
    for blocks in earlier:
        for e in range(entries):
            place = lax.bitwise_xor(tensor, masks[e] ^ 1)
            out_ref[place] = blocks[place]
    batch = 4
    for lead in range(0, entries, batch):
        part = range(lead, min(lead + batch, entries))
        turned = [
            jnp.transpose(rows_padded(query_ref[e].astype(jnp.float32), HEAD_DIM)).astype(
                jnp.bfloat16
            )
            for e in part
        ]
        for k, e in enumerate(part):
            scores = None
            for n in range(seq_count):
                score = jnp.dot(
                    kc_ref[n, heads[e]], turned[k], preferred_element_type=jnp.float32
                )
                scores = score if n == 0 else jnp.where(lane < n * per_seq, scores, score)
            scores_buf[k] = jnp.where(live, scores, negative)
        tops = [
            jnp.maximum(jnp.max(scores_buf[k], axis=0, keepdims=True), 0.1 * negative)
            for k in range(len(part))
        ]
        for k, e in enumerate(part):
            weights = jnp.exp((scores_buf[k] - tops[k]) * inv_root)
            total = jnp.sum(weights, axis=0, keepdims=True)
            out_ref[owners[e], mean_rows:, :] = pieces_of(tops[k] * inv_root, total)
            weights_buf[k] = jnp.transpose(weights)
        for k, e in enumerate(part):
            sums = [
                jnp.dot(
                    weights_buf[k, n * per_seq : (n + 1) * per_seq, :].astype(jnp.bfloat16),
                    vc_ref[n, heads[e]],
                    preferred_element_type=jnp.float32,
                )
                for n in range(seq_count)
            ]
            sums = rows_padded(jnp.concatenate(sums, axis=0), mean_rows)
            out_ref[owners[e], 0:mean_rows, :] = sums.astype(jnp.bfloat16)


def merge_kernel(seq_count, blocks_ref, fresh_ref, level_ref, wo_ref, out_ref, wide):
    peers, folded, lanes = out_ref.shape
    heads = wide.shape[0]
    held_rows = fresh_ref.shape[0]
    rows = held_rows // heads
    steps = rows // seq_count
    folds = folded // rows
    per_seq = heads * steps
    mean_rows = padded(held_rows, 16)
    stats = [top_and_total(blocks_ref.at[b], held_rows) for b in range(peers)]
    stats.append((level_ref[0:1, :], level_ref[1:2, :]))
    top = functools.reduce(jnp.maximum, [stat[0] for stat in stats])
    factors = [jnp.exp(stat[0] - top) for stat in stats]
    total = functools.reduce(jnp.add, [factor * stat[1] for factor, stat in zip(factors, stats)])
    total = jnp.where(total > 0.0, total, 1.0)
    columns = turned_rows([factor / total for factor in factors])
    mixed = fresh_ref[...] * columns[0:held_rows, peers : peers + 1]
    for b in range(peers):
        mixed = mixed + (
            blocks_ref[b, 0:mean_rows, :].astype(jnp.float32)[0:held_rows]
            * columns[0:held_rows, b : b + 1]
        )
    for n in range(seq_count):
        for h in range(heads):
            first = n * per_seq + h * steps
            wide[h, pl.ds(n, steps, stride=seq_count), :] = mixed[first : first + steps]
    attention = jnp.concatenate([wide[h, 0:rows, :] for h in range(heads)], axis=1)
    attention = attention.astype(jnp.bfloat16)
    width = folds * lanes
    for p in range(peers):
        share = jnp.dot(
            attention,
            wo_ref[:, p * width : (p + 1) * width],
            preferred_element_type=jnp.float32,
        )
        if folds > 1:
            share = jnp.concatenate(
                [share[:, c * lanes : (c + 1) * lanes] for c in range(folds)], axis=0
            )
        out_ref[p] = share.astype(out_ref.dtype)


def sum_kernel(rest_ref, parts_ref, out_ref):
    total = functools.reduce(
        jnp.add, [parts_ref[b].astype(jnp.float32) for b in range(parts_ref.shape[0])]
    )
    rows = rest_ref.shape[0]
    steps, seqs, _ = out_ref.shape
    folds, lanes = total.shape[0] // rows, total.shape[1]
    for c in range(folds):
        columns = slice(c * lanes, (c + 1) * lanes)
        piece = total[c * rows : (c + 1) * rows] + rest_ref[:, columns]
        for s in range(steps):
            out_ref[s, :, columns] = piece[s * seqs : (s + 1) * seqs].astype(jnp.bfloat16)


def crossed(value, mask):
    pairs = [(source, source ^ mask) for source in range(lax.axis_size("tensor"))]
    return lax.ppermute(value, "tensor", pairs)


def exchanged(value):
    return lax.all_to_all(value, "tensor", split_axis=0, concat_axis=0, tiled=True)


def z_masks():
    masks = [lax.axis_size("tensor") // 2]
    while masks[-1] > 2:
        masks.append(masks[-1] // 2)
    return masks


def body(
    layer_input_hidden,
    rmsnorm_gain_weight,
    wq,
    wk,
    wv,
    wo,
    adapter_down_stored,
    adapter_up_query,
    adapter_up_value,
    adapter_block_owner,
    rotated_key_cache,
    cached_value_rows,
    cache_valid_lengths,
):
    f32, bf16 = jnp.float32, jnp.bfloat16
    shape = jax.ShapeDtypeStruct
    steps, seqs, model_width = layer_input_hidden.shape
    peers = lax.axis_size("tensor")
    tensor_index = lax.axis_index("tensor")
    rows = steps * seqs
    local_heads = wq.shape[1] // HEAD_DIM
    held_rows = rows * local_heads
    kv_width = wk.shape[1]
    width = model_width // peers
    group = QUERY_HEADS // KEY_VALUE_HEADS

    wq = lax.ppermute(wq, "replica", [(0, 0), (1, 1)])
    pairs = [(0, 1), (1, 0)]
    other_down = lax.ppermute(adapter_down_stored, "replica", pairs)
    other_up_query = lax.ppermute(adapter_up_query, "replica", pairs)
    other_up_value = lax.ppermute(adapter_up_value, "replica", pairs)

    normed, cosine, sine, rest, reach, own_shrunk, features = kernel_call(
        functools.partial(norm_kernel, peers, local_heads),
        (
            shape((rows, model_width), bf16),
            shape((rows, HEAD_DIM), f32),
            shape((rows, HEAD_DIM), f32),
            shape((rows, width), f32),
            shape((8, HEAD_DIM), jnp.int32),
            shape((rows, 2 * ADAPTER_RANK), f32),
            shape((rows, adapter_down_stored.shape[0]), bf16),
        ),
        [far] * 5,
        (vmem,) * 7,
        [
            pltpu.SMEM(cache_valid_lengths.shape, jnp.int32),
            pltpu.SMEM(adapter_block_owner.shape, jnp.int32),
            pltpu.VMEM(layer_input_hidden.shape, bf16),
            pltpu.VMEM(adapter_down_stored.shape, bf16),
            pltpu.VMEM(rmsnorm_gain_weight.shape, bf16),
            pltpu.SemaphoreType.DMA((5,)),
        ],
        limit=8,
    )(
        cache_valid_lengths, adapter_block_owner, layer_input_hidden, adapter_down_stored,
        rmsnorm_gain_weight,
    )
    own_shrunk, other_down, other_up_query, other_up_value = lax.optimization_barrier(
        (own_shrunk, other_down, other_up_query, other_up_value)
    )
    partial, normed = kernel_call(
        shrink_kernel,
        (shape((rows, 2 * ADAPTER_RANK), f32), shape((rows, model_width), bf16)),
        [vmem] * 4,
        (vmem, vmem),
        limit=4,
    )(features, other_down, own_shrunk, normed)

    for mask in [1] + z_masks()[:-1]:
        partial = partial + crossed(partial, mask)
    shrink_parts = [partial, crossed(partial, 2)]

    key_sum = jnp.dot(normed, wk, preferred_element_type=f32)
    value_sum = jnp.dot(normed, wv, preferred_element_type=f32)
    query_sum = kernel_call(
        query_kernel,
        shape((rows, wq.shape[1]), f32),
        [vmem, vmem],
        vmem,
        limit=4,
        moved=wq.size,
        flops=2 * rows * wq.size,
    )(normed, wq)

    queries, key_raw, value_raw = kernel_call(
        functools.partial(finish_kernel, seqs),
        (
            shape((held_rows, HEAD_DIM), bf16),
            shape((rows, kv_width), bf16),
            shape((rows, kv_width), bf16),
        ),
        [vmem] * (9 + len(shrink_parts)),
        (vmem,) * 3,
        [
            pltpu.VMEM((local_heads, padded(rows, 8), HEAD_DIM), f32),
            pltpu.VMEM((held_rows, HEAD_DIM), f32),
        ],
        limit=4,
    )(
        query_sum, key_sum, value_sum, adapter_up_query, other_up_query,
        adapter_up_value, other_up_value, cosine, sine, *shrink_parts,
    )
    if kv_width != HEAD_DIM:
        kv_index = tensor_index * local_heads // group

        def own_head(value):
            heads = lax.all_gather(value, "tensor", axis=1, tiled=True)
            return lax.dynamic_slice_in_dim(heads, kv_index * HEAD_DIM, HEAD_DIM, 1)

        key_raw, value_raw = own_head(key_raw), own_head(value_raw)

    met = crossed(queries, z_masks()[0])
    fresh, fresh_level, queries = kernel_call(
        functools.partial(fresh_kernel, seqs),
        (
            shape((held_rows, HEAD_DIM), f32),
            shape((8, HEAD_DIM), f32),
            shape((held_rows, HEAD_DIM), bf16),
        ),
        [vmem] * 5,
        (vmem,) * 3,
        limit=4,
    )(queries, key_raw, value_raw, cosine, sine)
    held, masks = jnp.stack([queries, met]), [0, z_masks()[0]]
    for mask in z_masks()[1:]:
        held = jnp.concatenate([held, crossed(held, mask)])
        masks = masks + [mask ^ other for other in masks]
    others = crossed(held, 1)

    span = rotated_key_cache.shape[2]
    blocks_shape = shape((peers, padded(held_rows, 16) + 16, HEAD_DIM), bf16)
    buffers = [pltpu.VMEM((4, span, HEAD_DIM), f32), pltpu.VMEM((4, HEAD_DIM, span), f32)]

    def cache_part(its_masks, *operands):
        return kernel_call(
            functools.partial(cache_kernel, its_masks),
            blocks_shape,
            [vmem] * (3 + len(operands)),
            vmem,
            buffers,
            limit=6,
        )(reach, operands[0], rotated_key_cache, cached_value_rows, *operands[1:])

    even_blocks = cache_part(masks, held)
    blocks = cache_part([mask ^ 1 for mask in masks], others, even_blocks)

    folds = width // 256 if (rows * (width // 256)) % 16 == 0 else 1
    shares = kernel_call(
        functools.partial(merge_kernel, seqs),
        shape((peers, rows * folds, width // folds), bf16),
        [vmem] * 4,
        vmem,
        [pltpu.VMEM((local_heads, padded(rows, 8), HEAD_DIM), f32)],
        limit=6,
    )(exchanged(blocks), fresh, fresh_level, wo)
    return kernel_call(
        sum_kernel,
        shape((steps, seqs, width), bf16),
        [vmem] * 2,
        vmem,
        limit=4,
    )(rest, exchanged(shares))


def solution(mesh):
    return jax.shard_map(
        body,
        mesh=mesh,
        in_specs=(
            P(None, ("groups", "replica"), None),
            P(),
            P(None, "tensor"),
            P(None, "tensor"),
            P(None, "tensor"),
            P("tensor", None),
            P(("replica", "tensor"), None),
            P("replica", "tensor"),
            P("replica", "tensor"),
            P(),
            P(("groups", "replica"), None, "tensor", None),
            P(("groups", "replica"), None, "tensor", None),
            P(("groups", "replica")),
        ),
        out_specs=P(None, ("groups", "replica"), "tensor"),
        check_vma=False,
    )
```

```python
import functools
import math

import jax
import jax.numpy as jnp
from jax import lax
from jax.experimental import pallas as pl
from jax.experimental.pallas import tpu as pltpu
from jax.sharding import PartitionSpec as P

QUERY_HEADS = 64
KEY_VALUE_HEADS = 8
HEAD_DIM = 128
ADAPTER_RANK = 64


adapter_scale = 2.0
rope_base = 500000.0
negative = -1e30
inv_root = 1.0 / math.sqrt(HEAD_DIM)
MIB = 1 << 20

vmem = pl.BlockSpec(memory_space=pltpu.VMEM)
smem = pl.BlockSpec(memory_space=pltpu.SMEM)
far = pl.BlockSpec(memory_space=pl.ANY)


def padded(count, multiple):
    return -(-count // multiple) * multiple


def rows_padded(value, rows):
    if value.shape[0] == rows:
        return value
    filler = jnp.zeros((rows - value.shape[0],) + value.shape[1:], value.dtype)
    return jnp.concatenate([value, filler], axis=0)


def kernel_call(kernel, outs, specs, out_specs, scratch=(), limit=16, moved=0, flops=0):
    call = pl.pallas_call(
        kernel,
        out_shape=outs,
        in_specs=specs,
        out_specs=out_specs,
        scratch_shapes=list(scratch),
        compiler_params=pltpu.CompilerParams(vmem_limit_bytes=limit * MIB),
        cost_estimate=pl.CostEstimate(flops=flops, bytes_accessed=moved, transcendentals=0),
    )

    def run(*operands):
        return call(
            *[
                pltpu.with_memory_space_constraint(operand, pltpu.HBM) if spec is far else operand
                for operand, spec in zip(operands, specs)
            ]
        )

    return run


def fetches(pairs, sem):
    copies = [
        pltpu.make_async_copy(far_ref, near, sem.at[k]) for k, (far_ref, near) in enumerate(pairs)
    ]
    for copy in copies:
        copy.start()
    return copies


def features_of(normed_ref, owner_ref, held, block_rows):
    place = jnp.int32(0)
    for j in range(owner_ref.shape[0]):
        place = jnp.where(owner_ref[j] == held, jnp.int32(j), place)
    return normed_ref[:, pl.ds(pl.multiple_of(place * block_rows, block_rows), block_rows)]


def norm_kernel(
    peers, heads, lengths_ref, owner_ref, x_ref, down_ref, gain_ref, beside_ref,
    normed_ref, cos_ref, sin_ref, rest_ref, reach_ref, shrunk_ref, features_ref,
    lengths, owner, x_buf, down_buf, gain, sem,
):
    copies = fetches(
        [
            (lengths_ref, lengths),
            (owner_ref, owner),
            (x_ref, x_buf),
            (down_ref, down_buf),
            (gain_ref, gain),
        ],
        sem,
    )
    steps, seqs, _ = x_ref.shape
    rows, width = rest_ref.shape
    half = HEAD_DIM // 2
    row = lax.broadcasted_iota(jnp.int32, (rows, HEAD_DIM), 0)
    lane = lax.broadcasted_iota(jnp.int32, (rows, HEAD_DIM), 1)
    copies[0].wait()
    positions = jnp.zeros((rows, HEAD_DIM), jnp.int32)
    for s in range(steps):
        for n in range(seqs):
            positions = jnp.where(row == s * seqs + n, lengths[n] + s, positions)
    low = lane < half
    exponent = jnp.where(low, lane, lane - half).astype(jnp.float32) * (2.0 / HEAD_DIM)
    angles = positions.astype(jnp.float32) * jnp.exp(exponent * -math.log(rope_base))
    sine = jnp.sin(angles)
    cos_ref[...] = jnp.cos(angles)
    sin_ref[...] = jnp.where(low, -sine, sine)
    place = lax.broadcasted_iota(jnp.int32, reach_ref.shape, 1)
    reach = jnp.zeros(reach_ref.shape, jnp.int32)
    per_seq = heads * steps
    for n in range(seqs):
        mine = jnp.logical_and(place >= n * per_seq, place < (n + 1) * per_seq)
        reach = jnp.where(mine, lengths[n], reach)
    reach_ref[...] = reach
    copies[2].wait()
    values = jnp.concatenate([x_buf[s].astype(jnp.float32) for s in range(steps)], axis=0)
    factor = lax.rsqrt(jnp.mean(values * values, axis=-1, keepdims=True) + 1e-05)
    copies[4].wait()
    normed = values * factor * gain[...].astype(jnp.float32).reshape(1, -1)
    normed_ref[...] = normed.astype(jnp.bfloat16)
    replica, tensor = lax.axis_index("replica"), lax.axis_index("tensor")
    for s in range(steps):
        part = x_buf[s, :, pl.ds(pl.multiple_of(tensor * width, width), width)]
        rest_ref[s * seqs : (s + 1) * seqs, :] = part.astype(jnp.float32)
    copies[1].wait()
    copies[3].wait()
    block_rows = down_ref.shape[0]
    features_ref[...] = features_of(
        normed_ref, owner, (1 - replica) * peers + tensor, block_rows
    )
    shrunk_ref[...] = jnp.dot(
        features_of(normed_ref, owner, replica * peers + tensor, block_rows),
        down_buf[...],
        preferred_element_type=jnp.float32,
    )


def shrink_kernel(
    features_ref, other_ref, own_ref, normed_ref, beside_ref, out_ref, normed_out
):
    normed_out[...] = normed_ref[...]
    out_ref[...] = own_ref[...] + jnp.dot(
        features_ref[...], other_ref[...], preferred_element_type=jnp.float32
    )


def query_kernel(normed_ref, wq_ref, out_ref):
    out_ref[...] = jnp.dot(normed_ref[...], wq_ref[...], preferred_element_type=jnp.float32)


def rotated(values, cosine, sine):
    half = HEAD_DIM // 2
    turned = jnp.concatenate([values[:, half:], values[:, :half]], axis=1)
    return values * cosine + turned * sine


def finish_kernel(
    seq_count, acc_ref, key_ref, value_ref, uq_own, uq_other, uv_own, uv_other,
    cos_ref, sin_ref, beside_ref, *parts_and_outs,
):
    parts, (query_ref, keyout_ref, valueout_ref, wide, tall) = parts_and_outs[:-5], parts_and_outs[-5:]
    first = lax.axis_index("replica") == 0
    rows = acc_ref.shape[0]
    steps = rows // seq_count
    heads = acc_ref.shape[1] // HEAD_DIM
    shrunk = functools.reduce(jnp.add, [part[...] for part in parts])
    shrunk = shrunk.astype(jnp.bfloat16).astype(jnp.float32)
    half = ADAPTER_RANK // 2

    def lifted(low, high, own, other):
        mine = jnp.where(first, low, high).astype(jnp.bfloat16)
        theirs = jnp.where(first, high, low).astype(jnp.bfloat16)
        return adapter_scale * (
            jnp.dot(mine, own[...], preferred_element_type=jnp.float32)
            + jnp.dot(theirs, other[...], preferred_element_type=jnp.float32)
        )

    raw = acc_ref[...] + lifted(shrunk[:, :half], shrunk[:, half : 2 * half], uq_own, uq_other)
    raw = raw.astype(jnp.bfloat16).astype(jnp.float32)
    cosine, sine = cos_ref[...], sin_ref[...]
    for h in range(heads):
        columns = slice(h * HEAD_DIM, (h + 1) * HEAD_DIM)
        wide[h, 0:rows, :] = rotated(raw[:, columns], cosine, sine)
    for n in range(seq_count):
        for h in range(heads):
            tall[pl.ds((n * heads + h) * steps, steps), :] = wide[
                h, pl.ds(n, steps, stride=seq_count), :
            ]
    query_ref[...] = tall[...].astype(jnp.bfloat16)
    keyout_ref[...] = key_ref[...].astype(jnp.bfloat16)
    value = value_ref[...] + lifted(
        shrunk[:, 2 * half : 3 * half], shrunk[:, 3 * half :], uv_own, uv_other
    )
    valueout_ref[...] = value.astype(jnp.bfloat16)


def fresh_kernel(
    seq_count, query_ref, key_ref, value_ref, cos_ref, sin_ref, beside_ref,
    fresh_ref, level_ref, query_out,
):
    lane = lax.broadcasted_iota(jnp.int32, (1, HEAD_DIM), 1)
    columns = []
    steps = key_ref.shape[0] // seq_count
    per_seq = fresh_ref.shape[0] // seq_count
    for peer in range(query_out.shape[0]):
        query_out[peer] = query_ref[...]
    queries = query_ref[...].astype(jnp.float32)
    keys = rotated(key_ref[...].astype(jnp.float32), cos_ref[...], sin_ref[...])
    keys = keys.astype(jnp.bfloat16).astype(jnp.float32)
    values = value_ref[...].astype(jnp.float32)
    step = lax.rem(lax.broadcasted_iota(jnp.int32, (per_seq, 1), 0), steps)
    for n in range(seq_count):
        rows = slice(n * per_seq, (n + 1) * per_seq)
        query = queries[rows]
        scores = []
        for t in range(steps):
            place = t * seq_count + n
            score = jnp.sum(query * keys[place : place + 1], axis=-1, keepdims=True) * inv_root
            scores.append(jnp.where(step >= t, score, negative))
        top = functools.reduce(jnp.maximum, scores)
        weights = [
            jnp.where(step >= t, jnp.exp(score - top), 0.0) for t, score in enumerate(scores)
        ]
        total = functools.reduce(jnp.add, weights)
        summed = jnp.zeros((per_seq, HEAD_DIM), jnp.float32)
        for t, weight in enumerate(weights):
            place = t * seq_count + n
            summed = summed + weight.astype(jnp.bfloat16).astype(jnp.float32) * values[
                place : place + 1
            ]
        fresh_ref[rows, :] = summed
        columns.append(jnp.where(lane == 0, top, jnp.where(lane == 1, total, 0.0)))
    columns = rows_padded(jnp.concatenate(columns, axis=0), HEAD_DIM)
    level_ref[...] = jnp.transpose(columns)[0 : level_ref.shape[0], :]


def pieces_of(top, total):
    rows = lax.broadcasted_iota(jnp.int32, (16, HEAD_DIM), 0)
    packed = jnp.zeros((16, HEAD_DIM), jnp.float32)
    for first, left in ((0, top), (3, total)):
        for c in range(3):
            piece = left.astype(jnp.bfloat16).astype(jnp.float32)
            left = left - piece
            packed = jnp.where(rows == first + c, piece, packed)
    return packed.astype(jnp.bfloat16)


def top_and_total(part_ref, held_rows):
    pieces = part_ref[padded(held_rows, 16) :, :].astype(jnp.float32)
    return (
        pieces[0:1] + (pieces[1:2] + pieces[2:3]),
        pieces[3:4] + (pieces[4:5] + pieces[5:6]),
    )


def turned_rows(rows):
    count = padded(len(rows), 8)
    place = lax.broadcasted_iota(jnp.int32, (count, HEAD_DIM), 0)
    stacked = jnp.zeros((count, HEAD_DIM), jnp.float32)
    for k, row in enumerate(rows):
        stacked = jnp.where(place == k, row, stacked)
    return jnp.transpose(rows_padded(stacked, HEAD_DIM))


def cache_kernel(
    reach_ref, query_ref, kc_ref, vc_ref, beside_ref, out_ref, scores_buf, weights_buf
):
    peers, held_rows, _ = query_ref.shape
    seq_count, kv_heads, span, _ = kc_ref.shape
    per_seq = held_rows // seq_count
    mean_rows = padded(held_rows, 16)
    tensor = lax.axis_index("tensor")
    spots = tensor * span + lax.broadcasted_iota(jnp.int32, (span, HEAD_DIM), 0)
    live = spots < reach_ref[0:1, :]
    lane = lax.broadcasted_iota(jnp.int32, (span, HEAD_DIM), 1)
    heads = [e * kv_heads // peers for e in range(peers)]
    batch = 4
    for lead in range(0, peers, batch):
        part = range(lead, min(lead + batch, peers))
        turned = [
            jnp.transpose(rows_padded(query_ref[e].astype(jnp.float32), HEAD_DIM)).astype(
                jnp.bfloat16
            )
            for e in part
        ]
        for k, e in enumerate(part):
            scores = None
            for n in range(seq_count):
                score = jnp.dot(
                    kc_ref[n, heads[e]], turned[k], preferred_element_type=jnp.float32
                )
                scores = score if n == 0 else jnp.where(lane < n * per_seq, scores, score)
            scores_buf[k] = jnp.where(live, scores, negative)
        tops = [
            jnp.maximum(jnp.max(scores_buf[k], axis=0, keepdims=True), 0.1 * negative)
            for k in range(len(part))
        ]
        for k, e in enumerate(part):
            weights = jnp.exp((scores_buf[k] - tops[k]) * inv_root)
            total = jnp.sum(weights, axis=0, keepdims=True)
            out_ref[e, mean_rows:, :] = pieces_of(tops[k] * inv_root, total)
            weights_buf[k] = jnp.transpose(weights)
        for k, e in enumerate(part):
            sums = [
                jnp.dot(
                    weights_buf[k, n * per_seq : (n + 1) * per_seq, :].astype(jnp.bfloat16),
                    vc_ref[n, heads[e]],
                    preferred_element_type=jnp.float32,
                )
                for n in range(seq_count)
            ]
            sums = rows_padded(jnp.concatenate(sums, axis=0), mean_rows)
            out_ref[e, 0:mean_rows, :] = sums.astype(jnp.bfloat16)


def merge_kernel(seq_count, blocks_ref, fresh_ref, level_ref, wo_ref, out_ref, wide):
    peers, folded, lanes = out_ref.shape
    heads = wide.shape[0]
    held_rows = fresh_ref.shape[0]
    rows = held_rows // heads
    steps = rows // seq_count
    folds = folded // rows
    per_seq = heads * steps
    mean_rows = padded(held_rows, 16)
    stats = [top_and_total(blocks_ref.at[b], held_rows) for b in range(peers)]
    stats.append((level_ref[0:1, :], level_ref[1:2, :]))
    top = functools.reduce(jnp.maximum, [stat[0] for stat in stats])
    factors = [jnp.exp(stat[0] - top) for stat in stats]
    total = functools.reduce(jnp.add, [factor * stat[1] for factor, stat in zip(factors, stats)])
    total = jnp.where(total > 0.0, total, 1.0)
    columns = turned_rows([factor / total for factor in factors])
    mixed = fresh_ref[...] * columns[0:held_rows, peers : peers + 1]
    for b in range(peers):
        mixed = mixed + (
            blocks_ref[b, 0:mean_rows, :].astype(jnp.float32)[0:held_rows]
            * columns[0:held_rows, b : b + 1]
        )
    for n in range(seq_count):
        for h in range(heads):
            first = n * per_seq + h * steps
            wide[h, pl.ds(n, steps, stride=seq_count), :] = mixed[first : first + steps]
    attention = jnp.concatenate([wide[h, 0:rows, :] for h in range(heads)], axis=1)
    attention = attention.astype(jnp.bfloat16)
    width = folds * lanes
    for p in range(peers):
        share = jnp.dot(
            attention,
            wo_ref[:, p * width : (p + 1) * width],
            preferred_element_type=jnp.float32,
        )
        if folds > 1:
            share = jnp.concatenate(
                [share[:, c * lanes : (c + 1) * lanes] for c in range(folds)], axis=0
            )
        out_ref[p] = share.astype(out_ref.dtype)


def sum_kernel(rest_ref, parts_ref, out_ref):
    total = functools.reduce(
        jnp.add, [parts_ref[b].astype(jnp.float32) for b in range(parts_ref.shape[0])]
    )
    rows = rest_ref.shape[0]
    steps, seqs, _ = out_ref.shape
    folds, lanes = total.shape[0] // rows, total.shape[1]
    for c in range(folds):
        columns = slice(c * lanes, (c + 1) * lanes)
        piece = total[c * rows : (c + 1) * rows] + rest_ref[:, columns]
        for s in range(steps):
            out_ref[s, :, columns] = piece[s * seqs : (s + 1) * seqs].astype(jnp.bfloat16)


def crossed(value, mask):
    pairs = [(source, source ^ mask) for source in range(lax.axis_size("tensor"))]
    return lax.ppermute(value, "tensor", pairs)


def exchanged(value):
    return lax.all_to_all(value, "tensor", split_axis=0, concat_axis=0, tiled=True)


def z_masks():
    masks = [lax.axis_size("tensor") // 2]
    while masks[-1] > 2:
        masks.append(masks[-1] // 2)
    return masks


def body(
    layer_input_hidden,
    rmsnorm_gain_weight,
    wq,
    wk,
    wv,
    wo,
    adapter_down_stored,
    adapter_up_query,
    adapter_up_value,
    adapter_block_owner,
    rotated_key_cache,
    cached_value_rows,
    cache_valid_lengths,
):
    f32, bf16 = jnp.float32, jnp.bfloat16
    shape = jax.ShapeDtypeStruct
    steps, seqs, model_width = layer_input_hidden.shape
    peers = lax.axis_size("tensor")
    tensor_index = lax.axis_index("tensor")
    rows = steps * seqs
    local_heads = wq.shape[1] // HEAD_DIM
    held_rows = rows * local_heads
    kv_width = wk.shape[1]
    width = model_width // peers
    group = QUERY_HEADS // KEY_VALUE_HEADS

    pairs = [(0, 1), (1, 0)]
    other_down = lax.ppermute(adapter_down_stored, "replica", pairs)
    other_up_query = lax.ppermute(adapter_up_query, "replica", pairs)
    other_up_value = lax.ppermute(adapter_up_value, "replica", pairs)

    normed, cosine, sine, rest, reach, own_shrunk, features = kernel_call(
        functools.partial(norm_kernel, peers, local_heads),
        (
            shape((rows, model_width), bf16),
            shape((rows, HEAD_DIM), f32),
            shape((rows, HEAD_DIM), f32),
            shape((rows, width), f32),
            shape((8, HEAD_DIM), jnp.int32),
            shape((rows, 2 * ADAPTER_RANK), f32),
            shape((rows, adapter_down_stored.shape[0]), bf16),
        ),
        [far] * 6,
        (vmem,) * 7,
        [
            pltpu.SMEM(cache_valid_lengths.shape, jnp.int32),
            pltpu.SMEM(adapter_block_owner.shape, jnp.int32),
            pltpu.VMEM(layer_input_hidden.shape, bf16),
            pltpu.VMEM(adapter_down_stored.shape, bf16),
            pltpu.VMEM(rmsnorm_gain_weight.shape, bf16),
            pltpu.SemaphoreType.DMA((5,)),
        ],
        limit=8,
    )(
        cache_valid_lengths, adapter_block_owner, layer_input_hidden, adapter_down_stored,
        rmsnorm_gain_weight, wo,
    )
    own_shrunk, other_down, other_up_query, other_up_value = lax.optimization_barrier(
        (own_shrunk, other_down, other_up_query, other_up_value)
    )
    partial, normed = kernel_call(
        shrink_kernel,
        (shape((rows, 2 * ADAPTER_RANK), f32), shape((rows, model_width), bf16)),
        [vmem] * 4 + [far],
        (vmem, vmem),
        limit=4,
    )(features, other_down, own_shrunk, normed, wo)

    for mask in [1] + z_masks()[:-1]:
        partial = partial + crossed(partial, mask)
    shrink_parts = [partial, crossed(partial, 2)]

    key_sum = jnp.dot(normed, wk, preferred_element_type=f32)
    value_sum = jnp.dot(normed, wv, preferred_element_type=f32)
    query_sum = kernel_call(
        query_kernel,
        shape((rows, wq.shape[1]), f32),
        [vmem, vmem],
        vmem,
        limit=4,
        moved=wq.size,
        flops=2 * rows * wq.size,
    )(normed, wq)

    queries, key_raw, value_raw = kernel_call(
        functools.partial(finish_kernel, seqs),
        (
            shape((held_rows, HEAD_DIM), bf16),
            shape((rows, kv_width), bf16),
            shape((rows, kv_width), bf16),
        ),
        [vmem] * 9 + [far] + [vmem] * len(shrink_parts),
        (vmem,) * 3,
        [
            pltpu.VMEM((local_heads, padded(rows, 8), HEAD_DIM), f32),
            pltpu.VMEM((held_rows, HEAD_DIM), f32),
        ],
        limit=4,
    )(
        query_sum, key_sum, value_sum, adapter_up_query, other_up_query,
        adapter_up_value, other_up_value, cosine, sine, wq, *shrink_parts,
    )
    if kv_width != HEAD_DIM:
        kv_index = tensor_index * local_heads // group

        def own_head(value):
            heads = lax.all_gather(value, "tensor", axis=1, tiled=True)
            return lax.dynamic_slice_in_dim(heads, kv_index * HEAD_DIM, HEAD_DIM, 1)

        key_raw, value_raw = own_head(key_raw), own_head(value_raw)

    fresh, fresh_level, queries = kernel_call(
        functools.partial(fresh_kernel, seqs),
        (
            shape((held_rows, HEAD_DIM), f32),
            shape((8, HEAD_DIM), f32),
            shape((peers, held_rows, HEAD_DIM), bf16),
        ),
        [vmem] * 5 + [far],
        (vmem,) * 3,
        limit=4,
    )(queries, key_raw, value_raw, cosine, sine, wq)
    span = rotated_key_cache.shape[2]
    blocks_shape = shape((peers, padded(held_rows, 16) + 16, HEAD_DIM), bf16)
    buffers = [pltpu.VMEM((4, span, HEAD_DIM), f32), pltpu.VMEM((4, HEAD_DIM, span), f32)]
    blocks = kernel_call(
        cache_kernel,
        blocks_shape,
        [vmem] * 4 + [far],
        vmem,
        buffers,
        limit=6,
    )(reach, exchanged(queries), rotated_key_cache, cached_value_rows, wq)

    folds = width // 256 if (rows * (width // 256)) % 16 == 0 else 1
    shares = kernel_call(
        functools.partial(merge_kernel, seqs),
        shape((peers, rows * folds, width // folds), bf16),
        [vmem] * 4,
        vmem,
        [pltpu.VMEM((local_heads, padded(rows, 8), HEAD_DIM), f32)],
        limit=6,
    )(exchanged(blocks), fresh, fresh_level, wo)
    return kernel_call(
        sum_kernel,
        shape((steps, seqs, width), bf16),
        [vmem] * 2,
        vmem,
        limit=4,
    )(rest, exchanged(shares))


def solution(mesh):
    return jax.shard_map(
        body,
        mesh=mesh,
        in_specs=(
            P(None, ("groups", "replica"), None),
            P(),
            P(None, "tensor"),
            P(None, "tensor"),
            P(None, "tensor"),
            P("tensor", None),
            P(("replica", "tensor"), None),
            P("replica", "tensor"),
            P("replica", "tensor"),
            P(),
            P(("groups", "replica"), None, "tensor", None),
            P(("groups", "replica"), None, "tensor", None),
            P(("groups", "replica")),
        ),
        out_specs=P(None, ("groups", "replica"), "tensor"),
        check_vma=False,
    )
```

```python
import functools
import math

import jax
import jax.numpy as jnp
from jax import lax
from jax.experimental import pallas as pl
from jax.experimental.pallas import tpu as pltpu
from jax.sharding import PartitionSpec as P

QUERY_HEADS = 64
KEY_VALUE_HEADS = 8
HEAD_DIM = 128
ADAPTER_RANK = 64


adapter_scale = 2.0
rope_base = 500000.0
negative = -1e30
inv_root = 1.0 / math.sqrt(HEAD_DIM)
MIB = 1 << 20

vmem = pl.BlockSpec(memory_space=pltpu.VMEM)
smem = pl.BlockSpec(memory_space=pltpu.SMEM)
far = pl.BlockSpec(memory_space=pl.ANY)


def padded(count, multiple):
    return -(-count // multiple) * multiple


def rows_padded(value, rows):
    if value.shape[0] == rows:
        return value
    filler = jnp.zeros((rows - value.shape[0],) + value.shape[1:], value.dtype)
    return jnp.concatenate([value, filler], axis=0)


def kernel_call(kernel, outs, specs, out_specs, scratch=(), limit=16, moved=0, flops=0):
    call = pl.pallas_call(
        kernel,
        out_shape=outs,
        in_specs=specs,
        out_specs=out_specs,
        scratch_shapes=list(scratch),
        compiler_params=pltpu.CompilerParams(vmem_limit_bytes=limit * MIB),
        cost_estimate=pl.CostEstimate(flops=flops, bytes_accessed=moved, transcendentals=0),
    )

    def run(*operands):
        return call(
            *[
                pltpu.with_memory_space_constraint(operand, pltpu.HBM) if spec is far else operand
                for operand, spec in zip(operands, specs)
            ]
        )

    return run


def fetches(pairs, sem):
    copies = [
        pltpu.make_async_copy(far_ref, near, sem.at[k]) for k, (far_ref, near) in enumerate(pairs)
    ]
    for copy in copies:
        copy.start()
    return copies


def features_of(normed_ref, owner_ref, held, block_rows):
    place = jnp.int32(0)
    for j in range(owner_ref.shape[0]):
        place = jnp.where(owner_ref[j] == held, jnp.int32(j), place)
    return normed_ref[:, pl.ds(pl.multiple_of(place * block_rows, block_rows), block_rows)]


def norm_kernel(
    peers, heads, lengths_ref, owner_ref, x_ref, down_ref, gain_ref, beside_ref,
    normed_ref, cos_ref, sin_ref, rest_ref, reach_ref, shrunk_ref, features_ref,
    lengths, owner, x_buf, down_buf, gain, sem,
):
    copies = fetches(
        [
            (lengths_ref, lengths),
            (owner_ref, owner),
            (x_ref, x_buf),
            (down_ref, down_buf),
            (gain_ref, gain),
        ],
        sem,
    )
    steps, seqs, _ = x_ref.shape
    rows, width = rest_ref.shape
    half = HEAD_DIM // 2
    row = lax.broadcasted_iota(jnp.int32, (rows, HEAD_DIM), 0)
    lane = lax.broadcasted_iota(jnp.int32, (rows, HEAD_DIM), 1)
    copies[0].wait()
    positions = jnp.zeros((rows, HEAD_DIM), jnp.int32)
    for s in range(steps):
        for n in range(seqs):
            positions = jnp.where(row == s * seqs + n, lengths[n] + s, positions)
    low = lane < half
    exponent = jnp.where(low, lane, lane - half).astype(jnp.float32) * (2.0 / HEAD_DIM)
    angles = positions.astype(jnp.float32) * jnp.exp(exponent * -math.log(rope_base))
    sine = jnp.sin(angles)
    cos_ref[...] = jnp.cos(angles)
    sin_ref[...] = jnp.where(low, -sine, sine)
    place = lax.broadcasted_iota(jnp.int32, reach_ref.shape, 1)
    reach = jnp.zeros(reach_ref.shape, jnp.int32)
    per_seq = heads * steps
    for n in range(seqs):
        mine = jnp.logical_and(place >= n * per_seq, place < (n + 1) * per_seq)
        reach = jnp.where(mine, lengths[n], reach)
    reach_ref[...] = reach
    copies[2].wait()
    values = jnp.concatenate([x_buf[s].astype(jnp.float32) for s in range(steps)], axis=0)
    factor = lax.rsqrt(jnp.mean(values * values, axis=-1, keepdims=True) + 1e-05)
    copies[4].wait()
    normed = values * factor * gain[...].astype(jnp.float32).reshape(1, -1)
    normed_ref[...] = normed.astype(jnp.bfloat16)
    replica, tensor = lax.axis_index("replica"), lax.axis_index("tensor")
    for s in range(steps):
        part = x_buf[s, :, pl.ds(pl.multiple_of(tensor * width, width), width)]
        rest_ref[s * seqs : (s + 1) * seqs, :] = part.astype(jnp.float32)
    copies[1].wait()
    copies[3].wait()
    block_rows = down_ref.shape[0]
    features_ref[...] = features_of(
        normed_ref, owner, (1 - replica) * peers + tensor, block_rows
    )
    shrunk_ref[...] = jnp.dot(
        features_of(normed_ref, owner, replica * peers + tensor, block_rows),
        down_buf[...],
        preferred_element_type=jnp.float32,
    )


def shrink_kernel(
    features_ref, other_ref, own_ref, normed_ref, beside_ref, out_ref, normed_out
):
    normed_out[...] = normed_ref[...]
    out_ref[...] = own_ref[...] + jnp.dot(
        features_ref[...], other_ref[...], preferred_element_type=jnp.float32
    )


def query_kernel(normed_ref, wq_ref, far_ref, after_ref, out_ref, far_out):
    far_out[...] = far_ref[...]
    out_ref[...] = jnp.dot(normed_ref[...], wq_ref[...], preferred_element_type=jnp.float32)


def rotated(values, cosine, sine):
    half = HEAD_DIM // 2
    turned = jnp.concatenate([values[:, half:], values[:, :half]], axis=1)
    return values * cosine + turned * sine


def pack_kernel(acc_ref, partial_ref, beside_ref, out_ref, tall):
    rows = acc_ref.shape[0]
    heads = acc_ref.shape[1] // HEAD_DIM
    for h in range(heads):
        tall[h * rows : (h + 1) * rows, :] = acc_ref[:, h * HEAD_DIM : (h + 1) * HEAD_DIM]
    held_rows = padded(heads * rows, 16)
    if held_rows > heads * rows:
        tall[heads * rows : held_rows, :] = jnp.zeros(
            (held_rows - heads * rows, HEAD_DIM), jnp.float32
        )
    left = partial_ref[...]
    for c in range(3):
        piece = left.astype(jnp.bfloat16).astype(jnp.float32)
        left = left - piece
        tall[held_rows + c * rows : held_rows + (c + 1) * rows, :] = piece
    end = held_rows + 3 * rows
    if out_ref.shape[0] > end:
        tall[end:, :] = jnp.zeros((out_ref.shape[0] - end, HEAD_DIM), jnp.float32)
    out_ref[...] = tall[...].astype(jnp.bfloat16)


def finish_kernel(
    seq_count, acc_ref, partial_ref, met_ref, key_ref, value_ref, uq_own, uq_other, far_own,
    far_other, uv_own, uv_other, cos_ref, sin_ref, beside_ref,
    query_ref, keyout_ref, valueout_ref, wide, tall,
):
    first = lax.axis_index("replica") == 0
    rows = acc_ref.shape[0]
    steps = rows // seq_count
    heads = acc_ref.shape[1] // HEAD_DIM
    held_rows = padded(heads * rows, 16)
    met = met_ref[...].astype(jnp.float32)
    pieces = [met[held_rows + c * rows : held_rows + (c + 1) * rows] for c in range(3)]
    shrunk = partial_ref[...] + (pieces[0] + (pieces[1] + pieces[2]))
    shrunk = shrunk.astype(jnp.bfloat16).astype(jnp.float32)
    half = ADAPTER_RANK // 2

    def lifted(low, high, own, other):
        mine = jnp.where(first, low, high).astype(jnp.bfloat16)
        theirs = jnp.where(first, high, low).astype(jnp.bfloat16)
        return adapter_scale * (
            jnp.dot(mine, own[...], preferred_element_type=jnp.float32)
            + jnp.dot(theirs, other[...], preferred_element_type=jnp.float32)
        )

    low, high = shrunk[:, :half], shrunk[:, half : 2 * half]
    cosine, sine = cos_ref[...], sin_ref[...]
    for e, (own, other) in enumerate(((uq_own, uq_other), (far_own, far_other))):
        lora = lifted(low, high, own, other)
        for h in range(heads):
            columns = slice(h * HEAD_DIM, (h + 1) * HEAD_DIM)
            base = acc_ref[:, columns] if e == 0 else met[h * rows : (h + 1) * rows]
            raw = (base + lora[:, columns]).astype(jnp.bfloat16).astype(jnp.float32)
            wide[e, h, 0:rows, :] = rotated(raw, cosine, sine)
        for n in range(seq_count):
            for h in range(heads):
                tall[e, pl.ds((n * heads + h) * steps, steps), :] = wide[
                    e, h, pl.ds(n, steps, stride=seq_count), :
                ]
        query_ref[e] = tall[e].astype(jnp.bfloat16)
    keyout_ref[...] = key_ref[...].astype(jnp.bfloat16)
    value = value_ref[...] + lifted(
        shrunk[:, 2 * half : 3 * half], shrunk[:, 3 * half :], uv_own, uv_other
    )
    valueout_ref[...] = value.astype(jnp.bfloat16)


def fresh_kernel(
    seq_count, query_ref, key_ref, value_ref, cos_ref, sin_ref, beside_ref,
    fresh_ref, level_ref,
):
    lane = lax.broadcasted_iota(jnp.int32, (1, HEAD_DIM), 1)
    columns = []
    steps = key_ref.shape[0] // seq_count
    per_seq = fresh_ref.shape[0] // seq_count
    queries = query_ref[0].astype(jnp.float32)
    keys = rotated(key_ref[...].astype(jnp.float32), cos_ref[...], sin_ref[...])
    keys = keys.astype(jnp.bfloat16).astype(jnp.float32)
    values = value_ref[...].astype(jnp.float32)
    step = lax.rem(lax.broadcasted_iota(jnp.int32, (per_seq, 1), 0), steps)
    for n in range(seq_count):
        rows = slice(n * per_seq, (n + 1) * per_seq)
        query = queries[rows]
        scores = []
        for t in range(steps):
            place = t * seq_count + n
            score = jnp.sum(query * keys[place : place + 1], axis=-1, keepdims=True) * inv_root
            scores.append(jnp.where(step >= t, score, negative))
        top = functools.reduce(jnp.maximum, scores)
        weights = [
            jnp.where(step >= t, jnp.exp(score - top), 0.0) for t, score in enumerate(scores)
        ]
        total = functools.reduce(jnp.add, weights)
        summed = jnp.zeros((per_seq, HEAD_DIM), jnp.float32)
        for t, weight in enumerate(weights):
            place = t * seq_count + n
            summed = summed + weight.astype(jnp.bfloat16).astype(jnp.float32) * values[
                place : place + 1
            ]
        fresh_ref[rows, :] = summed
        columns.append(jnp.where(lane == 0, top, jnp.where(lane == 1, total, 0.0)))
    columns = rows_padded(jnp.concatenate(columns, axis=0), HEAD_DIM)
    level_ref[...] = jnp.transpose(columns)[0 : level_ref.shape[0], :]


def pieces_of(top, total):
    rows = lax.broadcasted_iota(jnp.int32, (16, HEAD_DIM), 0)
    packed = jnp.zeros((16, HEAD_DIM), jnp.float32)
    for first, left in ((0, top), (3, total)):
        for c in range(3):
            piece = left.astype(jnp.bfloat16).astype(jnp.float32)
            left = left - piece
            packed = jnp.where(rows == first + c, piece, packed)
    return packed.astype(jnp.bfloat16)


def top_and_total(part_ref, held_rows):
    pieces = part_ref[padded(held_rows, 16) :, :].astype(jnp.float32)
    return (
        pieces[0:1] + (pieces[1:2] + pieces[2:3]),
        pieces[3:4] + (pieces[4:5] + pieces[5:6]),
    )


def turned_rows(rows):
    count = padded(len(rows), 8)
    place = lax.broadcasted_iota(jnp.int32, (count, HEAD_DIM), 0)
    stacked = jnp.zeros((count, HEAD_DIM), jnp.float32)
    for k, row in enumerate(rows):
        stacked = jnp.where(place == k, row, stacked)
    return jnp.transpose(rows_padded(stacked, HEAD_DIM))


def cache_kernel(
    masks, reach_ref, query_ref, kc_ref, vc_ref, beside_ref, *refs
):
    *earlier, out_ref, scores_buf, weights_buf = refs
    entries, held_rows, _ = query_ref.shape
    seq_count, kv_heads, span, _ = kc_ref.shape
    peers = 2 * entries
    per_seq = held_rows // seq_count
    mean_rows = padded(held_rows, 16)
    tensor = lax.axis_index("tensor")
    spots = tensor * span + lax.broadcasted_iota(jnp.int32, (span, HEAD_DIM), 0)
    live = spots < reach_ref[0:1, :]
    lane = lax.broadcasted_iota(jnp.int32, (span, HEAD_DIM), 1)
    owners = [lax.bitwise_xor(tensor, mask) for mask in masks]
    heads = [owner * kv_heads // peers for owner in owners]
    for blocks in earlier:
        for e in range(entries):
            place = lax.bitwise_xor(tensor, masks[e] ^ 1)
            out_ref[place] = blocks[place]
    batch = 4
    for lead in range(0, entries, batch):
        part = range(lead, min(lead + batch, entries))
        turned = [
            jnp.transpose(rows_padded(query_ref[e].astype(jnp.float32), HEAD_DIM)).astype(
                jnp.bfloat16
            )
            for e in part
        ]
        for k, e in enumerate(part):
            scores = None
            for n in range(seq_count):
                score = jnp.dot(
                    kc_ref[n, heads[e]], turned[k], preferred_element_type=jnp.float32
                )
                scores = score if n == 0 else jnp.where(lane < n * per_seq, scores, score)
            scores_buf[k] = jnp.where(live, scores, negative)
        tops = [
            jnp.maximum(jnp.max(scores_buf[k], axis=0, keepdims=True), 0.1 * negative)
            for k in range(len(part))
        ]
        for k, e in enumerate(part):
            weights = jnp.exp((scores_buf[k] - tops[k]) * inv_root)
            total = jnp.sum(weights, axis=0, keepdims=True)
            out_ref[owners[e], mean_rows:, :] = pieces_of(tops[k] * inv_root, total)
            weights_buf[k] = jnp.transpose(weights)
        for k, e in enumerate(part):
            sums = [
                jnp.dot(
                    weights_buf[k, n * per_seq : (n + 1) * per_seq, :].astype(jnp.bfloat16),
                    vc_ref[n, heads[e]],
                    preferred_element_type=jnp.float32,
                )
                for n in range(seq_count)
            ]
            sums = rows_padded(jnp.concatenate(sums, axis=0), mean_rows)
            out_ref[owners[e], 0:mean_rows, :] = sums.astype(jnp.bfloat16)


def merge_kernel(seq_count, blocks_ref, fresh_ref, level_ref, wo_ref, out_ref, wide):
    peers, folded, lanes = out_ref.shape
    heads = wide.shape[0]
    held_rows = fresh_ref.shape[0]
    rows = held_rows // heads
    steps = rows // seq_count
    folds = folded // rows
    per_seq = heads * steps
    mean_rows = padded(held_rows, 16)
    stats = [top_and_total(blocks_ref.at[b], held_rows) for b in range(peers)]
    stats.append((level_ref[0:1, :], level_ref[1:2, :]))
    top = functools.reduce(jnp.maximum, [stat[0] for stat in stats])
    factors = [jnp.exp(stat[0] - top) for stat in stats]
    total = functools.reduce(jnp.add, [factor * stat[1] for factor, stat in zip(factors, stats)])
    total = jnp.where(total > 0.0, total, 1.0)
    columns = turned_rows([factor / total for factor in factors])
    mixed = fresh_ref[...] * columns[0:held_rows, peers : peers + 1]
    for b in range(peers):
        mixed = mixed + (
            blocks_ref[b, 0:mean_rows, :].astype(jnp.float32)[0:held_rows]
            * columns[0:held_rows, b : b + 1]
        )
    for n in range(seq_count):
        for h in range(heads):
            first = n * per_seq + h * steps
            wide[h, pl.ds(n, steps, stride=seq_count), :] = mixed[first : first + steps]
    attention = jnp.concatenate([wide[h, 0:rows, :] for h in range(heads)], axis=1)
    attention = attention.astype(jnp.bfloat16)
    width = folds * lanes
    for p in range(peers):
        share = jnp.dot(
            attention,
            wo_ref[:, p * width : (p + 1) * width],
            preferred_element_type=jnp.float32,
        )
        if folds > 1:
            share = jnp.concatenate(
                [share[:, c * lanes : (c + 1) * lanes] for c in range(folds)], axis=0
            )
        out_ref[p] = share.astype(out_ref.dtype)


def sum_kernel(rest_ref, parts_ref, out_ref):
    total = functools.reduce(
        jnp.add, [parts_ref[b].astype(jnp.float32) for b in range(parts_ref.shape[0])]
    )
    rows = rest_ref.shape[0]
    steps, seqs, _ = out_ref.shape
    folds, lanes = total.shape[0] // rows, total.shape[1]
    for c in range(folds):
        columns = slice(c * lanes, (c + 1) * lanes)
        piece = total[c * rows : (c + 1) * rows] + rest_ref[:, columns]
        for s in range(steps):
            out_ref[s, :, columns] = piece[s * seqs : (s + 1) * seqs].astype(jnp.bfloat16)


def crossed(value, mask):
    pairs = [(source, source ^ mask) for source in range(lax.axis_size("tensor"))]
    return lax.ppermute(value, "tensor", pairs)


def exchanged(value):
    return lax.all_to_all(value, "tensor", split_axis=0, concat_axis=0, tiled=True)


def near_masks():
    masks = [2]
    while 4 * masks[-1] < lax.axis_size("tensor"):
        masks.append(2 * masks[-1])
    return masks


def body(
    layer_input_hidden,
    rmsnorm_gain_weight,
    wq,
    wk,
    wv,
    wo,
    adapter_down_stored,
    adapter_up_query,
    adapter_up_value,
    adapter_block_owner,
    rotated_key_cache,
    cached_value_rows,
    cache_valid_lengths,
):
    f32, bf16 = jnp.float32, jnp.bfloat16
    shape = jax.ShapeDtypeStruct
    steps, seqs, model_width = layer_input_hidden.shape
    peers = lax.axis_size("tensor")
    tensor_index = lax.axis_index("tensor")
    rows = steps * seqs
    local_heads = wq.shape[1] // HEAD_DIM
    held_rows = rows * local_heads
    kv_width = wk.shape[1]
    width = model_width // peers
    group = QUERY_HEADS // KEY_VALUE_HEADS

    pairs = [(0, 1), (1, 0)]
    other_down = lax.ppermute(adapter_down_stored, "replica", pairs)
    other_up_query = lax.ppermute(adapter_up_query, "replica", pairs)
    far_up_query = crossed(adapter_up_query, peers // 2)
    other_up_value = lax.ppermute(adapter_up_value, "replica", pairs)

    normed, cosine, sine, rest, reach, own_shrunk, features = kernel_call(
        functools.partial(norm_kernel, peers, local_heads),
        (
            shape((rows, model_width), bf16),
            shape((rows, HEAD_DIM), f32),
            shape((rows, HEAD_DIM), f32),
            shape((rows, width), f32),
            shape((8, HEAD_DIM), jnp.int32),
            shape((rows, 2 * ADAPTER_RANK), f32),
            shape((rows, adapter_down_stored.shape[0]), bf16),
        ),
        [far] * 6,
        (vmem,) * 7,
        [
            pltpu.SMEM(cache_valid_lengths.shape, jnp.int32),
            pltpu.SMEM(adapter_block_owner.shape, jnp.int32),
            pltpu.VMEM(layer_input_hidden.shape, bf16),
            pltpu.VMEM(adapter_down_stored.shape, bf16),
            pltpu.VMEM(rmsnorm_gain_weight.shape, bf16),
            pltpu.SemaphoreType.DMA((5,)),
        ],
        limit=8,
    )(
        cache_valid_lengths, adapter_block_owner, layer_input_hidden, adapter_down_stored,
        rmsnorm_gain_weight, wo,
    )
    own_shrunk, other_down, other_up_query, other_up_value = lax.optimization_barrier(
        (own_shrunk, other_down, other_up_query, other_up_value)
    )
    partial, normed = kernel_call(
        shrink_kernel,
        (shape((rows, 2 * ADAPTER_RANK), f32), shape((rows, model_width), bf16)),
        [vmem] * 4 + [far],
        (vmem, vmem),
        limit=4,
    )(features, other_down, own_shrunk, normed, wo)

    partial = after = partial + crossed(partial, 1)
    for mask in near_masks():
        partial = partial + crossed(partial, mask)

    key_sum = jnp.dot(normed, wk, preferred_element_type=f32)
    value_sum = jnp.dot(normed, wv, preferred_element_type=f32)
    query_sum, far_up_query = kernel_call(
        query_kernel,
        (shape((rows, wq.shape[1]), f32), shape(far_up_query.shape, bf16)),
        [vmem] * 4,
        (vmem, vmem),
        limit=4,
        moved=wq.size,
        flops=2 * rows * wq.size,
    )(normed, wq, far_up_query, after)
    other_far_up_query = lax.ppermute(far_up_query, "replica", pairs)

    packed_rows = padded(held_rows, 16) + padded(3 * rows, 16)
    packed = kernel_call(
        pack_kernel,
        shape((packed_rows, HEAD_DIM), bf16),
        [vmem, vmem, far],
        vmem,
        [pltpu.VMEM((packed_rows, HEAD_DIM), f32)],
        limit=4,
    )(query_sum, partial, wq)
    queries, key_raw, value_raw = kernel_call(
        functools.partial(finish_kernel, seqs),
        (
            shape((2, held_rows, HEAD_DIM), bf16),
            shape((rows, kv_width), bf16),
            shape((rows, kv_width), bf16),
        ),
        [vmem] * 13 + [far],
        (vmem,) * 3,
        [
            pltpu.VMEM((2, local_heads, padded(rows, 8), HEAD_DIM), f32),
            pltpu.VMEM((2, held_rows, HEAD_DIM), f32),
        ],
        limit=4,
    )(
        query_sum, partial, crossed(packed, peers // 2), key_sum, value_sum, adapter_up_query,
        other_up_query, far_up_query, other_far_up_query, adapter_up_value, other_up_value,
        cosine, sine, wq,
    )

    if kv_width != HEAD_DIM:
        kv_index = tensor_index * local_heads // group

        def own_head(value):
            heads = lax.all_gather(value, "tensor", axis=1, tiled=True)
            return lax.dynamic_slice_in_dim(heads, kv_index * HEAD_DIM, HEAD_DIM, 1)

        key_raw, value_raw = own_head(key_raw), own_head(value_raw)

    fresh, fresh_level = kernel_call(
        functools.partial(fresh_kernel, seqs),
        (shape((held_rows, HEAD_DIM), f32), shape((8, HEAD_DIM), f32)),
        [vmem] * 5 + [far],
        (vmem, vmem),
        limit=4,
    )(queries, key_raw, value_raw, cosine, sine, wq)
    held, masks = queries, [0, peers // 2]
    for mask in near_masks()[::-1]:
        held = jnp.concatenate([held, crossed(held, mask)])
        masks = masks + [mask ^ other for other in masks]
    others = crossed(held, 1)

    span = rotated_key_cache.shape[2]
    blocks_shape = shape((peers, padded(held_rows, 16) + 16, HEAD_DIM), bf16)
    buffers = [pltpu.VMEM((4, span, HEAD_DIM), f32), pltpu.VMEM((4, HEAD_DIM, span), f32)]

    def cache_part(its_masks, *operands):
        return kernel_call(
            functools.partial(cache_kernel, its_masks),
            blocks_shape,
            [vmem] * 4 + [far] + [vmem] * (len(operands) - 1),
            vmem,
            buffers,
            limit=6,
        )(reach, operands[0], rotated_key_cache, cached_value_rows, wq, *operands[1:])

    even_blocks = cache_part(masks, held)
    blocks = cache_part([mask ^ 1 for mask in masks], others, even_blocks)

    folds = width // 256 if (rows * (width // 256)) % 16 == 0 else 1
    shares = kernel_call(
        functools.partial(merge_kernel, seqs),
        shape((peers, rows * folds, width // folds), bf16),
        [vmem] * 4,
        vmem,
        [pltpu.VMEM((local_heads, padded(rows, 8), HEAD_DIM), f32)],
        limit=6,
    )(exchanged(blocks), fresh, fresh_level, wo)
    return kernel_call(
        sum_kernel,
        shape((steps, seqs, width), bf16),
        [vmem] * 2,
        vmem,
        limit=4,
    )(rest, exchanged(shares))


def solution(mesh):
    return jax.shard_map(
        body,
        mesh=mesh,
        in_specs=(
            P(None, ("groups", "replica"), None),
            P(),
            P(None, "tensor"),
            P(None, "tensor"),
            P(None, "tensor"),
            P("tensor", None),
            P(("replica", "tensor"), None),
            P("replica", "tensor"),
            P("replica", "tensor"),
            P(),
            P(("groups", "replica"), None, "tensor", None),
            P(("groups", "replica"), None, "tensor", None),
            P(("groups", "replica")),
        ),
        out_specs=P(None, ("groups", "replica"), "tensor"),
        check_vma=False,
    )
```

```python
import functools
import math

import jax
import jax.numpy as jnp
from jax import lax
from jax.experimental import pallas as pl
from jax.experimental.pallas import tpu as pltpu
from jax.sharding import PartitionSpec as P

QUERY_HEADS = 64
KEY_VALUE_HEADS = 8
HEAD_DIM = 128
ADAPTER_RANK = 64


adapter_scale = 2.0
rope_base = 500000.0
negative = -1e30
inv_root = 1.0 / math.sqrt(HEAD_DIM)
MIB = 1 << 20

vmem = pl.BlockSpec(memory_space=pltpu.VMEM)
smem = pl.BlockSpec(memory_space=pltpu.SMEM)
far = pl.BlockSpec(memory_space=pl.ANY)


def padded(count, multiple):
    return -(-count // multiple) * multiple


def rows_padded(value, rows):
    if value.shape[0] == rows:
        return value
    filler = jnp.zeros((rows - value.shape[0],) + value.shape[1:], value.dtype)
    return jnp.concatenate([value, filler], axis=0)


def kernel_call(kernel, outs, specs, out_specs, scratch=(), limit=16, moved=0, flops=0):
    call = pl.pallas_call(
        kernel,
        out_shape=outs,
        in_specs=specs,
        out_specs=out_specs,
        scratch_shapes=list(scratch),
        compiler_params=pltpu.CompilerParams(vmem_limit_bytes=limit * MIB),
        cost_estimate=pl.CostEstimate(flops=flops, bytes_accessed=moved, transcendentals=0),
    )

    def run(*operands):
        return call(
            *[
                pltpu.with_memory_space_constraint(operand, pltpu.HBM) if spec is far else operand
                for operand, spec in zip(operands, specs)
            ]
        )

    return run


def fetches(pairs, sem):
    copies = [
        pltpu.make_async_copy(far_ref, near, sem.at[k]) for k, (far_ref, near) in enumerate(pairs)
    ]
    for copy in copies:
        copy.start()
    return copies


def features_of(normed_ref, owner_ref, held, block_rows):
    place = jnp.int32(0)
    for j in range(owner_ref.shape[0]):
        place = jnp.where(owner_ref[j] == held, jnp.int32(j), place)
    return normed_ref[:, pl.ds(pl.multiple_of(place * block_rows, block_rows), block_rows)]


def norm_kernel(
    peers, heads, lengths_ref, owner_ref, x_ref, down_ref, gain_ref, beside_ref,
    normed_ref, cos_ref, sin_ref, rest_ref, reach_ref, shrunk_ref, features_ref,
    lengths, owner, x_buf, down_buf, gain, sem,
):
    copies = fetches(
        [
            (lengths_ref, lengths),
            (owner_ref, owner),
            (x_ref, x_buf),
            (down_ref, down_buf),
            (gain_ref, gain),
        ],
        sem,
    )
    steps, seqs, _ = x_ref.shape
    rows, width = rest_ref.shape
    half = HEAD_DIM // 2
    row = lax.broadcasted_iota(jnp.int32, (rows, HEAD_DIM), 0)
    lane = lax.broadcasted_iota(jnp.int32, (rows, HEAD_DIM), 1)
    copies[0].wait()
    positions = jnp.zeros((rows, HEAD_DIM), jnp.int32)
    for s in range(steps):
        for n in range(seqs):
            positions = jnp.where(row == s * seqs + n, lengths[n] + s, positions)
    low = lane < half
    exponent = jnp.where(low, lane, lane - half).astype(jnp.float32) * (2.0 / HEAD_DIM)
    angles = positions.astype(jnp.float32) * jnp.exp(exponent * -math.log(rope_base))
    sine = jnp.sin(angles)
    cos_ref[...] = jnp.cos(angles)
    sin_ref[...] = jnp.where(low, -sine, sine)
    place = lax.broadcasted_iota(jnp.int32, reach_ref.shape, 1)
    reach = jnp.zeros(reach_ref.shape, jnp.int32)
    per_seq = heads * steps
    for n in range(seqs):
        mine = jnp.logical_and(place >= n * per_seq, place < (n + 1) * per_seq)
        reach = jnp.where(mine, lengths[n], reach)
    reach_ref[...] = reach
    copies[2].wait()
    values = jnp.concatenate([x_buf[s].astype(jnp.float32) for s in range(steps)], axis=0)
    factor = lax.rsqrt(jnp.mean(values * values, axis=-1, keepdims=True) + 1e-05)
    copies[4].wait()
    normed = values * factor * gain[...].astype(jnp.float32).reshape(1, -1)
    normed_ref[...] = normed.astype(jnp.bfloat16)
    replica, tensor = lax.axis_index("replica"), lax.axis_index("tensor")
    for s in range(steps):
        part = x_buf[s, :, pl.ds(pl.multiple_of(tensor * width, width), width)]
        rest_ref[s * seqs : (s + 1) * seqs, :] = part.astype(jnp.float32)
    copies[1].wait()
    copies[3].wait()
    block_rows = down_ref.shape[0]
    features_ref[...] = features_of(
        normed_ref, owner, (1 - replica) * peers + tensor, block_rows
    )
    shrunk_ref[...] = jnp.dot(
        features_of(normed_ref, owner, replica * peers + tensor, block_rows),
        down_buf[...],
        preferred_element_type=jnp.float32,
    )


def shrink_kernel(
    features_ref, other_ref, own_ref, normed_ref, beside_ref, out_ref, normed_out
):
    normed_out[...] = normed_ref[...]
    out_ref[...] = own_ref[...] + jnp.dot(
        features_ref[...], other_ref[...], preferred_element_type=jnp.float32
    )


def query_kernel(normed_ref, wq_ref, far_ref, after_ref, out_ref, far_out):
    far_out[...] = far_ref[...]
    out_ref[...] = jnp.dot(normed_ref[...], wq_ref[...], preferred_element_type=jnp.float32)


def rotated(values, cosine, sine):
    half = HEAD_DIM // 2
    turned = jnp.concatenate([values[:, half:], values[:, :half]], axis=1)
    return values * cosine + turned * sine


def pack_kernel(acc_ref, partial_ref, beside_ref, out_ref, tall):
    rows = acc_ref.shape[0]
    heads = acc_ref.shape[1] // HEAD_DIM
    for h in range(heads):
        tall[h * rows : (h + 1) * rows, :] = acc_ref[:, h * HEAD_DIM : (h + 1) * HEAD_DIM]
    held_rows = padded(heads * rows, 16)
    if held_rows > heads * rows:
        tall[heads * rows : held_rows, :] = jnp.zeros(
            (held_rows - heads * rows, HEAD_DIM), jnp.float32
        )
    left = partial_ref[...]
    for c in range(3):
        piece = left.astype(jnp.bfloat16).astype(jnp.float32)
        left = left - piece
        tall[held_rows + c * rows : held_rows + (c + 1) * rows, :] = piece
    end = held_rows + 3 * rows
    if out_ref.shape[0] > end:
        tall[end:, :] = jnp.zeros((out_ref.shape[0] - end, HEAD_DIM), jnp.float32)
    out_ref[...] = tall[...].astype(jnp.bfloat16)


def finish_kernel(
    seq_count, acc_ref, partial_ref, met_ref, key_ref, value_ref, uq_own, uq_other, far_own,
    far_other, uv_own, uv_other, cos_ref, sin_ref, beside_ref,
    query_ref, keyout_ref, valueout_ref, wide, tall,
):
    first = lax.axis_index("replica") == 0
    rows = acc_ref.shape[0]
    steps = rows // seq_count
    heads = acc_ref.shape[1] // HEAD_DIM
    held_rows = padded(heads * rows, 16)
    met = met_ref[...].astype(jnp.float32)
    pieces = [met[held_rows + c * rows : held_rows + (c + 1) * rows] for c in range(3)]
    shrunk = partial_ref[...] + (pieces[0] + (pieces[1] + pieces[2]))
    shrunk = shrunk.astype(jnp.bfloat16).astype(jnp.float32)
    half = ADAPTER_RANK // 2

    def lifted(low, high, own, other):
        mine = jnp.where(first, low, high).astype(jnp.bfloat16)
        theirs = jnp.where(first, high, low).astype(jnp.bfloat16)
        return adapter_scale * (
            jnp.dot(mine, own[...], preferred_element_type=jnp.float32)
            + jnp.dot(theirs, other[...], preferred_element_type=jnp.float32)
        )

    low, high = shrunk[:, :half], shrunk[:, half : 2 * half]
    cosine, sine = cos_ref[...], sin_ref[...]
    for e, (own, other) in enumerate(((uq_own, uq_other), (far_own, far_other))):
        lora = lifted(low, high, own, other)
        for h in range(heads):
            columns = slice(h * HEAD_DIM, (h + 1) * HEAD_DIM)
            base = acc_ref[:, columns] if e == 0 else met[h * rows : (h + 1) * rows]
            raw = (base + lora[:, columns]).astype(jnp.bfloat16).astype(jnp.float32)
            wide[e, h, 0:rows, :] = rotated(raw, cosine, sine)
        for n in range(seq_count):
            for h in range(heads):
                tall[e, pl.ds((n * heads + h) * steps, steps), :] = wide[
                    e, h, pl.ds(n, steps, stride=seq_count), :
                ]
        query_ref[e] = tall[e].astype(jnp.bfloat16)
    keyout_ref[...] = key_ref[...].astype(jnp.bfloat16)
    value = value_ref[...] + lifted(
        shrunk[:, 2 * half : 3 * half], shrunk[:, 3 * half :], uv_own, uv_other
    )
    valueout_ref[...] = value.astype(jnp.bfloat16)


def fresh_kernel(
    seq_count, query_ref, key_ref, value_ref, cos_ref, sin_ref, beside_ref,
    fresh_ref, level_ref,
):
    lane = lax.broadcasted_iota(jnp.int32, (1, HEAD_DIM), 1)
    columns = []
    steps = key_ref.shape[0] // seq_count
    per_seq = fresh_ref.shape[0] // seq_count
    queries = query_ref[0].astype(jnp.float32)
    keys = rotated(key_ref[...].astype(jnp.float32), cos_ref[...], sin_ref[...])
    keys = keys.astype(jnp.bfloat16).astype(jnp.float32)
    values = value_ref[...].astype(jnp.float32)
    step = lax.rem(lax.broadcasted_iota(jnp.int32, (per_seq, 1), 0), steps)
    for n in range(seq_count):
        rows = slice(n * per_seq, (n + 1) * per_seq)
        query = queries[rows]
        scores = []
        for t in range(steps):
            place = t * seq_count + n
            score = jnp.sum(query * keys[place : place + 1], axis=-1, keepdims=True) * inv_root
            scores.append(jnp.where(step >= t, score, negative))
        top = functools.reduce(jnp.maximum, scores)
        weights = [
            jnp.where(step >= t, jnp.exp(score - top), 0.0) for t, score in enumerate(scores)
        ]
        total = functools.reduce(jnp.add, weights)
        summed = jnp.zeros((per_seq, HEAD_DIM), jnp.float32)
        for t, weight in enumerate(weights):
            place = t * seq_count + n
            summed = summed + weight.astype(jnp.bfloat16).astype(jnp.float32) * values[
                place : place + 1
            ]
        fresh_ref[rows, :] = summed
        columns.append(jnp.where(lane == 0, top, jnp.where(lane == 1, total, 0.0)))
    columns = rows_padded(jnp.concatenate(columns, axis=0), HEAD_DIM)
    level_ref[...] = jnp.transpose(columns)[0 : level_ref.shape[0], :]


def pieces_of(top, total):
    rows = lax.broadcasted_iota(jnp.int32, (16, HEAD_DIM), 0)
    packed = jnp.zeros((16, HEAD_DIM), jnp.float32)
    for first, left in ((0, top), (3, total)):
        for c in range(3):
            piece = left.astype(jnp.bfloat16).astype(jnp.float32)
            left = left - piece
            packed = jnp.where(rows == first + c, piece, packed)
    return packed.astype(jnp.bfloat16)


def top_and_total(part_ref, held_rows):
    pieces = part_ref[padded(held_rows, 16) :, :].astype(jnp.float32)
    return (
        pieces[0:1] + (pieces[1:2] + pieces[2:3]),
        pieces[3:4] + (pieces[4:5] + pieces[5:6]),
    )


def turned_rows(rows):
    count = padded(len(rows), 8)
    place = lax.broadcasted_iota(jnp.int32, (count, HEAD_DIM), 0)
    stacked = jnp.zeros((count, HEAD_DIM), jnp.float32)
    for k, row in enumerate(rows):
        stacked = jnp.where(place == k, row, stacked)
    return jnp.transpose(rows_padded(stacked, HEAD_DIM))


def cache_kernel(
    masks, reach_ref, query_ref, kc_ref, vc_ref, beside_ref, after_ref, *refs
):
    *earlier, out_ref, scores_buf, weights_buf = refs
    entries, held_rows, _ = query_ref.shape
    seq_count, kv_heads, span, _ = kc_ref.shape
    peers = 2 * entries
    per_seq = held_rows // seq_count
    mean_rows = padded(held_rows, 16)
    tensor = lax.axis_index("tensor")
    spots = tensor * span + lax.broadcasted_iota(jnp.int32, (span, HEAD_DIM), 0)
    live = spots < reach_ref[0:1, :]
    lane = lax.broadcasted_iota(jnp.int32, (span, HEAD_DIM), 1)
    owners = [lax.bitwise_xor(tensor, mask) for mask in masks]
    heads = [owner * kv_heads // peers for owner in owners]
    for blocks in earlier:
        for e in range(entries):
            place = lax.bitwise_xor(tensor, masks[e] ^ 1)
            out_ref[place] = blocks[place]
    batch = 4
    for lead in range(0, entries, batch):
        part = range(lead, min(lead + batch, entries))
        turned = [
            jnp.transpose(rows_padded(query_ref[e].astype(jnp.float32), HEAD_DIM)).astype(
                jnp.bfloat16
            )
            for e in part
        ]
        for k, e in enumerate(part):
            scores = None
            for n in range(seq_count):
                score = jnp.dot(
                    kc_ref[n, heads[e]], turned[k], preferred_element_type=jnp.float32
                )
                scores = score if n == 0 else jnp.where(lane < n * per_seq, scores, score)
            scores_buf[k] = jnp.where(live, scores, negative)
        tops = [
            jnp.maximum(jnp.max(scores_buf[k], axis=0, keepdims=True), 0.1 * negative)
            for k in range(len(part))
        ]
        for k, e in enumerate(part):
            weights = jnp.exp((scores_buf[k] - tops[k]) * inv_root)
            total = jnp.sum(weights, axis=0, keepdims=True)
            out_ref[owners[e], mean_rows:, :] = pieces_of(tops[k] * inv_root, total)
            weights_buf[k] = jnp.transpose(weights)
        for k, e in enumerate(part):
            sums = [
                jnp.dot(
                    weights_buf[k, n * per_seq : (n + 1) * per_seq, :].astype(jnp.bfloat16),
                    vc_ref[n, heads[e]],
                    preferred_element_type=jnp.float32,
                )
                for n in range(seq_count)
            ]
            sums = rows_padded(jnp.concatenate(sums, axis=0), mean_rows)
            out_ref[owners[e], 0:mean_rows, :] = sums.astype(jnp.bfloat16)


def merge_kernel(seq_count, blocks_ref, fresh_ref, level_ref, wo_ref, out_ref, wide):
    peers, folded, lanes = out_ref.shape
    heads = wide.shape[0]
    held_rows = fresh_ref.shape[0]
    rows = held_rows // heads
    steps = rows // seq_count
    folds = folded // rows
    per_seq = heads * steps
    mean_rows = padded(held_rows, 16)
    stats = [top_and_total(blocks_ref.at[b], held_rows) for b in range(peers)]
    stats.append((level_ref[0:1, :], level_ref[1:2, :]))
    top = functools.reduce(jnp.maximum, [stat[0] for stat in stats])
    factors = [jnp.exp(stat[0] - top) for stat in stats]
    total = functools.reduce(jnp.add, [factor * stat[1] for factor, stat in zip(factors, stats)])
    total = jnp.where(total > 0.0, total, 1.0)
    columns = turned_rows([factor / total for factor in factors])
    mixed = fresh_ref[...] * columns[0:held_rows, peers : peers + 1]
    for b in range(peers):
        mixed = mixed + (
            blocks_ref[b, 0:mean_rows, :].astype(jnp.float32)[0:held_rows]
            * columns[0:held_rows, b : b + 1]
        )
    for n in range(seq_count):
        for h in range(heads):
            first = n * per_seq + h * steps
            wide[h, pl.ds(n, steps, stride=seq_count), :] = mixed[first : first + steps]
    attention = jnp.concatenate([wide[h, 0:rows, :] for h in range(heads)], axis=1)
    attention = attention.astype(jnp.bfloat16)
    width = folds * lanes
    for p in range(peers):
        share = jnp.dot(
            attention,
            wo_ref[:, p * width : (p + 1) * width],
            preferred_element_type=jnp.float32,
        )
        if folds > 1:
            share = jnp.concatenate(
                [share[:, c * lanes : (c + 1) * lanes] for c in range(folds)], axis=0
            )
        out_ref[p] = share.astype(out_ref.dtype)


def sum_kernel(rest_ref, parts_ref, out_ref):
    total = functools.reduce(
        jnp.add, [parts_ref[b].astype(jnp.float32) for b in range(parts_ref.shape[0])]
    )
    rows = rest_ref.shape[0]
    steps, seqs, _ = out_ref.shape
    folds, lanes = total.shape[0] // rows, total.shape[1]
    for c in range(folds):
        columns = slice(c * lanes, (c + 1) * lanes)
        piece = total[c * rows : (c + 1) * rows] + rest_ref[:, columns]
        for s in range(steps):
            out_ref[s, :, columns] = piece[s * seqs : (s + 1) * seqs].astype(jnp.bfloat16)


def crossed(value, mask):
    pairs = [(source, source ^ mask) for source in range(lax.axis_size("tensor"))]
    return lax.ppermute(value, "tensor", pairs)


def exchanged(value):
    return lax.all_to_all(value, "tensor", split_axis=0, concat_axis=0, tiled=True)


def near_masks():
    masks = [2]
    while 4 * masks[-1] < lax.axis_size("tensor"):
        masks.append(2 * masks[-1])
    return masks


def body(
    layer_input_hidden,
    rmsnorm_gain_weight,
    wq,
    wk,
    wv,
    wo,
    adapter_down_stored,
    adapter_up_query,
    adapter_up_value,
    adapter_block_owner,
    rotated_key_cache,
    cached_value_rows,
    cache_valid_lengths,
):
    f32, bf16 = jnp.float32, jnp.bfloat16
    shape = jax.ShapeDtypeStruct
    steps, seqs, model_width = layer_input_hidden.shape
    peers = lax.axis_size("tensor")
    tensor_index = lax.axis_index("tensor")
    rows = steps * seqs
    local_heads = wq.shape[1] // HEAD_DIM
    held_rows = rows * local_heads
    kv_width = wk.shape[1]
    width = model_width // peers
    group = QUERY_HEADS // KEY_VALUE_HEADS

    pairs = [(0, 1), (1, 0)]
    other_down = lax.ppermute(adapter_down_stored, "replica", pairs)
    other_up_query = lax.ppermute(adapter_up_query, "replica", pairs)
    far_up_query = crossed(adapter_up_query, peers // 2)
    other_up_value = lax.ppermute(adapter_up_value, "replica", pairs)

    normed, cosine, sine, rest, reach, own_shrunk, features = kernel_call(
        functools.partial(norm_kernel, peers, local_heads),
        (
            shape((rows, model_width), bf16),
            shape((rows, HEAD_DIM), f32),
            shape((rows, HEAD_DIM), f32),
            shape((rows, width), f32),
            shape((8, HEAD_DIM), jnp.int32),
            shape((rows, 2 * ADAPTER_RANK), f32),
            shape((rows, adapter_down_stored.shape[0]), bf16),
        ),
        [far] * 6,
        (vmem,) * 7,
        [
            pltpu.SMEM(cache_valid_lengths.shape, jnp.int32),
            pltpu.SMEM(adapter_block_owner.shape, jnp.int32),
            pltpu.VMEM(layer_input_hidden.shape, bf16),
            pltpu.VMEM(adapter_down_stored.shape, bf16),
            pltpu.VMEM(rmsnorm_gain_weight.shape, bf16),
            pltpu.SemaphoreType.DMA((5,)),
        ],
        limit=8,
    )(
        cache_valid_lengths, adapter_block_owner, layer_input_hidden, adapter_down_stored,
        rmsnorm_gain_weight, wo,
    )
    own_shrunk, other_down, other_up_query, other_up_value = lax.optimization_barrier(
        (own_shrunk, other_down, other_up_query, other_up_value)
    )
    partial, normed = kernel_call(
        shrink_kernel,
        (shape((rows, 2 * ADAPTER_RANK), f32), shape((rows, model_width), bf16)),
        [vmem] * 4 + [far],
        (vmem, vmem),
        limit=4,
    )(features, other_down, own_shrunk, normed, wo)

    partial = after = partial + crossed(partial, 1)
    for mask in near_masks():
        partial = partial + crossed(partial, mask)

    key_sum = jnp.dot(normed, wk, preferred_element_type=f32)
    value_sum = jnp.dot(normed, wv, preferred_element_type=f32)
    query_sum, far_up_query = kernel_call(
        query_kernel,
        (shape((rows, wq.shape[1]), f32), shape(far_up_query.shape, bf16)),
        [vmem] * 4,
        (vmem, vmem),
        limit=4,
        moved=wq.size,
        flops=2 * rows * wq.size,
    )(normed, wq, far_up_query, after)
    other_far_up_query = lax.ppermute(far_up_query, "replica", pairs)

    packed_rows = padded(held_rows, 16) + padded(3 * rows, 16)
    packed = kernel_call(
        pack_kernel,
        shape((packed_rows, HEAD_DIM), bf16),
        [vmem, vmem, far],
        vmem,
        [pltpu.VMEM((packed_rows, HEAD_DIM), f32)],
        limit=4,
    )(query_sum, partial, wq)
    queries, key_raw, value_raw = kernel_call(
        functools.partial(finish_kernel, seqs),
        (
            shape((2, held_rows, HEAD_DIM), bf16),
            shape((rows, kv_width), bf16),
            shape((rows, kv_width), bf16),
        ),
        [vmem] * 13 + [far],
        (vmem,) * 3,
        [
            pltpu.VMEM((2, local_heads, padded(rows, 8), HEAD_DIM), f32),
            pltpu.VMEM((2, held_rows, HEAD_DIM), f32),
        ],
        limit=4,
    )(
        query_sum, partial, crossed(packed, peers // 2), key_sum, value_sum, adapter_up_query,
        other_up_query, far_up_query, other_far_up_query, adapter_up_value, other_up_value,
        cosine, sine, wq,
    )

    if kv_width != HEAD_DIM:
        kv_index = tensor_index * local_heads // group

        def own_head(value):
            heads = lax.all_gather(value, "tensor", axis=1, tiled=True)
            return lax.dynamic_slice_in_dim(heads, kv_index * HEAD_DIM, HEAD_DIM, 1)

        key_raw, value_raw = own_head(key_raw), own_head(value_raw)

    fresh, fresh_level = kernel_call(
        functools.partial(fresh_kernel, seqs),
        (shape((held_rows, HEAD_DIM), f32), shape((8, HEAD_DIM), f32)),
        [vmem] * 5 + [far],
        (vmem, vmem),
        limit=4,
    )(queries, key_raw, value_raw, cosine, sine, wq)
    held, masks = queries, [0, peers // 2]
    for mask in near_masks()[::-1]:
        held = jnp.concatenate([held, crossed(held, mask)])
        masks = masks + [mask ^ other for other in masks]
    others = crossed(held, 1)

    span = rotated_key_cache.shape[2]
    blocks_shape = shape((peers, padded(held_rows, 16) + 16, HEAD_DIM), bf16)
    buffers = [pltpu.VMEM((4, span, HEAD_DIM), f32), pltpu.VMEM((4, HEAD_DIM, span), f32)]

    def cache_part(its_masks, *operands):
        return kernel_call(
            functools.partial(cache_kernel, its_masks),
            blocks_shape,
            [vmem] * 4 + [far] + [vmem] * len(operands),
            vmem,
            buffers,
            limit=6,
        )(
            reach, operands[0], rotated_key_cache, cached_value_rows, wq, fresh_level,
            *operands[1:],
        )

    even_blocks = cache_part(masks, held)
    blocks = cache_part([mask ^ 1 for mask in masks], others, even_blocks)

    folds = width // 256 if (rows * (width // 256)) % 16 == 0 else 1
    shares = kernel_call(
        functools.partial(merge_kernel, seqs),
        shape((peers, rows * folds, width // folds), bf16),
        [vmem] * 4,
        vmem,
        [pltpu.VMEM((local_heads, padded(rows, 8), HEAD_DIM), f32)],
        limit=6,
    )(exchanged(blocks), fresh, fresh_level, wo)
    return kernel_call(
        sum_kernel,
        shape((steps, seqs, width), bf16),
        [vmem] * 2,
        vmem,
        limit=4,
    )(rest, exchanged(shares))


def solution(mesh):
    return jax.shard_map(
        body,
        mesh=mesh,
        in_specs=(
            P(None, ("groups", "replica"), None),
            P(),
            P(None, "tensor"),
            P(None, "tensor"),
            P(None, "tensor"),
            P("tensor", None),
            P(("replica", "tensor"), None),
            P("replica", "tensor"),
            P("replica", "tensor"),
            P(),
            P(("groups", "replica"), None, "tensor", None),
            P(("groups", "replica"), None, "tensor", None),
            P(("groups", "replica")),
        ),
        out_specs=P(None, ("groups", "replica"), "tensor"),
        check_vma=False,
    )
```

```python
import functools
import math

import jax
import jax.numpy as jnp
from jax import lax
from jax.experimental import pallas as pl
from jax.experimental.pallas import tpu as pltpu
from jax.sharding import PartitionSpec as P

QUERY_HEADS = 64
KEY_VALUE_HEADS = 8
HEAD_DIM = 128
ADAPTER_RANK = 64


adapter_scale = 2.0
rope_base = 500000.0
negative = -1e30
inv_root = 1.0 / math.sqrt(HEAD_DIM)
MIB = 1 << 20

vmem = pl.BlockSpec(memory_space=pltpu.VMEM)
smem = pl.BlockSpec(memory_space=pltpu.SMEM)
far = pl.BlockSpec(memory_space=pl.ANY)


def padded(count, multiple):
    return -(-count // multiple) * multiple


def rows_padded(value, rows):
    if value.shape[0] == rows:
        return value
    filler = jnp.zeros((rows - value.shape[0],) + value.shape[1:], value.dtype)
    return jnp.concatenate([value, filler], axis=0)


def kernel_call(kernel, outs, specs, out_specs, scratch=(), limit=16, moved=0, flops=0):
    call = pl.pallas_call(
        kernel,
        out_shape=outs,
        in_specs=specs,
        out_specs=out_specs,
        scratch_shapes=list(scratch),
        compiler_params=pltpu.CompilerParams(vmem_limit_bytes=limit * MIB),
        cost_estimate=pl.CostEstimate(flops=flops, bytes_accessed=moved, transcendentals=0),
    )

    def run(*operands):
        return call(
            *[
                pltpu.with_memory_space_constraint(operand, pltpu.HBM) if spec is far else operand
                for operand, spec in zip(operands, specs)
            ]
        )

    return run


def fetches(pairs, sem):
    copies = [
        pltpu.make_async_copy(far_ref, near, sem.at[k]) for k, (far_ref, near) in enumerate(pairs)
    ]
    for copy in copies:
        copy.start()
    return copies


def features_of(normed_ref, owner_ref, held, block_rows):
    place = jnp.int32(0)
    for j in range(owner_ref.shape[0]):
        place = jnp.where(owner_ref[j] == held, jnp.int32(j), place)
    return normed_ref[:, pl.ds(pl.multiple_of(place * block_rows, block_rows), block_rows)]


def norm_kernel(
    peers, heads, lengths_ref, owner_ref, x_ref, down_ref, gain_ref, beside_ref,
    normed_ref, cos_ref, sin_ref, rest_ref, reach_ref, shrunk_ref, features_ref,
    lengths, owner, x_buf, down_buf, gain, sem,
):
    copies = fetches(
        [
            (lengths_ref, lengths),
            (owner_ref, owner),
            (x_ref, x_buf),
            (down_ref, down_buf),
            (gain_ref, gain),
        ],
        sem,
    )
    steps, seqs, _ = x_ref.shape
    rows, width = rest_ref.shape
    half = HEAD_DIM // 2
    row = lax.broadcasted_iota(jnp.int32, (rows, HEAD_DIM), 0)
    lane = lax.broadcasted_iota(jnp.int32, (rows, HEAD_DIM), 1)
    copies[0].wait()
    positions = jnp.zeros((rows, HEAD_DIM), jnp.int32)
    for s in range(steps):
        for n in range(seqs):
            positions = jnp.where(row == s * seqs + n, lengths[n] + s, positions)
    low = lane < half
    exponent = jnp.where(low, lane, lane - half).astype(jnp.float32) * (2.0 / HEAD_DIM)
    angles = positions.astype(jnp.float32) * jnp.exp(exponent * -math.log(rope_base))
    sine = jnp.sin(angles)
    cos_ref[...] = jnp.cos(angles)
    sin_ref[...] = jnp.where(low, -sine, sine)
    place = lax.broadcasted_iota(jnp.int32, reach_ref.shape, 1)
    reach = jnp.zeros(reach_ref.shape, jnp.int32)
    per_seq = heads * steps
    for n in range(seqs):
        mine = jnp.logical_and(place >= n * per_seq, place < (n + 1) * per_seq)
        reach = jnp.where(mine, lengths[n], reach)
    reach_ref[...] = reach
    copies[2].wait()
    values = jnp.concatenate([x_buf[s].astype(jnp.float32) for s in range(steps)], axis=0)
    factor = lax.rsqrt(jnp.mean(values * values, axis=-1, keepdims=True) + 1e-05)
    copies[4].wait()
    normed = values * factor * gain[...].astype(jnp.float32).reshape(1, -1)
    normed_ref[...] = normed.astype(jnp.bfloat16)
    replica, tensor = lax.axis_index("replica"), lax.axis_index("tensor")
    for s in range(steps):
        part = x_buf[s, :, pl.ds(pl.multiple_of(tensor * width, width), width)]
        rest_ref[s * seqs : (s + 1) * seqs, :] = part.astype(jnp.float32)
    copies[1].wait()
    copies[3].wait()
    block_rows = down_ref.shape[0]
    features_ref[...] = features_of(
        normed_ref, owner, (1 - replica) * peers + tensor, block_rows
    )
    shrunk_ref[...] = jnp.dot(
        features_of(normed_ref, owner, replica * peers + tensor, block_rows),
        down_buf[...],
        preferred_element_type=jnp.float32,
    )


def shrink_kernel(
    features_ref, other_ref, own_ref, normed_ref, up_ref, beside_ref, out_ref, normed_out, up_out
):
    normed_out[...] = normed_ref[...]
    up_out[...] = up_ref[...]
    out_ref[...] = own_ref[...] + jnp.dot(
        features_ref[...], other_ref[...], preferred_element_type=jnp.float32
    )


def query_kernel(normed_ref, wq_ref, after_ref, out_ref):
    out_ref[...] = jnp.dot(normed_ref[...], wq_ref[...], preferred_element_type=jnp.float32)


def rotated(values, cosine, sine):
    half = HEAD_DIM // 2
    turned = jnp.concatenate([values[:, half:], values[:, :half]], axis=1)
    return values * cosine + turned * sine


def pack_kernel(acc_ref, partial_ref, beside_ref, out_ref, tall):
    rows = acc_ref.shape[0]
    heads = acc_ref.shape[1] // HEAD_DIM
    for h in range(heads):
        tall[h * rows : (h + 1) * rows, :] = acc_ref[:, h * HEAD_DIM : (h + 1) * HEAD_DIM]
    held_rows = padded(heads * rows, 16)
    if held_rows > heads * rows:
        tall[heads * rows : held_rows, :] = jnp.zeros(
            (held_rows - heads * rows, HEAD_DIM), jnp.float32
        )
    left = partial_ref[...]
    for c in range(3):
        piece = left.astype(jnp.bfloat16).astype(jnp.float32)
        left = left - piece
        tall[held_rows + c * rows : held_rows + (c + 1) * rows, :] = piece
    end = held_rows + 3 * rows
    if out_ref.shape[0] > end:
        tall[end:, :] = jnp.zeros((out_ref.shape[0] - end, HEAD_DIM), jnp.float32)
    out_ref[...] = tall[...].astype(jnp.bfloat16)


def finish_kernel(
    seq_count, acc_ref, partial_ref, met_ref, key_ref, value_ref, uq_own, uq_other, far_own,
    far_other, uv_own, uv_other, cos_ref, sin_ref, beside_ref,
    query_ref, keyout_ref, valueout_ref, wide, tall,
):
    first = lax.axis_index("replica") == 0
    rows = acc_ref.shape[0]
    steps = rows // seq_count
    heads = acc_ref.shape[1] // HEAD_DIM
    held_rows = padded(heads * rows, 16)
    met = met_ref[...].astype(jnp.float32)
    pieces = [met[held_rows + c * rows : held_rows + (c + 1) * rows] for c in range(3)]
    shrunk = partial_ref[...] + (pieces[0] + (pieces[1] + pieces[2]))
    shrunk = shrunk.astype(jnp.bfloat16).astype(jnp.float32)
    half = ADAPTER_RANK // 2

    def lifted(low, high, own, other):
        mine = jnp.where(first, low, high).astype(jnp.bfloat16)
        theirs = jnp.where(first, high, low).astype(jnp.bfloat16)
        return adapter_scale * (
            jnp.dot(mine, own[...], preferred_element_type=jnp.float32)
            + jnp.dot(theirs, other[...], preferred_element_type=jnp.float32)
        )

    low, high = shrunk[:, :half], shrunk[:, half : 2 * half]
    cosine, sine = cos_ref[...], sin_ref[...]
    for e, (own, other) in enumerate(((uq_own, uq_other), (far_own, far_other))):
        lora = lifted(low, high, own, other)
        for h in range(heads):
            columns = slice(h * HEAD_DIM, (h + 1) * HEAD_DIM)
            base = acc_ref[:, columns] if e == 0 else met[h * rows : (h + 1) * rows]
            raw = (base + lora[:, columns]).astype(jnp.bfloat16).astype(jnp.float32)
            wide[e, h, 0:rows, :] = rotated(raw, cosine, sine)
        for n in range(seq_count):
            for h in range(heads):
                tall[e, pl.ds((n * heads + h) * steps, steps), :] = wide[
                    e, h, pl.ds(n, steps, stride=seq_count), :
                ]
        query_ref[e] = tall[e].astype(jnp.bfloat16)
    keyout_ref[...] = key_ref[...].astype(jnp.bfloat16)
    value = value_ref[...] + lifted(
        shrunk[:, 2 * half : 3 * half], shrunk[:, 3 * half :], uv_own, uv_other
    )
    valueout_ref[...] = value.astype(jnp.bfloat16)


def fresh_kernel(
    seq_count, query_ref, key_ref, value_ref, cos_ref, sin_ref, beside_ref,
    fresh_ref, level_ref,
):
    lane = lax.broadcasted_iota(jnp.int32, (1, HEAD_DIM), 1)
    columns = []
    steps = key_ref.shape[0] // seq_count
    per_seq = fresh_ref.shape[0] // seq_count
    queries = query_ref[0].astype(jnp.float32)
    keys = rotated(key_ref[...].astype(jnp.float32), cos_ref[...], sin_ref[...])
    keys = keys.astype(jnp.bfloat16).astype(jnp.float32)
    values = value_ref[...].astype(jnp.float32)
    step = lax.rem(lax.broadcasted_iota(jnp.int32, (per_seq, 1), 0), steps)
    for n in range(seq_count):
        rows = slice(n * per_seq, (n + 1) * per_seq)
        query = queries[rows]
        scores = []
        for t in range(steps):
            place = t * seq_count + n
            score = jnp.sum(query * keys[place : place + 1], axis=-1, keepdims=True) * inv_root
            scores.append(jnp.where(step >= t, score, negative))
        top = functools.reduce(jnp.maximum, scores)
        weights = [
            jnp.where(step >= t, jnp.exp(score - top), 0.0) for t, score in enumerate(scores)
        ]
        total = functools.reduce(jnp.add, weights)
        summed = jnp.zeros((per_seq, HEAD_DIM), jnp.float32)
        for t, weight in enumerate(weights):
            place = t * seq_count + n
            summed = summed + weight.astype(jnp.bfloat16).astype(jnp.float32) * values[
                place : place + 1
            ]
        fresh_ref[rows, :] = summed
        columns.append(jnp.where(lane == 0, top, jnp.where(lane == 1, total, 0.0)))
    columns = rows_padded(jnp.concatenate(columns, axis=0), HEAD_DIM)
    level_ref[...] = jnp.transpose(columns)[0 : level_ref.shape[0], :]


def pieces_of(top, total):
    rows = lax.broadcasted_iota(jnp.int32, (16, HEAD_DIM), 0)
    packed = jnp.zeros((16, HEAD_DIM), jnp.float32)
    for first, left in ((0, top), (3, total)):
        for c in range(3):
            piece = left.astype(jnp.bfloat16).astype(jnp.float32)
            left = left - piece
            packed = jnp.where(rows == first + c, piece, packed)
    return packed.astype(jnp.bfloat16)


def top_and_total(part_ref, held_rows):
    pieces = part_ref[padded(held_rows, 16) :, :].astype(jnp.float32)
    return (
        pieces[0:1] + (pieces[1:2] + pieces[2:3]),
        pieces[3:4] + (pieces[4:5] + pieces[5:6]),
    )


def turned_rows(rows):
    count = padded(len(rows), 8)
    place = lax.broadcasted_iota(jnp.int32, (count, HEAD_DIM), 0)
    stacked = jnp.zeros((count, HEAD_DIM), jnp.float32)
    for k, row in enumerate(rows):
        stacked = jnp.where(place == k, row, stacked)
    return jnp.transpose(rows_padded(stacked, HEAD_DIM))


def cache_kernel(
    masks, reach_ref, query_ref, kc_ref, vc_ref, beside_ref, after_ref, *refs
):
    *earlier, out_ref, scores_buf, weights_buf = refs
    entries, held_rows, _ = query_ref.shape
    seq_count, kv_heads, span, _ = kc_ref.shape
    peers = 2 * entries
    per_seq = held_rows // seq_count
    mean_rows = padded(held_rows, 16)
    tensor = lax.axis_index("tensor")
    spots = tensor * span + lax.broadcasted_iota(jnp.int32, (span, HEAD_DIM), 0)
    live = spots < reach_ref[0:1, :]
    lane = lax.broadcasted_iota(jnp.int32, (span, HEAD_DIM), 1)
    owners = [lax.bitwise_xor(tensor, mask) for mask in masks]
    heads = [owner * kv_heads // peers for owner in owners]
    for blocks in earlier:
        for e in range(entries):
            place = lax.bitwise_xor(tensor, masks[e] ^ 1)
            out_ref[place] = blocks[place]
    batch = 4
    for lead in range(0, entries, batch):
        part = range(lead, min(lead + batch, entries))
        turned = [
            jnp.transpose(rows_padded(query_ref[e].astype(jnp.float32), HEAD_DIM)).astype(
                jnp.bfloat16
            )
            for e in part
        ]
        for k, e in enumerate(part):
            scores = None
            for n in range(seq_count):
                score = jnp.dot(
                    kc_ref[n, heads[e]], turned[k], preferred_element_type=jnp.float32
                )
                scores = score if n == 0 else jnp.where(lane < n * per_seq, scores, score)
            scores_buf[k] = jnp.where(live, scores, negative)
        tops = [
            jnp.maximum(jnp.max(scores_buf[k], axis=0, keepdims=True), 0.1 * negative)
            for k in range(len(part))
        ]
        for k, e in enumerate(part):
            weights = jnp.exp((scores_buf[k] - tops[k]) * inv_root)
            total = jnp.sum(weights, axis=0, keepdims=True)
            out_ref[owners[e], mean_rows:, :] = pieces_of(tops[k] * inv_root, total)
            weights_buf[k] = jnp.transpose(weights)
        for k, e in enumerate(part):
            sums = [
                jnp.dot(
                    weights_buf[k, n * per_seq : (n + 1) * per_seq, :].astype(jnp.bfloat16),
                    vc_ref[n, heads[e]],
                    preferred_element_type=jnp.float32,
                )
                for n in range(seq_count)
            ]
            sums = rows_padded(jnp.concatenate(sums, axis=0), mean_rows)
            out_ref[owners[e], 0:mean_rows, :] = sums.astype(jnp.bfloat16)


def merge_kernel(seq_count, blocks_ref, fresh_ref, level_ref, wo_ref, out_ref, wide):
    peers, folded, lanes = out_ref.shape
    heads = wide.shape[0]
    held_rows = fresh_ref.shape[0]
    rows = held_rows // heads
    steps = rows // seq_count
    folds = folded // rows
    per_seq = heads * steps
    mean_rows = padded(held_rows, 16)
    stats = [top_and_total(blocks_ref.at[b], held_rows) for b in range(peers)]
    stats.append((level_ref[0:1, :], level_ref[1:2, :]))
    top = functools.reduce(jnp.maximum, [stat[0] for stat in stats])
    factors = [jnp.exp(stat[0] - top) for stat in stats]
    total = functools.reduce(jnp.add, [factor * stat[1] for factor, stat in zip(factors, stats)])
    total = jnp.where(total > 0.0, total, 1.0)
    columns = turned_rows([factor / total for factor in factors])
    mixed = fresh_ref[...] * columns[0:held_rows, peers : peers + 1]
    for b in range(peers):
        mixed = mixed + (
            blocks_ref[b, 0:mean_rows, :].astype(jnp.float32)[0:held_rows]
            * columns[0:held_rows, b : b + 1]
        )
    for n in range(seq_count):
        for h in range(heads):
            first = n * per_seq + h * steps
            wide[h, pl.ds(n, steps, stride=seq_count), :] = mixed[first : first + steps]
    attention = jnp.concatenate([wide[h, 0:rows, :] for h in range(heads)], axis=1)
    attention = attention.astype(jnp.bfloat16)
    width = folds * lanes
    for p in range(peers):
        share = jnp.dot(
            attention,
            wo_ref[:, p * width : (p + 1) * width],
            preferred_element_type=jnp.float32,
        )
        if folds > 1:
            share = jnp.concatenate(
                [share[:, c * lanes : (c + 1) * lanes] for c in range(folds)], axis=0
            )
        out_ref[p] = share.astype(out_ref.dtype)


def sum_kernel(rest_ref, parts_ref, out_ref):
    total = functools.reduce(
        jnp.add, [parts_ref[b].astype(jnp.float32) for b in range(parts_ref.shape[0])]
    )
    rows = rest_ref.shape[0]
    steps, seqs, _ = out_ref.shape
    folds, lanes = total.shape[0] // rows, total.shape[1]
    for c in range(folds):
        columns = slice(c * lanes, (c + 1) * lanes)
        piece = total[c * rows : (c + 1) * rows] + rest_ref[:, columns]
        for s in range(steps):
            out_ref[s, :, columns] = piece[s * seqs : (s + 1) * seqs].astype(jnp.bfloat16)


def crossed(value, mask):
    pairs = [(source, source ^ mask) for source in range(lax.axis_size("tensor"))]
    return lax.ppermute(value, "tensor", pairs)


def exchanged(value):
    return lax.all_to_all(value, "tensor", split_axis=0, concat_axis=0, tiled=True)


def near_masks():
    masks = [2]
    while 4 * masks[-1] < lax.axis_size("tensor"):
        masks.append(2 * masks[-1])
    return masks


def body(
    layer_input_hidden,
    rmsnorm_gain_weight,
    wq,
    wk,
    wv,
    wo,
    adapter_down_stored,
    adapter_up_query,
    adapter_up_value,
    adapter_block_owner,
    rotated_key_cache,
    cached_value_rows,
    cache_valid_lengths,
):
    f32, bf16 = jnp.float32, jnp.bfloat16
    shape = jax.ShapeDtypeStruct
    steps, seqs, model_width = layer_input_hidden.shape
    peers = lax.axis_size("tensor")
    tensor_index = lax.axis_index("tensor")
    rows = steps * seqs
    local_heads = wq.shape[1] // HEAD_DIM
    held_rows = rows * local_heads
    kv_width = wk.shape[1]
    width = model_width // peers
    group = QUERY_HEADS // KEY_VALUE_HEADS

    pairs = [(0, 1), (1, 0)]
    other_down = lax.ppermute(adapter_down_stored, "replica", pairs)
    other_up_query = lax.ppermute(adapter_up_query, "replica", pairs)
    other_up_value = lax.ppermute(adapter_up_value, "replica", pairs)

    normed, cosine, sine, rest, reach, own_shrunk, features = kernel_call(
        functools.partial(norm_kernel, peers, local_heads),
        (
            shape((rows, model_width), bf16),
            shape((rows, HEAD_DIM), f32),
            shape((rows, HEAD_DIM), f32),
            shape((rows, width), f32),
            shape((8, HEAD_DIM), jnp.int32),
            shape((rows, 2 * ADAPTER_RANK), f32),
            shape((rows, adapter_down_stored.shape[0]), bf16),
        ),
        [far] * 6,
        (vmem,) * 7,
        [
            pltpu.SMEM(cache_valid_lengths.shape, jnp.int32),
            pltpu.SMEM(adapter_block_owner.shape, jnp.int32),
            pltpu.VMEM(layer_input_hidden.shape, bf16),
            pltpu.VMEM(adapter_down_stored.shape, bf16),
            pltpu.VMEM(rmsnorm_gain_weight.shape, bf16),
            pltpu.SemaphoreType.DMA((5,)),
        ],
        limit=8,
    )(
        cache_valid_lengths, adapter_block_owner, layer_input_hidden, adapter_down_stored,
        rmsnorm_gain_weight, wo,
    )
    own_shrunk, other_down, other_up_query, other_up_value = lax.optimization_barrier(
        (own_shrunk, other_down, other_up_query, other_up_value)
    )
    partial, normed, up_query = kernel_call(
        shrink_kernel,
        (
            shape((rows, 2 * ADAPTER_RANK), f32),
            shape((rows, model_width), bf16),
            shape(adapter_up_query.shape, bf16),
        ),
        [vmem] * 5 + [far],
        (vmem,) * 3,
        limit=4,
    )(features, other_down, own_shrunk, normed, adapter_up_query, wo)

    partial = after = partial + crossed(partial, 1)
    far_up_query = crossed(up_query, peers // 2)
    for mask in near_masks():
        partial = partial + crossed(partial, mask)

    key_sum = jnp.dot(normed, wk, preferred_element_type=f32)
    value_sum = jnp.dot(normed, wv, preferred_element_type=f32)
    query_sum = kernel_call(
        query_kernel,
        shape((rows, wq.shape[1]), f32),
        [vmem] * 3,
        vmem,
        limit=4,
        moved=wq.size,
        flops=2 * rows * wq.size,
    )(normed, wq, after)
    other_far_up_query = lax.ppermute(far_up_query, "replica", pairs)

    packed_rows = padded(held_rows, 16) + padded(3 * rows, 16)
    packed = kernel_call(
        pack_kernel,
        shape((packed_rows, HEAD_DIM), bf16),
        [vmem, vmem, far],
        vmem,
        [pltpu.VMEM((packed_rows, HEAD_DIM), f32)],
        limit=4,
    )(query_sum, partial, wq)
    queries, key_raw, value_raw = kernel_call(
        functools.partial(finish_kernel, seqs),
        (
            shape((2, held_rows, HEAD_DIM), bf16),
            shape((rows, kv_width), bf16),
            shape((rows, kv_width), bf16),
        ),
        [vmem] * 13 + [far],
        (vmem,) * 3,
        [
            pltpu.VMEM((2, local_heads, padded(rows, 8), HEAD_DIM), f32),
            pltpu.VMEM((2, held_rows, HEAD_DIM), f32),
        ],
        limit=4,
    )(
        query_sum, partial, crossed(packed, peers // 2), key_sum, value_sum, up_query,
        other_up_query, far_up_query, other_far_up_query, adapter_up_value, other_up_value,
        cosine, sine, wq,
    )

    if kv_width != HEAD_DIM:
        kv_index = tensor_index * local_heads // group

        def own_head(value):
            heads = lax.all_gather(value, "tensor", axis=1, tiled=True)
            return lax.dynamic_slice_in_dim(heads, kv_index * HEAD_DIM, HEAD_DIM, 1)

        key_raw, value_raw = own_head(key_raw), own_head(value_raw)

    fresh, fresh_level = kernel_call(
        functools.partial(fresh_kernel, seqs),
        (shape((held_rows, HEAD_DIM), f32), shape((8, HEAD_DIM), f32)),
        [vmem] * 5 + [far],
        (vmem, vmem),
        limit=4,
    )(queries, key_raw, value_raw, cosine, sine, wq)
    held, masks = queries, [0, peers // 2]
    for mask in near_masks()[::-1]:
        held = jnp.concatenate([held, crossed(held, mask)])
        masks = masks + [mask ^ other for other in masks]
    others = crossed(held, 1)

    span = rotated_key_cache.shape[2]
    blocks_shape = shape((peers, padded(held_rows, 16) + 16, HEAD_DIM), bf16)
    buffers = [pltpu.VMEM((4, span, HEAD_DIM), f32), pltpu.VMEM((4, HEAD_DIM, span), f32)]

    def cache_part(its_masks, *operands):
        return kernel_call(
            functools.partial(cache_kernel, its_masks),
            blocks_shape,
            [vmem] * 4 + [far] + [vmem] * len(operands),
            vmem,
            buffers,
            limit=6,
        )(
            reach, operands[0], rotated_key_cache, cached_value_rows, wq, fresh_level,
            *operands[1:],
        )

    even_blocks = cache_part(masks, held)
    blocks = cache_part([mask ^ 1 for mask in masks], others, even_blocks)

    folds = width // 256 if (rows * (width // 256)) % 16 == 0 else 1
    shares = kernel_call(
        functools.partial(merge_kernel, seqs),
        shape((peers, rows * folds, width // folds), bf16),
        [vmem] * 4,
        vmem,
        [pltpu.VMEM((local_heads, padded(rows, 8), HEAD_DIM), f32)],
        limit=6,
    )(exchanged(blocks), fresh, fresh_level, wo)
    return kernel_call(
        sum_kernel,
        shape((steps, seqs, width), bf16),
        [vmem] * 2,
        vmem,
        limit=4,
    )(rest, exchanged(shares))


def solution(mesh):
    return jax.shard_map(
        body,
        mesh=mesh,
        in_specs=(
            P(None, ("groups", "replica"), None),
            P(),
            P(None, "tensor"),
            P(None, "tensor"),
            P(None, "tensor"),
            P("tensor", None),
            P(("replica", "tensor"), None),
            P("replica", "tensor"),
            P("replica", "tensor"),
            P(),
            P(("groups", "replica"), None, "tensor", None),
            P(("groups", "replica"), None, "tensor", None),
            P(("groups", "replica")),
        ),
        out_specs=P(None, ("groups", "replica"), "tensor"),
        check_vma=False,
    )
```

```python
import functools
import math

import jax
import jax.numpy as jnp
from jax import lax
from jax.experimental import pallas as pl
from jax.experimental.pallas import tpu as pltpu
from jax.sharding import PartitionSpec as P

QUERY_HEADS = 64
KEY_VALUE_HEADS = 8
HEAD_DIM = 128
ADAPTER_RANK = 64


adapter_scale = 2.0
rope_base = 500000.0
negative = -1e30
inv_root = 1.0 / math.sqrt(HEAD_DIM)
MIB = 1 << 20

vmem = pl.BlockSpec(memory_space=pltpu.VMEM)
smem = pl.BlockSpec(memory_space=pltpu.SMEM)
far = pl.BlockSpec(memory_space=pl.ANY)


def padded(count, multiple):
    return -(-count // multiple) * multiple


def rows_padded(value, rows):
    if value.shape[0] == rows:
        return value
    filler = jnp.zeros((rows - value.shape[0],) + value.shape[1:], value.dtype)
    return jnp.concatenate([value, filler], axis=0)


def kernel_call(kernel, outs, specs, out_specs, scratch=(), limit=16, moved=0, flops=0):
    call = pl.pallas_call(
        kernel,
        out_shape=outs,
        in_specs=specs,
        out_specs=out_specs,
        scratch_shapes=list(scratch),
        compiler_params=pltpu.CompilerParams(vmem_limit_bytes=limit * MIB),
        cost_estimate=pl.CostEstimate(flops=flops, bytes_accessed=moved, transcendentals=0),
    )

    def run(*operands):
        return call(
            *[
                pltpu.with_memory_space_constraint(operand, pltpu.HBM) if spec is far else operand
                for operand, spec in zip(operands, specs)
            ]
        )

    return run


def fetches(pairs, sem):
    copies = [
        pltpu.make_async_copy(far_ref, near, sem.at[k]) for k, (far_ref, near) in enumerate(pairs)
    ]
    for copy in copies:
        copy.start()
    return copies


def features_of(normed_ref, owner_ref, held, block_rows):
    place = jnp.int32(0)
    for j in range(owner_ref.shape[0]):
        place = jnp.where(owner_ref[j] == held, jnp.int32(j), place)
    return normed_ref[:, pl.ds(pl.multiple_of(place * block_rows, block_rows), block_rows)]


def norm_kernel(
    peers, heads, lengths_ref, owner_ref, x_ref, down_ref, gain_ref, beside_ref,
    normed_ref, cos_ref, sin_ref, rest_ref, reach_ref, shrunk_ref, features_ref,
    lengths, owner, x_buf, down_buf, gain, sem,
):
    copies = fetches(
        [
            (lengths_ref, lengths),
            (owner_ref, owner),
            (x_ref, x_buf),
            (down_ref, down_buf),
            (gain_ref, gain),
        ],
        sem,
    )
    steps, seqs, _ = x_ref.shape
    rows, width = rest_ref.shape
    half = HEAD_DIM // 2
    row = lax.broadcasted_iota(jnp.int32, (rows, HEAD_DIM), 0)
    lane = lax.broadcasted_iota(jnp.int32, (rows, HEAD_DIM), 1)
    copies[0].wait()
    positions = jnp.zeros((rows, HEAD_DIM), jnp.int32)
    for s in range(steps):
        for n in range(seqs):
            positions = jnp.where(row == s * seqs + n, lengths[n] + s, positions)
    low = lane < half
    exponent = jnp.where(low, lane, lane - half).astype(jnp.float32) * (2.0 / HEAD_DIM)
    angles = positions.astype(jnp.float32) * jnp.exp(exponent * -math.log(rope_base))
    sine = jnp.sin(angles)
    cos_ref[...] = jnp.cos(angles)
    sin_ref[...] = jnp.where(low, -sine, sine)
    place = lax.broadcasted_iota(jnp.int32, reach_ref.shape, 1)
    reach = jnp.zeros(reach_ref.shape, jnp.int32)
    per_seq = heads * steps
    for n in range(seqs):
        mine = jnp.logical_and(place >= n * per_seq, place < (n + 1) * per_seq)
        reach = jnp.where(mine, lengths[n], reach)
    reach_ref[...] = reach
    copies[2].wait()
    values = jnp.concatenate([x_buf[s].astype(jnp.float32) for s in range(steps)], axis=0)
    factor = lax.rsqrt(jnp.mean(values * values, axis=-1, keepdims=True) + 1e-05)
    copies[4].wait()
    normed = values * factor * gain[...].astype(jnp.float32).reshape(1, -1)
    normed_ref[...] = normed.astype(jnp.bfloat16)
    replica, tensor = lax.axis_index("replica"), lax.axis_index("tensor")
    for s in range(steps):
        part = x_buf[s, :, pl.ds(pl.multiple_of(tensor * width, width), width)]
        rest_ref[s * seqs : (s + 1) * seqs, :] = part.astype(jnp.float32)
    copies[1].wait()
    copies[3].wait()
    block_rows = down_ref.shape[0]
    features_ref[...] = features_of(
        normed_ref, owner, (1 - replica) * peers + tensor, block_rows
    )
    shrunk_ref[...] = jnp.dot(
        features_of(normed_ref, owner, replica * peers + tensor, block_rows),
        down_buf[...],
        preferred_element_type=jnp.float32,
    )


def shrink_kernel(
    features_ref, other_ref, own_ref, normed_ref, up_ref, beside_ref, out_ref, normed_out, up_out
):
    normed_out[...] = normed_ref[...]
    up_out[...] = up_ref[...]
    out_ref[...] = own_ref[...] + jnp.dot(
        features_ref[...], other_ref[...], preferred_element_type=jnp.float32
    )


def query_kernel(normed_ref, wq_ref, out_ref):
    out_ref[...] = jnp.dot(normed_ref[...], wq_ref[...], preferred_element_type=jnp.float32)


def rotated(values, cosine, sine):
    half = HEAD_DIM // 2
    turned = jnp.concatenate([values[:, half:], values[:, :half]], axis=1)
    return values * cosine + turned * sine


def pack_kernel(acc_ref, partial_ref, beside_ref, out_ref, tall):
    rows = acc_ref.shape[0]
    heads = acc_ref.shape[1] // HEAD_DIM
    for h in range(heads):
        tall[h * rows : (h + 1) * rows, :] = acc_ref[:, h * HEAD_DIM : (h + 1) * HEAD_DIM]
    held_rows = padded(heads * rows, 16)
    if held_rows > heads * rows:
        tall[heads * rows : held_rows, :] = jnp.zeros(
            (held_rows - heads * rows, HEAD_DIM), jnp.float32
        )
    left = partial_ref[...]
    for c in range(3):
        piece = left.astype(jnp.bfloat16).astype(jnp.float32)
        left = left - piece
        tall[held_rows + c * rows : held_rows + (c + 1) * rows, :] = piece
    end = held_rows + 3 * rows
    if out_ref.shape[0] > end:
        tall[end:, :] = jnp.zeros((out_ref.shape[0] - end, HEAD_DIM), jnp.float32)
    out_ref[...] = tall[...].astype(jnp.bfloat16)


def finish_kernel(
    seq_count, acc_ref, partial_ref, met_ref, key_ref, value_ref, uq_own, uq_other, far_own,
    far_other, uv_own, uv_other, cos_ref, sin_ref, beside_ref,
    query_ref, keyout_ref, valueout_ref, wide, tall,
):
    first = lax.axis_index("replica") == 0
    rows = acc_ref.shape[0]
    steps = rows // seq_count
    heads = acc_ref.shape[1] // HEAD_DIM
    held_rows = padded(heads * rows, 16)
    met = met_ref[...].astype(jnp.float32)
    pieces = [met[held_rows + c * rows : held_rows + (c + 1) * rows] for c in range(3)]
    shrunk = partial_ref[...] + (pieces[0] + (pieces[1] + pieces[2]))
    shrunk = shrunk.astype(jnp.bfloat16).astype(jnp.float32)
    half = ADAPTER_RANK // 2

    def lifted(low, high, own, other):
        mine = jnp.where(first, low, high).astype(jnp.bfloat16)
        theirs = jnp.where(first, high, low).astype(jnp.bfloat16)
        return adapter_scale * (
            jnp.dot(mine, own[...], preferred_element_type=jnp.float32)
            + jnp.dot(theirs, other[...], preferred_element_type=jnp.float32)
        )

    low, high = shrunk[:, :half], shrunk[:, half : 2 * half]
    cosine, sine = cos_ref[...], sin_ref[...]
    for e, (own, other) in enumerate(((uq_own, uq_other), (far_own, far_other))):
        lora = lifted(low, high, own, other)
        for h in range(heads):
            columns = slice(h * HEAD_DIM, (h + 1) * HEAD_DIM)
            base = acc_ref[:, columns] if e == 0 else met[h * rows : (h + 1) * rows]
            raw = (base + lora[:, columns]).astype(jnp.bfloat16).astype(jnp.float32)
            wide[e, h, 0:rows, :] = rotated(raw, cosine, sine)
        for n in range(seq_count):
            for h in range(heads):
                tall[e, pl.ds((n * heads + h) * steps, steps), :] = wide[
                    e, h, pl.ds(n, steps, stride=seq_count), :
                ]
        query_ref[e] = tall[e].astype(jnp.bfloat16)
    keyout_ref[...] = key_ref[...].astype(jnp.bfloat16)
    value = value_ref[...] + lifted(
        shrunk[:, 2 * half : 3 * half], shrunk[:, 3 * half :], uv_own, uv_other
    )
    valueout_ref[...] = value.astype(jnp.bfloat16)


def fresh_kernel(
    seq_count, query_ref, key_ref, value_ref, cos_ref, sin_ref, beside_ref,
    fresh_ref, level_ref,
):
    lane = lax.broadcasted_iota(jnp.int32, (1, HEAD_DIM), 1)
    columns = []
    steps = key_ref.shape[0] // seq_count
    per_seq = fresh_ref.shape[0] // seq_count
    queries = query_ref[0].astype(jnp.float32)
    keys = rotated(key_ref[...].astype(jnp.float32), cos_ref[...], sin_ref[...])
    keys = keys.astype(jnp.bfloat16).astype(jnp.float32)
    values = value_ref[...].astype(jnp.float32)
    step = lax.rem(lax.broadcasted_iota(jnp.int32, (per_seq, 1), 0), steps)
    for n in range(seq_count):
        rows = slice(n * per_seq, (n + 1) * per_seq)
        query = queries[rows]
        scores = []
        for t in range(steps):
            place = t * seq_count + n
            score = jnp.sum(query * keys[place : place + 1], axis=-1, keepdims=True) * inv_root
            scores.append(jnp.where(step >= t, score, negative))
        top = functools.reduce(jnp.maximum, scores)
        weights = [
            jnp.where(step >= t, jnp.exp(score - top), 0.0) for t, score in enumerate(scores)
        ]
        total = functools.reduce(jnp.add, weights)
        summed = jnp.zeros((per_seq, HEAD_DIM), jnp.float32)
        for t, weight in enumerate(weights):
            place = t * seq_count + n
            summed = summed + weight.astype(jnp.bfloat16).astype(jnp.float32) * values[
                place : place + 1
            ]
        fresh_ref[rows, :] = summed
        columns.append(jnp.where(lane == 0, top, jnp.where(lane == 1, total, 0.0)))
    columns = rows_padded(jnp.concatenate(columns, axis=0), HEAD_DIM)
    level_ref[...] = jnp.transpose(columns)[0 : level_ref.shape[0], :]


def pieces_of(top, total):
    rows = lax.broadcasted_iota(jnp.int32, (16, HEAD_DIM), 0)
    packed = jnp.zeros((16, HEAD_DIM), jnp.float32)
    for first, left in ((0, top), (3, total)):
        for c in range(3):
            piece = left.astype(jnp.bfloat16).astype(jnp.float32)
            left = left - piece
            packed = jnp.where(rows == first + c, piece, packed)
    return packed.astype(jnp.bfloat16)


def top_and_total(part_ref, held_rows):
    pieces = part_ref[padded(held_rows, 16) :, :].astype(jnp.float32)
    return (
        pieces[0:1] + (pieces[1:2] + pieces[2:3]),
        pieces[3:4] + (pieces[4:5] + pieces[5:6]),
    )


def turned_rows(rows):
    count = padded(len(rows), 8)
    place = lax.broadcasted_iota(jnp.int32, (count, HEAD_DIM), 0)
    stacked = jnp.zeros((count, HEAD_DIM), jnp.float32)
    for k, row in enumerate(rows):
        stacked = jnp.where(place == k, row, stacked)
    return jnp.transpose(rows_padded(stacked, HEAD_DIM))


def cache_kernel(
    masks, taken, reach_ref, kc_ref, vc_ref, beside_ref, after_ref, *refs
):
    *refs, out_ref, scores_buf, weights_buf = refs
    earlier, query_refs = (refs[:1], refs[1:]) if taken else ([], refs)
    entries, peers = len(masks), out_ref.shape[0]
    each, held_rows, _ = query_refs[0].shape
    seq_count, kv_heads, span, _ = kc_ref.shape
    per_seq = held_rows // seq_count
    mean_rows = padded(held_rows, 16)
    tensor = lax.axis_index("tensor")
    spots = tensor * span + lax.broadcasted_iota(jnp.int32, (span, HEAD_DIM), 0)
    live = spots < reach_ref[0:1, :]
    lane = lax.broadcasted_iota(jnp.int32, (span, HEAD_DIM), 1)
    owners = [lax.bitwise_xor(tensor, mask) for mask in masks]
    heads = [owner * kv_heads // peers for owner in owners]
    for blocks in earlier:
        for mask in taken:
            place = lax.bitwise_xor(tensor, mask)
            out_ref[place] = blocks[place]
    batch = scores_buf.shape[0]
    for lead in range(0, entries, batch):
        part = range(lead, min(lead + batch, entries))
        turned = [
            jnp.transpose(
                rows_padded(query_refs[e // each][e % each].astype(jnp.float32), HEAD_DIM)
            ).astype(jnp.bfloat16)
            for e in part
        ]
        for k, e in enumerate(part):
            scores = None
            for n in range(seq_count):
                score = jnp.dot(
                    kc_ref[n, heads[e]], turned[k], preferred_element_type=jnp.float32
                )
                scores = score if n == 0 else jnp.where(lane < n * per_seq, scores, score)
            scores_buf[k] = jnp.where(live, scores, negative)
        tops = [
            jnp.maximum(jnp.max(scores_buf[k], axis=0, keepdims=True), 0.1 * negative)
            for k in range(len(part))
        ]
        for k, e in enumerate(part):
            weights = jnp.exp((scores_buf[k] - tops[k]) * inv_root)
            total = jnp.sum(weights, axis=0, keepdims=True)
            out_ref[owners[e], mean_rows:, :] = pieces_of(tops[k] * inv_root, total)
            weights_buf[k] = jnp.transpose(weights)
        for k, e in enumerate(part):
            sums = [
                jnp.dot(
                    weights_buf[k, n * per_seq : (n + 1) * per_seq, :].astype(jnp.bfloat16),
                    vc_ref[n, heads[e]],
                    preferred_element_type=jnp.float32,
                )
                for n in range(seq_count)
            ]
            sums = rows_padded(jnp.concatenate(sums, axis=0), mean_rows)
            out_ref[owners[e], 0:mean_rows, :] = sums.astype(jnp.bfloat16)


def merge_kernel(seq_count, blocks_ref, fresh_ref, level_ref, wo_ref, out_ref, wide):
    peers, folded, lanes = out_ref.shape
    heads = wide.shape[0]
    held_rows = fresh_ref.shape[0]
    rows = held_rows // heads
    steps = rows // seq_count
    folds = folded // rows
    per_seq = heads * steps
    mean_rows = padded(held_rows, 16)
    stats = [top_and_total(blocks_ref.at[b], held_rows) for b in range(peers)]
    stats.append((level_ref[0:1, :], level_ref[1:2, :]))
    top = functools.reduce(jnp.maximum, [stat[0] for stat in stats])
    factors = [jnp.exp(stat[0] - top) for stat in stats]
    total = functools.reduce(jnp.add, [factor * stat[1] for factor, stat in zip(factors, stats)])
    total = jnp.where(total > 0.0, total, 1.0)
    columns = turned_rows([factor / total for factor in factors])
    mixed = fresh_ref[...] * columns[0:held_rows, peers : peers + 1]
    for b in range(peers):
        mixed = mixed + (
            blocks_ref[b, 0:mean_rows, :].astype(jnp.float32)[0:held_rows]
            * columns[0:held_rows, b : b + 1]
        )
    for n in range(seq_count):
        for h in range(heads):
            first = n * per_seq + h * steps
            wide[h, pl.ds(n, steps, stride=seq_count), :] = mixed[first : first + steps]
    attention = jnp.concatenate([wide[h, 0:rows, :] for h in range(heads)], axis=1)
    attention = attention.astype(jnp.bfloat16)
    width = folds * lanes
    for p in range(peers):
        share = jnp.dot(
            attention,
            wo_ref[:, p * width : (p + 1) * width],
            preferred_element_type=jnp.float32,
        )
        if folds > 1:
            share = jnp.concatenate(
                [share[:, c * lanes : (c + 1) * lanes] for c in range(folds)], axis=0
            )
        out_ref[p] = share.astype(out_ref.dtype)


def sum_kernel(rest_ref, parts_ref, out_ref):
    total = functools.reduce(
        jnp.add, [parts_ref[b].astype(jnp.float32) for b in range(parts_ref.shape[0])]
    )
    rows = rest_ref.shape[0]
    steps, seqs, _ = out_ref.shape
    folds, lanes = total.shape[0] // rows, total.shape[1]
    for c in range(folds):
        columns = slice(c * lanes, (c + 1) * lanes)
        piece = total[c * rows : (c + 1) * rows] + rest_ref[:, columns]
        for s in range(steps):
            out_ref[s, :, columns] = piece[s * seqs : (s + 1) * seqs].astype(jnp.bfloat16)


def crossed(value, mask):
    pairs = [(source, source ^ mask) for source in range(lax.axis_size("tensor"))]
    return lax.ppermute(value, "tensor", pairs)


def exchanged(value):
    return lax.all_to_all(value, "tensor", split_axis=0, concat_axis=0, tiled=True)


def near_masks():
    masks = [2]
    while 4 * masks[-1] < lax.axis_size("tensor"):
        masks.append(2 * masks[-1])
    return masks


def body(
    layer_input_hidden,
    rmsnorm_gain_weight,
    wq,
    wk,
    wv,
    wo,
    adapter_down_stored,
    adapter_up_query,
    adapter_up_value,
    adapter_block_owner,
    rotated_key_cache,
    cached_value_rows,
    cache_valid_lengths,
):
    f32, bf16 = jnp.float32, jnp.bfloat16
    shape = jax.ShapeDtypeStruct
    steps, seqs, model_width = layer_input_hidden.shape
    peers = lax.axis_size("tensor")
    tensor_index = lax.axis_index("tensor")
    rows = steps * seqs
    local_heads = wq.shape[1] // HEAD_DIM
    held_rows = rows * local_heads
    kv_width = wk.shape[1]
    width = model_width // peers
    group = QUERY_HEADS // KEY_VALUE_HEADS

    pairs = [(0, 1), (1, 0)]
    other_down = lax.ppermute(adapter_down_stored, "replica", pairs)
    other_up_query = lax.ppermute(adapter_up_query, "replica", pairs)
    other_up_value = lax.ppermute(adapter_up_value, "replica", pairs)

    normed, cosine, sine, rest, reach, own_shrunk, features = kernel_call(
        functools.partial(norm_kernel, peers, local_heads),
        (
            shape((rows, model_width), bf16),
            shape((rows, HEAD_DIM), f32),
            shape((rows, HEAD_DIM), f32),
            shape((rows, width), f32),
            shape((8, HEAD_DIM), jnp.int32),
            shape((rows, 2 * ADAPTER_RANK), f32),
            shape((rows, adapter_down_stored.shape[0]), bf16),
        ),
        [far] * 6,
        (vmem,) * 7,
        [
            pltpu.SMEM(cache_valid_lengths.shape, jnp.int32),
            pltpu.SMEM(adapter_block_owner.shape, jnp.int32),
            pltpu.VMEM(layer_input_hidden.shape, bf16),
            pltpu.VMEM(adapter_down_stored.shape, bf16),
            pltpu.VMEM(rmsnorm_gain_weight.shape, bf16),
            pltpu.SemaphoreType.DMA((5,)),
        ],
        limit=8,
    )(
        cache_valid_lengths, adapter_block_owner, layer_input_hidden, adapter_down_stored,
        rmsnorm_gain_weight, wo,
    )
    own_shrunk, other_down, other_up_query, other_up_value = lax.optimization_barrier(
        (own_shrunk, other_down, other_up_query, other_up_value)
    )
    partial, normed, up_query = kernel_call(
        shrink_kernel,
        (
            shape((rows, 2 * ADAPTER_RANK), f32),
            shape((rows, model_width), bf16),
            shape(adapter_up_query.shape, bf16),
        ),
        [vmem] * 5 + [far],
        (vmem,) * 3,
        limit=4,
    )(features, other_down, own_shrunk, normed, adapter_up_query, wo)

    partial = functools.reduce(jnp.add, [partial] + [crossed(partial, m) for m in (1, 2, 3)])
    far_up_query = crossed(up_query, peers // 2)
    for mask in near_masks()[1:]:
        partial = partial + crossed(partial, mask)

    key_sum = jnp.dot(normed, wk, preferred_element_type=f32)
    value_sum = jnp.dot(normed, wv, preferred_element_type=f32)
    query_sum = kernel_call(
        query_kernel,
        shape((rows, wq.shape[1]), f32),
        [vmem] * 2,
        vmem,
        limit=4,
        moved=wq.size,
        flops=2 * rows * wq.size,
    )(normed, wq)
    other_far_up_query = lax.ppermute(far_up_query, "replica", pairs)

    packed_rows = padded(held_rows, 16) + padded(3 * rows, 16)
    packed = kernel_call(
        pack_kernel,
        shape((packed_rows, HEAD_DIM), bf16),
        [vmem, vmem, far],
        vmem,
        [pltpu.VMEM((packed_rows, HEAD_DIM), f32)],
        limit=4,
    )(query_sum, partial, wq)
    queries, key_raw, value_raw = kernel_call(
        functools.partial(finish_kernel, seqs),
        (
            shape((2, held_rows, HEAD_DIM), bf16),
            shape((rows, kv_width), bf16),
            shape((rows, kv_width), bf16),
        ),
        [vmem] * 13 + [far],
        (vmem,) * 3,
        [
            pltpu.VMEM((2, local_heads, padded(rows, 8), HEAD_DIM), f32),
            pltpu.VMEM((2, held_rows, HEAD_DIM), f32),
        ],
        limit=4,
    )(
        query_sum, partial, crossed(packed, peers // 2), key_sum, value_sum, up_query,
        other_up_query, far_up_query, other_far_up_query, adapter_up_value, other_up_value,
        cosine, sine, wq,
    )

    if kv_width != HEAD_DIM:
        kv_index = tensor_index * local_heads // group

        def own_head(value):
            heads = lax.all_gather(value, "tensor", axis=1, tiled=True)
            return lax.dynamic_slice_in_dim(heads, kv_index * HEAD_DIM, HEAD_DIM, 1)

        key_raw, value_raw = own_head(key_raw), own_head(value_raw)

    fresh, fresh_level = kernel_call(
        functools.partial(fresh_kernel, seqs),
        (shape((held_rows, HEAD_DIM), f32), shape((8, HEAD_DIM), f32)),
        [vmem] * 5 + [far],
        (vmem, vmem),
        limit=4,
    )(queries, key_raw, value_raw, cosine, sine, wq)
    held, masks = queries, [0, peers // 2]
    for mask in near_masks()[:0:-1]:
        held = jnp.concatenate([held, crossed(held, mask)])
        masks = masks + [mask ^ other for other in masks]
    others = [crossed(held, m) for m in (1, 2, 3)]

    span = rotated_key_cache.shape[2]
    blocks_shape = shape((peers, padded(held_rows, 16) + 16, HEAD_DIM), bf16)
    buffers = [pltpu.VMEM((3, span, HEAD_DIM), f32), pltpu.VMEM((3, HEAD_DIM, span), f32)]

    def cache_part(its_masks, taken, *operands):
        return kernel_call(
            functools.partial(cache_kernel, its_masks, taken),
            blocks_shape,
            [vmem] * 3 + [far] + [vmem] * (1 + len(operands)),
            vmem,
            buffers,
            limit=6,
        )(reach, rotated_key_cache, cached_value_rows, wq, fresh_level, *operands)

    near_blocks = cache_part(masks, [], held)
    other_masks = [mask ^ m for m in (1, 2, 3) for mask in masks]
    blocks = cache_part(other_masks, masks, near_blocks, *others)

    folds = width // 256 if (rows * (width // 256)) % 16 == 0 else 1
    shares = kernel_call(
        functools.partial(merge_kernel, seqs),
        shape((peers, rows * folds, width // folds), bf16),
        [vmem] * 4,
        vmem,
        [pltpu.VMEM((local_heads, padded(rows, 8), HEAD_DIM), f32)],
        limit=6,
    )(exchanged(blocks), fresh, fresh_level, wo)
    return kernel_call(
        sum_kernel,
        shape((steps, seqs, width), bf16),
        [vmem] * 2,
        vmem,
        limit=4,
    )(rest, exchanged(shares))


def solution(mesh):
    return jax.shard_map(
        body,
        mesh=mesh,
        in_specs=(
            P(None, ("groups", "replica"), None),
            P(),
            P(None, "tensor"),
            P(None, "tensor"),
            P(None, "tensor"),
            P("tensor", None),
            P(("replica", "tensor"), None),
            P("replica", "tensor"),
            P("replica", "tensor"),
            P(),
            P(("groups", "replica"), None, "tensor", None),
            P(("groups", "replica"), None, "tensor", None),
            P(("groups", "replica")),
        ),
        out_specs=P(None, ("groups", "replica"), "tensor"),
        check_vma=False,
    )
```

```python
import functools
import math

import jax
import jax.numpy as jnp
from jax import lax
from jax.experimental import pallas as pl
from jax.experimental.pallas import tpu as pltpu
from jax.sharding import PartitionSpec as P

QUERY_HEADS = 64
KEY_VALUE_HEADS = 8
HEAD_DIM = 128
ADAPTER_RANK = 64


adapter_scale = 2.0
rope_base = 500000.0
negative = -1e30
inv_root = 1.0 / math.sqrt(HEAD_DIM)
MIB = 1 << 20

vmem = pl.BlockSpec(memory_space=pltpu.VMEM)
smem = pl.BlockSpec(memory_space=pltpu.SMEM)
far = pl.BlockSpec(memory_space=pl.ANY)


def padded(count, multiple):
    return -(-count // multiple) * multiple


def rows_padded(value, rows):
    if value.shape[0] == rows:
        return value
    filler = jnp.zeros((rows - value.shape[0],) + value.shape[1:], value.dtype)
    return jnp.concatenate([value, filler], axis=0)


def kernel_call(kernel, outs, specs, out_specs, scratch=(), limit=16, moved=0, flops=0):
    call = pl.pallas_call(
        kernel,
        out_shape=outs,
        in_specs=specs,
        out_specs=out_specs,
        scratch_shapes=list(scratch),
        compiler_params=pltpu.CompilerParams(vmem_limit_bytes=limit * MIB),
        cost_estimate=pl.CostEstimate(flops=flops, bytes_accessed=moved, transcendentals=0),
    )

    def run(*operands):
        return call(
            *[
                pltpu.with_memory_space_constraint(operand, pltpu.HBM) if spec is far else operand
                for operand, spec in zip(operands, specs)
            ]
        )

    return run


def fetches(pairs, sem):
    copies = [
        pltpu.make_async_copy(far_ref, near, sem.at[k]) for k, (far_ref, near) in enumerate(pairs)
    ]
    for copy in copies:
        copy.start()
    return copies


def features_of(normed_ref, owner_ref, held, block_rows):
    place = jnp.int32(0)
    for j in range(owner_ref.shape[0]):
        place = jnp.where(owner_ref[j] == held, jnp.int32(j), place)
    return normed_ref[:, pl.ds(pl.multiple_of(place * block_rows, block_rows), block_rows)]


def norm_kernel(
    peers, heads, lengths_ref, owner_ref, x_ref, down_ref, gain_ref, beside_ref,
    normed_ref, cos_ref, sin_ref, rest_ref, reach_ref, shrunk_ref, features_ref,
    lengths, owner, x_buf, down_buf, gain, sem,
):
    copies = fetches(
        [
            (lengths_ref, lengths),
            (owner_ref, owner),
            (x_ref, x_buf),
            (down_ref, down_buf),
            (gain_ref, gain),
        ],
        sem,
    )
    steps, seqs, _ = x_ref.shape
    rows, width = rest_ref.shape
    half = HEAD_DIM // 2
    row = lax.broadcasted_iota(jnp.int32, (rows, HEAD_DIM), 0)
    lane = lax.broadcasted_iota(jnp.int32, (rows, HEAD_DIM), 1)
    copies[0].wait()
    positions = jnp.zeros((rows, HEAD_DIM), jnp.int32)
    for s in range(steps):
        for n in range(seqs):
            positions = jnp.where(row == s * seqs + n, lengths[n] + s, positions)
    low = lane < half
    exponent = jnp.where(low, lane, lane - half).astype(jnp.float32) * (2.0 / HEAD_DIM)
    angles = positions.astype(jnp.float32) * jnp.exp(exponent * -math.log(rope_base))
    sine = jnp.sin(angles)
    cos_ref[...] = jnp.cos(angles)
    sin_ref[...] = jnp.where(low, -sine, sine)
    place = lax.broadcasted_iota(jnp.int32, reach_ref.shape, 1)
    reach = jnp.zeros(reach_ref.shape, jnp.int32)
    per_seq = heads * steps
    for n in range(seqs):
        mine = jnp.logical_and(place >= n * per_seq, place < (n + 1) * per_seq)
        reach = jnp.where(mine, lengths[n], reach)
    reach_ref[...] = reach
    copies[2].wait()
    values = jnp.concatenate([x_buf[s].astype(jnp.float32) for s in range(steps)], axis=0)
    factor = lax.rsqrt(jnp.mean(values * values, axis=-1, keepdims=True) + 1e-05)
    copies[4].wait()
    normed = values * factor * gain[...].astype(jnp.float32).reshape(1, -1)
    normed_ref[...] = normed.astype(jnp.bfloat16)
    replica, tensor = lax.axis_index("replica"), lax.axis_index("tensor")
    for s in range(steps):
        part = x_buf[s, :, pl.ds(pl.multiple_of(tensor * width, width), width)]
        rest_ref[s * seqs : (s + 1) * seqs, :] = part.astype(jnp.float32)
    copies[1].wait()
    copies[3].wait()
    block_rows = down_ref.shape[0]
    features_ref[...] = features_of(
        normed_ref, owner, (1 - replica) * peers + tensor, block_rows
    )
    shrunk_ref[...] = jnp.dot(
        features_of(normed_ref, owner, replica * peers + tensor, block_rows),
        down_buf[...],
        preferred_element_type=jnp.float32,
    )


def shrink_kernel(
    features_ref, other_ref, own_ref, normed_ref, up_ref, beside_ref, out_ref, normed_out, up_out
):
    normed_out[...] = normed_ref[...]
    up_out[...] = up_ref[...]
    out_ref[...] = own_ref[...] + jnp.dot(
        features_ref[...], other_ref[...], preferred_element_type=jnp.float32
    )


def query_kernel(normed_ref, wq_ref, after_ref, out_ref):
    out_ref[...] = jnp.dot(normed_ref[...], wq_ref[...], preferred_element_type=jnp.float32)


def rotated(values, cosine, sine):
    half = HEAD_DIM // 2
    turned = jnp.concatenate([values[:, half:], values[:, :half]], axis=1)
    return values * cosine + turned * sine


def pack_kernel(acc_ref, partial_ref, beside_ref, out_ref, tall):
    rows = acc_ref.shape[0]
    heads = acc_ref.shape[1] // HEAD_DIM
    for h in range(heads):
        tall[h * rows : (h + 1) * rows, :] = acc_ref[:, h * HEAD_DIM : (h + 1) * HEAD_DIM]
    held_rows = padded(heads * rows, 16)
    if held_rows > heads * rows:
        tall[heads * rows : held_rows, :] = jnp.zeros(
            (held_rows - heads * rows, HEAD_DIM), jnp.float32
        )
    left = partial_ref[...]
    for c in range(3):
        piece = left.astype(jnp.bfloat16).astype(jnp.float32)
        left = left - piece
        tall[held_rows + c * rows : held_rows + (c + 1) * rows, :] = piece
    end = held_rows + 3 * rows
    if out_ref.shape[0] > end:
        tall[end:, :] = jnp.zeros((out_ref.shape[0] - end, HEAD_DIM), jnp.float32)
    out_ref[...] = tall[...].astype(jnp.bfloat16)


def finish_kernel(
    seq_count, acc_ref, partial_ref, met_ref, key_ref, value_ref, uq_own, uq_other, far_own,
    far_other, uv_own, uv_other, cos_ref, sin_ref, beside_ref,
    query_ref, keyout_ref, valueout_ref, wide, tall,
):
    first = lax.axis_index("replica") == 0
    rows = acc_ref.shape[0]
    steps = rows // seq_count
    heads = acc_ref.shape[1] // HEAD_DIM
    held_rows = padded(heads * rows, 16)
    met = met_ref[...].astype(jnp.float32)
    pieces = [met[held_rows + c * rows : held_rows + (c + 1) * rows] for c in range(3)]
    shrunk = partial_ref[...] + (pieces[0] + (pieces[1] + pieces[2]))
    shrunk = shrunk.astype(jnp.bfloat16).astype(jnp.float32)
    half = ADAPTER_RANK // 2

    def lifted(low, high, own, other):
        mine = jnp.where(first, low, high).astype(jnp.bfloat16)
        theirs = jnp.where(first, high, low).astype(jnp.bfloat16)
        return adapter_scale * (
            jnp.dot(mine, own[...], preferred_element_type=jnp.float32)
            + jnp.dot(theirs, other[...], preferred_element_type=jnp.float32)
        )

    low, high = shrunk[:, :half], shrunk[:, half : 2 * half]
    cosine, sine = cos_ref[...], sin_ref[...]
    for e, (own, other) in enumerate(((uq_own, uq_other), (far_own, far_other))):
        lora = lifted(low, high, own, other)
        for h in range(heads):
            columns = slice(h * HEAD_DIM, (h + 1) * HEAD_DIM)
            base = acc_ref[:, columns] if e == 0 else met[h * rows : (h + 1) * rows]
            raw = (base + lora[:, columns]).astype(jnp.bfloat16).astype(jnp.float32)
            wide[e, h, 0:rows, :] = rotated(raw, cosine, sine)
        for n in range(seq_count):
            for h in range(heads):
                tall[e, pl.ds((n * heads + h) * steps, steps), :] = wide[
                    e, h, pl.ds(n, steps, stride=seq_count), :
                ]
        query_ref[e] = tall[e].astype(jnp.bfloat16)
    keyout_ref[...] = key_ref[...].astype(jnp.bfloat16)
    value = value_ref[...] + lifted(
        shrunk[:, 2 * half : 3 * half], shrunk[:, 3 * half :], uv_own, uv_other
    )
    valueout_ref[...] = value.astype(jnp.bfloat16)


def fresh_kernel(
    seq_count, query_ref, key_ref, value_ref, cos_ref, sin_ref, beside_ref,
    fresh_ref, level_ref,
):
    lane = lax.broadcasted_iota(jnp.int32, (1, HEAD_DIM), 1)
    columns = []
    steps = key_ref.shape[0] // seq_count
    per_seq = fresh_ref.shape[0] // seq_count
    queries = query_ref[0].astype(jnp.float32)
    keys = rotated(key_ref[...].astype(jnp.float32), cos_ref[...], sin_ref[...])
    keys = keys.astype(jnp.bfloat16).astype(jnp.float32)
    values = value_ref[...].astype(jnp.float32)
    step = lax.rem(lax.broadcasted_iota(jnp.int32, (per_seq, 1), 0), steps)
    for n in range(seq_count):
        rows = slice(n * per_seq, (n + 1) * per_seq)
        query = queries[rows]
        scores = []
        for t in range(steps):
            place = t * seq_count + n
            score = jnp.sum(query * keys[place : place + 1], axis=-1, keepdims=True) * inv_root
            scores.append(jnp.where(step >= t, score, negative))
        top = functools.reduce(jnp.maximum, scores)
        weights = [
            jnp.where(step >= t, jnp.exp(score - top), 0.0) for t, score in enumerate(scores)
        ]
        total = functools.reduce(jnp.add, weights)
        summed = jnp.zeros((per_seq, HEAD_DIM), jnp.float32)
        for t, weight in enumerate(weights):
            place = t * seq_count + n
            summed = summed + weight.astype(jnp.bfloat16).astype(jnp.float32) * values[
                place : place + 1
            ]
        fresh_ref[rows, :] = summed
        columns.append(jnp.where(lane == 0, top, jnp.where(lane == 1, total, 0.0)))
    columns = rows_padded(jnp.concatenate(columns, axis=0), HEAD_DIM)
    level_ref[...] = jnp.transpose(columns)[0 : level_ref.shape[0], :]


def pieces_of(top, total):
    rows = lax.broadcasted_iota(jnp.int32, (16, HEAD_DIM), 0)
    packed = jnp.zeros((16, HEAD_DIM), jnp.float32)
    for first, left in ((0, top), (3, total)):
        for c in range(3):
            piece = left.astype(jnp.bfloat16).astype(jnp.float32)
            left = left - piece
            packed = jnp.where(rows == first + c, piece, packed)
    return packed.astype(jnp.bfloat16)


def top_and_total(part_ref, held_rows):
    pieces = part_ref[padded(held_rows, 16) :, :].astype(jnp.float32)
    return (
        pieces[0:1] + (pieces[1:2] + pieces[2:3]),
        pieces[3:4] + (pieces[4:5] + pieces[5:6]),
    )


def turned_rows(rows):
    count = padded(len(rows), 8)
    place = lax.broadcasted_iota(jnp.int32, (count, HEAD_DIM), 0)
    stacked = jnp.zeros((count, HEAD_DIM), jnp.float32)
    for k, row in enumerate(rows):
        stacked = jnp.where(place == k, row, stacked)
    return jnp.transpose(rows_padded(stacked, HEAD_DIM))


def cache_kernel(
    masks, taken, reach_ref, kc_ref, vc_ref, beside_ref, after_ref, *refs
):
    *refs, out_ref, scores_buf, weights_buf = refs
    earlier, query_refs = (refs[:1], refs[1:]) if taken else ([], refs)
    entries, peers = len(masks), out_ref.shape[0]
    each, held_rows, _ = query_refs[0].shape
    seq_count, kv_heads, span, _ = kc_ref.shape
    per_seq = held_rows // seq_count
    mean_rows = padded(held_rows, 16)
    tensor = lax.axis_index("tensor")
    spots = tensor * span + lax.broadcasted_iota(jnp.int32, (span, HEAD_DIM), 0)
    live = spots < reach_ref[0:1, :]
    lane = lax.broadcasted_iota(jnp.int32, (span, HEAD_DIM), 1)
    owners = [lax.bitwise_xor(tensor, mask) for mask in masks]
    heads = [owner * kv_heads // peers for owner in owners]
    for blocks in earlier:
        for mask in taken:
            place = lax.bitwise_xor(tensor, mask)
            out_ref[place] = blocks[place]
    batch = scores_buf.shape[0]
    for lead in range(0, entries, batch):
        part = range(lead, min(lead + batch, entries))
        turned = [
            jnp.transpose(
                rows_padded(query_refs[e // each][e % each].astype(jnp.float32), HEAD_DIM)
            ).astype(jnp.bfloat16)
            for e in part
        ]
        for k, e in enumerate(part):
            scores = None
            for n in range(seq_count):
                score = jnp.dot(
                    kc_ref[n, heads[e]], turned[k], preferred_element_type=jnp.float32
                )
                scores = score if n == 0 else jnp.where(lane < n * per_seq, scores, score)
            scores_buf[k] = jnp.where(live, scores, negative)
        tops = [
            jnp.maximum(jnp.max(scores_buf[k], axis=0, keepdims=True), 0.1 * negative)
            for k in range(len(part))
        ]
        for k, e in enumerate(part):
            weights = jnp.exp((scores_buf[k] - tops[k]) * inv_root)
            total = jnp.sum(weights, axis=0, keepdims=True)
            out_ref[owners[e], mean_rows:, :] = pieces_of(tops[k] * inv_root, total)
            weights_buf[k] = jnp.transpose(weights)
        for k, e in enumerate(part):
            sums = [
                jnp.dot(
                    weights_buf[k, n * per_seq : (n + 1) * per_seq, :].astype(jnp.bfloat16),
                    vc_ref[n, heads[e]],
                    preferred_element_type=jnp.float32,
                )
                for n in range(seq_count)
            ]
            sums = rows_padded(jnp.concatenate(sums, axis=0), mean_rows)
            out_ref[owners[e], 0:mean_rows, :] = sums.astype(jnp.bfloat16)


def merge_kernel(seq_count, blocks_ref, fresh_ref, level_ref, wo_ref, out_ref, wide):
    peers, folded, lanes = out_ref.shape
    heads = wide.shape[0]
    held_rows = fresh_ref.shape[0]
    rows = held_rows // heads
    steps = rows // seq_count
    folds = folded // rows
    per_seq = heads * steps
    mean_rows = padded(held_rows, 16)
    stats = [top_and_total(blocks_ref.at[b], held_rows) for b in range(peers)]
    stats.append((level_ref[0:1, :], level_ref[1:2, :]))
    top = functools.reduce(jnp.maximum, [stat[0] for stat in stats])
    factors = [jnp.exp(stat[0] - top) for stat in stats]
    total = functools.reduce(jnp.add, [factor * stat[1] for factor, stat in zip(factors, stats)])
    total = jnp.where(total > 0.0, total, 1.0)
    columns = turned_rows([factor / total for factor in factors])
    mixed = fresh_ref[...] * columns[0:held_rows, peers : peers + 1]
    for b in range(peers):
        mixed = mixed + (
            blocks_ref[b, 0:mean_rows, :].astype(jnp.float32)[0:held_rows]
            * columns[0:held_rows, b : b + 1]
        )
    for n in range(seq_count):
        for h in range(heads):
            first = n * per_seq + h * steps
            wide[h, pl.ds(n, steps, stride=seq_count), :] = mixed[first : first + steps]
    attention = jnp.concatenate([wide[h, 0:rows, :] for h in range(heads)], axis=1)
    attention = attention.astype(jnp.bfloat16)
    width = folds * lanes
    for p in range(peers):
        share = jnp.dot(
            attention,
            wo_ref[:, p * width : (p + 1) * width],
            preferred_element_type=jnp.float32,
        )
        if folds > 1:
            share = jnp.concatenate(
                [share[:, c * lanes : (c + 1) * lanes] for c in range(folds)], axis=0
            )
        out_ref[p] = share.astype(out_ref.dtype)


def sum_kernel(rest_ref, parts_ref, out_ref):
    total = functools.reduce(
        jnp.add, [parts_ref[b].astype(jnp.float32) for b in range(parts_ref.shape[0])]
    )
    rows = rest_ref.shape[0]
    steps, seqs, _ = out_ref.shape
    folds, lanes = total.shape[0] // rows, total.shape[1]
    for c in range(folds):
        columns = slice(c * lanes, (c + 1) * lanes)
        piece = total[c * rows : (c + 1) * rows] + rest_ref[:, columns]
        for s in range(steps):
            out_ref[s, :, columns] = piece[s * seqs : (s + 1) * seqs].astype(jnp.bfloat16)


def crossed(value, mask):
    pairs = [(source, source ^ mask) for source in range(lax.axis_size("tensor"))]
    return lax.ppermute(value, "tensor", pairs)


def exchanged(value):
    return lax.all_to_all(value, "tensor", split_axis=0, concat_axis=0, tiled=True)


def near_masks():
    masks = [2]
    while 4 * masks[-1] < lax.axis_size("tensor"):
        masks.append(2 * masks[-1])
    return masks


def body(
    layer_input_hidden,
    rmsnorm_gain_weight,
    wq,
    wk,
    wv,
    wo,
    adapter_down_stored,
    adapter_up_query,
    adapter_up_value,
    adapter_block_owner,
    rotated_key_cache,
    cached_value_rows,
    cache_valid_lengths,
):
    f32, bf16 = jnp.float32, jnp.bfloat16
    shape = jax.ShapeDtypeStruct
    steps, seqs, model_width = layer_input_hidden.shape
    peers = lax.axis_size("tensor")
    tensor_index = lax.axis_index("tensor")
    rows = steps * seqs
    local_heads = wq.shape[1] // HEAD_DIM
    held_rows = rows * local_heads
    kv_width = wk.shape[1]
    width = model_width // peers
    group = QUERY_HEADS // KEY_VALUE_HEADS

    pairs = [(0, 1), (1, 0)]
    other_down = lax.ppermute(adapter_down_stored, "replica", pairs)
    other_up_query = lax.ppermute(adapter_up_query, "replica", pairs)
    other_up_value = lax.ppermute(adapter_up_value, "replica", pairs)

    normed, cosine, sine, rest, reach, own_shrunk, features = kernel_call(
        functools.partial(norm_kernel, peers, local_heads),
        (
            shape((rows, model_width), bf16),
            shape((rows, HEAD_DIM), f32),
            shape((rows, HEAD_DIM), f32),
            shape((rows, width), f32),
            shape((8, HEAD_DIM), jnp.int32),
            shape((rows, 2 * ADAPTER_RANK), f32),
            shape((rows, adapter_down_stored.shape[0]), bf16),
        ),
        [far] * 6,
        (vmem,) * 7,
        [
            pltpu.SMEM(cache_valid_lengths.shape, jnp.int32),
            pltpu.SMEM(adapter_block_owner.shape, jnp.int32),
            pltpu.VMEM(layer_input_hidden.shape, bf16),
            pltpu.VMEM(adapter_down_stored.shape, bf16),
            pltpu.VMEM(rmsnorm_gain_weight.shape, bf16),
            pltpu.SemaphoreType.DMA((5,)),
        ],
        limit=8,
    )(
        cache_valid_lengths, adapter_block_owner, layer_input_hidden, adapter_down_stored,
        rmsnorm_gain_weight, wo,
    )
    own_shrunk, other_down, other_up_query, other_up_value = lax.optimization_barrier(
        (own_shrunk, other_down, other_up_query, other_up_value)
    )
    partial, normed, up_query = kernel_call(
        shrink_kernel,
        (
            shape((rows, 2 * ADAPTER_RANK), f32),
            shape((rows, model_width), bf16),
            shape(adapter_up_query.shape, bf16),
        ),
        [vmem] * 5 + [far],
        (vmem,) * 3,
        limit=4,
    )(features, other_down, own_shrunk, normed, adapter_up_query, wo)

    met = [crossed(partial, m) for m in (1, 2, 3)]
    partial = functools.reduce(jnp.add, [partial] + met)
    far_up_query = crossed(up_query, peers // 2)
    for mask in near_masks()[1:]:
        partial = partial + crossed(partial, mask)

    key_sum = jnp.dot(normed, wk, preferred_element_type=f32)
    value_sum = jnp.dot(normed, wv, preferred_element_type=f32)
    query_sum = kernel_call(
        query_kernel,
        shape((rows, wq.shape[1]), f32),
        [vmem] * 3,
        vmem,
        limit=4,
        moved=wq.size,
        flops=2 * rows * wq.size,
    )(normed, wq, met[0])
    other_far_up_query = lax.ppermute(far_up_query, "replica", pairs)

    packed_rows = padded(held_rows, 16) + padded(3 * rows, 16)
    packed = kernel_call(
        pack_kernel,
        shape((packed_rows, HEAD_DIM), bf16),
        [vmem, vmem, far],
        vmem,
        [pltpu.VMEM((packed_rows, HEAD_DIM), f32)],
        limit=4,
    )(query_sum, partial, wq)
    queries, key_raw, value_raw = kernel_call(
        functools.partial(finish_kernel, seqs),
        (
            shape((2, held_rows, HEAD_DIM), bf16),
            shape((rows, kv_width), bf16),
            shape((rows, kv_width), bf16),
        ),
        [vmem] * 13 + [far],
        (vmem,) * 3,
        [
            pltpu.VMEM((2, local_heads, padded(rows, 8), HEAD_DIM), f32),
            pltpu.VMEM((2, held_rows, HEAD_DIM), f32),
        ],
        limit=4,
    )(
        query_sum, partial, crossed(packed, peers // 2), key_sum, value_sum, up_query,
        other_up_query, far_up_query, other_far_up_query, adapter_up_value, other_up_value,
        cosine, sine, wq,
    )

    if kv_width != HEAD_DIM:
        kv_index = tensor_index * local_heads // group

        def own_head(value):
            heads = lax.all_gather(value, "tensor", axis=1, tiled=True)
            return lax.dynamic_slice_in_dim(heads, kv_index * HEAD_DIM, HEAD_DIM, 1)

        key_raw, value_raw = own_head(key_raw), own_head(value_raw)

    fresh, fresh_level = kernel_call(
        functools.partial(fresh_kernel, seqs),
        (shape((held_rows, HEAD_DIM), f32), shape((8, HEAD_DIM), f32)),
        [vmem] * 5 + [far],
        (vmem, vmem),
        limit=4,
    )(queries, key_raw, value_raw, cosine, sine, wq)
    held, masks = queries, [0, peers // 2]
    for mask in near_masks()[:0:-1]:
        held = jnp.concatenate([held, crossed(held, mask)])
        masks = masks + [mask ^ other for other in masks]
    others = [crossed(held, m) for m in (1, 2, 3)]

    span = rotated_key_cache.shape[2]
    blocks_shape = shape((peers, padded(held_rows, 16) + 16, HEAD_DIM), bf16)
    buffers = [pltpu.VMEM((3, span, HEAD_DIM), f32), pltpu.VMEM((3, HEAD_DIM, span), f32)]

    def cache_part(its_masks, taken, *operands):
        return kernel_call(
            functools.partial(cache_kernel, its_masks, taken),
            blocks_shape,
            [vmem] * 3 + [far] + [vmem] * (1 + len(operands)),
            vmem,
            buffers,
            limit=6,
        )(reach, rotated_key_cache, cached_value_rows, wq, fresh_level, *operands)

    near_blocks = cache_part(masks, [], held)
    other_masks = [mask ^ m for m in (1, 2, 3) for mask in masks]
    blocks = cache_part(other_masks, masks, near_blocks, *others)

    folds = width // 256 if (rows * (width // 256)) % 16 == 0 else 1
    shares = kernel_call(
        functools.partial(merge_kernel, seqs),
        shape((peers, rows * folds, width // folds), bf16),
        [vmem] * 4,
        vmem,
        [pltpu.VMEM((local_heads, padded(rows, 8), HEAD_DIM), f32)],
        limit=6,
    )(exchanged(blocks), fresh, fresh_level, wo)
    return kernel_call(
        sum_kernel,
        shape((steps, seqs, width), bf16),
        [vmem] * 2,
        vmem,
        limit=4,
    )(rest, exchanged(shares))


def solution(mesh):
    return jax.shard_map(
        body,
        mesh=mesh,
        in_specs=(
            P(None, ("groups", "replica"), None),
            P(),
            P(None, "tensor"),
            P(None, "tensor"),
            P(None, "tensor"),
            P("tensor", None),
            P(("replica", "tensor"), None),
            P("replica", "tensor"),
            P("replica", "tensor"),
            P(),
            P(("groups", "replica"), None, "tensor", None),
            P(("groups", "replica"), None, "tensor", None),
            P(("groups", "replica")),
        ),
        out_specs=P(None, ("groups", "replica"), "tensor"),
        check_vma=False,
    )
```

```python
import functools
import math

import jax
import jax.numpy as jnp
from jax import lax
from jax.experimental import pallas as pl
from jax.experimental.pallas import tpu as pltpu
from jax.sharding import PartitionSpec as P

QUERY_HEADS = 64
KEY_VALUE_HEADS = 8
HEAD_DIM = 128
ADAPTER_RANK = 64


adapter_scale = 2.0
rope_base = 500000.0
negative = -1e30
inv_root = 1.0 / math.sqrt(HEAD_DIM)
MIB = 1 << 20

vmem = pl.BlockSpec(memory_space=pltpu.VMEM)
smem = pl.BlockSpec(memory_space=pltpu.SMEM)
far = pl.BlockSpec(memory_space=pl.ANY)


def padded(count, multiple):
    return -(-count // multiple) * multiple


def rows_padded(value, rows):
    if value.shape[0] == rows:
        return value
    filler = jnp.zeros((rows - value.shape[0],) + value.shape[1:], value.dtype)
    return jnp.concatenate([value, filler], axis=0)


def kernel_call(kernel, outs, specs, out_specs, scratch=(), limit=16, moved=0, flops=0):
    call = pl.pallas_call(
        kernel,
        out_shape=outs,
        in_specs=specs,
        out_specs=out_specs,
        scratch_shapes=list(scratch),
        compiler_params=pltpu.CompilerParams(vmem_limit_bytes=limit * MIB),
        cost_estimate=pl.CostEstimate(flops=flops, bytes_accessed=moved, transcendentals=0),
    )

    def run(*operands):
        return call(
            *[
                pltpu.with_memory_space_constraint(operand, pltpu.HBM) if spec is far else operand
                for operand, spec in zip(operands, specs)
            ]
        )

    return run


def fetches(pairs, sem):
    copies = [
        pltpu.make_async_copy(far_ref, near, sem.at[k]) for k, (far_ref, near) in enumerate(pairs)
    ]
    for copy in copies:
        copy.start()
    return copies


def features_of(normed_ref, owner_ref, held, block_rows):
    place = jnp.int32(0)
    for j in range(owner_ref.shape[0]):
        place = jnp.where(owner_ref[j] == held, jnp.int32(j), place)
    return normed_ref[:, pl.ds(pl.multiple_of(place * block_rows, block_rows), block_rows)]


def norm_kernel(
    peers, heads, lengths_ref, owner_ref, x_ref, down_ref, gain_ref, beside_ref,
    normed_ref, cos_ref, sin_ref, rest_ref, reach_ref, shrunk_ref, features_ref,
    lengths, owner, x_buf, down_buf, gain, sem,
):
    copies = fetches(
        [
            (lengths_ref, lengths),
            (owner_ref, owner),
            (x_ref, x_buf),
            (down_ref, down_buf),
            (gain_ref, gain),
        ],
        sem,
    )
    steps, seqs, _ = x_ref.shape
    rows, width = rest_ref.shape
    half = HEAD_DIM // 2
    row = lax.broadcasted_iota(jnp.int32, (rows, HEAD_DIM), 0)
    lane = lax.broadcasted_iota(jnp.int32, (rows, HEAD_DIM), 1)
    copies[0].wait()
    positions = jnp.zeros((rows, HEAD_DIM), jnp.int32)
    for s in range(steps):
        for n in range(seqs):
            positions = jnp.where(row == s * seqs + n, lengths[n] + s, positions)
    low = lane < half
    exponent = jnp.where(low, lane, lane - half).astype(jnp.float32) * (2.0 / HEAD_DIM)
    angles = positions.astype(jnp.float32) * jnp.exp(exponent * -math.log(rope_base))
    sine = jnp.sin(angles)
    cos_ref[...] = jnp.cos(angles)
    sin_ref[...] = jnp.where(low, -sine, sine)
    place = lax.broadcasted_iota(jnp.int32, reach_ref.shape, 1)
    reach = jnp.zeros(reach_ref.shape, jnp.int32)
    per_seq = heads * steps
    for n in range(seqs):
        mine = jnp.logical_and(place >= n * per_seq, place < (n + 1) * per_seq)
        reach = jnp.where(mine, lengths[n], reach)
    reach_ref[...] = reach
    copies[2].wait()
    values = jnp.concatenate([x_buf[s].astype(jnp.float32) for s in range(steps)], axis=0)
    factor = lax.rsqrt(jnp.mean(values * values, axis=-1, keepdims=True) + 1e-05)
    copies[4].wait()
    normed = values * factor * gain[...].astype(jnp.float32).reshape(1, -1)
    normed_ref[...] = normed.astype(jnp.bfloat16)
    replica, tensor = lax.axis_index("replica"), lax.axis_index("tensor")
    for s in range(steps):
        part = x_buf[s, :, pl.ds(pl.multiple_of(tensor * width, width), width)]
        rest_ref[s * seqs : (s + 1) * seqs, :] = part.astype(jnp.float32)
    copies[1].wait()
    copies[3].wait()
    block_rows = down_ref.shape[0]
    features_ref[...] = features_of(
        normed_ref, owner, (1 - replica) * peers + tensor, block_rows
    )
    shrunk_ref[...] = jnp.dot(
        features_of(normed_ref, owner, replica * peers + tensor, block_rows),
        down_buf[...],
        preferred_element_type=jnp.float32,
    )


def shrink_kernel(
    features_ref, other_ref, own_ref, normed_ref, up_ref, beside_ref, out_ref, normed_out, up_out
):
    normed_out[...] = normed_ref[...]
    up_out[...] = up_ref[...]
    out_ref[...] = own_ref[...] + jnp.dot(
        features_ref[...], other_ref[...], preferred_element_type=jnp.float32
    )


def query_kernel(normed_ref, wq_ref, after_ref, out_ref):
    out_ref[...] = jnp.dot(normed_ref[...], wq_ref[...], preferred_element_type=jnp.float32)


def rotated(values, cosine, sine):
    half = HEAD_DIM // 2
    turned = jnp.concatenate([values[:, half:], values[:, :half]], axis=1)
    return values * cosine + turned * sine


def pack_kernel(acc_ref, partial_ref, beside_ref, out_ref, tall):
    rows = acc_ref.shape[0]
    heads = acc_ref.shape[1] // HEAD_DIM
    for h in range(heads):
        tall[h * rows : (h + 1) * rows, :] = acc_ref[:, h * HEAD_DIM : (h + 1) * HEAD_DIM]
    held_rows = padded(heads * rows, 16)
    if held_rows > heads * rows:
        tall[heads * rows : held_rows, :] = jnp.zeros(
            (held_rows - heads * rows, HEAD_DIM), jnp.float32
        )
    left = partial_ref[...]
    for c in range(3):
        piece = left.astype(jnp.bfloat16).astype(jnp.float32)
        left = left - piece
        tall[held_rows + c * rows : held_rows + (c + 1) * rows, :] = piece
    end = held_rows + 3 * rows
    if out_ref.shape[0] > end:
        tall[end:, :] = jnp.zeros((out_ref.shape[0] - end, HEAD_DIM), jnp.float32)
    out_ref[...] = tall[...].astype(jnp.bfloat16)


def finish_kernel(
    seq_count, acc_ref, partial_ref, met_ref, key_ref, value_ref, uq_own, uq_other, far_own,
    far_other, uv_own, uv_other, cos_ref, sin_ref, beside_ref,
    query_ref, keyout_ref, valueout_ref, wide, tall,
):
    first = lax.axis_index("replica") == 0
    rows = acc_ref.shape[0]
    steps = rows // seq_count
    heads = acc_ref.shape[1] // HEAD_DIM
    held_rows = padded(heads * rows, 16)
    met = met_ref[...].astype(jnp.float32)
    pieces = [met[held_rows + c * rows : held_rows + (c + 1) * rows] for c in range(3)]
    shrunk = partial_ref[...] + (pieces[0] + (pieces[1] + pieces[2]))
    shrunk = shrunk.astype(jnp.bfloat16).astype(jnp.float32)
    half = ADAPTER_RANK // 2

    def lifted(low, high, own, other):
        mine = jnp.where(first, low, high).astype(jnp.bfloat16)
        theirs = jnp.where(first, high, low).astype(jnp.bfloat16)
        return adapter_scale * (
            jnp.dot(mine, own[...], preferred_element_type=jnp.float32)
            + jnp.dot(theirs, other[...], preferred_element_type=jnp.float32)
        )

    low, high = shrunk[:, :half], shrunk[:, half : 2 * half]
    cosine, sine = cos_ref[...], sin_ref[...]
    for e, (own, other) in enumerate(((uq_own, uq_other), (far_own, far_other))):
        lora = lifted(low, high, own, other)
        for h in range(heads):
            columns = slice(h * HEAD_DIM, (h + 1) * HEAD_DIM)
            base = acc_ref[:, columns] if e == 0 else met[h * rows : (h + 1) * rows]
            raw = (base + lora[:, columns]).astype(jnp.bfloat16).astype(jnp.float32)
            wide[e, h, 0:rows, :] = rotated(raw, cosine, sine)
        for n in range(seq_count):
            for h in range(heads):
                tall[e, pl.ds((n * heads + h) * steps, steps), :] = wide[
                    e, h, pl.ds(n, steps, stride=seq_count), :
                ]
        query_ref[e] = tall[e].astype(jnp.bfloat16)
    keyout_ref[...] = key_ref[...].astype(jnp.bfloat16)
    value = value_ref[...] + lifted(
        shrunk[:, 2 * half : 3 * half], shrunk[:, 3 * half :], uv_own, uv_other
    )
    valueout_ref[...] = value.astype(jnp.bfloat16)


def fresh_kernel(
    seq_count, query_ref, key_ref, value_ref, cos_ref, sin_ref, fresh_ref, level_ref
):
    lane = lax.broadcasted_iota(jnp.int32, (1, HEAD_DIM), 1)
    columns = []
    steps = key_ref.shape[0] // seq_count
    per_seq = fresh_ref.shape[0] // seq_count
    queries = query_ref[0].astype(jnp.float32)
    keys = rotated(key_ref[...].astype(jnp.float32), cos_ref[...], sin_ref[...])
    keys = keys.astype(jnp.bfloat16).astype(jnp.float32)
    values = value_ref[...].astype(jnp.float32)
    step = lax.rem(lax.broadcasted_iota(jnp.int32, (per_seq, 1), 0), steps)
    for n in range(seq_count):
        rows = slice(n * per_seq, (n + 1) * per_seq)
        query = queries[rows]
        scores = []
        for t in range(steps):
            place = t * seq_count + n
            score = jnp.sum(query * keys[place : place + 1], axis=-1, keepdims=True) * inv_root
            scores.append(jnp.where(step >= t, score, negative))
        top = functools.reduce(jnp.maximum, scores)
        weights = [
            jnp.where(step >= t, jnp.exp(score - top), 0.0) for t, score in enumerate(scores)
        ]
        total = functools.reduce(jnp.add, weights)
        summed = jnp.zeros((per_seq, HEAD_DIM), jnp.float32)
        for t, weight in enumerate(weights):
            place = t * seq_count + n
            summed = summed + weight.astype(jnp.bfloat16).astype(jnp.float32) * values[
                place : place + 1
            ]
        fresh_ref[rows, :] = summed
        columns.append(jnp.where(lane == 0, top, jnp.where(lane == 1, total, 0.0)))
    columns = rows_padded(jnp.concatenate(columns, axis=0), HEAD_DIM)
    level_ref[...] = jnp.transpose(columns)[0 : level_ref.shape[0], :]


def pieces_of(top, total):
    rows = lax.broadcasted_iota(jnp.int32, (16, HEAD_DIM), 0)
    packed = jnp.zeros((16, HEAD_DIM), jnp.float32)
    for first, left in ((0, top), (3, total)):
        for c in range(3):
            piece = left.astype(jnp.bfloat16).astype(jnp.float32)
            left = left - piece
            packed = jnp.where(rows == first + c, piece, packed)
    return packed.astype(jnp.bfloat16)


def top_and_total(part_ref, held_rows):
    pieces = part_ref[padded(held_rows, 16) :, :].astype(jnp.float32)
    return (
        pieces[0:1] + (pieces[1:2] + pieces[2:3]),
        pieces[3:4] + (pieces[4:5] + pieces[5:6]),
    )


def turned_rows(rows):
    count = padded(len(rows), 8)
    place = lax.broadcasted_iota(jnp.int32, (count, HEAD_DIM), 0)
    stacked = jnp.zeros((count, HEAD_DIM), jnp.float32)
    for k, row in enumerate(rows):
        stacked = jnp.where(place == k, row, stacked)
    return jnp.transpose(rows_padded(stacked, HEAD_DIM))


def cache_kernel(
    masks, taken, reach_ref, kc_ref, vc_ref, beside_ref, after_ref, *refs
):
    *refs, out_ref, scores_buf, weights_buf = refs
    earlier, query_refs = (refs[:1], refs[1:]) if taken else ([], refs)
    entries, peers = len(masks), out_ref.shape[0]
    each, held_rows, _ = query_refs[0].shape
    seq_count, kv_heads, span, _ = kc_ref.shape
    per_seq = held_rows // seq_count
    mean_rows = padded(held_rows, 16)
    tensor = lax.axis_index("tensor")
    spots = tensor * span + lax.broadcasted_iota(jnp.int32, (span, HEAD_DIM), 0)
    live = spots < reach_ref[0:1, :]
    lane = lax.broadcasted_iota(jnp.int32, (span, HEAD_DIM), 1)
    owners = [lax.bitwise_xor(tensor, mask) for mask in masks]
    heads = [owner * kv_heads // peers for owner in owners]
    for blocks in earlier:
        for mask in taken:
            place = lax.bitwise_xor(tensor, mask)
            out_ref[place] = blocks[place]
    batch = scores_buf.shape[0]
    for lead in range(0, entries, batch):
        part = range(lead, min(lead + batch, entries))
        turned = [
            jnp.transpose(
                rows_padded(query_refs[e // each][e % each].astype(jnp.float32), HEAD_DIM)
            ).astype(jnp.bfloat16)
            for e in part
        ]
        for k, e in enumerate(part):
            scores = None
            for n in range(seq_count):
                score = jnp.dot(
                    kc_ref[n, heads[e]], turned[k], preferred_element_type=jnp.float32
                )
                scores = score if n == 0 else jnp.where(lane < n * per_seq, scores, score)
            scores_buf[k] = jnp.where(live, scores, negative)
        tops = [
            jnp.maximum(jnp.max(scores_buf[k], axis=0, keepdims=True), 0.1 * negative)
            for k in range(len(part))
        ]
        for k, e in enumerate(part):
            weights = jnp.exp((scores_buf[k] - tops[k]) * inv_root)
            total = jnp.sum(weights, axis=0, keepdims=True)
            out_ref[owners[e], mean_rows:, :] = pieces_of(tops[k] * inv_root, total)
            weights_buf[k] = jnp.transpose(weights)
        for k, e in enumerate(part):
            sums = [
                jnp.dot(
                    weights_buf[k, n * per_seq : (n + 1) * per_seq, :].astype(jnp.bfloat16),
                    vc_ref[n, heads[e]],
                    preferred_element_type=jnp.float32,
                )
                for n in range(seq_count)
            ]
            sums = rows_padded(jnp.concatenate(sums, axis=0), mean_rows)
            out_ref[owners[e], 0:mean_rows, :] = sums.astype(jnp.bfloat16)


def merge_kernel(seq_count, blocks_ref, fresh_ref, level_ref, wo_ref, out_ref, wide):
    peers, folded, lanes = out_ref.shape
    heads = wide.shape[0]
    held_rows = fresh_ref.shape[0]
    rows = held_rows // heads
    steps = rows // seq_count
    folds = folded // rows
    per_seq = heads * steps
    mean_rows = padded(held_rows, 16)
    stats = [top_and_total(blocks_ref.at[b], held_rows) for b in range(peers)]
    stats.append((level_ref[0:1, :], level_ref[1:2, :]))
    top = functools.reduce(jnp.maximum, [stat[0] for stat in stats])
    factors = [jnp.exp(stat[0] - top) for stat in stats]
    total = functools.reduce(jnp.add, [factor * stat[1] for factor, stat in zip(factors, stats)])
    total = jnp.where(total > 0.0, total, 1.0)
    columns = turned_rows([factor / total for factor in factors])
    mixed = fresh_ref[...] * columns[0:held_rows, peers : peers + 1]
    for b in range(peers):
        mixed = mixed + (
            blocks_ref[b, 0:mean_rows, :].astype(jnp.float32)[0:held_rows]
            * columns[0:held_rows, b : b + 1]
        )
    for n in range(seq_count):
        for h in range(heads):
            first = n * per_seq + h * steps
            wide[h, pl.ds(n, steps, stride=seq_count), :] = mixed[first : first + steps]
    attention = jnp.concatenate([wide[h, 0:rows, :] for h in range(heads)], axis=1)
    attention = attention.astype(jnp.bfloat16)
    width = folds * lanes
    for p in range(peers):
        share = jnp.dot(
            attention,
            wo_ref[:, p * width : (p + 1) * width],
            preferred_element_type=jnp.float32,
        )
        if folds > 1:
            share = jnp.concatenate(
                [share[:, c * lanes : (c + 1) * lanes] for c in range(folds)], axis=0
            )
        out_ref[p] = share.astype(out_ref.dtype)


def sum_kernel(rest_ref, parts_ref, out_ref):
    total = functools.reduce(
        jnp.add, [parts_ref[b].astype(jnp.float32) for b in range(parts_ref.shape[0])]
    )
    rows = rest_ref.shape[0]
    steps, seqs, _ = out_ref.shape
    folds, lanes = total.shape[0] // rows, total.shape[1]
    for c in range(folds):
        columns = slice(c * lanes, (c + 1) * lanes)
        piece = total[c * rows : (c + 1) * rows] + rest_ref[:, columns]
        for s in range(steps):
            out_ref[s, :, columns] = piece[s * seqs : (s + 1) * seqs].astype(jnp.bfloat16)


def crossed(value, mask):
    pairs = [(source, source ^ mask) for source in range(lax.axis_size("tensor"))]
    return lax.ppermute(value, "tensor", pairs)


def exchanged(value):
    return lax.all_to_all(value, "tensor", split_axis=0, concat_axis=0, tiled=True)


def near_masks():
    masks = [2]
    while 4 * masks[-1] < lax.axis_size("tensor"):
        masks.append(2 * masks[-1])
    return masks


def body(
    layer_input_hidden,
    rmsnorm_gain_weight,
    wq,
    wk,
    wv,
    wo,
    adapter_down_stored,
    adapter_up_query,
    adapter_up_value,
    adapter_block_owner,
    rotated_key_cache,
    cached_value_rows,
    cache_valid_lengths,
):
    f32, bf16 = jnp.float32, jnp.bfloat16
    shape = jax.ShapeDtypeStruct
    steps, seqs, model_width = layer_input_hidden.shape
    peers = lax.axis_size("tensor")
    tensor_index = lax.axis_index("tensor")
    rows = steps * seqs
    local_heads = wq.shape[1] // HEAD_DIM
    held_rows = rows * local_heads
    kv_width = wk.shape[1]
    width = model_width // peers
    group = QUERY_HEADS // KEY_VALUE_HEADS

    pairs = [(0, 1), (1, 0)]
    other_down = lax.ppermute(adapter_down_stored, "replica", pairs)
    other_up_query = lax.ppermute(adapter_up_query, "replica", pairs)
    other_up_value = lax.ppermute(adapter_up_value, "replica", pairs)

    normed, cosine, sine, rest, reach, own_shrunk, features = kernel_call(
        functools.partial(norm_kernel, peers, local_heads),
        (
            shape((rows, model_width), bf16),
            shape((rows, HEAD_DIM), f32),
            shape((rows, HEAD_DIM), f32),
            shape((rows, width), f32),
            shape((8, HEAD_DIM), jnp.int32),
            shape((rows, 2 * ADAPTER_RANK), f32),
            shape((rows, adapter_down_stored.shape[0]), bf16),
        ),
        [far] * 6,
        (vmem,) * 7,
        [
            pltpu.SMEM(cache_valid_lengths.shape, jnp.int32),
            pltpu.SMEM(adapter_block_owner.shape, jnp.int32),
            pltpu.VMEM(layer_input_hidden.shape, bf16),
            pltpu.VMEM(adapter_down_stored.shape, bf16),
            pltpu.VMEM(rmsnorm_gain_weight.shape, bf16),
            pltpu.SemaphoreType.DMA((5,)),
        ],
        limit=8,
    )(
        cache_valid_lengths, adapter_block_owner, layer_input_hidden, adapter_down_stored,
        rmsnorm_gain_weight, wo,
    )
    own_shrunk, other_down, other_up_query, other_up_value = lax.optimization_barrier(
        (own_shrunk, other_down, other_up_query, other_up_value)
    )
    partial, normed, up_query = kernel_call(
        shrink_kernel,
        (
            shape((rows, 2 * ADAPTER_RANK), f32),
            shape((rows, model_width), bf16),
            shape(adapter_up_query.shape, bf16),
        ),
        [vmem] * 5 + [far],
        (vmem,) * 3,
        limit=4,
    )(features, other_down, own_shrunk, normed, adapter_up_query, wo)

    partial = after = partial + crossed(partial, 1)
    far_up_query = crossed(up_query, peers // 2)
    for mask in near_masks():
        partial = partial + crossed(partial, mask)

    key_sum = jnp.dot(normed, wk, preferred_element_type=f32)
    value_sum = jnp.dot(normed, wv, preferred_element_type=f32)
    query_sum = kernel_call(
        query_kernel,
        shape((rows, wq.shape[1]), f32),
        [vmem] * 3,
        vmem,
        limit=4,
        moved=wq.size,
        flops=2 * rows * wq.size,
    )(normed, wq, after)
    other_far_up_query = lax.ppermute(far_up_query, "replica", pairs)

    packed_rows = padded(held_rows, 16) + padded(3 * rows, 16)
    packed = kernel_call(
        pack_kernel,
        shape((packed_rows, HEAD_DIM), bf16),
        [vmem, vmem, far],
        vmem,
        [pltpu.VMEM((packed_rows, HEAD_DIM), f32)],
        limit=4,
    )(query_sum, partial, wq)
    queries, key_raw, value_raw = kernel_call(
        functools.partial(finish_kernel, seqs),
        (
            shape((2, held_rows, HEAD_DIM), bf16),
            shape((rows, kv_width), bf16),
            shape((rows, kv_width), bf16),
        ),
        [vmem] * 13 + [far],
        (vmem,) * 3,
        [
            pltpu.VMEM((2, local_heads, padded(rows, 8), HEAD_DIM), f32),
            pltpu.VMEM((2, held_rows, HEAD_DIM), f32),
        ],
        limit=4,
    )(
        query_sum, partial, crossed(packed, peers // 2), key_sum, value_sum, up_query,
        other_up_query, far_up_query, other_far_up_query, adapter_up_value, other_up_value,
        cosine, sine, wq,
    )

    if kv_width != HEAD_DIM:
        kv_index = tensor_index * local_heads // group

        def own_head(value):
            heads = lax.all_gather(value, "tensor", axis=1, tiled=True)
            return lax.dynamic_slice_in_dim(heads, kv_index * HEAD_DIM, HEAD_DIM, 1)

        key_raw, value_raw = own_head(key_raw), own_head(value_raw)

    fresh, fresh_level = kernel_call(
        functools.partial(fresh_kernel, seqs),
        (shape((held_rows, HEAD_DIM), f32), shape((8, HEAD_DIM), f32)),
        [vmem] * 5,
        (vmem, vmem),
        limit=4,
    )(queries, key_raw, value_raw, cosine, sine)
    held, masks = queries, [0, peers // 2]
    for mask in near_masks()[:0:-1]:
        held = jnp.concatenate([held, crossed(held, mask)])
        masks = masks + [mask ^ other for other in masks]
    others = [crossed(held, m) for m in (1, 2, 3)]

    span = rotated_key_cache.shape[2]
    blocks_shape = shape((peers, padded(held_rows, 16) + 16, HEAD_DIM), bf16)
    buffers = [pltpu.VMEM((3, span, HEAD_DIM), f32), pltpu.VMEM((3, HEAD_DIM, span), f32)]

    def cache_part(its_masks, taken, *operands):
        return kernel_call(
            functools.partial(cache_kernel, its_masks, taken),
            blocks_shape,
            [vmem] * 3 + [far] + [vmem] * (1 + len(operands)),
            vmem,
            buffers,
            limit=6,
        )(reach, rotated_key_cache, cached_value_rows, wq, fresh_level, *operands)

    near_blocks = cache_part(masks, [], held)
    other_masks = [mask ^ m for m in (1, 2, 3) for mask in masks]
    blocks = cache_part(other_masks, masks, near_blocks, *others)

    folds = width // 256 if (rows * (width // 256)) % 16 == 0 else 1
    shares = kernel_call(
        functools.partial(merge_kernel, seqs),
        shape((peers, rows * folds, width // folds), bf16),
        [vmem] * 4,
        vmem,
        [pltpu.VMEM((local_heads, padded(rows, 8), HEAD_DIM), f32)],
        limit=6,
    )(exchanged(blocks), fresh, fresh_level, wo)
    return kernel_call(
        sum_kernel,
        shape((steps, seqs, width), bf16),
        [vmem] * 2,
        vmem,
        limit=4,
    )(rest, exchanged(shares))


def solution(mesh):
    return jax.shard_map(
        body,
        mesh=mesh,
        in_specs=(
            P(None, ("groups", "replica"), None),
            P(),
            P(None, "tensor"),
            P(None, "tensor"),
            P(None, "tensor"),
            P("tensor", None),
            P(("replica", "tensor"), None),
            P("replica", "tensor"),
            P("replica", "tensor"),
            P(),
            P(("groups", "replica"), None, "tensor", None),
            P(("groups", "replica"), None, "tensor", None),
            P(("groups", "replica")),
        ),
        out_specs=P(None, ("groups", "replica"), "tensor"),
        check_vma=False,
    )
```

```python
import functools
import math

import jax
import jax.numpy as jnp
from jax import lax
from jax.experimental import pallas as pl
from jax.experimental.pallas import tpu as pltpu
from jax.sharding import PartitionSpec as P

QUERY_HEADS = 64
KEY_VALUE_HEADS = 8
HEAD_DIM = 128
ADAPTER_RANK = 64


adapter_scale = 2.0
rope_base = 500000.0
negative = -1e30
inv_root = 1.0 / math.sqrt(HEAD_DIM)
MIB = 1 << 20

vmem = pl.BlockSpec(memory_space=pltpu.VMEM)
smem = pl.BlockSpec(memory_space=pltpu.SMEM)
far = pl.BlockSpec(memory_space=pl.ANY)


def padded(count, multiple):
    return -(-count // multiple) * multiple


def rows_padded(value, rows):
    if value.shape[0] == rows:
        return value
    filler = jnp.zeros((rows - value.shape[0],) + value.shape[1:], value.dtype)
    return jnp.concatenate([value, filler], axis=0)


def kernel_call(kernel, outs, specs, out_specs, scratch=(), limit=16, moved=0, flops=0):
    call = pl.pallas_call(
        kernel,
        out_shape=outs,
        in_specs=specs,
        out_specs=out_specs,
        scratch_shapes=list(scratch),
        compiler_params=pltpu.CompilerParams(vmem_limit_bytes=limit * MIB),
        cost_estimate=pl.CostEstimate(flops=flops, bytes_accessed=moved, transcendentals=0),
    )

    def run(*operands):
        return call(
            *[
                pltpu.with_memory_space_constraint(operand, pltpu.HBM) if spec is far else operand
                for operand, spec in zip(operands, specs)
            ]
        )

    return run


def fetches(pairs, sem):
    copies = [
        pltpu.make_async_copy(far_ref, near, sem.at[k]) for k, (far_ref, near) in enumerate(pairs)
    ]
    for copy in copies:
        copy.start()
    return copies


def features_of(normed_ref, owner_ref, held, block_rows):
    place = jnp.int32(0)
    for j in range(owner_ref.shape[0]):
        place = jnp.where(owner_ref[j] == held, jnp.int32(j), place)
    return normed_ref[:, pl.ds(pl.multiple_of(place * block_rows, block_rows), block_rows)]


def norm_kernel(
    peers, heads, lengths_ref, owner_ref, x_ref, down_ref, gain_ref, beside_ref,
    normed_ref, cos_ref, sin_ref, rest_ref, reach_ref, shrunk_ref, features_ref,
    lengths, owner, x_buf, down_buf, gain, sem,
):
    copies = fetches(
        [
            (lengths_ref, lengths),
            (owner_ref, owner),
            (x_ref, x_buf),
            (down_ref, down_buf),
            (gain_ref, gain),
        ],
        sem,
    )
    steps, seqs, _ = x_ref.shape
    rows, width = rest_ref.shape
    half = HEAD_DIM // 2
    row = lax.broadcasted_iota(jnp.int32, (rows, HEAD_DIM), 0)
    lane = lax.broadcasted_iota(jnp.int32, (rows, HEAD_DIM), 1)
    copies[0].wait()
    positions = jnp.zeros((rows, HEAD_DIM), jnp.int32)
    for s in range(steps):
        for n in range(seqs):
            positions = jnp.where(row == s * seqs + n, lengths[n] + s, positions)
    low = lane < half
    exponent = jnp.where(low, lane, lane - half).astype(jnp.float32) * (2.0 / HEAD_DIM)
    angles = positions.astype(jnp.float32) * jnp.exp(exponent * -math.log(rope_base))
    sine = jnp.sin(angles)
    cos_ref[...] = jnp.cos(angles)
    sin_ref[...] = jnp.where(low, -sine, sine)
    place = lax.broadcasted_iota(jnp.int32, reach_ref.shape, 1)
    reach = jnp.zeros(reach_ref.shape, jnp.int32)
    per_seq = heads * steps
    for n in range(seqs):
        mine = jnp.logical_and(place >= n * per_seq, place < (n + 1) * per_seq)
        reach = jnp.where(mine, lengths[n], reach)
    reach_ref[...] = reach
    copies[2].wait()
    values = jnp.concatenate([x_buf[s].astype(jnp.float32) for s in range(steps)], axis=0)
    factor = lax.rsqrt(jnp.mean(values * values, axis=-1, keepdims=True) + 1e-05)
    copies[4].wait()
    normed = values * factor * gain[...].astype(jnp.float32).reshape(1, -1)
    normed_ref[...] = normed.astype(jnp.bfloat16)
    replica, tensor = lax.axis_index("replica"), lax.axis_index("tensor")
    for s in range(steps):
        part = x_buf[s, :, pl.ds(pl.multiple_of(tensor * width, width), width)]
        rest_ref[s * seqs : (s + 1) * seqs, :] = part.astype(jnp.float32)
    copies[1].wait()
    copies[3].wait()
    block_rows = down_ref.shape[0]
    features_ref[...] = features_of(
        normed_ref, owner, (1 - replica) * peers + tensor, block_rows
    )
    shrunk_ref[...] = jnp.dot(
        features_of(normed_ref, owner, replica * peers + tensor, block_rows),
        down_buf[...],
        preferred_element_type=jnp.float32,
    )


def shrink_kernel(
    features_ref, other_ref, own_ref, normed_ref, up_ref, beside_ref, out_ref, normed_out, up_out
):
    normed_out[...] = normed_ref[...]
    up_out[...] = up_ref[...]
    out_ref[...] = own_ref[...] + jnp.dot(
        features_ref[...], other_ref[...], preferred_element_type=jnp.float32
    )


def query_kernel(normed_ref, wq_ref, after_ref, out_ref):
    out_ref[...] = jnp.dot(normed_ref[...], wq_ref[...], preferred_element_type=jnp.float32)


def rotated(values, cosine, sine):
    half = HEAD_DIM // 2
    turned = jnp.concatenate([values[:, half:], values[:, :half]], axis=1)
    return values * cosine + turned * sine


def pack_kernel(acc_ref, partial_ref, beside_ref, out_ref, tall):
    rows = acc_ref.shape[0]
    heads = acc_ref.shape[1] // HEAD_DIM
    for h in range(heads):
        tall[h * rows : (h + 1) * rows, :] = acc_ref[:, h * HEAD_DIM : (h + 1) * HEAD_DIM]
    held_rows = padded(heads * rows, 16)
    if held_rows > heads * rows:
        tall[heads * rows : held_rows, :] = jnp.zeros(
            (held_rows - heads * rows, HEAD_DIM), jnp.float32
        )
    left = partial_ref[...]
    for c in range(3):
        piece = left.astype(jnp.bfloat16).astype(jnp.float32)
        left = left - piece
        tall[held_rows + c * rows : held_rows + (c + 1) * rows, :] = piece
    end = held_rows + 3 * rows
    if out_ref.shape[0] > end:
        tall[end:, :] = jnp.zeros((out_ref.shape[0] - end, HEAD_DIM), jnp.float32)
    out_ref[...] = tall[...].astype(jnp.bfloat16)


def finish_kernel(
    seq_count, acc_ref, partial_ref, met_ref, key_ref, value_ref, uq_own, uq_other, far_own,
    far_other, uv_own, uv_other, cos_ref, sin_ref, beside_ref,
    query_ref, keyout_ref, valueout_ref, wide, tall,
):
    first = lax.axis_index("replica") == 0
    rows = acc_ref.shape[0]
    steps = rows // seq_count
    heads = acc_ref.shape[1] // HEAD_DIM
    held_rows = padded(heads * rows, 16)
    met = met_ref[...].astype(jnp.float32)
    pieces = [met[held_rows + c * rows : held_rows + (c + 1) * rows] for c in range(3)]
    shrunk = partial_ref[...] + (pieces[0] + (pieces[1] + pieces[2]))
    shrunk = shrunk.astype(jnp.bfloat16).astype(jnp.float32)
    half = ADAPTER_RANK // 2

    def lifted(low, high, own, other):
        mine = jnp.where(first, low, high).astype(jnp.bfloat16)
        theirs = jnp.where(first, high, low).astype(jnp.bfloat16)
        return adapter_scale * (
            jnp.dot(mine, own[...], preferred_element_type=jnp.float32)
            + jnp.dot(theirs, other[...], preferred_element_type=jnp.float32)
        )

    low, high = shrunk[:, :half], shrunk[:, half : 2 * half]
    cosine, sine = cos_ref[...], sin_ref[...]
    for e, (own, other) in enumerate(((uq_own, uq_other), (far_own, far_other))):
        lora = lifted(low, high, own, other)
        for h in range(heads):
            columns = slice(h * HEAD_DIM, (h + 1) * HEAD_DIM)
            base = acc_ref[:, columns] if e == 0 else met[h * rows : (h + 1) * rows]
            raw = (base + lora[:, columns]).astype(jnp.bfloat16).astype(jnp.float32)
            wide[e, h, 0:rows, :] = rotated(raw, cosine, sine)
        for n in range(seq_count):
            for h in range(heads):
                tall[e, pl.ds((n * heads + h) * steps, steps), :] = wide[
                    e, h, pl.ds(n, steps, stride=seq_count), :
                ]
        query_ref[e] = tall[e].astype(jnp.bfloat16)
    keyout_ref[...] = key_ref[...].astype(jnp.bfloat16)
    value = value_ref[...] + lifted(
        shrunk[:, 2 * half : 3 * half], shrunk[:, 3 * half :], uv_own, uv_other
    )
    valueout_ref[...] = value.astype(jnp.bfloat16)


def fresh_kernel(
    seq_count, query_ref, key_ref, value_ref, cos_ref, sin_ref, fresh_ref, level_ref
):
    lane = lax.broadcasted_iota(jnp.int32, (1, HEAD_DIM), 1)
    columns = []
    steps = key_ref.shape[0] // seq_count
    per_seq = fresh_ref.shape[0] // seq_count
    queries = query_ref[0].astype(jnp.float32)
    keys = rotated(key_ref[...].astype(jnp.float32), cos_ref[...], sin_ref[...])
    keys = keys.astype(jnp.bfloat16).astype(jnp.float32)
    values = value_ref[...].astype(jnp.float32)
    step = lax.rem(lax.broadcasted_iota(jnp.int32, (per_seq, 1), 0), steps)
    for n in range(seq_count):
        rows = slice(n * per_seq, (n + 1) * per_seq)
        query = queries[rows]
        scores = []
        for t in range(steps):
            place = t * seq_count + n
            score = jnp.sum(query * keys[place : place + 1], axis=-1, keepdims=True) * inv_root
            scores.append(jnp.where(step >= t, score, negative))
        top = functools.reduce(jnp.maximum, scores)
        weights = [
            jnp.where(step >= t, jnp.exp(score - top), 0.0) for t, score in enumerate(scores)
        ]
        total = functools.reduce(jnp.add, weights)
        summed = jnp.zeros((per_seq, HEAD_DIM), jnp.float32)
        for t, weight in enumerate(weights):
            place = t * seq_count + n
            summed = summed + weight.astype(jnp.bfloat16).astype(jnp.float32) * values[
                place : place + 1
            ]
        fresh_ref[rows, :] = summed
        columns.append(jnp.where(lane == 0, top, jnp.where(lane == 1, total, 0.0)))
    columns = rows_padded(jnp.concatenate(columns, axis=0), HEAD_DIM)
    level_ref[...] = jnp.transpose(columns)[0 : level_ref.shape[0], :]


def pieces_of(top, total):
    rows = lax.broadcasted_iota(jnp.int32, (16, HEAD_DIM), 0)
    packed = jnp.zeros((16, HEAD_DIM), jnp.float32)
    for first, left in ((0, top), (3, total)):
        for c in range(3):
            piece = left.astype(jnp.bfloat16).astype(jnp.float32)
            left = left - piece
            packed = jnp.where(rows == first + c, piece, packed)
    return packed.astype(jnp.bfloat16)


def top_and_total(part_ref, held_rows):
    pieces = part_ref[padded(held_rows, 16) :, :].astype(jnp.float32)
    return (
        pieces[0:1] + (pieces[1:2] + pieces[2:3]),
        pieces[3:4] + (pieces[4:5] + pieces[5:6]),
    )


def turned_rows(rows):
    count = padded(len(rows), 8)
    place = lax.broadcasted_iota(jnp.int32, (count, HEAD_DIM), 0)
    stacked = jnp.zeros((count, HEAD_DIM), jnp.float32)
    for k, row in enumerate(rows):
        stacked = jnp.where(place == k, row, stacked)
    return jnp.transpose(rows_padded(stacked, HEAD_DIM))


def cache_kernel(
    masks, taken, reach_ref, kc_ref, vc_ref, beside_ref, after_ref, *refs
):
    *refs, out_ref, scores_buf, weights_buf = refs
    earlier, query_refs = (refs[:1], refs[1:]) if taken else ([], refs)
    entries, peers = len(masks), out_ref.shape[0]
    each, held_rows, _ = query_refs[0].shape
    seq_count, kv_heads, span, _ = kc_ref.shape
    per_seq = held_rows // seq_count
    mean_rows = padded(held_rows, 16)
    tensor = lax.axis_index("tensor")
    spots = tensor * span + lax.broadcasted_iota(jnp.int32, (span, HEAD_DIM), 0)
    live = spots < reach_ref[0:1, :]
    lane = lax.broadcasted_iota(jnp.int32, (span, HEAD_DIM), 1)
    owners = [lax.bitwise_xor(tensor, mask) for mask in masks]
    heads = [owner * kv_heads // peers for owner in owners]
    for blocks in earlier:
        for mask in taken:
            place = lax.bitwise_xor(tensor, mask)
            out_ref[place] = blocks[place]
    batch = scores_buf.shape[0]
    for lead in range(0, entries, batch):
        part = range(lead, min(lead + batch, entries))
        turned = [
            jnp.transpose(
                rows_padded(query_refs[e // each][e % each].astype(jnp.float32), HEAD_DIM)
            ).astype(jnp.bfloat16)
            for e in part
        ]
        for k, e in enumerate(part):
            scores = None
            for n in range(seq_count):
                score = jnp.dot(
                    kc_ref[n, heads[e]], turned[k], preferred_element_type=jnp.float32
                )
                scores = score if n == 0 else jnp.where(lane < n * per_seq, scores, score)
            scores_buf[k] = jnp.where(live, scores, negative)
        tops = [
            jnp.maximum(jnp.max(scores_buf[k], axis=0, keepdims=True), 0.1 * negative)
            for k in range(len(part))
        ]
        for k, e in enumerate(part):
            weights = jnp.exp((scores_buf[k] - tops[k]) * inv_root)
            total = jnp.sum(weights, axis=0, keepdims=True)
            out_ref[owners[e], mean_rows:, :] = pieces_of(tops[k] * inv_root, total)
            weights_buf[k] = jnp.transpose(weights)
        for k, e in enumerate(part):
            sums = [
                jnp.dot(
                    weights_buf[k, n * per_seq : (n + 1) * per_seq, :].astype(jnp.bfloat16),
                    vc_ref[n, heads[e]],
                    preferred_element_type=jnp.float32,
                )
                for n in range(seq_count)
            ]
            sums = rows_padded(jnp.concatenate(sums, axis=0), mean_rows)
            out_ref[owners[e], 0:mean_rows, :] = sums.astype(jnp.bfloat16)


def merge_kernel(seq_count, blocks_ref, fresh_ref, level_ref, wo_ref, out_ref, wide):
    peers, folded, lanes = out_ref.shape
    heads = wide.shape[0]
    held_rows = fresh_ref.shape[0]
    rows = held_rows // heads
    steps = rows // seq_count
    folds = folded // rows
    per_seq = heads * steps
    mean_rows = padded(held_rows, 16)
    stats = [top_and_total(blocks_ref.at[b], held_rows) for b in range(peers)]
    stats.append((level_ref[0:1, :], level_ref[1:2, :]))
    top = functools.reduce(jnp.maximum, [stat[0] for stat in stats])
    factors = [jnp.exp(stat[0] - top) for stat in stats]
    total = functools.reduce(jnp.add, [factor * stat[1] for factor, stat in zip(factors, stats)])
    total = jnp.where(total > 0.0, total, 1.0)
    columns = turned_rows([factor / total for factor in factors])
    mixed = fresh_ref[...] * columns[0:held_rows, peers : peers + 1]
    for b in range(peers):
        mixed = mixed + (
            blocks_ref[b, 0:mean_rows, :].astype(jnp.float32)[0:held_rows]
            * columns[0:held_rows, b : b + 1]
        )
    for n in range(seq_count):
        for h in range(heads):
            first = n * per_seq + h * steps
            wide[h, pl.ds(n, steps, stride=seq_count), :] = mixed[first : first + steps]
    attention = jnp.concatenate([wide[h, 0:rows, :] for h in range(heads)], axis=1)
    attention = attention.astype(jnp.bfloat16)
    width = folds * lanes
    for p in range(peers):
        share = jnp.dot(
            attention,
            wo_ref[:, p * width : (p + 1) * width],
            preferred_element_type=jnp.float32,
        )
        if folds > 1:
            share = jnp.concatenate(
                [share[:, c * lanes : (c + 1) * lanes] for c in range(folds)], axis=0
            )
        out_ref[p] = share.astype(out_ref.dtype)


def sum_kernel(rest_ref, parts_ref, out_ref):
    total = functools.reduce(
        jnp.add, [parts_ref[b].astype(jnp.float32) for b in range(parts_ref.shape[0])]
    )
    rows = rest_ref.shape[0]
    steps, seqs, _ = out_ref.shape
    folds, lanes = total.shape[0] // rows, total.shape[1]
    for c in range(folds):
        columns = slice(c * lanes, (c + 1) * lanes)
        piece = total[c * rows : (c + 1) * rows] + rest_ref[:, columns]
        for s in range(steps):
            out_ref[s, :, columns] = piece[s * seqs : (s + 1) * seqs].astype(jnp.bfloat16)


def crossed(value, mask):
    pairs = [(source, source ^ mask) for source in range(lax.axis_size("tensor"))]
    return lax.ppermute(value, "tensor", pairs)


def exchanged(value):
    return lax.all_to_all(value, "tensor", split_axis=0, concat_axis=0, tiled=True)


def near_masks():
    masks = [2]
    while 4 * masks[-1] < lax.axis_size("tensor"):
        masks.append(2 * masks[-1])
    return masks


def body(
    layer_input_hidden,
    rmsnorm_gain_weight,
    wq,
    wk,
    wv,
    wo,
    adapter_down_stored,
    adapter_up_query,
    adapter_up_value,
    adapter_block_owner,
    rotated_key_cache,
    cached_value_rows,
    cache_valid_lengths,
):
    f32, bf16 = jnp.float32, jnp.bfloat16
    shape = jax.ShapeDtypeStruct
    steps, seqs, model_width = layer_input_hidden.shape
    peers = lax.axis_size("tensor")
    tensor_index = lax.axis_index("tensor")
    rows = steps * seqs
    local_heads = wq.shape[1] // HEAD_DIM
    held_rows = rows * local_heads
    kv_width = wk.shape[1]
    width = model_width // peers
    group = QUERY_HEADS // KEY_VALUE_HEADS

    pairs = [(0, 1), (1, 0)]
    other_down = lax.ppermute(adapter_down_stored, "replica", pairs)
    other_up_query = lax.ppermute(adapter_up_query, "replica", pairs)
    other_up_value = lax.ppermute(adapter_up_value, "replica", pairs)

    normed, cosine, sine, rest, reach, own_shrunk, features = kernel_call(
        functools.partial(norm_kernel, peers, local_heads),
        (
            shape((rows, model_width), bf16),
            shape((rows, HEAD_DIM), f32),
            shape((rows, HEAD_DIM), f32),
            shape((rows, width), f32),
            shape((8, HEAD_DIM), jnp.int32),
            shape((rows, 2 * ADAPTER_RANK), f32),
            shape((rows, adapter_down_stored.shape[0]), bf16),
        ),
        [far] * 6,
        (vmem,) * 7,
        [
            pltpu.SMEM(cache_valid_lengths.shape, jnp.int32),
            pltpu.SMEM(adapter_block_owner.shape, jnp.int32),
            pltpu.VMEM(layer_input_hidden.shape, bf16),
            pltpu.VMEM(adapter_down_stored.shape, bf16),
            pltpu.VMEM(rmsnorm_gain_weight.shape, bf16),
            pltpu.SemaphoreType.DMA((5,)),
        ],
        limit=8,
    )(
        cache_valid_lengths, adapter_block_owner, layer_input_hidden, adapter_down_stored,
        rmsnorm_gain_weight, wo,
    )
    own_shrunk, other_down, other_up_query, other_up_value = lax.optimization_barrier(
        (own_shrunk, other_down, other_up_query, other_up_value)
    )
    partial, normed, up_query = kernel_call(
        shrink_kernel,
        (
            shape((rows, 2 * ADAPTER_RANK), f32),
            shape((rows, model_width), bf16),
            shape(adapter_up_query.shape, bf16),
        ),
        [vmem] * 5 + [far],
        (vmem,) * 3,
        limit=4,
    )(features, other_down, own_shrunk, normed, adapter_up_query, wo)

    partial = after = partial + crossed(partial, 1)
    far_up_query = crossed(up_query, peers // 2)
    for mask in near_masks():
        partial = partial + crossed(partial, mask)

    key_sum = jnp.dot(normed, wk, preferred_element_type=f32)
    value_sum = jnp.dot(normed, wv, preferred_element_type=f32)
    query_sum = kernel_call(
        query_kernel,
        shape((rows, wq.shape[1]), f32),
        [vmem] * 3,
        vmem,
        limit=4,
        moved=wq.size,
        flops=2 * rows * wq.size,
    )(normed, wq, after)
    other_far_up_query = lax.ppermute(far_up_query, "replica", pairs)

    packed_rows = padded(held_rows, 16) + padded(3 * rows, 16)
    packed = kernel_call(
        pack_kernel,
        shape((packed_rows, HEAD_DIM), bf16),
        [vmem, vmem, far],
        vmem,
        [pltpu.VMEM((packed_rows, HEAD_DIM), f32)],
        limit=4,
    )(query_sum, partial, wq)
    queries, key_raw, value_raw = kernel_call(
        functools.partial(finish_kernel, seqs),
        (
            shape((2, held_rows, HEAD_DIM), bf16),
            shape((rows, kv_width), bf16),
            shape((rows, kv_width), bf16),
        ),
        [vmem] * 13 + [far],
        (vmem,) * 3,
        [
            pltpu.VMEM((2, local_heads, padded(rows, 8), HEAD_DIM), f32),
            pltpu.VMEM((2, held_rows, HEAD_DIM), f32),
        ],
        limit=4,
    )(
        query_sum, partial, crossed(packed, peers // 2), key_sum, value_sum, up_query,
        other_up_query, far_up_query, other_far_up_query, adapter_up_value, other_up_value,
        cosine, sine, wq,
    )

    if kv_width != HEAD_DIM:
        kv_index = tensor_index * local_heads // group

        def own_head(value):
            heads = lax.all_gather(value, "tensor", axis=1, tiled=True)
            return lax.dynamic_slice_in_dim(heads, kv_index * HEAD_DIM, HEAD_DIM, 1)

        key_raw, value_raw = own_head(key_raw), own_head(value_raw)

    fresh, fresh_level = kernel_call(
        functools.partial(fresh_kernel, seqs),
        (shape((held_rows, HEAD_DIM), f32), shape((8, HEAD_DIM), f32)),
        [vmem] * 5,
        (vmem, vmem),
        limit=4,
    )(queries, key_raw, value_raw, cosine, sine)
    held, masks = queries, [0, peers // 2]
    for mask in near_masks()[:0:-1]:
        held = jnp.concatenate([held, crossed(held, mask)])
        masks = masks + [mask ^ other for other in masks]
    others = {m: crossed(held, m) for m in (1, 2, 3)}

    span = rotated_key_cache.shape[2]
    blocks_shape = shape((peers, padded(held_rows, 16) + 16, HEAD_DIM), bf16)
    buffers = [pltpu.VMEM((4, span, HEAD_DIM), f32), pltpu.VMEM((4, HEAD_DIM, span), f32)]

    def cache_part(its_masks, taken, *operands):
        return kernel_call(
            functools.partial(cache_kernel, its_masks, taken),
            blocks_shape,
            [vmem] * 3 + [far] + [vmem] * (1 + len(operands)),
            vmem,
            buffers,
            limit=6,
        )(reach, rotated_key_cache, cached_value_rows, wq, fresh_level, *operands)

    blocks, taken = cache_part(masks, [], held), masks
    for met in ((2, 3), (1,)):
        its_masks = [mask ^ m for m in met for mask in masks]
        blocks = cache_part(its_masks, taken, blocks, *[others[m] for m in met])
        taken = taken + its_masks

    folds = width // 256 if (rows * (width // 256)) % 16 == 0 else 1
    shares = kernel_call(
        functools.partial(merge_kernel, seqs),
        shape((peers, rows * folds, width // folds), bf16),
        [vmem] * 4,
        vmem,
        [pltpu.VMEM((local_heads, padded(rows, 8), HEAD_DIM), f32)],
        limit=6,
    )(exchanged(blocks), fresh, fresh_level, wo)
    return kernel_call(
        sum_kernel,
        shape((steps, seqs, width), bf16),
        [vmem] * 2,
        vmem,
        limit=4,
    )(rest, exchanged(shares))


def solution(mesh):
    return jax.shard_map(
        body,
        mesh=mesh,
        in_specs=(
            P(None, ("groups", "replica"), None),
            P(),
            P(None, "tensor"),
            P(None, "tensor"),
            P(None, "tensor"),
            P("tensor", None),
            P(("replica", "tensor"), None),
            P("replica", "tensor"),
            P("replica", "tensor"),
            P(),
            P(("groups", "replica"), None, "tensor", None),
            P(("groups", "replica"), None, "tensor", None),
            P(("groups", "replica")),
        ),
        out_specs=P(None, ("groups", "replica"), "tensor"),
        check_vma=False,
    )
```

```python
import functools
import math

import jax
import jax.numpy as jnp
from jax import lax
from jax.experimental import pallas as pl
from jax.experimental.pallas import tpu as pltpu
from jax.sharding import PartitionSpec as P

QUERY_HEADS = 64
KEY_VALUE_HEADS = 8
HEAD_DIM = 128
ADAPTER_RANK = 64


adapter_scale = 2.0
rope_base = 500000.0
negative = -1e30
inv_root = 1.0 / math.sqrt(HEAD_DIM)
MIB = 1 << 20

vmem = pl.BlockSpec(memory_space=pltpu.VMEM)
smem = pl.BlockSpec(memory_space=pltpu.SMEM)
far = pl.BlockSpec(memory_space=pl.ANY)


def padded(count, multiple):
    return -(-count // multiple) * multiple


def rows_padded(value, rows):
    if value.shape[0] == rows:
        return value
    filler = jnp.zeros((rows - value.shape[0],) + value.shape[1:], value.dtype)
    return jnp.concatenate([value, filler], axis=0)


def kernel_call(kernel, outs, specs, out_specs, scratch=(), limit=16, moved=0, flops=0):
    call = pl.pallas_call(
        kernel,
        out_shape=outs,
        in_specs=specs,
        out_specs=out_specs,
        scratch_shapes=list(scratch),
        compiler_params=pltpu.CompilerParams(vmem_limit_bytes=limit * MIB),
        cost_estimate=pl.CostEstimate(flops=flops, bytes_accessed=moved, transcendentals=0),
    )

    def run(*operands):
        return call(
            *[
                pltpu.with_memory_space_constraint(operand, pltpu.HBM) if spec is far else operand
                for operand, spec in zip(operands, specs)
            ]
        )

    return run


def fetches(pairs, sem):
    copies = [
        pltpu.make_async_copy(far_ref, near, sem.at[k]) for k, (far_ref, near) in enumerate(pairs)
    ]
    for copy in copies:
        copy.start()
    return copies


def features_of(normed_ref, owner_ref, held, block_rows):
    place = jnp.int32(0)
    for j in range(owner_ref.shape[0]):
        place = jnp.where(owner_ref[j] == held, jnp.int32(j), place)
    return normed_ref[:, pl.ds(pl.multiple_of(place * block_rows, block_rows), block_rows)]


def norm_kernel(
    peers, heads, lengths_ref, owner_ref, x_ref, down_ref, gain_ref, beside_ref,
    normed_ref, cos_ref, sin_ref, rest_ref, reach_ref, shrunk_ref, features_ref,
    lengths, owner, x_buf, down_buf, gain, sem,
):
    copies = fetches(
        [
            (lengths_ref, lengths),
            (owner_ref, owner),
            (x_ref, x_buf),
            (down_ref, down_buf),
            (gain_ref, gain),
        ],
        sem,
    )
    steps, seqs, _ = x_ref.shape
    rows, width = rest_ref.shape
    half = HEAD_DIM // 2
    row = lax.broadcasted_iota(jnp.int32, (rows, HEAD_DIM), 0)
    lane = lax.broadcasted_iota(jnp.int32, (rows, HEAD_DIM), 1)
    copies[0].wait()
    positions = jnp.zeros((rows, HEAD_DIM), jnp.int32)
    for s in range(steps):
        for n in range(seqs):
            positions = jnp.where(row == s * seqs + n, lengths[n] + s, positions)
    low = lane < half
    exponent = jnp.where(low, lane, lane - half).astype(jnp.float32) * (2.0 / HEAD_DIM)
    angles = positions.astype(jnp.float32) * jnp.exp(exponent * -math.log(rope_base))
    sine = jnp.sin(angles)
    cos_ref[...] = jnp.cos(angles)
    sin_ref[...] = jnp.where(low, -sine, sine)
    place = lax.broadcasted_iota(jnp.int32, reach_ref.shape, 1)
    reach = jnp.zeros(reach_ref.shape, jnp.int32)
    per_seq = heads * steps
    for n in range(seqs):
        mine = jnp.logical_and(place >= n * per_seq, place < (n + 1) * per_seq)
        reach = jnp.where(mine, lengths[n], reach)
    reach_ref[...] = reach
    copies[2].wait()
    values = jnp.concatenate([x_buf[s].astype(jnp.float32) for s in range(steps)], axis=0)
    factor = lax.rsqrt(jnp.mean(values * values, axis=-1, keepdims=True) + 1e-05)
    copies[4].wait()
    normed = values * factor * gain[...].astype(jnp.float32).reshape(1, -1)
    normed_ref[...] = normed.astype(jnp.bfloat16)
    replica, tensor = lax.axis_index("replica"), lax.axis_index("tensor")
    columns = pl.ds(pl.multiple_of(tensor * width, width), width)
    rest = [x_buf[s, :, columns].astype(jnp.float32) for s in range(steps)]
    rest_ref[...] = jnp.concatenate(rest, axis=0)
    copies[1].wait()
    copies[3].wait()
    block_rows = down_ref.shape[0]
    features_ref[...] = features_of(
        normed_ref, owner, (1 - replica) * peers + tensor, block_rows
    )
    shrunk_ref[...] = jnp.dot(
        features_of(normed_ref, owner, replica * peers + tensor, block_rows),
        down_buf[...],
        preferred_element_type=jnp.float32,
    )


def shrink_kernel(
    features_ref, other_ref, own_ref, normed_ref, up_ref, beside_ref, out_ref, normed_out, up_out
):
    normed_out[...] = normed_ref[...]
    up_out[...] = up_ref[...]
    out_ref[...] = own_ref[...] + jnp.dot(
        features_ref[...], other_ref[...], preferred_element_type=jnp.float32
    )


def query_kernel(normed_ref, wq_ref, after_ref, out_ref):
    out_ref[...] = jnp.dot(normed_ref[...], wq_ref[...], preferred_element_type=jnp.float32)


def rotated(values, cosine, sine):
    half = HEAD_DIM // 2
    turned = jnp.concatenate([values[:, half:], values[:, :half]], axis=1)
    return values * cosine + turned * sine


def pack_kernel(acc_ref, partial_ref, beside_ref, out_ref, tall):
    rows = acc_ref.shape[0]
    heads = acc_ref.shape[1] // HEAD_DIM
    for h in range(heads):
        tall[h * rows : (h + 1) * rows, :] = acc_ref[:, h * HEAD_DIM : (h + 1) * HEAD_DIM]
    held_rows = padded(heads * rows, 16)
    if held_rows > heads * rows:
        tall[heads * rows : held_rows, :] = jnp.zeros(
            (held_rows - heads * rows, HEAD_DIM), jnp.float32
        )
    left = partial_ref[...]
    for c in range(3):
        piece = left.astype(jnp.bfloat16).astype(jnp.float32)
        left = left - piece
        tall[held_rows + c * rows : held_rows + (c + 1) * rows, :] = piece
    end = held_rows + 3 * rows
    if out_ref.shape[0] > end:
        tall[end:, :] = jnp.zeros((out_ref.shape[0] - end, HEAD_DIM), jnp.float32)
    out_ref[...] = tall[...].astype(jnp.bfloat16)


def finish_kernel(
    seq_count, acc_ref, partial_ref, met_ref, key_ref, value_ref, uq_own, uq_other, far_own,
    far_other, uv_own, uv_other, cos_ref, sin_ref, beside_ref,
    query_ref, keyout_ref, valueout_ref, wide, tall,
):
    first = lax.axis_index("replica") == 0
    rows = acc_ref.shape[0]
    steps = rows // seq_count
    heads = acc_ref.shape[1] // HEAD_DIM
    held_rows = padded(heads * rows, 16)
    met = met_ref[...].astype(jnp.float32)
    pieces = [met[held_rows + c * rows : held_rows + (c + 1) * rows] for c in range(3)]
    shrunk = partial_ref[...] + (pieces[0] + (pieces[1] + pieces[2]))
    shrunk = shrunk.astype(jnp.bfloat16).astype(jnp.float32)
    half = ADAPTER_RANK // 2

    def lifted(low, high, own, other):
        mine = jnp.where(first, low, high).astype(jnp.bfloat16)
        theirs = jnp.where(first, high, low).astype(jnp.bfloat16)
        return adapter_scale * (
            jnp.dot(mine, own[...], preferred_element_type=jnp.float32)
            + jnp.dot(theirs, other[...], preferred_element_type=jnp.float32)
        )

    low, high = shrunk[:, :half], shrunk[:, half : 2 * half]
    cosine, sine = cos_ref[...], sin_ref[...]
    for e, (own, other) in enumerate(((uq_own, uq_other), (far_own, far_other))):
        lora = lifted(low, high, own, other)
        for h in range(heads):
            columns = slice(h * HEAD_DIM, (h + 1) * HEAD_DIM)
            base = acc_ref[:, columns] if e == 0 else met[h * rows : (h + 1) * rows]
            raw = (base + lora[:, columns]).astype(jnp.bfloat16).astype(jnp.float32)
            wide[e, h, 0:rows, :] = rotated(raw, cosine, sine)
        for n in range(seq_count):
            for h in range(heads):
                tall[e, pl.ds((n * heads + h) * steps, steps), :] = wide[
                    e, h, pl.ds(n, steps, stride=seq_count), :
                ]
        query_ref[e] = tall[e, 0 : heads * rows, :].astype(jnp.bfloat16)
    keyout_ref[...] = key_ref[...].astype(jnp.bfloat16)
    value = value_ref[...] + lifted(
        shrunk[:, 2 * half : 3 * half], shrunk[:, 3 * half :], uv_own, uv_other
    )
    valueout_ref[...] = value.astype(jnp.bfloat16)


def fresh_kernel(
    seq_count, query_ref, key_ref, value_ref, cos_ref, sin_ref, fresh_ref, level_ref
):
    lane = lax.broadcasted_iota(jnp.int32, (1, HEAD_DIM), 1)
    columns = []
    steps = key_ref.shape[0] // seq_count
    per_seq = fresh_ref.shape[0] // seq_count
    queries = query_ref[0].astype(jnp.float32)
    keys = rotated(key_ref[...].astype(jnp.float32), cos_ref[...], sin_ref[...])
    keys = keys.astype(jnp.bfloat16).astype(jnp.float32)
    values = value_ref[...].astype(jnp.float32)
    step = lax.rem(lax.broadcasted_iota(jnp.int32, (per_seq, 1), 0), steps)
    for n in range(seq_count):
        rows = slice(n * per_seq, (n + 1) * per_seq)
        query = queries[rows]
        scores = []
        for t in range(steps):
            place = t * seq_count + n
            score = jnp.sum(query * keys[place : place + 1], axis=-1, keepdims=True) * inv_root
            scores.append(jnp.where(step >= t, score, negative))
        top = functools.reduce(jnp.maximum, scores)
        weights = [
            jnp.where(step >= t, jnp.exp(score - top), 0.0) for t, score in enumerate(scores)
        ]
        total = functools.reduce(jnp.add, weights)
        summed = jnp.zeros((per_seq, HEAD_DIM), jnp.float32)
        for t, weight in enumerate(weights):
            place = t * seq_count + n
            summed = summed + weight.astype(jnp.bfloat16).astype(jnp.float32) * values[
                place : place + 1
            ]
        fresh_ref[rows, :] = summed
        columns.append(jnp.where(lane == 0, top, jnp.where(lane == 1, total, 0.0)))
    columns = rows_padded(jnp.concatenate(columns, axis=0), HEAD_DIM)
    level_ref[...] = jnp.transpose(columns)[0 : level_ref.shape[0], :]


def pieces_of(top, total):
    rows = lax.broadcasted_iota(jnp.int32, (16, HEAD_DIM), 0)
    packed = jnp.zeros((16, HEAD_DIM), jnp.float32)
    for first, left in ((0, top), (3, total)):
        for c in range(3):
            piece = left.astype(jnp.bfloat16).astype(jnp.float32)
            left = left - piece
            packed = jnp.where(rows == first + c, piece, packed)
    return packed.astype(jnp.bfloat16)


def top_and_total(part_ref, held_rows):
    pieces = part_ref[padded(held_rows, 16) :, :].astype(jnp.float32)
    return (
        pieces[0:1] + (pieces[1:2] + pieces[2:3]),
        pieces[3:4] + (pieces[4:5] + pieces[5:6]),
    )


def turned_rows(rows):
    count = padded(len(rows), 8)
    place = lax.broadcasted_iota(jnp.int32, (count, HEAD_DIM), 0)
    stacked = jnp.zeros((count, HEAD_DIM), jnp.float32)
    for k, row in enumerate(rows):
        stacked = jnp.where(place == k, row, stacked)
    return jnp.transpose(rows_padded(stacked, HEAD_DIM))


def cache_kernel(
    masks, taken, reach_ref, kc_ref, vc_ref, beside_ref, after_ref, *refs
):
    *refs, out_ref, scores_buf, weights_buf = refs
    earlier, query_refs = (refs[:1], refs[1:]) if taken else ([], refs)
    entries, peers = len(masks), out_ref.shape[0]
    each, held_rows, _ = query_refs[0].shape
    seq_count, kv_heads, span, _ = kc_ref.shape
    per_seq = held_rows // seq_count
    mean_rows = padded(held_rows, 16)
    tensor = lax.axis_index("tensor")
    spots = tensor * span + lax.broadcasted_iota(jnp.int32, (span, HEAD_DIM), 0)
    live = spots < reach_ref[0:1, :]
    lane = lax.broadcasted_iota(jnp.int32, (span, HEAD_DIM), 1)
    owners = [lax.bitwise_xor(tensor, mask) for mask in masks]
    heads = [owner * kv_heads // peers for owner in owners]
    for blocks in earlier:
        for mask in taken:
            place = lax.bitwise_xor(tensor, mask)
            out_ref[place] = blocks[place]
    batch = scores_buf.shape[0]
    for lead in range(0, entries, batch):
        part = range(lead, min(lead + batch, entries))
        turned = [
            jnp.transpose(
                rows_padded(query_refs[e // each][e % each].astype(jnp.float32), HEAD_DIM)
            ).astype(jnp.bfloat16)
            for e in part
        ]
        for k, e in enumerate(part):
            scores = None
            for n in range(seq_count):
                score = jnp.dot(
                    kc_ref[n, heads[e]], turned[k], preferred_element_type=jnp.float32
                )
                scores = score if n == 0 else jnp.where(lane < n * per_seq, scores, score)
            scores_buf[k] = jnp.where(live, scores, negative)
        tops = [
            jnp.maximum(jnp.max(scores_buf[k], axis=0, keepdims=True), 0.1 * negative)
            for k in range(len(part))
        ]
        for k, e in enumerate(part):
            weights = jnp.exp((scores_buf[k] - tops[k]) * inv_root)
            total = jnp.sum(weights, axis=0, keepdims=True)
            out_ref[owners[e], mean_rows:, :] = pieces_of(tops[k] * inv_root, total)
            weights_buf[k] = jnp.transpose(weights)
        for k, e in enumerate(part):
            sums = [
                jnp.dot(
                    weights_buf[k, n * per_seq : (n + 1) * per_seq, :].astype(jnp.bfloat16),
                    vc_ref[n, heads[e]],
                    preferred_element_type=jnp.float32,
                )
                for n in range(seq_count)
            ]
            sums = rows_padded(jnp.concatenate(sums, axis=0), mean_rows)
            out_ref[owners[e], 0:mean_rows, :] = sums.astype(jnp.bfloat16)


def merge_kernel(seq_count, blocks_ref, fresh_ref, level_ref, wo_ref, out_ref, wide):
    peers, folded, lanes = out_ref.shape
    heads = wide.shape[0]
    held_rows = fresh_ref.shape[0]
    rows = held_rows // heads
    steps = rows // seq_count
    folds = folded // rows
    per_seq = heads * steps
    mean_rows = padded(held_rows, 16)
    stats = [top_and_total(blocks_ref.at[b], held_rows) for b in range(peers)]
    stats.append((level_ref[0:1, :], level_ref[1:2, :]))
    top = functools.reduce(jnp.maximum, [stat[0] for stat in stats])
    factors = [jnp.exp(stat[0] - top) for stat in stats]
    total = functools.reduce(jnp.add, [factor * stat[1] for factor, stat in zip(factors, stats)])
    total = jnp.where(total > 0.0, total, 1.0)
    columns = turned_rows([factor / total for factor in factors])
    mixed = fresh_ref[...] * columns[0:held_rows, peers : peers + 1]
    for b in range(peers):
        mixed = mixed + (
            blocks_ref[b, 0:mean_rows, :].astype(jnp.float32)[0:held_rows]
            * columns[0:held_rows, b : b + 1]
        )
    for n in range(seq_count):
        for h in range(heads):
            first = n * per_seq + h * steps
            wide[h, pl.ds(n, steps, stride=seq_count), :] = mixed[first : first + steps]
    attention = jnp.concatenate([wide[h, 0:rows, :] for h in range(heads)], axis=1)
    attention = attention.astype(jnp.bfloat16)
    width = folds * lanes
    for p in range(peers):
        share = jnp.dot(
            attention,
            wo_ref[:, p * width : (p + 1) * width],
            preferred_element_type=jnp.float32,
        )
        if folds > 1:
            share = jnp.concatenate(
                [share[:, c * lanes : (c + 1) * lanes] for c in range(folds)], axis=0
            )
        out_ref[p] = share.astype(out_ref.dtype)


def sum_kernel(rest_ref, parts_ref, out_ref):
    total = functools.reduce(
        jnp.add, [parts_ref[b].astype(jnp.float32) for b in range(parts_ref.shape[0])]
    )
    rows = rest_ref.shape[0]
    steps, seqs, _ = out_ref.shape
    folds, lanes = total.shape[0] // rows, total.shape[1]
    for c in range(folds):
        columns = slice(c * lanes, (c + 1) * lanes)
        piece = total[c * rows : (c + 1) * rows] + rest_ref[:, columns]
        for s in range(steps):
            out_ref[s, :, columns] = piece[s * seqs : (s + 1) * seqs].astype(jnp.bfloat16)


def crossed(value, mask):
    pairs = [(source, source ^ mask) for source in range(lax.axis_size("tensor"))]
    return lax.ppermute(value, "tensor", pairs)


def exchanged(value):
    return lax.all_to_all(value, "tensor", split_axis=0, concat_axis=0, tiled=True)


def near_masks():
    masks = [2]
    while 4 * masks[-1] < lax.axis_size("tensor"):
        masks.append(2 * masks[-1])
    return masks


def body(
    layer_input_hidden,
    rmsnorm_gain_weight,
    wq,
    wk,
    wv,
    wo,
    adapter_down_stored,
    adapter_up_query,
    adapter_up_value,
    adapter_block_owner,
    rotated_key_cache,
    cached_value_rows,
    cache_valid_lengths,
):
    f32, bf16 = jnp.float32, jnp.bfloat16
    shape = jax.ShapeDtypeStruct
    steps, seqs, model_width = layer_input_hidden.shape
    peers = lax.axis_size("tensor")
    tensor_index = lax.axis_index("tensor")
    rows = steps * seqs
    local_heads = wq.shape[1] // HEAD_DIM
    held_rows = rows * local_heads
    kv_width = wk.shape[1]
    width = model_width // peers
    group = QUERY_HEADS // KEY_VALUE_HEADS

    pairs = [(0, 1), (1, 0)]
    other_down = lax.ppermute(adapter_down_stored, "replica", pairs)
    other_up_query = lax.ppermute(adapter_up_query, "replica", pairs)
    other_up_value = lax.ppermute(adapter_up_value, "replica", pairs)

    normed, cosine, sine, rest, reach, own_shrunk, features = kernel_call(
        functools.partial(norm_kernel, peers, local_heads),
        (
            shape((rows, model_width), bf16),
            shape((rows, HEAD_DIM), f32),
            shape((rows, HEAD_DIM), f32),
            shape((rows, width), f32),
            shape((8, HEAD_DIM), jnp.int32),
            shape((rows, 2 * ADAPTER_RANK), f32),
            shape((rows, adapter_down_stored.shape[0]), bf16),
        ),
        [far] * 6,
        (vmem,) * 7,
        [
            pltpu.SMEM(cache_valid_lengths.shape, jnp.int32),
            pltpu.SMEM(adapter_block_owner.shape, jnp.int32),
            pltpu.VMEM(layer_input_hidden.shape, bf16),
            pltpu.VMEM(adapter_down_stored.shape, bf16),
            pltpu.VMEM(rmsnorm_gain_weight.shape, bf16),
            pltpu.SemaphoreType.DMA((5,)),
        ],
        limit=8,
    )(
        cache_valid_lengths, adapter_block_owner, layer_input_hidden, adapter_down_stored,
        rmsnorm_gain_weight, wo,
    )
    own_shrunk, other_down, other_up_query, other_up_value = lax.optimization_barrier(
        (own_shrunk, other_down, other_up_query, other_up_value)
    )
    partial, normed, up_query = kernel_call(
        shrink_kernel,
        (
            shape((rows, 2 * ADAPTER_RANK), f32),
            shape((rows, model_width), bf16),
            shape(adapter_up_query.shape, bf16),
        ),
        [vmem] * 5 + [far],
        (vmem,) * 3,
        limit=4,
    )(features, other_down, own_shrunk, normed, adapter_up_query, wo)

    partial = after = partial + crossed(partial, 1)
    far_up_query = crossed(up_query, peers // 2)
    for mask in near_masks():
        partial = partial + crossed(partial, mask)

    key_sum = jnp.dot(normed, wk, preferred_element_type=f32)
    value_sum = jnp.dot(normed, wv, preferred_element_type=f32)
    query_sum = kernel_call(
        query_kernel,
        shape((rows, wq.shape[1]), f32),
        [vmem] * 3,
        vmem,
        limit=4,
        moved=wq.size,
        flops=2 * rows * wq.size,
    )(normed, wq, after)
    other_far_up_query = lax.ppermute(far_up_query, "replica", pairs)

    strided_rows = padded(max(rows, 8 * seqs), 8)
    packed_rows = padded(held_rows, 16) + padded(3 * rows, 16)
    packed = kernel_call(
        pack_kernel,
        shape((packed_rows, HEAD_DIM), bf16),
        [vmem, vmem, far],
        vmem,
        [pltpu.VMEM((packed_rows, HEAD_DIM), f32)],
        limit=4,
    )(query_sum, partial, wq)
    queries, key_raw, value_raw = kernel_call(
        functools.partial(finish_kernel, seqs),
        (
            shape((2, held_rows, HEAD_DIM), bf16),
            shape((rows, kv_width), bf16),
            shape((rows, kv_width), bf16),
        ),
        [vmem] * 13 + [far],
        (vmem,) * 3,
        [
            pltpu.VMEM((2, local_heads, strided_rows, HEAD_DIM), f32),
            pltpu.VMEM((2, padded(held_rows, 8) + 8, HEAD_DIM), f32),
        ],
        limit=4,
    )(
        query_sum, partial, crossed(packed, peers // 2), key_sum, value_sum, up_query,
        other_up_query, far_up_query, other_far_up_query, adapter_up_value, other_up_value,
        cosine, sine, wq,
    )

    if kv_width != HEAD_DIM:
        kv_index = tensor_index * local_heads // group

        def own_head(value):
            heads = lax.all_gather(value, "tensor", axis=1, tiled=True)
            return lax.dynamic_slice_in_dim(heads, kv_index * HEAD_DIM, HEAD_DIM, 1)

        key_raw, value_raw = own_head(key_raw), own_head(value_raw)

    fresh, fresh_level = kernel_call(
        functools.partial(fresh_kernel, seqs),
        (shape((held_rows, HEAD_DIM), f32), shape((8, HEAD_DIM), f32)),
        [vmem] * 5,
        (vmem, vmem),
        limit=4,
    )(queries, key_raw, value_raw, cosine, sine)
    held, masks = queries, [0, peers // 2]
    for mask in near_masks()[:0:-1]:
        held = jnp.concatenate([held, crossed(held, mask)])
        masks = masks + [mask ^ other for other in masks]
    others = {m: crossed(held, m) for m in (1, 2, 3)}

    span = rotated_key_cache.shape[2]
    blocks_shape = shape((peers, padded(held_rows, 16) + 16, HEAD_DIM), bf16)
    buffers = [pltpu.VMEM((4, span, HEAD_DIM), f32), pltpu.VMEM((4, HEAD_DIM, span), f32)]

    def cache_part(its_masks, taken, *operands):
        return kernel_call(
            functools.partial(cache_kernel, its_masks, taken),
            blocks_shape,
            [vmem] * 3 + [far] + [vmem] * (1 + len(operands)),
            vmem,
            buffers,
            limit=6,
        )(reach, rotated_key_cache, cached_value_rows, wq, fresh_level, *operands)

    blocks, taken = cache_part(masks, [], held), masks
    for met in ((2, 3), (1,)):
        its_masks = [mask ^ m for m in met for mask in masks]
        blocks = cache_part(its_masks, taken, blocks, *[others[m] for m in met])
        taken = taken + its_masks

    folds = width // 256 if (rows * (width // 256)) % 16 == 0 else 1
    shares = kernel_call(
        functools.partial(merge_kernel, seqs),
        shape((peers, rows * folds, width // folds), bf16),
        [vmem] * 4,
        vmem,
        [pltpu.VMEM((local_heads, strided_rows, HEAD_DIM), f32)],
        limit=6,
    )(exchanged(blocks), fresh, fresh_level, wo)
    return kernel_call(
        sum_kernel,
        shape((steps, seqs, width), bf16),
        [vmem] * 2,
        vmem,
        limit=4,
    )(rest, exchanged(shares))


def solution(mesh):
    return jax.shard_map(
        body,
        mesh=mesh,
        in_specs=(
            P(None, ("groups", "replica"), None),
            P(),
            P(None, "tensor"),
            P(None, "tensor"),
            P(None, "tensor"),
            P("tensor", None),
            P(("replica", "tensor"), None),
            P("replica", "tensor"),
            P("replica", "tensor"),
            P(),
            P(("groups", "replica"), None, "tensor", None),
            P(("groups", "replica"), None, "tensor", None),
            P(("groups", "replica")),
        ),
        out_specs=P(None, ("groups", "replica"), "tensor"),
        check_vma=False,
    )
```

```python
import functools
import math

import jax
import jax.numpy as jnp
from jax import lax
from jax.experimental import pallas as pl
from jax.experimental.pallas import tpu as pltpu
from jax.sharding import PartitionSpec as P

QUERY_HEADS = 64
KEY_VALUE_HEADS = 8
HEAD_DIM = 128
ADAPTER_RANK = 64


adapter_scale = 2.0
rope_base = 500000.0
negative = -1e30
inv_root = 1.0 / math.sqrt(HEAD_DIM)
MIB = 1 << 20

vmem = pl.BlockSpec(memory_space=pltpu.VMEM)
smem = pl.BlockSpec(memory_space=pltpu.SMEM)
far = pl.BlockSpec(memory_space=pl.ANY)


def padded(count, multiple):
    return -(-count // multiple) * multiple


def rows_padded(value, rows):
    if value.shape[0] == rows:
        return value
    filler = jnp.zeros((rows - value.shape[0],) + value.shape[1:], value.dtype)
    return jnp.concatenate([value, filler], axis=0)


def kernel_call(kernel, outs, specs, out_specs, scratch=(), limit=16, moved=0, flops=0):
    call = pl.pallas_call(
        kernel,
        out_shape=outs,
        in_specs=specs,
        out_specs=out_specs,
        scratch_shapes=list(scratch),
        compiler_params=pltpu.CompilerParams(vmem_limit_bytes=limit * MIB),
        cost_estimate=pl.CostEstimate(flops=flops, bytes_accessed=moved, transcendentals=0),
    )

    def run(*operands):
        return call(
            *[
                pltpu.with_memory_space_constraint(operand, pltpu.HBM) if spec is far else operand
                for operand, spec in zip(operands, specs)
            ]
        )

    return run


def fetches(pairs, sem):
    copies = [
        pltpu.make_async_copy(far_ref, near, sem.at[k]) for k, (far_ref, near) in enumerate(pairs)
    ]
    for copy in copies:
        copy.start()
    return copies


def features_of(normed_ref, owner_ref, held, block_rows):
    place = jnp.int32(0)
    for j in range(owner_ref.shape[0]):
        place = jnp.where(owner_ref[j] == held, jnp.int32(j), place)
    return normed_ref[:, pl.ds(pl.multiple_of(place * block_rows, block_rows), block_rows)]


def norm_kernel(
    peers, heads, lengths_ref, owner_ref, x_ref, down_ref, gain_ref, beside_ref,
    normed_ref, cos_ref, sin_ref, rest_ref, reach_ref, shrunk_ref, features_ref,
    lengths, owner, x_buf, down_buf, gain, sem,
):
    copies = fetches(
        [
            (lengths_ref, lengths),
            (owner_ref, owner),
            (x_ref, x_buf),
            (down_ref, down_buf),
            (gain_ref, gain),
        ],
        sem,
    )
    steps, seqs, _ = x_ref.shape
    rows, width = rest_ref.shape
    half = HEAD_DIM // 2
    row = lax.broadcasted_iota(jnp.int32, (rows, HEAD_DIM), 0)
    lane = lax.broadcasted_iota(jnp.int32, (rows, HEAD_DIM), 1)
    copies[0].wait()
    positions = jnp.zeros((rows, HEAD_DIM), jnp.int32)
    for s in range(steps):
        for n in range(seqs):
            positions = jnp.where(row == s * seqs + n, lengths[n] + s, positions)
    low = lane < half
    exponent = jnp.where(low, lane, lane - half).astype(jnp.float32) * (2.0 / HEAD_DIM)
    angles = positions.astype(jnp.float32) * jnp.exp(exponent * -math.log(rope_base))
    sine = jnp.sin(angles)
    cos_ref[...] = jnp.cos(angles)
    sin_ref[...] = jnp.where(low, -sine, sine)
    place = lax.broadcasted_iota(jnp.int32, reach_ref.shape, 1)
    reach = jnp.zeros(reach_ref.shape, jnp.int32)
    per_seq = heads * steps
    for n in range(seqs):
        mine = jnp.logical_and(place >= n * per_seq, place < (n + 1) * per_seq)
        reach = jnp.where(mine, lengths[n], reach)
    reach_ref[...] = reach
    copies[2].wait()
    values = jnp.concatenate([x_buf[s].astype(jnp.float32) for s in range(steps)], axis=0)
    factor = lax.rsqrt(jnp.mean(values * values, axis=-1, keepdims=True) + 1e-05)
    copies[4].wait()
    normed = values * factor * gain[...].astype(jnp.float32).reshape(1, -1)
    normed_ref[...] = normed.astype(jnp.bfloat16)
    replica, tensor = lax.axis_index("replica"), lax.axis_index("tensor")
    columns = pl.ds(pl.multiple_of(tensor * width, width), width)
    rest = [x_buf[s, :, columns].astype(jnp.float32) for s in range(steps)]
    rest_ref[...] = jnp.concatenate(rest, axis=0)
    copies[1].wait()
    copies[3].wait()
    block_rows = down_ref.shape[0]
    features_ref[...] = features_of(
        normed_ref, owner, (1 - replica) * peers + tensor, block_rows
    )
    shrunk_ref[...] = jnp.dot(
        features_of(normed_ref, owner, replica * peers + tensor, block_rows),
        down_buf[...],
        preferred_element_type=jnp.float32,
    )


def shrink_kernel(
    features_ref, other_ref, own_ref, normed_ref, beside_ref, out_ref, normed_out
):
    normed_out[...] = normed_ref[...]
    out_ref[...] = own_ref[...] + jnp.dot(
        features_ref[...], other_ref[...], preferred_element_type=jnp.float32
    )


def query_kernel(normed_ref, wq_ref, far_ref, out_ref, far_out):
    far_out[...] = far_ref[...]
    out_ref[...] = jnp.dot(normed_ref[...], wq_ref[...], preferred_element_type=jnp.float32)


def rotated(values, cosine, sine):
    half = HEAD_DIM // 2
    turned = jnp.concatenate([values[:, half:], values[:, :half]], axis=1)
    return values * cosine + turned * sine


def pack_kernel(acc_ref, partial_ref, beside_ref, out_ref, tall):
    rows = acc_ref.shape[0]
    heads = acc_ref.shape[1] // HEAD_DIM
    for h in range(heads):
        tall[h * rows : (h + 1) * rows, :] = acc_ref[:, h * HEAD_DIM : (h + 1) * HEAD_DIM]
    held_rows = padded(heads * rows, 16)
    if held_rows > heads * rows:
        tall[heads * rows : held_rows, :] = jnp.zeros(
            (held_rows - heads * rows, HEAD_DIM), jnp.float32
        )
    left = partial_ref[...]
    for c in range(3):
        piece = left.astype(jnp.bfloat16).astype(jnp.float32)
        left = left - piece
        tall[held_rows + c * rows : held_rows + (c + 1) * rows, :] = piece
    end = held_rows + 3 * rows
    if out_ref.shape[0] > end:
        tall[end:, :] = jnp.zeros((out_ref.shape[0] - end, HEAD_DIM), jnp.float32)
    out_ref[...] = tall[...].astype(jnp.bfloat16)


def finish_kernel(
    seq_count, acc_ref, partial_ref, met_ref, key_ref, value_ref, uq_own, uq_other, far_own,
    far_other, uv_own, uv_other, cos_ref, sin_ref, beside_ref,
    query_ref, keyout_ref, valueout_ref, wide, tall,
):
    first = lax.axis_index("replica") == 0
    rows = acc_ref.shape[0]
    steps = rows // seq_count
    heads = acc_ref.shape[1] // HEAD_DIM
    held_rows = padded(heads * rows, 16)
    met = met_ref[...].astype(jnp.float32)
    pieces = [met[held_rows + c * rows : held_rows + (c + 1) * rows] for c in range(3)]
    shrunk = partial_ref[...] + (pieces[0] + (pieces[1] + pieces[2]))
    shrunk = shrunk.astype(jnp.bfloat16).astype(jnp.float32)
    half = ADAPTER_RANK // 2

    def lifted(low, high, own, other):
        mine = jnp.where(first, low, high).astype(jnp.bfloat16)
        theirs = jnp.where(first, high, low).astype(jnp.bfloat16)
        return adapter_scale * (
            jnp.dot(mine, own[...], preferred_element_type=jnp.float32)
            + jnp.dot(theirs, other[...], preferred_element_type=jnp.float32)
        )

    low, high = shrunk[:, :half], shrunk[:, half : 2 * half]
    cosine, sine = cos_ref[...], sin_ref[...]
    for e, (own, other) in enumerate(((uq_own, uq_other), (far_own, far_other))):
        lora = lifted(low, high, own, other)
        for h in range(heads):
            columns = slice(h * HEAD_DIM, (h + 1) * HEAD_DIM)
            base = acc_ref[:, columns] if e == 0 else met[h * rows : (h + 1) * rows]
            raw = (base + lora[:, columns]).astype(jnp.bfloat16).astype(jnp.float32)
            wide[e, h, 0:rows, :] = rotated(raw, cosine, sine)
        for n in range(seq_count):
            for h in range(heads):
                tall[e, pl.ds((n * heads + h) * steps, steps), :] = wide[
                    e, h, pl.ds(n, steps, stride=seq_count), :
                ]
        query_ref[e] = tall[e, 0 : heads * rows, :].astype(jnp.bfloat16)
    keyout_ref[...] = key_ref[...].astype(jnp.bfloat16)
    value = value_ref[...] + lifted(
        shrunk[:, 2 * half : 3 * half], shrunk[:, 3 * half :], uv_own, uv_other
    )
    valueout_ref[...] = value.astype(jnp.bfloat16)


def fresh_kernel(
    seq_count, query_ref, key_ref, value_ref, cos_ref, sin_ref, fresh_ref, level_ref
):
    lane = lax.broadcasted_iota(jnp.int32, (1, HEAD_DIM), 1)
    columns = []
    steps = key_ref.shape[0] // seq_count
    per_seq = fresh_ref.shape[0] // seq_count
    queries = query_ref[0].astype(jnp.float32)
    keys = rotated(key_ref[...].astype(jnp.float32), cos_ref[...], sin_ref[...])
    keys = keys.astype(jnp.bfloat16).astype(jnp.float32)
    values = value_ref[...].astype(jnp.float32)
    step = lax.rem(lax.broadcasted_iota(jnp.int32, (per_seq, 1), 0), steps)
    for n in range(seq_count):
        rows = slice(n * per_seq, (n + 1) * per_seq)
        query = queries[rows]
        scores = []
        for t in range(steps):
            place = t * seq_count + n
            score = jnp.sum(query * keys[place : place + 1], axis=-1, keepdims=True) * inv_root
            scores.append(jnp.where(step >= t, score, negative))
        top = functools.reduce(jnp.maximum, scores)
        weights = [
            jnp.where(step >= t, jnp.exp(score - top), 0.0) for t, score in enumerate(scores)
        ]
        total = functools.reduce(jnp.add, weights)
        summed = jnp.zeros((per_seq, HEAD_DIM), jnp.float32)
        for t, weight in enumerate(weights):
            place = t * seq_count + n
            summed = summed + weight.astype(jnp.bfloat16).astype(jnp.float32) * values[
                place : place + 1
            ]
        fresh_ref[rows, :] = summed
        columns.append(jnp.where(lane == 0, top, jnp.where(lane == 1, total, 0.0)))
    columns = rows_padded(jnp.concatenate(columns, axis=0), HEAD_DIM)
    level_ref[...] = jnp.transpose(columns)[0 : level_ref.shape[0], :]


def pieces_of(top, total):
    rows = lax.broadcasted_iota(jnp.int32, (16, HEAD_DIM), 0)
    packed = jnp.zeros((16, HEAD_DIM), jnp.float32)
    for first, left in ((0, top), (3, total)):
        for c in range(3):
            piece = left.astype(jnp.bfloat16).astype(jnp.float32)
            left = left - piece
            packed = jnp.where(rows == first + c, piece, packed)
    return packed.astype(jnp.bfloat16)


def top_and_total(part_ref, held_rows):
    pieces = part_ref[padded(held_rows, 16) :, :].astype(jnp.float32)
    return (
        pieces[0:1] + (pieces[1:2] + pieces[2:3]),
        pieces[3:4] + (pieces[4:5] + pieces[5:6]),
    )


def turned_rows(rows):
    count = padded(len(rows), 8)
    place = lax.broadcasted_iota(jnp.int32, (count, HEAD_DIM), 0)
    stacked = jnp.zeros((count, HEAD_DIM), jnp.float32)
    for k, row in enumerate(rows):
        stacked = jnp.where(place == k, row, stacked)
    return jnp.transpose(rows_padded(stacked, HEAD_DIM))


def cache_kernel(
    masks, taken, reach_ref, kc_ref, vc_ref, beside_ref, after_ref, *refs
):
    *refs, out_ref, scores_buf, weights_buf = refs
    earlier, query_refs = (refs[:1], refs[1:]) if taken else ([], refs)
    entries, peers = len(masks), out_ref.shape[0]
    each, held_rows, _ = query_refs[0].shape
    seq_count, kv_heads, span, _ = kc_ref.shape
    per_seq = held_rows // seq_count
    mean_rows = padded(held_rows, 16)
    tensor = lax.axis_index("tensor")
    spots = tensor * span + lax.broadcasted_iota(jnp.int32, (span, HEAD_DIM), 0)
    live = spots < reach_ref[0:1, :]
    lane = lax.broadcasted_iota(jnp.int32, (span, HEAD_DIM), 1)
    owners = [lax.bitwise_xor(tensor, mask) for mask in masks]
    heads = [owner * kv_heads // peers for owner in owners]
    for blocks in earlier:
        for mask in taken:
            place = lax.bitwise_xor(tensor, mask)
            out_ref[place] = blocks[place]
    batch = scores_buf.shape[0]
    for lead in range(0, entries, batch):
        part = range(lead, min(lead + batch, entries))
        turned = [
            jnp.transpose(
                rows_padded(query_refs[e // each][e % each].astype(jnp.float32), HEAD_DIM)
            ).astype(jnp.bfloat16)
            for e in part
        ]
        for k, e in enumerate(part):
            scores = None
            for n in range(seq_count):
                score = jnp.dot(
                    kc_ref[n, heads[e]], turned[k], preferred_element_type=jnp.float32
                )
                scores = score if n == 0 else jnp.where(lane < n * per_seq, scores, score)
            scores_buf[k] = jnp.where(live, scores, negative)
        tops = [
            jnp.maximum(jnp.max(scores_buf[k], axis=0, keepdims=True), 0.1 * negative)
            for k in range(len(part))
        ]
        for k, e in enumerate(part):
            weights = jnp.exp((scores_buf[k] - tops[k]) * inv_root)
            total = jnp.sum(weights, axis=0, keepdims=True)
            out_ref[owners[e], mean_rows:, :] = pieces_of(tops[k] * inv_root, total)
            weights_buf[k] = jnp.transpose(weights)
        for k, e in enumerate(part):
            sums = [
                jnp.dot(
                    weights_buf[k, n * per_seq : (n + 1) * per_seq, :].astype(jnp.bfloat16),
                    vc_ref[n, heads[e]],
                    preferred_element_type=jnp.float32,
                )
                for n in range(seq_count)
            ]
            sums = rows_padded(jnp.concatenate(sums, axis=0), mean_rows)
            out_ref[owners[e], 0:mean_rows, :] = sums.astype(jnp.bfloat16)


def merge_kernel(seq_count, blocks_ref, fresh_ref, level_ref, wo_ref, out_ref, wide):
    peers, folded, lanes = out_ref.shape
    heads = wide.shape[0]
    held_rows = fresh_ref.shape[0]
    rows = held_rows // heads
    steps = rows // seq_count
    folds = folded // rows
    per_seq = heads * steps
    mean_rows = padded(held_rows, 16)
    stats = [top_and_total(blocks_ref.at[b], held_rows) for b in range(peers)]
    stats.append((level_ref[0:1, :], level_ref[1:2, :]))
    top = functools.reduce(jnp.maximum, [stat[0] for stat in stats])
    factors = [jnp.exp(stat[0] - top) for stat in stats]
    total = functools.reduce(jnp.add, [factor * stat[1] for factor, stat in zip(factors, stats)])
    total = jnp.where(total > 0.0, total, 1.0)
    columns = turned_rows([factor / total for factor in factors])
    mixed = fresh_ref[...] * columns[0:held_rows, peers : peers + 1]
    for b in range(peers):
        mixed = mixed + (
            blocks_ref[b, 0:mean_rows, :].astype(jnp.float32)[0:held_rows]
            * columns[0:held_rows, b : b + 1]
        )
    for n in range(seq_count):
        for h in range(heads):
            first = n * per_seq + h * steps
            wide[h, pl.ds(n, steps, stride=seq_count), :] = mixed[first : first + steps]
    attention = jnp.concatenate([wide[h, 0:rows, :] for h in range(heads)], axis=1)
    attention = attention.astype(jnp.bfloat16)
    width = folds * lanes
    for p in range(peers):
        share = jnp.dot(
            attention,
            wo_ref[:, p * width : (p + 1) * width],
            preferred_element_type=jnp.float32,
        )
        if folds > 1:
            share = jnp.concatenate(
                [share[:, c * lanes : (c + 1) * lanes] for c in range(folds)], axis=0
            )
        out_ref[p] = share.astype(out_ref.dtype)


def sum_kernel(rest_ref, parts_ref, out_ref):
    total = functools.reduce(
        jnp.add, [parts_ref[b].astype(jnp.float32) for b in range(parts_ref.shape[0])]
    )
    rows = rest_ref.shape[0]
    steps, seqs, _ = out_ref.shape
    folds, lanes = total.shape[0] // rows, total.shape[1]
    for c in range(folds):
        columns = slice(c * lanes, (c + 1) * lanes)
        piece = total[c * rows : (c + 1) * rows] + rest_ref[:, columns]
        for s in range(steps):
            out_ref[s, :, columns] = piece[s * seqs : (s + 1) * seqs].astype(jnp.bfloat16)


def crossed(value, mask):
    pairs = [(source, source ^ mask) for source in range(lax.axis_size("tensor"))]
    return lax.ppermute(value, "tensor", pairs)


def exchanged(value):
    return lax.all_to_all(value, "tensor", split_axis=0, concat_axis=0, tiled=True)


def near_masks():
    masks = [2]
    while 4 * masks[-1] < lax.axis_size("tensor"):
        masks.append(2 * masks[-1])
    return masks


def body(
    layer_input_hidden,
    rmsnorm_gain_weight,
    wq,
    wk,
    wv,
    wo,
    adapter_down_stored,
    adapter_up_query,
    adapter_up_value,
    adapter_block_owner,
    rotated_key_cache,
    cached_value_rows,
    cache_valid_lengths,
):
    f32, bf16 = jnp.float32, jnp.bfloat16
    shape = jax.ShapeDtypeStruct
    steps, seqs, model_width = layer_input_hidden.shape
    peers = lax.axis_size("tensor")
    tensor_index = lax.axis_index("tensor")
    rows = steps * seqs
    local_heads = wq.shape[1] // HEAD_DIM
    held_rows = rows * local_heads
    kv_width = wk.shape[1]
    width = model_width // peers
    group = QUERY_HEADS // KEY_VALUE_HEADS

    pairs = [(0, 1), (1, 0)]
    other_down = lax.ppermute(adapter_down_stored, "replica", pairs)
    other_up_query = lax.ppermute(adapter_up_query, "replica", pairs)
    other_up_value = lax.ppermute(adapter_up_value, "replica", pairs)
    far_up_query = crossed(adapter_up_query, peers // 2)

    normed, cosine, sine, rest, reach, own_shrunk, features = kernel_call(
        functools.partial(norm_kernel, peers, local_heads),
        (
            shape((rows, model_width), bf16),
            shape((rows, HEAD_DIM), f32),
            shape((rows, HEAD_DIM), f32),
            shape((rows, width), f32),
            shape((8, HEAD_DIM), jnp.int32),
            shape((rows, 2 * ADAPTER_RANK), f32),
            shape((rows, adapter_down_stored.shape[0]), bf16),
        ),
        [far] * 6,
        (vmem,) * 7,
        [
            pltpu.SMEM(cache_valid_lengths.shape, jnp.int32),
            pltpu.SMEM(adapter_block_owner.shape, jnp.int32),
            pltpu.VMEM(layer_input_hidden.shape, bf16),
            pltpu.VMEM(adapter_down_stored.shape, bf16),
            pltpu.VMEM(rmsnorm_gain_weight.shape, bf16),
            pltpu.SemaphoreType.DMA((5,)),
        ],
        limit=8,
    )(
        cache_valid_lengths, adapter_block_owner, layer_input_hidden, adapter_down_stored,
        rmsnorm_gain_weight, wo,
    )
    own_shrunk, other_down, other_up_query, other_up_value = lax.optimization_barrier(
        (own_shrunk, other_down, other_up_query, other_up_value)
    )
    partial, normed = kernel_call(
        shrink_kernel,
        (shape((rows, 2 * ADAPTER_RANK), f32), shape((rows, model_width), bf16)),
        [vmem] * 4 + [far],
        (vmem, vmem),
        limit=4,
    )(features, other_down, own_shrunk, normed, wo)

    partial = functools.reduce(jnp.add, [partial] + [crossed(partial, m) for m in (1, 2, 3)])
    for mask in near_masks()[1:]:
        partial = partial + crossed(partial, mask)

    key_sum = jnp.dot(normed, wk, preferred_element_type=f32)
    value_sum = jnp.dot(normed, wv, preferred_element_type=f32)
    query_sum, far_up_query = kernel_call(
        query_kernel,
        (shape((rows, wq.shape[1]), f32), shape(far_up_query.shape, bf16)),
        [vmem] * 3,
        (vmem, vmem),
        limit=4,
        moved=wq.size,
        flops=2 * rows * wq.size,
    )(normed, wq, far_up_query)
    other_far_up_query = lax.ppermute(far_up_query, "replica", pairs)

    strided_rows = padded(max(rows, 8 * seqs), 8)
    packed_rows = padded(held_rows, 16) + padded(3 * rows, 16)
    packed = kernel_call(
        pack_kernel,
        shape((packed_rows, HEAD_DIM), bf16),
        [vmem, vmem, far],
        vmem,
        [pltpu.VMEM((packed_rows, HEAD_DIM), f32)],
        limit=4,
    )(query_sum, partial, wq)
    queries, key_raw, value_raw = kernel_call(
        functools.partial(finish_kernel, seqs),
        (
            shape((2, held_rows, HEAD_DIM), bf16),
            shape((rows, kv_width), bf16),
            shape((rows, kv_width), bf16),
        ),
        [vmem] * 13 + [far],
        (vmem,) * 3,
        [
            pltpu.VMEM((2, local_heads, strided_rows, HEAD_DIM), f32),
            pltpu.VMEM((2, padded(held_rows, 8) + 8, HEAD_DIM), f32),
        ],
        limit=4,
    )(
        query_sum, partial, crossed(packed, peers // 2), key_sum, value_sum, adapter_up_query,
        other_up_query, far_up_query, other_far_up_query, adapter_up_value, other_up_value,
        cosine, sine, wq,
    )

    if kv_width != HEAD_DIM:
        kv_index = tensor_index * local_heads // group

        def own_head(value):
            heads = lax.all_gather(value, "tensor", axis=1, tiled=True)
            return lax.dynamic_slice_in_dim(heads, kv_index * HEAD_DIM, HEAD_DIM, 1)

        key_raw, value_raw = own_head(key_raw), own_head(value_raw)

    fresh, fresh_level = kernel_call(
        functools.partial(fresh_kernel, seqs),
        (shape((held_rows, HEAD_DIM), f32), shape((8, HEAD_DIM), f32)),
        [vmem] * 5,
        (vmem, vmem),
        limit=4,
    )(queries, key_raw, value_raw, cosine, sine)
    held, masks = queries, [0, peers // 2]
    for mask in near_masks()[:0:-1]:
        held = jnp.concatenate([held, crossed(held, mask)])
        masks = masks + [mask ^ other for other in masks]
    others = {m: crossed(held, m) for m in (1, 2, 3)}

    span = rotated_key_cache.shape[2]
    blocks_shape = shape((peers, padded(held_rows, 16) + 16, HEAD_DIM), bf16)
    buffers = [pltpu.VMEM((4, span, HEAD_DIM), f32), pltpu.VMEM((4, HEAD_DIM, span), f32)]

    def cache_part(its_masks, taken, *operands):
        return kernel_call(
            functools.partial(cache_kernel, its_masks, taken),
            blocks_shape,
            [vmem] * 3 + [far] + [vmem] * (1 + len(operands)),
            vmem,
            buffers,
            limit=6,
        )(reach, rotated_key_cache, cached_value_rows, wq, fresh_level, *operands)

    blocks, taken = cache_part(masks, [], held), masks
    for met in ((2, 3), (1,)):
        its_masks = [mask ^ m for m in met for mask in masks]
        blocks = cache_part(its_masks, taken, blocks, *[others[m] for m in met])
        taken = taken + its_masks

    folds = width // 256 if (rows * (width // 256)) % 16 == 0 else 1
    shares = kernel_call(
        functools.partial(merge_kernel, seqs),
        shape((peers, rows * folds, width // folds), bf16),
        [vmem] * 4,
        vmem,
        [pltpu.VMEM((local_heads, strided_rows, HEAD_DIM), f32)],
        limit=6,
    )(exchanged(blocks), fresh, fresh_level, wo)
    return kernel_call(
        sum_kernel,
        shape((steps, seqs, width), bf16),
        [vmem] * 2,
        vmem,
        limit=4,
    )(rest, exchanged(shares))


def solution(mesh):
    return jax.shard_map(
        body,
        mesh=mesh,
        in_specs=(
            P(None, ("groups", "replica"), None),
            P(),
            P(None, "tensor"),
            P(None, "tensor"),
            P(None, "tensor"),
            P("tensor", None),
            P(("replica", "tensor"), None),
            P("replica", "tensor"),
            P("replica", "tensor"),
            P(),
            P(("groups", "replica"), None, "tensor", None),
            P(("groups", "replica"), None, "tensor", None),
            P(("groups", "replica")),
        ),
        out_specs=P(None, ("groups", "replica"), "tensor"),
        check_vma=False,
    )
```

```python
import functools
import math

import jax
import jax.numpy as jnp
from jax import lax
from jax.experimental import pallas as pl
from jax.experimental.pallas import tpu as pltpu
from jax.sharding import PartitionSpec as P

QUERY_HEADS = 64
KEY_VALUE_HEADS = 8
HEAD_DIM = 128
ADAPTER_RANK = 64


adapter_scale = 2.0
rope_base = 500000.0
negative = -1e30
inv_root = 1.0 / math.sqrt(HEAD_DIM)
MIB = 1 << 20

vmem = pl.BlockSpec(memory_space=pltpu.VMEM)
smem = pl.BlockSpec(memory_space=pltpu.SMEM)
far = pl.BlockSpec(memory_space=pl.ANY)


def padded(count, multiple):
    return -(-count // multiple) * multiple


def rows_padded(value, rows):
    if value.shape[0] == rows:
        return value
    filler = jnp.zeros((rows - value.shape[0],) + value.shape[1:], value.dtype)
    return jnp.concatenate([value, filler], axis=0)


def kernel_call(
    kernel, outs, specs, out_specs, scratch=(), limit=16, moved=0, flops=0, aliases=None
):
    call = pl.pallas_call(
        kernel,
        out_shape=outs,
        in_specs=specs,
        out_specs=out_specs,
        scratch_shapes=list(scratch),
        input_output_aliases=aliases or {},
        compiler_params=pltpu.CompilerParams(vmem_limit_bytes=limit * MIB),
        cost_estimate=pl.CostEstimate(flops=flops, bytes_accessed=moved, transcendentals=0),
    )

    def run(*operands):
        return call(
            *[
                pltpu.with_memory_space_constraint(operand, pltpu.HBM) if spec is far else operand
                for operand, spec in zip(operands, specs)
            ]
        )

    return run


def fetches(pairs, sem):
    copies = [
        pltpu.make_async_copy(far_ref, near, sem.at[k]) for k, (far_ref, near) in enumerate(pairs)
    ]
    for copy in copies:
        copy.start()
    return copies


def features_of(normed_ref, owner_ref, held, block_rows):
    place = jnp.int32(0)
    for j in range(owner_ref.shape[0]):
        place = jnp.where(owner_ref[j] == held, jnp.int32(j), place)
    return normed_ref[:, pl.ds(pl.multiple_of(place * block_rows, block_rows), block_rows)]


def norm_kernel(
    peers, heads, lengths_ref, owner_ref, x_ref, down_ref, gain_ref, beside_ref,
    normed_ref, cos_ref, sin_ref, rest_ref, reach_ref, shrunk_ref, features_ref,
    lengths, owner, x_buf, down_buf, gain, sem,
):
    copies = fetches(
        [
            (lengths_ref, lengths),
            (owner_ref, owner),
            (x_ref, x_buf),
            (down_ref, down_buf),
            (gain_ref, gain),
        ],
        sem,
    )
    steps, seqs, _ = x_ref.shape
    rows, width = rest_ref.shape
    half = HEAD_DIM // 2
    row = lax.broadcasted_iota(jnp.int32, (rows, HEAD_DIM), 0)
    lane = lax.broadcasted_iota(jnp.int32, (rows, HEAD_DIM), 1)
    copies[0].wait()
    positions = jnp.zeros((rows, HEAD_DIM), jnp.int32)
    for s in range(steps):
        for n in range(seqs):
            positions = jnp.where(row == s * seqs + n, lengths[n] + s, positions)
    low = lane < half
    exponent = jnp.where(low, lane, lane - half).astype(jnp.float32) * (2.0 / HEAD_DIM)
    angles = positions.astype(jnp.float32) * jnp.exp(exponent * -math.log(rope_base))
    sine = jnp.sin(angles)
    cos_ref[...] = jnp.cos(angles)
    sin_ref[...] = jnp.where(low, -sine, sine)
    place = lax.broadcasted_iota(jnp.int32, reach_ref.shape, 1)
    reach = jnp.zeros(reach_ref.shape, jnp.int32)
    per_seq = heads * steps
    for n in range(seqs):
        mine = jnp.logical_and(place >= n * per_seq, place < (n + 1) * per_seq)
        reach = jnp.where(mine, lengths[n], reach)
    reach_ref[...] = reach
    copies[2].wait()
    values = jnp.concatenate([x_buf[s].astype(jnp.float32) for s in range(steps)], axis=0)
    factor = lax.rsqrt(jnp.mean(values * values, axis=-1, keepdims=True) + 1e-05)
    copies[4].wait()
    normed = values * factor * gain[...].astype(jnp.float32).reshape(1, -1)
    normed_ref[...] = normed.astype(jnp.bfloat16)
    replica, tensor = lax.axis_index("replica"), lax.axis_index("tensor")
    columns = pl.ds(pl.multiple_of(tensor * width, width), width)
    rest = [x_buf[s, :, columns].astype(jnp.float32) for s in range(steps)]
    rest_ref[...] = jnp.concatenate(rest, axis=0)
    copies[1].wait()
    copies[3].wait()
    block_rows = down_ref.shape[0]
    features_ref[...] = features_of(
        normed_ref, owner, (1 - replica) * peers + tensor, block_rows
    )
    shrunk_ref[...] = jnp.dot(
        features_of(normed_ref, owner, replica * peers + tensor, block_rows),
        down_buf[...],
        preferred_element_type=jnp.float32,
    )


def shrink_kernel(
    features_ref, other_ref, own_ref, normed_ref, up_ref, beside_ref, out_ref, normed_out, up_out
):
    normed_out[...] = normed_ref[...]
    up_out[...] = up_ref[...]
    out_ref[...] = own_ref[...] + jnp.dot(
        features_ref[...], other_ref[...], preferred_element_type=jnp.float32
    )


def query_kernel(normed_ref, wq_ref, after_ref, out_ref):
    out_ref[...] = jnp.dot(normed_ref[...], wq_ref[...], preferred_element_type=jnp.float32)


def rotated(values, cosine, sine):
    half = HEAD_DIM // 2
    turned = jnp.concatenate([values[:, half:], values[:, :half]], axis=1)
    return values * cosine + turned * sine


def pack_kernel(acc_ref, partial_ref, beside_ref, out_ref, tall):
    rows = acc_ref.shape[0]
    heads = acc_ref.shape[1] // HEAD_DIM
    for h in range(heads):
        tall[h * rows : (h + 1) * rows, :] = acc_ref[:, h * HEAD_DIM : (h + 1) * HEAD_DIM]
    held_rows = padded(heads * rows, 16)
    if held_rows > heads * rows:
        tall[heads * rows : held_rows, :] = jnp.zeros(
            (held_rows - heads * rows, HEAD_DIM), jnp.float32
        )
    left = partial_ref[...]
    for c in range(3):
        piece = left.astype(jnp.bfloat16).astype(jnp.float32)
        left = left - piece
        tall[held_rows + c * rows : held_rows + (c + 1) * rows, :] = piece
    end = held_rows + 3 * rows
    if out_ref.shape[0] > end:
        tall[end:, :] = jnp.zeros((out_ref.shape[0] - end, HEAD_DIM), jnp.float32)
    out_ref[...] = tall[...].astype(jnp.bfloat16)


def finish_kernel(
    seq_count, acc_ref, partial_ref, met_ref, key_ref, value_ref, uq_own, uq_other, far_own,
    far_other, uv_own, uv_other, cos_ref, sin_ref, beside_ref,
    query_ref, keyout_ref, valueout_ref, wide, tall,
):
    first = lax.axis_index("replica") == 0
    rows = acc_ref.shape[0]
    steps = rows // seq_count
    heads = acc_ref.shape[1] // HEAD_DIM
    held_rows = padded(heads * rows, 16)
    met = met_ref[...].astype(jnp.float32)
    pieces = [met[held_rows + c * rows : held_rows + (c + 1) * rows] for c in range(3)]
    shrunk = partial_ref[...] + (pieces[0] + (pieces[1] + pieces[2]))
    shrunk = shrunk.astype(jnp.bfloat16).astype(jnp.float32)
    half = ADAPTER_RANK // 2

    def lifted(low, high, own, other):
        mine = jnp.where(first, low, high).astype(jnp.bfloat16)
        theirs = jnp.where(first, high, low).astype(jnp.bfloat16)
        return adapter_scale * (
            jnp.dot(mine, own[...], preferred_element_type=jnp.float32)
            + jnp.dot(theirs, other[...], preferred_element_type=jnp.float32)
        )

    low, high = shrunk[:, :half], shrunk[:, half : 2 * half]
    cosine, sine = cos_ref[...], sin_ref[...]
    for e, (own, other) in enumerate(((uq_own, uq_other), (far_own, far_other))):
        lora = lifted(low, high, own, other)
        for h in range(heads):
            columns = slice(h * HEAD_DIM, (h + 1) * HEAD_DIM)
            base = acc_ref[:, columns] if e == 0 else met[h * rows : (h + 1) * rows]
            raw = (base + lora[:, columns]).astype(jnp.bfloat16).astype(jnp.float32)
            wide[e, h, 0:rows, :] = rotated(raw, cosine, sine)
        for n in range(seq_count):
            for h in range(heads):
                tall[e, pl.ds((n * heads + h) * steps, steps), :] = wide[
                    e, h, pl.ds(n, steps, stride=seq_count), :
                ]
        query_ref[e] = tall[e, 0 : heads * rows, :].astype(jnp.bfloat16)
    keyout_ref[...] = key_ref[...].astype(jnp.bfloat16)
    value = value_ref[...] + lifted(
        shrunk[:, 2 * half : 3 * half], shrunk[:, 3 * half :], uv_own, uv_other
    )
    valueout_ref[...] = value.astype(jnp.bfloat16)


def fresh_kernel(
    seq_count, query_ref, key_ref, value_ref, cos_ref, sin_ref, fresh_ref, level_ref
):
    lane = lax.broadcasted_iota(jnp.int32, (1, HEAD_DIM), 1)
    columns = []
    steps = key_ref.shape[0] // seq_count
    per_seq = fresh_ref.shape[0] // seq_count
    queries = query_ref[0].astype(jnp.float32)
    keys = rotated(key_ref[...].astype(jnp.float32), cos_ref[...], sin_ref[...])
    keys = keys.astype(jnp.bfloat16).astype(jnp.float32)
    values = value_ref[...].astype(jnp.float32)
    step = lax.rem(lax.broadcasted_iota(jnp.int32, (per_seq, 1), 0), steps)
    for n in range(seq_count):
        rows = slice(n * per_seq, (n + 1) * per_seq)
        query = queries[rows]
        scores = []
        for t in range(steps):
            place = t * seq_count + n
            score = jnp.sum(query * keys[place : place + 1], axis=-1, keepdims=True) * inv_root
            scores.append(jnp.where(step >= t, score, negative))
        top = functools.reduce(jnp.maximum, scores)
        weights = [
            jnp.where(step >= t, jnp.exp(score - top), 0.0) for t, score in enumerate(scores)
        ]
        total = functools.reduce(jnp.add, weights)
        summed = jnp.zeros((per_seq, HEAD_DIM), jnp.float32)
        for t, weight in enumerate(weights):
            place = t * seq_count + n
            summed = summed + weight.astype(jnp.bfloat16).astype(jnp.float32) * values[
                place : place + 1
            ]
        fresh_ref[rows, :] = summed
        columns.append(jnp.where(lane == 0, top, jnp.where(lane == 1, total, 0.0)))
    columns = rows_padded(jnp.concatenate(columns, axis=0), HEAD_DIM)
    level_ref[...] = jnp.transpose(columns)[0 : level_ref.shape[0], :]


def pieces_of(top, total):
    rows = lax.broadcasted_iota(jnp.int32, (16, HEAD_DIM), 0)
    packed = jnp.zeros((16, HEAD_DIM), jnp.float32)
    for first, left in ((0, top), (3, total)):
        for c in range(3):
            piece = left.astype(jnp.bfloat16).astype(jnp.float32)
            left = left - piece
            packed = jnp.where(rows == first + c, piece, packed)
    return packed.astype(jnp.bfloat16)


def top_and_total(part_ref, held_rows):
    pieces = part_ref[padded(held_rows, 16) :, :].astype(jnp.float32)
    return (
        pieces[0:1] + (pieces[1:2] + pieces[2:3]),
        pieces[3:4] + (pieces[4:5] + pieces[5:6]),
    )


def turned_rows(rows):
    count = padded(len(rows), 8)
    place = lax.broadcasted_iota(jnp.int32, (count, HEAD_DIM), 0)
    stacked = jnp.zeros((count, HEAD_DIM), jnp.float32)
    for k, row in enumerate(rows):
        stacked = jnp.where(place == k, row, stacked)
    return jnp.transpose(rows_padded(stacked, HEAD_DIM))


def cache_kernel(
    masks, goes_on, reach_ref, kc_ref, vc_ref, beside_ref, after_ref, *refs
):
    *refs, out_ref, scores_buf, weights_buf = refs
    query_refs = refs[1:] if goes_on else refs
    entries, peers = len(masks), out_ref.shape[0]
    each, held_rows, _ = query_refs[0].shape
    seq_count, kv_heads, span, _ = kc_ref.shape
    per_seq = held_rows // seq_count
    mean_rows = padded(held_rows, 16)
    tensor = lax.axis_index("tensor")
    spots = tensor * span + lax.broadcasted_iota(jnp.int32, (span, HEAD_DIM), 0)
    live = spots < reach_ref[0:1, :]
    lane = lax.broadcasted_iota(jnp.int32, (span, HEAD_DIM), 1)
    owners = [lax.bitwise_xor(tensor, mask) for mask in masks]
    heads = [owner * kv_heads // peers for owner in owners]
    batch = scores_buf.shape[0]
    for lead in range(0, entries, batch):
        part = range(lead, min(lead + batch, entries))
        turned = [
            jnp.transpose(
                rows_padded(query_refs[e // each][e % each].astype(jnp.float32), HEAD_DIM)
            ).astype(jnp.bfloat16)
            for e in part
        ]
        for k, e in enumerate(part):
            scores = None
            for n in range(seq_count):
                score = jnp.dot(
                    kc_ref[n, heads[e]], turned[k], preferred_element_type=jnp.float32
                )
                scores = score if n == 0 else jnp.where(lane < n * per_seq, scores, score)
            scores_buf[k] = jnp.where(live, scores, negative)
        tops = [
            jnp.maximum(jnp.max(scores_buf[k], axis=0, keepdims=True), 0.1 * negative)
            for k in range(len(part))
        ]
        for k, e in enumerate(part):
            weights = jnp.exp((scores_buf[k] - tops[k]) * inv_root)
            total = jnp.sum(weights, axis=0, keepdims=True)
            out_ref[owners[e], mean_rows:, :] = pieces_of(tops[k] * inv_root, total)
            weights_buf[k] = jnp.transpose(weights)
        for k, e in enumerate(part):
            sums = [
                jnp.dot(
                    weights_buf[k, n * per_seq : (n + 1) * per_seq, :].astype(jnp.bfloat16),
                    vc_ref[n, heads[e]],
                    preferred_element_type=jnp.float32,
                )
                for n in range(seq_count)
            ]
            sums = rows_padded(jnp.concatenate(sums, axis=0), mean_rows)
            out_ref[owners[e], 0:mean_rows, :] = sums.astype(jnp.bfloat16)


def merge_kernel(seq_count, blocks_ref, fresh_ref, level_ref, wo_ref, out_ref, wide):
    peers, folded, lanes = out_ref.shape
    heads = wide.shape[0]
    held_rows = fresh_ref.shape[0]
    rows = held_rows // heads
    steps = rows // seq_count
    folds = folded // rows
    per_seq = heads * steps
    mean_rows = padded(held_rows, 16)
    stats = [top_and_total(blocks_ref.at[b], held_rows) for b in range(peers)]
    stats.append((level_ref[0:1, :], level_ref[1:2, :]))
    top = functools.reduce(jnp.maximum, [stat[0] for stat in stats])
    factors = [jnp.exp(stat[0] - top) for stat in stats]
    total = functools.reduce(jnp.add, [factor * stat[1] for factor, stat in zip(factors, stats)])
    total = jnp.where(total > 0.0, total, 1.0)
    columns = turned_rows([factor / total for factor in factors])
    mixed = fresh_ref[...] * columns[0:held_rows, peers : peers + 1]
    for b in range(peers):
        mixed = mixed + (
            blocks_ref[b, 0:mean_rows, :].astype(jnp.float32)[0:held_rows]
            * columns[0:held_rows, b : b + 1]
        )
    for n in range(seq_count):
        for h in range(heads):
            first = n * per_seq + h * steps
            wide[h, pl.ds(n, steps, stride=seq_count), :] = mixed[first : first + steps]
    attention = jnp.concatenate([wide[h, 0:rows, :] for h in range(heads)], axis=1)
    attention = attention.astype(jnp.bfloat16)
    width = folds * lanes
    for p in range(peers):
        share = jnp.dot(
            attention,
            wo_ref[:, p * width : (p + 1) * width],
            preferred_element_type=jnp.float32,
        )
        if folds > 1:
            share = jnp.concatenate(
                [share[:, c * lanes : (c + 1) * lanes] for c in range(folds)], axis=0
            )
        out_ref[p] = share.astype(out_ref.dtype)


def sum_kernel(rest_ref, parts_ref, out_ref):
    total = functools.reduce(
        jnp.add, [parts_ref[b].astype(jnp.float32) for b in range(parts_ref.shape[0])]
    )
    rows = rest_ref.shape[0]
    steps, seqs, _ = out_ref.shape
    folds, lanes = total.shape[0] // rows, total.shape[1]
    for c in range(folds):
        columns = slice(c * lanes, (c + 1) * lanes)
        piece = total[c * rows : (c + 1) * rows] + rest_ref[:, columns]
        for s in range(steps):
            out_ref[s, :, columns] = piece[s * seqs : (s + 1) * seqs].astype(jnp.bfloat16)


def crossed(value, mask):
    pairs = [(source, source ^ mask) for source in range(lax.axis_size("tensor"))]
    return lax.ppermute(value, "tensor", pairs)


def exchanged(value):
    return lax.all_to_all(value, "tensor", split_axis=0, concat_axis=0, tiled=True)


def near_masks():
    masks = [2]
    while 4 * masks[-1] < lax.axis_size("tensor"):
        masks.append(2 * masks[-1])
    return masks


def body(
    layer_input_hidden,
    rmsnorm_gain_weight,
    wq,
    wk,
    wv,
    wo,
    adapter_down_stored,
    adapter_up_query,
    adapter_up_value,
    adapter_block_owner,
    rotated_key_cache,
    cached_value_rows,
    cache_valid_lengths,
):
    f32, bf16 = jnp.float32, jnp.bfloat16
    shape = jax.ShapeDtypeStruct
    steps, seqs, model_width = layer_input_hidden.shape
    peers = lax.axis_size("tensor")
    tensor_index = lax.axis_index("tensor")
    rows = steps * seqs
    local_heads = wq.shape[1] // HEAD_DIM
    held_rows = rows * local_heads
    kv_width = wk.shape[1]
    width = model_width // peers
    group = QUERY_HEADS // KEY_VALUE_HEADS

    pairs = [(0, 1), (1, 0)]
    other_down = lax.ppermute(adapter_down_stored, "replica", pairs)
    other_up_query = lax.ppermute(adapter_up_query, "replica", pairs)
    other_up_value = lax.ppermute(adapter_up_value, "replica", pairs)

    normed, cosine, sine, rest, reach, own_shrunk, features = kernel_call(
        functools.partial(norm_kernel, peers, local_heads),
        (
            shape((rows, model_width), bf16),
            shape((rows, HEAD_DIM), f32),
            shape((rows, HEAD_DIM), f32),
            shape((rows, width), f32),
            shape((8, HEAD_DIM), jnp.int32),
            shape((rows, 2 * ADAPTER_RANK), f32),
            shape((rows, adapter_down_stored.shape[0]), bf16),
        ),
        [far] * 6,
        (vmem,) * 7,
        [
            pltpu.SMEM(cache_valid_lengths.shape, jnp.int32),
            pltpu.SMEM(adapter_block_owner.shape, jnp.int32),
            pltpu.VMEM(layer_input_hidden.shape, bf16),
            pltpu.VMEM(adapter_down_stored.shape, bf16),
            pltpu.VMEM(rmsnorm_gain_weight.shape, bf16),
            pltpu.SemaphoreType.DMA((5,)),
        ],
        limit=8,
    )(
        cache_valid_lengths, adapter_block_owner, layer_input_hidden, adapter_down_stored,
        rmsnorm_gain_weight, wo,
    )
    own_shrunk, other_down, other_up_query, other_up_value = lax.optimization_barrier(
        (own_shrunk, other_down, other_up_query, other_up_value)
    )
    partial, normed, up_query = kernel_call(
        shrink_kernel,
        (
            shape((rows, 2 * ADAPTER_RANK), f32),
            shape((rows, model_width), bf16),
            shape(adapter_up_query.shape, bf16),
        ),
        [vmem] * 5 + [far],
        (vmem,) * 3,
        limit=4,
    )(features, other_down, own_shrunk, normed, adapter_up_query, wo)

    partial = after = partial + crossed(partial, 1)
    far_up_query = crossed(up_query, peers // 2)
    for mask in near_masks():
        partial = partial + crossed(partial, mask)

    key_sum = jnp.dot(normed, wk, preferred_element_type=f32)
    value_sum = jnp.dot(normed, wv, preferred_element_type=f32)
    query_sum = kernel_call(
        query_kernel,
        shape((rows, wq.shape[1]), f32),
        [vmem] * 3,
        vmem,
        limit=4,
        moved=wq.size,
        flops=2 * rows * wq.size,
    )(normed, wq, after)
    other_far_up_query = lax.ppermute(far_up_query, "replica", pairs)

    strided_rows = padded(max(rows, 8 * seqs), 8)
    packed_rows = padded(held_rows, 16) + padded(3 * rows, 16)
    packed = kernel_call(
        pack_kernel,
        shape((packed_rows, HEAD_DIM), bf16),
        [vmem, vmem, far],
        vmem,
        [pltpu.VMEM((packed_rows, HEAD_DIM), f32)],
        limit=4,
    )(query_sum, partial, wq)
    queries, key_raw, value_raw = kernel_call(
        functools.partial(finish_kernel, seqs),
        (
            shape((2, held_rows, HEAD_DIM), bf16),
            shape((rows, kv_width), bf16),
            shape((rows, kv_width), bf16),
        ),
        [vmem] * 13 + [far],
        (vmem,) * 3,
        [
            pltpu.VMEM((2, local_heads, strided_rows, HEAD_DIM), f32),
            pltpu.VMEM((2, padded(held_rows, 8) + 8, HEAD_DIM), f32),
        ],
        limit=4,
    )(
        query_sum, partial, crossed(packed, peers // 2), key_sum, value_sum, up_query,
        other_up_query, far_up_query, other_far_up_query, adapter_up_value, other_up_value,
        cosine, sine, wq,
    )

    if kv_width != HEAD_DIM:
        kv_index = tensor_index * local_heads // group

        def own_head(value):
            heads = lax.all_gather(value, "tensor", axis=1, tiled=True)
            return lax.dynamic_slice_in_dim(heads, kv_index * HEAD_DIM, HEAD_DIM, 1)

        key_raw, value_raw = own_head(key_raw), own_head(value_raw)

    fresh, fresh_level = kernel_call(
        functools.partial(fresh_kernel, seqs),
        (shape((held_rows, HEAD_DIM), f32), shape((8, HEAD_DIM), f32)),
        [vmem] * 5,
        (vmem, vmem),
        limit=4,
    )(queries, key_raw, value_raw, cosine, sine)
    held, masks = queries, [0, peers // 2]
    for mask in near_masks()[:0:-1]:
        held = jnp.concatenate([held, crossed(held, mask)])
        masks = masks + [mask ^ other for other in masks]
    others = {m: crossed(held, m) for m in (1, 2, 3)}

    span = rotated_key_cache.shape[2]
    blocks_shape = shape((peers, padded(held_rows, 16) + 16, HEAD_DIM), bf16)
    buffers = [pltpu.VMEM((4, span, HEAD_DIM), f32), pltpu.VMEM((4, HEAD_DIM, span), f32)]

    def cache_part(its_masks, goes_on, *operands):
        return kernel_call(
            functools.partial(cache_kernel, its_masks, goes_on),
            blocks_shape,
            [vmem] * 3 + [far] + [vmem] * (1 + len(operands)),
            vmem,
            buffers,
            limit=6,
            aliases={5: 0} if goes_on else None,
        )(reach, rotated_key_cache, cached_value_rows, wq, fresh_level, *operands)

    blocks = cache_part(masks, False, held)
    for met in ((2, 3), (1,)):
        its_masks = [mask ^ m for m in met for mask in masks]
        blocks = cache_part(its_masks, True, blocks, *[others[m] for m in met])

    folds = width // 256 if (rows * (width // 256)) % 16 == 0 else 1
    shares = kernel_call(
        functools.partial(merge_kernel, seqs),
        shape((peers, rows * folds, width // folds), bf16),
        [vmem] * 4,
        vmem,
        [pltpu.VMEM((local_heads, strided_rows, HEAD_DIM), f32)],
        limit=6,
    )(exchanged(blocks), fresh, fresh_level, wo)
    return kernel_call(
        sum_kernel,
        shape((steps, seqs, width), bf16),
        [vmem] * 2,
        vmem,
        limit=4,
    )(rest, exchanged(shares))


def solution(mesh):
    return jax.shard_map(
        body,
        mesh=mesh,
        in_specs=(
            P(None, ("groups", "replica"), None),
            P(),
            P(None, "tensor"),
            P(None, "tensor"),
            P(None, "tensor"),
            P("tensor", None),
            P(("replica", "tensor"), None),
            P("replica", "tensor"),
            P("replica", "tensor"),
            P(),
            P(("groups", "replica"), None, "tensor", None),
            P(("groups", "replica"), None, "tensor", None),
            P(("groups", "replica")),
        ),
        out_specs=P(None, ("groups", "replica"), "tensor"),
        check_vma=False,
    )
```

```python
import functools
import math

import jax
import jax.numpy as jnp
from jax import lax
from jax.experimental import pallas as pl
from jax.experimental.pallas import tpu as pltpu
from jax.sharding import PartitionSpec as P

QUERY_HEADS = 64
KEY_VALUE_HEADS = 8
HEAD_DIM = 128
ADAPTER_RANK = 64


adapter_scale = 2.0
rope_base = 500000.0
negative = -1e30
inv_root = 1.0 / math.sqrt(HEAD_DIM)
MIB = 1 << 20

vmem = pl.BlockSpec(memory_space=pltpu.VMEM)
smem = pl.BlockSpec(memory_space=pltpu.SMEM)
far = pl.BlockSpec(memory_space=pl.ANY)


def padded(count, multiple):
    return -(-count // multiple) * multiple


def rows_padded(value, rows):
    if value.shape[0] == rows:
        return value
    filler = jnp.zeros((rows - value.shape[0],) + value.shape[1:], value.dtype)
    return jnp.concatenate([value, filler], axis=0)


def kernel_call(kernel, outs, specs, out_specs, scratch=(), limit=16, moved=0, flops=0):
    call = pl.pallas_call(
        kernel,
        out_shape=outs,
        in_specs=specs,
        out_specs=out_specs,
        scratch_shapes=list(scratch),
        compiler_params=pltpu.CompilerParams(vmem_limit_bytes=limit * MIB),
        cost_estimate=pl.CostEstimate(flops=flops, bytes_accessed=moved, transcendentals=0),
    )

    def run(*operands):
        return call(
            *[
                pltpu.with_memory_space_constraint(operand, pltpu.HBM) if spec is far else operand
                for operand, spec in zip(operands, specs)
            ]
        )

    return run


def fetches(pairs, sem):
    copies = [
        pltpu.make_async_copy(far_ref, near, sem.at[k]) for k, (far_ref, near) in enumerate(pairs)
    ]
    for copy in copies:
        copy.start()
    return copies


def features_of(normed_ref, owner_ref, held, block_rows):
    place = jnp.int32(0)
    for j in range(owner_ref.shape[0]):
        place = jnp.where(owner_ref[j] == held, jnp.int32(j), place)
    return normed_ref[:, pl.ds(pl.multiple_of(place * block_rows, block_rows), block_rows)]


def norm_kernel(
    peers, heads, lengths_ref, owner_ref, x_ref, down_ref, gain_ref, beside_ref,
    normed_ref, cos_ref, sin_ref, rest_ref, reach_ref, shrunk_ref, features_ref,
    lengths, owner, x_buf, down_buf, gain, sem,
):
    copies = fetches(
        [
            (lengths_ref, lengths),
            (owner_ref, owner),
            (x_ref, x_buf),
            (down_ref, down_buf),
            (gain_ref, gain),
        ],
        sem,
    )
    steps, seqs, _ = x_ref.shape
    rows, width = rest_ref.shape
    half = HEAD_DIM // 2
    row = lax.broadcasted_iota(jnp.int32, (rows, HEAD_DIM), 0)
    lane = lax.broadcasted_iota(jnp.int32, (rows, HEAD_DIM), 1)
    copies[0].wait()
    positions = jnp.zeros((rows, HEAD_DIM), jnp.int32)
    for s in range(steps):
        for n in range(seqs):
            positions = jnp.where(row == s * seqs + n, lengths[n] + s, positions)
    low = lane < half
    exponent = jnp.where(low, lane, lane - half).astype(jnp.float32) * (2.0 / HEAD_DIM)
    angles = positions.astype(jnp.float32) * jnp.exp(exponent * -math.log(rope_base))
    sine = jnp.sin(angles)
    cos_ref[...] = jnp.cos(angles)
    sin_ref[...] = jnp.where(low, -sine, sine)
    place = lax.broadcasted_iota(jnp.int32, reach_ref.shape, 1)
    reach = jnp.zeros(reach_ref.shape, jnp.int32)
    per_seq = heads * steps
    for n in range(seqs):
        mine = jnp.logical_and(place >= n * per_seq, place < (n + 1) * per_seq)
        reach = jnp.where(mine, lengths[n], reach)
    reach_ref[...] = reach
    copies[2].wait()
    values = jnp.concatenate([x_buf[s].astype(jnp.float32) for s in range(steps)], axis=0)
    factor = lax.rsqrt(jnp.mean(values * values, axis=-1, keepdims=True) + 1e-05)
    copies[4].wait()
    normed = values * factor * gain[...].astype(jnp.float32).reshape(1, -1)
    normed_ref[...] = normed.astype(jnp.bfloat16)
    replica, tensor = lax.axis_index("replica"), lax.axis_index("tensor")
    columns = pl.ds(pl.multiple_of(tensor * width, width), width)
    rest = [x_buf[s, :, columns].astype(jnp.float32) for s in range(steps)]
    rest_ref[...] = jnp.concatenate(rest, axis=0)
    copies[1].wait()
    copies[3].wait()
    block_rows = down_ref.shape[0]
    features_ref[...] = features_of(
        normed_ref, owner, (1 - replica) * peers + tensor, block_rows
    )
    shrunk_ref[...] = jnp.dot(
        features_of(normed_ref, owner, replica * peers + tensor, block_rows),
        down_buf[...],
        preferred_element_type=jnp.float32,
    )


def shrink_kernel(
    features_ref, other_ref, own_ref, normed_ref, up_ref, beside_ref, out_ref, normed_out, up_out
):
    normed_out[...] = normed_ref[...]
    up_out[...] = up_ref[...]
    out_ref[...] = own_ref[...] + jnp.dot(
        features_ref[...], other_ref[...], preferred_element_type=jnp.float32
    )


def query_kernel(normed_ref, wq_ref, after_ref, out_ref):
    out_ref[...] = jnp.dot(normed_ref[...], wq_ref[...], preferred_element_type=jnp.float32)


def rotated(values, cosine, sine):
    half = HEAD_DIM // 2
    turned = jnp.concatenate([values[:, half:], values[:, :half]], axis=1)
    return values * cosine + turned * sine


def pack_kernel(acc_ref, partial_ref, beside_ref, out_ref, tall):
    rows = acc_ref.shape[0]
    heads = acc_ref.shape[1] // HEAD_DIM
    for h in range(heads):
        tall[h * rows : (h + 1) * rows, :] = acc_ref[:, h * HEAD_DIM : (h + 1) * HEAD_DIM]
    held_rows = padded(heads * rows, 16)
    if held_rows > heads * rows:
        tall[heads * rows : held_rows, :] = jnp.zeros(
            (held_rows - heads * rows, HEAD_DIM), jnp.float32
        )
    left = partial_ref[...]
    for c in range(3):
        piece = left.astype(jnp.bfloat16).astype(jnp.float32)
        left = left - piece
        tall[held_rows + c * rows : held_rows + (c + 1) * rows, :] = piece
    end = held_rows + 3 * rows
    if out_ref.shape[0] > end:
        tall[end:, :] = jnp.zeros((out_ref.shape[0] - end, HEAD_DIM), jnp.float32)
    out_ref[...] = tall[...].astype(jnp.bfloat16)


def finish_kernel(
    seq_count, acc_ref, partial_ref, met_ref, key_ref, value_ref, uq_own, uq_other, far_own,
    far_other, uv_own, uv_other, cos_ref, sin_ref, beside_ref,
    query_ref, keyout_ref, valueout_ref, wide, tall,
):
    first = lax.axis_index("replica") == 0
    rows = acc_ref.shape[0]
    steps = rows // seq_count
    heads = acc_ref.shape[1] // HEAD_DIM
    held_rows = padded(heads * rows, 16)
    met = met_ref[...].astype(jnp.float32)
    pieces = [met[held_rows + c * rows : held_rows + (c + 1) * rows] for c in range(3)]
    shrunk = partial_ref[...] + (pieces[0] + (pieces[1] + pieces[2]))
    shrunk = shrunk.astype(jnp.bfloat16).astype(jnp.float32)
    half = ADAPTER_RANK // 2

    def lifted(low, high, own, other):
        mine = jnp.where(first, low, high).astype(jnp.bfloat16)
        theirs = jnp.where(first, high, low).astype(jnp.bfloat16)
        return adapter_scale * (
            jnp.dot(mine, own[...], preferred_element_type=jnp.float32)
            + jnp.dot(theirs, other[...], preferred_element_type=jnp.float32)
        )

    low, high = shrunk[:, :half], shrunk[:, half : 2 * half]
    cosine, sine = cos_ref[...], sin_ref[...]
    for e, (own, other) in enumerate(((uq_own, uq_other), (far_own, far_other))):
        lora = lifted(low, high, own, other)
        for h in range(heads):
            columns = slice(h * HEAD_DIM, (h + 1) * HEAD_DIM)
            base = acc_ref[:, columns] if e == 0 else met[h * rows : (h + 1) * rows]
            raw = (base + lora[:, columns]).astype(jnp.bfloat16).astype(jnp.float32)
            wide[e, h, 0:rows, :] = rotated(raw, cosine, sine)
        for n in range(seq_count):
            for h in range(heads):
                tall[e, pl.ds((n * heads + h) * steps, steps), :] = wide[
                    e, h, pl.ds(n, steps, stride=seq_count), :
                ]
        query_ref[e] = tall[e, 0 : heads * rows, :].astype(jnp.bfloat16)
    keyout_ref[...] = key_ref[...].astype(jnp.bfloat16)
    value = value_ref[...] + lifted(
        shrunk[:, 2 * half : 3 * half], shrunk[:, 3 * half :], uv_own, uv_other
    )
    valueout_ref[...] = value.astype(jnp.bfloat16)


def fresh_kernel(
    seq_count, query_ref, key_ref, value_ref, cos_ref, sin_ref, fresh_ref, level_ref
):
    lane = lax.broadcasted_iota(jnp.int32, (1, HEAD_DIM), 1)
    columns = []
    steps = key_ref.shape[0] // seq_count
    per_seq = fresh_ref.shape[0] // seq_count
    queries = query_ref[0].astype(jnp.float32)
    keys = rotated(key_ref[...].astype(jnp.float32), cos_ref[...], sin_ref[...])
    keys = keys.astype(jnp.bfloat16).astype(jnp.float32)
    values = value_ref[...].astype(jnp.float32)
    step = lax.rem(lax.broadcasted_iota(jnp.int32, (per_seq, 1), 0), steps)
    for n in range(seq_count):
        rows = slice(n * per_seq, (n + 1) * per_seq)
        query = queries[rows]
        scores = []
        for t in range(steps):
            place = t * seq_count + n
            score = jnp.sum(query * keys[place : place + 1], axis=-1, keepdims=True) * inv_root
            scores.append(jnp.where(step >= t, score, negative))
        top = functools.reduce(jnp.maximum, scores)
        weights = [
            jnp.where(step >= t, jnp.exp(score - top), 0.0) for t, score in enumerate(scores)
        ]
        total = functools.reduce(jnp.add, weights)
        summed = jnp.zeros((per_seq, HEAD_DIM), jnp.float32)
        for t, weight in enumerate(weights):
            place = t * seq_count + n
            summed = summed + weight.astype(jnp.bfloat16).astype(jnp.float32) * values[
                place : place + 1
            ]
        fresh_ref[rows, :] = summed
        columns.append(jnp.where(lane == 0, top, jnp.where(lane == 1, total, 0.0)))
    columns = rows_padded(jnp.concatenate(columns, axis=0), HEAD_DIM)
    level_ref[...] = jnp.transpose(columns)[0 : level_ref.shape[0], :]


def pieces_of(top, total):
    rows = lax.broadcasted_iota(jnp.int32, (16, HEAD_DIM), 0)
    packed = jnp.zeros((16, HEAD_DIM), jnp.float32)
    for first, left in ((0, top), (3, total)):
        for c in range(3):
            piece = left.astype(jnp.bfloat16).astype(jnp.float32)
            left = left - piece
            packed = jnp.where(rows == first + c, piece, packed)
    return packed.astype(jnp.bfloat16)


def top_and_total(part_ref, held_rows):
    pieces = part_ref[padded(held_rows, 16) :, :].astype(jnp.float32)
    return (
        pieces[0:1] + (pieces[1:2] + pieces[2:3]),
        pieces[3:4] + (pieces[4:5] + pieces[5:6]),
    )


def turned_rows(rows):
    count = padded(len(rows), 8)
    place = lax.broadcasted_iota(jnp.int32, (count, HEAD_DIM), 0)
    stacked = jnp.zeros((count, HEAD_DIM), jnp.float32)
    for k, row in enumerate(rows):
        stacked = jnp.where(place == k, row, stacked)
    return jnp.transpose(rows_padded(stacked, HEAD_DIM))


def cache_kernel(
    masks, taken, reach_ref, kc_ref, vc_ref, beside_ref, after_ref, *refs
):
    *refs, out_ref, scores_buf, weights_buf = refs
    earlier, query_refs = (refs[:1], refs[1:]) if taken else ([], refs)
    entries, peers = len(masks), out_ref.shape[0]
    each, held_rows, _ = query_refs[0].shape
    seq_count, kv_heads, span, _ = kc_ref.shape
    per_seq = held_rows // seq_count
    mean_rows = padded(held_rows, 16)
    tensor = lax.axis_index("tensor")
    spots = tensor * span + lax.broadcasted_iota(jnp.int32, (span, HEAD_DIM), 0)
    live = spots < reach_ref[0:1, :]
    lane = lax.broadcasted_iota(jnp.int32, (span, HEAD_DIM), 1)
    owners = [lax.bitwise_xor(tensor, mask) for mask in masks]
    heads = [owner * kv_heads // peers for owner in owners]
    for blocks in earlier:
        for mask in taken:
            place = lax.bitwise_xor(tensor, mask)
            out_ref[place] = blocks[place]
    batch = scores_buf.shape[0]
    for lead in range(0, entries, batch):
        part = range(lead, min(lead + batch, entries))
        queries = [rows_padded(query_refs[e // each][e % each], HEAD_DIM) for e in part]
        for k, e in enumerate(part):
            scores = None
            for n in range(seq_count):
                score = lax.dot_general(
                    kc_ref[n, heads[e]],
                    queries[k],
                    (((1,), (1,)), ((), ())),
                    preferred_element_type=jnp.float32,
                )
                scores = score if n == 0 else jnp.where(lane < n * per_seq, scores, score)
            scores_buf[k] = jnp.where(live, scores, negative)
        tops = [
            jnp.maximum(jnp.max(scores_buf[k], axis=0, keepdims=True), 0.1 * negative)
            for k in range(len(part))
        ]
        for k, e in enumerate(part):
            weights = jnp.exp((scores_buf[k] - tops[k]) * inv_root)
            total = jnp.sum(weights, axis=0, keepdims=True)
            out_ref[owners[e], mean_rows:, :] = pieces_of(tops[k] * inv_root, total)
            weights_buf[k] = jnp.transpose(weights)
        for k, e in enumerate(part):
            sums = [
                jnp.dot(
                    weights_buf[k, n * per_seq : (n + 1) * per_seq, :].astype(jnp.bfloat16),
                    vc_ref[n, heads[e]],
                    preferred_element_type=jnp.float32,
                )
                for n in range(seq_count)
            ]
            sums = rows_padded(jnp.concatenate(sums, axis=0), mean_rows)
            out_ref[owners[e], 0:mean_rows, :] = sums.astype(jnp.bfloat16)


def merge_kernel(seq_count, blocks_ref, fresh_ref, level_ref, wo_ref, out_ref, wide):
    peers, folded, lanes = out_ref.shape
    heads = wide.shape[0]
    held_rows = fresh_ref.shape[0]
    rows = held_rows // heads
    steps = rows // seq_count
    folds = folded // rows
    per_seq = heads * steps
    mean_rows = padded(held_rows, 16)
    stats = [top_and_total(blocks_ref.at[b], held_rows) for b in range(peers)]
    stats.append((level_ref[0:1, :], level_ref[1:2, :]))
    top = functools.reduce(jnp.maximum, [stat[0] for stat in stats])
    factors = [jnp.exp(stat[0] - top) for stat in stats]
    total = functools.reduce(jnp.add, [factor * stat[1] for factor, stat in zip(factors, stats)])
    total = jnp.where(total > 0.0, total, 1.0)
    columns = turned_rows([factor / total for factor in factors])
    mixed = fresh_ref[...] * columns[0:held_rows, peers : peers + 1]
    for b in range(peers):
        mixed = mixed + (
            blocks_ref[b, 0:mean_rows, :].astype(jnp.float32)[0:held_rows]
            * columns[0:held_rows, b : b + 1]
        )
    for n in range(seq_count):
        for h in range(heads):
            first = n * per_seq + h * steps
            wide[h, pl.ds(n, steps, stride=seq_count), :] = mixed[first : first + steps]
    attention = jnp.concatenate([wide[h, 0:rows, :] for h in range(heads)], axis=1)
    attention = attention.astype(jnp.bfloat16)
    width = folds * lanes
    for p in range(peers):
        share = jnp.dot(
            attention,
            wo_ref[:, p * width : (p + 1) * width],
            preferred_element_type=jnp.float32,
        )
        if folds > 1:
            share = jnp.concatenate(
                [share[:, c * lanes : (c + 1) * lanes] for c in range(folds)], axis=0
            )
        out_ref[p] = share.astype(out_ref.dtype)


def sum_kernel(rest_ref, parts_ref, out_ref):
    total = functools.reduce(
        jnp.add, [parts_ref[b].astype(jnp.float32) for b in range(parts_ref.shape[0])]
    )
    rows = rest_ref.shape[0]
    steps, seqs, _ = out_ref.shape
    folds, lanes = total.shape[0] // rows, total.shape[1]
    for c in range(folds):
        columns = slice(c * lanes, (c + 1) * lanes)
        piece = total[c * rows : (c + 1) * rows] + rest_ref[:, columns]
        for s in range(steps):
            out_ref[s, :, columns] = piece[s * seqs : (s + 1) * seqs].astype(jnp.bfloat16)


def crossed(value, mask):
    pairs = [(source, source ^ mask) for source in range(lax.axis_size("tensor"))]
    return lax.ppermute(value, "tensor", pairs)


def exchanged(value):
    return lax.all_to_all(value, "tensor", split_axis=0, concat_axis=0, tiled=True)


def near_masks():
    masks = [2]
    while 4 * masks[-1] < lax.axis_size("tensor"):
        masks.append(2 * masks[-1])
    return masks


def body(
    layer_input_hidden,
    rmsnorm_gain_weight,
    wq,
    wk,
    wv,
    wo,
    adapter_down_stored,
    adapter_up_query,
    adapter_up_value,
    adapter_block_owner,
    rotated_key_cache,
    cached_value_rows,
    cache_valid_lengths,
):
    f32, bf16 = jnp.float32, jnp.bfloat16
    shape = jax.ShapeDtypeStruct
    steps, seqs, model_width = layer_input_hidden.shape
    peers = lax.axis_size("tensor")
    tensor_index = lax.axis_index("tensor")
    rows = steps * seqs
    local_heads = wq.shape[1] // HEAD_DIM
    held_rows = rows * local_heads
    kv_width = wk.shape[1]
    width = model_width // peers
    group = QUERY_HEADS // KEY_VALUE_HEADS

    pairs = [(0, 1), (1, 0)]
    other_down = lax.ppermute(adapter_down_stored, "replica", pairs)
    other_up_query = lax.ppermute(adapter_up_query, "replica", pairs)
    other_up_value = lax.ppermute(adapter_up_value, "replica", pairs)

    normed, cosine, sine, rest, reach, own_shrunk, features = kernel_call(
        functools.partial(norm_kernel, peers, local_heads),
        (
            shape((rows, model_width), bf16),
            shape((rows, HEAD_DIM), f32),
            shape((rows, HEAD_DIM), f32),
            shape((rows, width), f32),
            shape((8, HEAD_DIM), jnp.int32),
            shape((rows, 2 * ADAPTER_RANK), f32),
            shape((rows, adapter_down_stored.shape[0]), bf16),
        ),
        [far] * 6,
        (vmem,) * 7,
        [
            pltpu.SMEM(cache_valid_lengths.shape, jnp.int32),
            pltpu.SMEM(adapter_block_owner.shape, jnp.int32),
            pltpu.VMEM(layer_input_hidden.shape, bf16),
            pltpu.VMEM(adapter_down_stored.shape, bf16),
            pltpu.VMEM(rmsnorm_gain_weight.shape, bf16),
            pltpu.SemaphoreType.DMA((5,)),
        ],
        limit=8,
    )(
        cache_valid_lengths, adapter_block_owner, layer_input_hidden, adapter_down_stored,
        rmsnorm_gain_weight, wo,
    )
    own_shrunk, other_down, other_up_query, other_up_value = lax.optimization_barrier(
        (own_shrunk, other_down, other_up_query, other_up_value)
    )
    partial, normed, up_query = kernel_call(
        shrink_kernel,
        (
            shape((rows, 2 * ADAPTER_RANK), f32),
            shape((rows, model_width), bf16),
            shape(adapter_up_query.shape, bf16),
        ),
        [vmem] * 5 + [far],
        (vmem,) * 3,
        limit=4,
    )(features, other_down, own_shrunk, normed, adapter_up_query, wo)

    partial = after = partial + crossed(partial, 1)
    far_up_query = crossed(up_query, peers // 2)
    for mask in near_masks():
        partial = partial + crossed(partial, mask)

    key_sum = jnp.dot(normed, wk, preferred_element_type=f32)
    value_sum = jnp.dot(normed, wv, preferred_element_type=f32)
    query_sum = kernel_call(
        query_kernel,
        shape((rows, wq.shape[1]), f32),
        [vmem] * 3,
        vmem,
        limit=4,
        moved=wq.size,
        flops=2 * rows * wq.size,
    )(normed, wq, after)
    other_far_up_query = lax.ppermute(far_up_query, "replica", pairs)

    strided_rows = padded(max(rows, 8 * seqs), 8)
    packed_rows = padded(held_rows, 16) + padded(3 * rows, 16)
    packed = kernel_call(
        pack_kernel,
        shape((packed_rows, HEAD_DIM), bf16),
        [vmem, vmem, far],
        vmem,
        [pltpu.VMEM((packed_rows, HEAD_DIM), f32)],
        limit=4,
    )(query_sum, partial, wq)
    queries, key_raw, value_raw = kernel_call(
        functools.partial(finish_kernel, seqs),
        (
            shape((2, held_rows, HEAD_DIM), bf16),
            shape((rows, kv_width), bf16),
            shape((rows, kv_width), bf16),
        ),
        [vmem] * 13 + [far],
        (vmem,) * 3,
        [
            pltpu.VMEM((2, local_heads, strided_rows, HEAD_DIM), f32),
            pltpu.VMEM((2, padded(held_rows, 8) + 8, HEAD_DIM), f32),
        ],
        limit=4,
    )(
        query_sum, partial, crossed(packed, peers // 2), key_sum, value_sum, up_query,
        other_up_query, far_up_query, other_far_up_query, adapter_up_value, other_up_value,
        cosine, sine, wq,
    )

    if kv_width != HEAD_DIM:
        kv_index = tensor_index * local_heads // group

        def own_head(value):
            heads = lax.all_gather(value, "tensor", axis=1, tiled=True)
            return lax.dynamic_slice_in_dim(heads, kv_index * HEAD_DIM, HEAD_DIM, 1)

        key_raw, value_raw = own_head(key_raw), own_head(value_raw)

    fresh, fresh_level = kernel_call(
        functools.partial(fresh_kernel, seqs),
        (shape((held_rows, HEAD_DIM), f32), shape((8, HEAD_DIM), f32)),
        [vmem] * 5,
        (vmem, vmem),
        limit=4,
    )(queries, key_raw, value_raw, cosine, sine)
    held, masks = queries, [0, peers // 2]
    for mask in near_masks()[:0:-1]:
        held = jnp.concatenate([held, crossed(held, mask)])
        masks = masks + [mask ^ other for other in masks]
    others = {m: crossed(held, m) for m in (1, 2, 3)}

    span = rotated_key_cache.shape[2]
    blocks_shape = shape((peers, padded(held_rows, 16) + 16, HEAD_DIM), bf16)
    buffers = [pltpu.VMEM((4, span, HEAD_DIM), f32), pltpu.VMEM((4, HEAD_DIM, span), f32)]

    def cache_part(its_masks, taken, *operands):
        return kernel_call(
            functools.partial(cache_kernel, its_masks, taken),
            blocks_shape,
            [vmem] * 3 + [far] + [vmem] * (1 + len(operands)),
            vmem,
            buffers,
            limit=6,
        )(reach, rotated_key_cache, cached_value_rows, wq, fresh_level, *operands)

    blocks, taken = cache_part(masks, [], held), masks
    for met in ((2, 3), (1,)):
        its_masks = [mask ^ m for m in met for mask in masks]
        blocks = cache_part(its_masks, taken, blocks, *[others[m] for m in met])
        taken = taken + its_masks

    folds = width // 256 if (rows * (width // 256)) % 16 == 0 else 1
    shares = kernel_call(
        functools.partial(merge_kernel, seqs),
        shape((peers, rows * folds, width // folds), bf16),
        [vmem] * 4,
        vmem,
        [pltpu.VMEM((local_heads, strided_rows, HEAD_DIM), f32)],
        limit=6,
    )(exchanged(blocks), fresh, fresh_level, wo)
    return kernel_call(
        sum_kernel,
        shape((steps, seqs, width), bf16),
        [vmem] * 2,
        vmem,
        limit=4,
    )(rest, exchanged(shares))


def solution(mesh):
    return jax.shard_map(
        body,
        mesh=mesh,
        in_specs=(
            P(None, ("groups", "replica"), None),
            P(),
            P(None, "tensor"),
            P(None, "tensor"),
            P(None, "tensor"),
            P("tensor", None),
            P(("replica", "tensor"), None),
            P("replica", "tensor"),
            P("replica", "tensor"),
            P(),
            P(("groups", "replica"), None, "tensor", None),
            P(("groups", "replica"), None, "tensor", None),
            P(("groups", "replica")),
        ),
        out_specs=P(None, ("groups", "replica"), "tensor"),
        check_vma=False,
    )
```

```python
import functools
import math

import jax
import jax.numpy as jnp
from jax import lax
from jax.experimental import pallas as pl
from jax.experimental.pallas import tpu as pltpu
from jax.sharding import PartitionSpec as P

QUERY_HEADS = 64
KEY_VALUE_HEADS = 8
HEAD_DIM = 128
ADAPTER_RANK = 64


adapter_scale = 2.0
rope_base = 500000.0
negative = -1e30
inv_root = 1.0 / math.sqrt(HEAD_DIM)
MIB = 1 << 20

vmem = pl.BlockSpec(memory_space=pltpu.VMEM)
smem = pl.BlockSpec(memory_space=pltpu.SMEM)
far = pl.BlockSpec(memory_space=pl.ANY)


def padded(count, multiple):
    return -(-count // multiple) * multiple


def rows_padded(value, rows):
    if value.shape[0] == rows:
        return value
    filler = jnp.zeros((rows - value.shape[0],) + value.shape[1:], value.dtype)
    return jnp.concatenate([value, filler], axis=0)


def kernel_call(kernel, outs, specs, out_specs, scratch=(), limit=16, moved=0, flops=0):
    call = pl.pallas_call(
        kernel,
        out_shape=outs,
        in_specs=specs,
        out_specs=out_specs,
        scratch_shapes=list(scratch),
        compiler_params=pltpu.CompilerParams(vmem_limit_bytes=limit * MIB),
        cost_estimate=pl.CostEstimate(flops=flops, bytes_accessed=moved, transcendentals=0),
    )

    def run(*operands):
        return call(
            *[
                pltpu.with_memory_space_constraint(operand, pltpu.HBM) if spec is far else operand
                for operand, spec in zip(operands, specs)
            ]
        )

    return run


def fetches(pairs, sem):
    copies = [
        pltpu.make_async_copy(far_ref, near, sem.at[k]) for k, (far_ref, near) in enumerate(pairs)
    ]
    for copy in copies:
        copy.start()
    return copies


def features_of(normed_ref, owner_ref, held, block_rows):
    place = jnp.int32(0)
    for j in range(owner_ref.shape[0]):
        place = jnp.where(owner_ref[j] == held, jnp.int32(j), place)
    return normed_ref[:, pl.ds(pl.multiple_of(place * block_rows, block_rows), block_rows)]


def norm_kernel(
    peers, heads, lengths_ref, owner_ref, x_ref, down_ref, gain_ref, beside_ref,
    normed_ref, cos_ref, sin_ref, rest_ref, reach_ref, shrunk_ref, features_ref,
    lengths, owner, x_buf, down_buf, gain, sem,
):
    copies = fetches(
        [
            (lengths_ref, lengths),
            (owner_ref, owner),
            (x_ref, x_buf),
            (down_ref, down_buf),
            (gain_ref, gain),
        ],
        sem,
    )
    steps, seqs, _ = x_ref.shape
    rows, width = rest_ref.shape
    half = HEAD_DIM // 2
    row = lax.broadcasted_iota(jnp.int32, (rows, HEAD_DIM), 0)
    lane = lax.broadcasted_iota(jnp.int32, (rows, HEAD_DIM), 1)
    copies[0].wait()
    positions = jnp.zeros((rows, HEAD_DIM), jnp.int32)
    for s in range(steps):
        for n in range(seqs):
            positions = jnp.where(row == s * seqs + n, lengths[n] + s, positions)
    low = lane < half
    exponent = jnp.where(low, lane, lane - half).astype(jnp.float32) * (2.0 / HEAD_DIM)
    angles = positions.astype(jnp.float32) * jnp.exp(exponent * -math.log(rope_base))
    sine = jnp.sin(angles)
    cos_ref[...] = jnp.cos(angles)
    sin_ref[...] = jnp.where(low, -sine, sine)
    place = lax.broadcasted_iota(jnp.int32, reach_ref.shape, 1)
    reach = jnp.zeros(reach_ref.shape, jnp.int32)
    per_seq = heads * steps
    for n in range(seqs):
        mine = jnp.logical_and(place >= n * per_seq, place < (n + 1) * per_seq)
        reach = jnp.where(mine, lengths[n], reach)
    reach_ref[...] = reach
    copies[2].wait()
    values = jnp.concatenate([x_buf[s].astype(jnp.float32) for s in range(steps)], axis=0)
    factor = lax.rsqrt(jnp.mean(values * values, axis=-1, keepdims=True) + 1e-05)
    copies[4].wait()
    normed = values * factor * gain[...].astype(jnp.float32).reshape(1, -1)
    normed_ref[...] = normed.astype(jnp.bfloat16)
    replica, tensor = lax.axis_index("replica"), lax.axis_index("tensor")
    columns = pl.ds(pl.multiple_of(tensor * width, width), width)
    rest = [x_buf[s, :, columns].astype(jnp.float32) for s in range(steps)]
    rest_ref[...] = jnp.concatenate(rest, axis=0)
    copies[1].wait()
    copies[3].wait()
    block_rows = down_ref.shape[0]
    features_ref[...] = features_of(
        normed_ref, owner, (1 - replica) * peers + tensor, block_rows
    )
    shrunk_ref[...] = jnp.dot(
        features_of(normed_ref, owner, replica * peers + tensor, block_rows),
        down_buf[...],
        preferred_element_type=jnp.float32,
    )


def shrink_kernel(
    features_ref, other_ref, own_ref, normed_ref, up_ref, beside_ref, out_ref, normed_out, up_out
):
    normed_out[...] = normed_ref[...]
    up_out[...] = up_ref[...]
    out_ref[...] = own_ref[...] + jnp.dot(
        features_ref[...], other_ref[...], preferred_element_type=jnp.float32
    )


def query_kernel(normed_ref, wq_ref, after_ref, out_ref):
    out_ref[...] = jnp.dot(normed_ref[...], wq_ref[...], preferred_element_type=jnp.float32)


def rotated(values, cosine, sine):
    half = HEAD_DIM // 2
    turned = jnp.concatenate([values[:, half:], values[:, :half]], axis=1)
    return values * cosine + turned * sine


def pack_kernel(acc_ref, partial_ref, beside_ref, out_ref, tall):
    rows = acc_ref.shape[0]
    heads = acc_ref.shape[1] // HEAD_DIM
    for h in range(heads):
        tall[h * rows : (h + 1) * rows, :] = acc_ref[:, h * HEAD_DIM : (h + 1) * HEAD_DIM]
    held_rows = padded(heads * rows, 16)
    if held_rows > heads * rows:
        tall[heads * rows : held_rows, :] = jnp.zeros(
            (held_rows - heads * rows, HEAD_DIM), jnp.float32
        )
    left = partial_ref[...]
    for c in range(3):
        piece = left.astype(jnp.bfloat16).astype(jnp.float32)
        left = left - piece
        tall[held_rows + c * rows : held_rows + (c + 1) * rows, :] = piece
    end = held_rows + 3 * rows
    if out_ref.shape[0] > end:
        tall[end:, :] = jnp.zeros((out_ref.shape[0] - end, HEAD_DIM), jnp.float32)
    out_ref[...] = tall[...].astype(jnp.bfloat16)


def finish_kernel(
    seq_count, acc_ref, partial_ref, met_ref, key_ref, value_ref, uq_own, uq_other, far_own,
    far_other, uv_own, uv_other, cos_ref, sin_ref, beside_ref,
    query_ref, keyout_ref, valueout_ref, wide, tall,
):
    first = lax.axis_index("replica") == 0
    rows = acc_ref.shape[0]
    steps = rows // seq_count
    heads = acc_ref.shape[1] // HEAD_DIM
    held_rows = padded(heads * rows, 16)
    met = met_ref[...].astype(jnp.float32)
    pieces = [met[held_rows + c * rows : held_rows + (c + 1) * rows] for c in range(3)]
    shrunk = partial_ref[...] + (pieces[0] + (pieces[1] + pieces[2]))
    shrunk = shrunk.astype(jnp.bfloat16).astype(jnp.float32)
    half = ADAPTER_RANK // 2

    def lifted(low, high, own, other):
        mine, theirs = jnp.where(first, low, high), jnp.where(first, high, low)
        both = jnp.concatenate([mine, theirs], axis=1).astype(jnp.bfloat16)
        ups = jnp.concatenate([own[...], other[...]], axis=0)
        return adapter_scale * jnp.dot(both, ups, preferred_element_type=jnp.float32)

    low, high = shrunk[:, :half], shrunk[:, half : 2 * half]
    cosine, sine = cos_ref[...], sin_ref[...]
    for e, (own, other) in enumerate(((uq_own, uq_other), (far_own, far_other))):
        lora = lifted(low, high, own, other)
        for h in range(heads):
            columns = slice(h * HEAD_DIM, (h + 1) * HEAD_DIM)
            base = acc_ref[:, columns] if e == 0 else met[h * rows : (h + 1) * rows]
            raw = (base + lora[:, columns]).astype(jnp.bfloat16).astype(jnp.float32)
            wide[e, h, 0:rows, :] = rotated(raw, cosine, sine)
        for n in range(seq_count):
            for h in range(heads):
                tall[e, pl.ds((n * heads + h) * steps, steps), :] = wide[
                    e, h, pl.ds(n, steps, stride=seq_count), :
                ]
        query_ref[e] = tall[e, 0 : heads * rows, :].astype(jnp.bfloat16)
    keyout_ref[...] = key_ref[...].astype(jnp.bfloat16)
    value = value_ref[...] + lifted(
        shrunk[:, 2 * half : 3 * half], shrunk[:, 3 * half :], uv_own, uv_other
    )
    valueout_ref[...] = value.astype(jnp.bfloat16)


def fresh_kernel(
    seq_count, query_ref, key_ref, value_ref, cos_ref, sin_ref, fresh_ref, level_ref
):
    lane = lax.broadcasted_iota(jnp.int32, (1, HEAD_DIM), 1)
    columns = []
    steps = key_ref.shape[0] // seq_count
    per_seq = fresh_ref.shape[0] // seq_count
    queries = query_ref[0].astype(jnp.float32)
    keys = rotated(key_ref[...].astype(jnp.float32), cos_ref[...], sin_ref[...])
    keys = keys.astype(jnp.bfloat16).astype(jnp.float32)
    values = value_ref[...].astype(jnp.float32)
    step = lax.rem(lax.broadcasted_iota(jnp.int32, (per_seq, 1), 0), steps)
    for n in range(seq_count):
        rows = slice(n * per_seq, (n + 1) * per_seq)
        query = queries[rows]
        scores = []
        for t in range(steps):
            place = t * seq_count + n
            score = jnp.sum(query * keys[place : place + 1], axis=-1, keepdims=True) * inv_root
            scores.append(jnp.where(step >= t, score, negative))
        top = functools.reduce(jnp.maximum, scores)
        weights = [
            jnp.where(step >= t, jnp.exp(score - top), 0.0) for t, score in enumerate(scores)
        ]
        total = functools.reduce(jnp.add, weights)
        summed = jnp.zeros((per_seq, HEAD_DIM), jnp.float32)
        for t, weight in enumerate(weights):
            place = t * seq_count + n
            summed = summed + weight.astype(jnp.bfloat16).astype(jnp.float32) * values[
                place : place + 1
            ]
        fresh_ref[rows, :] = summed
        columns.append(jnp.where(lane == 0, top, jnp.where(lane == 1, total, 0.0)))
    columns = rows_padded(jnp.concatenate(columns, axis=0), HEAD_DIM)
    level_ref[...] = jnp.transpose(columns)[0 : level_ref.shape[0], :]


def pieces_of(top, total):
    rows = lax.broadcasted_iota(jnp.int32, (16, HEAD_DIM), 0)
    packed = jnp.zeros((16, HEAD_DIM), jnp.float32)
    for first, left in ((0, top), (3, total)):
        for c in range(3):
            piece = left.astype(jnp.bfloat16).astype(jnp.float32)
            left = left - piece
            packed = jnp.where(rows == first + c, piece, packed)
    return packed.astype(jnp.bfloat16)


def top_and_total(part_ref, held_rows):
    pieces = part_ref[padded(held_rows, 16) :, :].astype(jnp.float32)
    return (
        pieces[0:1] + (pieces[1:2] + pieces[2:3]),
        pieces[3:4] + (pieces[4:5] + pieces[5:6]),
    )


def turned_rows(rows):
    count = padded(len(rows), 8)
    place = lax.broadcasted_iota(jnp.int32, (count, HEAD_DIM), 0)
    stacked = jnp.zeros((count, HEAD_DIM), jnp.float32)
    for k, row in enumerate(rows):
        stacked = jnp.where(place == k, row, stacked)
    return jnp.transpose(rows_padded(stacked, HEAD_DIM))


def cache_kernel(
    masks, taken, reach_ref, kc_ref, vc_ref, beside_ref, after_ref, *refs
):
    *refs, out_ref, scores_buf, weights_buf = refs
    earlier, query_refs = (refs[:1], refs[1:]) if taken else ([], refs)
    entries, peers = len(masks), out_ref.shape[0]
    each, held_rows, _ = query_refs[0].shape
    seq_count, kv_heads, span, _ = kc_ref.shape
    per_seq = held_rows // seq_count
    mean_rows = padded(held_rows, 16)
    tensor = lax.axis_index("tensor")
    spots = tensor * span + lax.broadcasted_iota(jnp.int32, (span, HEAD_DIM), 0)
    live = spots < reach_ref[0:1, :]
    lane = lax.broadcasted_iota(jnp.int32, (span, HEAD_DIM), 1)
    owners = [lax.bitwise_xor(tensor, mask) for mask in masks]
    heads = [owner * kv_heads // peers for owner in owners]
    for blocks in earlier:
        for mask in taken:
            place = lax.bitwise_xor(tensor, mask)
            out_ref[place] = blocks[place]
    batch = scores_buf.shape[0]
    for lead in range(0, entries, batch):
        part = range(lead, min(lead + batch, entries))
        queries = [rows_padded(query_refs[e // each][e % each], HEAD_DIM) for e in part]
        for k, e in enumerate(part):
            scores = None
            for n in range(seq_count):
                score = lax.dot_general(
                    kc_ref[n, heads[e]],
                    queries[k],
                    (((1,), (1,)), ((), ())),
                    preferred_element_type=jnp.float32,
                )
                scores = score if n == 0 else jnp.where(lane < n * per_seq, scores, score)
            scores_buf[k] = jnp.where(live, scores, negative)
        tops = [
            jnp.maximum(jnp.max(scores_buf[k], axis=0, keepdims=True), 0.1 * negative)
            for k in range(len(part))
        ]
        for k, e in enumerate(part):
            weights = jnp.exp((scores_buf[k] - tops[k]) * inv_root)
            total = jnp.sum(weights, axis=0, keepdims=True)
            out_ref[owners[e], mean_rows:, :] = pieces_of(tops[k] * inv_root, total)
            weights_buf[k] = jnp.transpose(weights)
        for k, e in enumerate(part):
            sums = [
                jnp.dot(
                    weights_buf[k, n * per_seq : (n + 1) * per_seq, :].astype(jnp.bfloat16),
                    vc_ref[n, heads[e]],
                    preferred_element_type=jnp.float32,
                )
                for n in range(seq_count)
            ]
            sums = rows_padded(jnp.concatenate(sums, axis=0), mean_rows)
            out_ref[owners[e], 0:mean_rows, :] = sums.astype(jnp.bfloat16)


def merge_kernel(seq_count, blocks_ref, fresh_ref, level_ref, wo_ref, out_ref, wide):
    peers, folded, lanes = out_ref.shape
    heads = wide.shape[0]
    held_rows = fresh_ref.shape[0]
    rows = held_rows // heads
    steps = rows // seq_count
    folds = folded // rows
    per_seq = heads * steps
    mean_rows = padded(held_rows, 16)
    stats = [top_and_total(blocks_ref.at[b], held_rows) for b in range(peers)]
    stats.append((level_ref[0:1, :], level_ref[1:2, :]))
    top = functools.reduce(jnp.maximum, [stat[0] for stat in stats])
    factors = [jnp.exp(stat[0] - top) for stat in stats]
    total = functools.reduce(jnp.add, [factor * stat[1] for factor, stat in zip(factors, stats)])
    total = jnp.where(total > 0.0, total, 1.0)
    columns = turned_rows([factor / total for factor in factors])
    mixed = fresh_ref[...] * columns[0:held_rows, peers : peers + 1]
    for b in range(peers):
        mixed = mixed + (
            blocks_ref[b, 0:mean_rows, :].astype(jnp.float32)[0:held_rows]
            * columns[0:held_rows, b : b + 1]
        )
    for n in range(seq_count):
        for h in range(heads):
            first = n * per_seq + h * steps
            wide[h, pl.ds(n, steps, stride=seq_count), :] = mixed[first : first + steps]
    attention = jnp.concatenate([wide[h, 0:rows, :] for h in range(heads)], axis=1)
    attention = attention.astype(jnp.bfloat16)
    width = folds * lanes
    for p in range(peers):
        share = jnp.dot(
            attention,
            wo_ref[:, p * width : (p + 1) * width],
            preferred_element_type=jnp.float32,
        )
        if folds > 1:
            share = jnp.concatenate(
                [share[:, c * lanes : (c + 1) * lanes] for c in range(folds)], axis=0
            )
        out_ref[p] = share.astype(out_ref.dtype)


def sum_kernel(rest_ref, parts_ref, out_ref):
    total = functools.reduce(
        jnp.add, [parts_ref[b].astype(jnp.float32) for b in range(parts_ref.shape[0])]
    )
    rows = rest_ref.shape[0]
    steps, seqs, _ = out_ref.shape
    folds, lanes = total.shape[0] // rows, total.shape[1]
    for c in range(folds):
        columns = slice(c * lanes, (c + 1) * lanes)
        piece = total[c * rows : (c + 1) * rows] + rest_ref[:, columns]
        for s in range(steps):
            out_ref[s, :, columns] = piece[s * seqs : (s + 1) * seqs].astype(jnp.bfloat16)


def crossed(value, mask):
    pairs = [(source, source ^ mask) for source in range(lax.axis_size("tensor"))]
    return lax.ppermute(value, "tensor", pairs)


def exchanged(value):
    return lax.all_to_all(value, "tensor", split_axis=0, concat_axis=0, tiled=True)


def near_masks():
    masks = [2]
    while 4 * masks[-1] < lax.axis_size("tensor"):
        masks.append(2 * masks[-1])
    return masks


def body(
    layer_input_hidden,
    rmsnorm_gain_weight,
    wq,
    wk,
    wv,
    wo,
    adapter_down_stored,
    adapter_up_query,
    adapter_up_value,
    adapter_block_owner,
    rotated_key_cache,
    cached_value_rows,
    cache_valid_lengths,
):
    f32, bf16 = jnp.float32, jnp.bfloat16
    shape = jax.ShapeDtypeStruct
    steps, seqs, model_width = layer_input_hidden.shape
    peers = lax.axis_size("tensor")
    tensor_index = lax.axis_index("tensor")
    rows = steps * seqs
    local_heads = wq.shape[1] // HEAD_DIM
    held_rows = rows * local_heads
    kv_width = wk.shape[1]
    width = model_width // peers
    group = QUERY_HEADS // KEY_VALUE_HEADS

    pairs = [(0, 1), (1, 0)]
    other_down = lax.ppermute(adapter_down_stored, "replica", pairs)
    other_up_query = lax.ppermute(adapter_up_query, "replica", pairs)
    other_up_value = lax.ppermute(adapter_up_value, "replica", pairs)

    normed, cosine, sine, rest, reach, own_shrunk, features = kernel_call(
        functools.partial(norm_kernel, peers, local_heads),
        (
            shape((rows, model_width), bf16),
            shape((rows, HEAD_DIM), f32),
            shape((rows, HEAD_DIM), f32),
            shape((rows, width), f32),
            shape((8, HEAD_DIM), jnp.int32),
            shape((rows, 2 * ADAPTER_RANK), f32),
            shape((rows, adapter_down_stored.shape[0]), bf16),
        ),
        [far] * 6,
        (vmem,) * 7,
        [
            pltpu.SMEM(cache_valid_lengths.shape, jnp.int32),
            pltpu.SMEM(adapter_block_owner.shape, jnp.int32),
            pltpu.VMEM(layer_input_hidden.shape, bf16),
            pltpu.VMEM(adapter_down_stored.shape, bf16),
            pltpu.VMEM(rmsnorm_gain_weight.shape, bf16),
            pltpu.SemaphoreType.DMA((5,)),
        ],
        limit=8,
    )(
        cache_valid_lengths, adapter_block_owner, layer_input_hidden, adapter_down_stored,
        rmsnorm_gain_weight, wo,
    )
    own_shrunk, other_down, other_up_query, other_up_value = lax.optimization_barrier(
        (own_shrunk, other_down, other_up_query, other_up_value)
    )
    partial, normed, up_query = kernel_call(
        shrink_kernel,
        (
            shape((rows, 2 * ADAPTER_RANK), f32),
            shape((rows, model_width), bf16),
            shape(adapter_up_query.shape, bf16),
        ),
        [vmem] * 5 + [far],
        (vmem,) * 3,
        limit=4,
    )(features, other_down, own_shrunk, normed, adapter_up_query, wo)

    partial = after = partial + crossed(partial, 1)
    far_up_query = crossed(up_query, peers // 2)
    for mask in near_masks():
        partial = partial + crossed(partial, mask)

    key_sum = jnp.dot(normed, wk, preferred_element_type=f32)
    value_sum = jnp.dot(normed, wv, preferred_element_type=f32)
    query_sum = kernel_call(
        query_kernel,
        shape((rows, wq.shape[1]), f32),
        [vmem] * 3,
        vmem,
        limit=4,
        moved=wq.size,
        flops=2 * rows * wq.size,
    )(normed, wq, after)
    other_far_up_query = lax.ppermute(far_up_query, "replica", pairs)

    strided_rows = padded(max(rows, 8 * seqs), 8)
    packed_rows = padded(held_rows, 16) + padded(3 * rows, 16)
    packed = kernel_call(
        pack_kernel,
        shape((packed_rows, HEAD_DIM), bf16),
        [vmem, vmem, far],
        vmem,
        [pltpu.VMEM((packed_rows, HEAD_DIM), f32)],
        limit=4,
    )(query_sum, partial, wq)
    queries, key_raw, value_raw = kernel_call(
        functools.partial(finish_kernel, seqs),
        (
            shape((2, held_rows, HEAD_DIM), bf16),
            shape((rows, kv_width), bf16),
            shape((rows, kv_width), bf16),
        ),
        [vmem] * 13 + [far],
        (vmem,) * 3,
        [
            pltpu.VMEM((2, local_heads, strided_rows, HEAD_DIM), f32),
            pltpu.VMEM((2, padded(held_rows, 8) + 8, HEAD_DIM), f32),
        ],
        limit=4,
    )(
        query_sum, partial, crossed(packed, peers // 2), key_sum, value_sum, up_query,
        other_up_query, far_up_query, other_far_up_query, adapter_up_value, other_up_value,
        cosine, sine, wq,
    )

    if kv_width != HEAD_DIM:
        kv_index = tensor_index * local_heads // group

        def own_head(value):
            heads = lax.all_gather(value, "tensor", axis=1, tiled=True)
            return lax.dynamic_slice_in_dim(heads, kv_index * HEAD_DIM, HEAD_DIM, 1)

        key_raw, value_raw = own_head(key_raw), own_head(value_raw)

    fresh, fresh_level = kernel_call(
        functools.partial(fresh_kernel, seqs),
        (shape((held_rows, HEAD_DIM), f32), shape((8, HEAD_DIM), f32)),
        [vmem] * 5,
        (vmem, vmem),
        limit=4,
    )(queries, key_raw, value_raw, cosine, sine)
    held, masks = queries, [0, peers // 2]
    for mask in near_masks()[:0:-1]:
        held = jnp.concatenate([held, crossed(held, mask)])
        masks = masks + [mask ^ other for other in masks]
    others = {m: crossed(held, m) for m in (1, 2, 3)}

    span = rotated_key_cache.shape[2]
    blocks_shape = shape((peers, padded(held_rows, 16) + 16, HEAD_DIM), bf16)
    buffers = [pltpu.VMEM((4, span, HEAD_DIM), f32), pltpu.VMEM((4, HEAD_DIM, span), f32)]

    def cache_part(its_masks, taken, *operands):
        return kernel_call(
            functools.partial(cache_kernel, its_masks, taken),
            blocks_shape,
            [vmem] * 3 + [far] + [vmem] * (1 + len(operands)),
            vmem,
            buffers,
            limit=6,
        )(reach, rotated_key_cache, cached_value_rows, wq, fresh_level, *operands)

    blocks, taken = cache_part(masks, [], held), masks
    for met in ((2, 3), (1,)):
        its_masks = [mask ^ m for m in met for mask in masks]
        blocks = cache_part(its_masks, taken, blocks, *[others[m] for m in met])
        taken = taken + its_masks

    folds = width // 256 if (rows * (width // 256)) % 16 == 0 else 1
    shares = kernel_call(
        functools.partial(merge_kernel, seqs),
        shape((peers, rows * folds, width // folds), bf16),
        [vmem] * 4,
        vmem,
        [pltpu.VMEM((local_heads, strided_rows, HEAD_DIM), f32)],
        limit=6,
    )(exchanged(blocks), fresh, fresh_level, wo)
    return kernel_call(
        sum_kernel,
        shape((steps, seqs, width), bf16),
        [vmem] * 2,
        vmem,
        limit=4,
    )(rest, exchanged(shares))


def solution(mesh):
    return jax.shard_map(
        body,
        mesh=mesh,
        in_specs=(
            P(None, ("groups", "replica"), None),
            P(),
            P(None, "tensor"),
            P(None, "tensor"),
            P(None, "tensor"),
            P("tensor", None),
            P(("replica", "tensor"), None),
            P("replica", "tensor"),
            P("replica", "tensor"),
            P(),
            P(("groups", "replica"), None, "tensor", None),
            P(("groups", "replica"), None, "tensor", None),
            P(("groups", "replica")),
        ),
        out_specs=P(None, ("groups", "replica"), "tensor"),
        check_vma=False,
    )
```
